32 devices in a mesh: dp: 4 (over y, core), fsdp: 8 (over z, x).
Axes of the slice: x: 2, y: 2, z: 4, core: 2. Of those that a mesh axis runs over, the one named last changes fastest.
Arguments:
- latents: bfloat16 [32, 384, 1536], P(('dp', 'fsdp')), may hold values from -6 to 6
- context: bfloat16 [32, 128, 768], P(('dp', 'fsdp')), may hold values from -6 to 6
- timestep: bfloat16 [32, 1536], P(('dp', 'fsdp')), may hold values from -6 to 6
- lengths: int32 [32], P(('dp', 'fsdp')), may hold values from 21 to 384, as said below
- cotangent: bfloat16 [32, 384, 1536], P(('dp', 'fsdp')), may hold values from -6 to 6
- mod_matrix: float32 [1536, 9216], P(('dp', 'fsdp')), may hold values from -0.25515518 to 0.25515518
- mod_first: float32 [1536, 9216], P(('dp', 'fsdp')), may hold values from -16 to 16
- mod_second: float32 [1536, 9216], P(('dp', 'fsdp')), may hold values from 0.73728 to 2.94912
- qkv_matrix: float32 [1536, 4608], P(('dp', 'fsdp')), may hold values from -0.09021098 to 0.09021098
- qkv_first: float32 [1536, 4608], P(('dp', 'fsdp')), may hold values from -16 to 16
- qkv_second: float32 [1536, 4608], P(('dp', 'fsdp')), may hold values from 0.73728 to 2.94912
- square_set: float32 [3, 1536, 1536], P(None, ('dp', 'fsdp')), may hold values from -2.8867513 to 2.8867513
- square_first: float32 [3, 1536, 1536], P(None, ('dp', 'fsdp')), may hold values from -16 to 16
- square_second: float32 [3, 1536, 1536], P(None, ('dp', 'fsdp')), may hold values from 0.73728 to 2.94912
- ctx_matrix: float32 [768, 3072], P(('dp', 'fsdp')), may hold values from -0.12757759 to 0.12757759
- ctx_first: float32 [768, 3072], P(('dp', 'fsdp')), may hold values from -16 to 16
- ctx_second: float32 [768, 3072], P(('dp', 'fsdp')), may hold values from 0.73728 to 2.94912
- ff_in: float32 [1536, 12288], P(('dp', 'fsdp')), may hold values from -0.25515518 to 0.25515518
- in_first: float32 [1536, 12288], P(('dp', 'fsdp')), may hold values from -16 to 16
- in_second: float32 [1536, 12288], P(('dp', 'fsdp')), may hold values from 0.73728 to 2.94912
- ff_down: float32 [6144, 1536], P(('dp', 'fsdp')), may hold values from -0.12757759 to 0.12757759
- down_first: float32 [6144, 1536], P(('dp', 'fsdp')), may hold values from -16 to 16
- down_second: float32 [6144, 1536], P(('dp', 'fsdp')), may hold values from 0.73728 to 2.94912
- norm_gains: float32 [3, 1536], P(None, ('dp', 'fsdp')), may hold values from 0.25 to 3.2
- gains_first: float32 [3, 1536], P(None, ('dp', 'fsdp')), may hold values from -16 to 16
- gains_second: float32 [3, 1536], P(None, ('dp', 'fsdp')), may hold values from 0.73728 to 2.94912
Outputs:
- block_out: bfloat16 [32, 384, 1536], P(('dp', 'fsdp'))
- latents_grad: bfloat16 [32, 384, 1536], P(('dp', 'fsdp'))
- mod_matrix_new: float32 [1536, 9216], P(('dp', 'fsdp'))
- mod_first_new: float32 [1536, 9216], P(('dp', 'fsdp'))
- mod_second_new: float32 [1536, 9216], P(('dp', 'fsdp'))
- qkv_matrix_new: float32 [1536, 4608], P(('dp', 'fsdp'))
- qkv_first_new: float32 [1536, 4608], P(('dp', 'fsdp'))
- qkv_second_new: float32 [1536, 4608], P(('dp', 'fsdp'))
- square_set_new: float32 [3, 1536, 1536], P(None, ('dp', 'fsdp'))
- square_first_new: float32 [3, 1536, 1536], P(None, ('dp', 'fsdp'))
- square_second_new: float32 [3, 1536, 1536], P(None, ('dp', 'fsdp'))
- ctx_matrix_new: float32 [768, 3072], P(('dp', 'fsdp'))
- ctx_first_new: float32 [768, 3072], P(('dp', 'fsdp'))
- ctx_second_new: float32 [768, 3072], P(('dp', 'fsdp'))
- ff_in_new: float32 [1536, 12288], P(('dp', 'fsdp'))
- in_first_new: float32 [1536, 12288], P(('dp', 'fsdp'))
- in_second_new: float32 [1536, 12288], P(('dp', 'fsdp'))
- ff_down_new: float32 [6144, 1536], P(('dp', 'fsdp'))
- down_first_new: float32 [6144, 1536], P(('dp', 'fsdp'))
- down_second_new: float32 [6144, 1536], P(('dp', 'fsdp'))
- norm_gains_new: float32 [3, 1536], P(None, ('dp', 'fsdp'))
- gains_first_new: float32 [3, 1536], P(None, ('dp', 'fsdp'))
- gains_second_new: float32 [3, 1536], P(None, ('dp', 'fsdp'))
- weight_norms: float32 [9], replicated
- update_norms: float32 [9], replicated
- stream_rms: float32 [4], replicated
The draws below stay inside these ranges and needn't reach their ends.
Inputs may be any that keep to these rules, and one draw needn't show every extreme that they name: `lengths`: the last clip is full.
All inputs are finite; a program needn't handle non-finite values.
Results may differ from the reference program's by a relative error of at most 0.018.
The reference program's roundings to bfloat16 on the way count: a program that leaves them out, or rounds other values in their place, can miss the bound.
Values may be sent and summed in bfloat16 or wider, within the bound.
A program may use at most 512 MiB of HBM per device.

```python
import math
import jax
import jax.numpy as jnp
from jax import lax

D = 1536
HEADS = 24
HEAD_DIM = 64
FF = 6144
CTX_DIM = 768
CTX = 128
CLIP_LEN = 384
STEP = 10
CLIPS = 32
N_DP = 4
N_FSDP = 8


def rising(count, ceiling):
    steps = jnp.arange(count, dtype=jnp.float32) / (count - 1)
    return 1.0 + (ceiling - 1.0) * steps


def ramped(key, rows, cols, fan, ceiling):
    noise = jnp.clip(jax.random.normal(key, (rows, cols), jnp.float32), -6.0, 6.0)
    spread = math.sqrt((ceiling * ceiling + ceiling + 1.0) / 3.0)
    return noise * rising(rows, ceiling)[:, None] / (spread * math.sqrt(fan))


def draw_lengths(key, part):
    key = jax.random.fold_in(key, 17)
    order = jnp.arange(CLIPS, dtype=jnp.int32)
    outer = order // N_FSDP
    inner = order % N_FSDP
    base = CLIP_LEN * (N_FSDP - 1 + 2 * inner) * (N_DP - 1 + 2 * outer) // (9 * (N_FSDP - 1) * (N_DP - 1))
    jitter = jax.random.randint(key, (CLIPS,), 0, CLIP_LEN // 8 + 2, dtype=jnp.int32)
    drawn = jnp.maximum(base - jitter, max(CLIP_LEN // 18, 1))
    return jnp.where(order == CLIPS - 1, CLIP_LEN, drawn).astype(jnp.int32)


def draw_mod_matrix(key, part):
    key = jax.random.fold_in(key, 11)
    ceiling = 3.0
    return ramped(key, D, 6 * D, D, ceiling)


def draw_qkv_matrix(key, part):
    key = jax.random.fold_in(key, 12)
    ceiling = 3.0
    return ramped(key, D, 3 * D, 8 * D, ceiling)


def draw_square_set(key, part):
    key = jax.random.fold_in(key, 13)
    ceiling = 3.0
    first_block = ramped(jax.random.fold_in(key, 1), D, D, 4 * D // CLIP_LEN, ceiling)
    second_block = ramped(jax.random.fold_in(key, 2), D, D, 8 * D, ceiling)
    third_block = ramped(jax.random.fold_in(key, 3), D, D, D // CTX, ceiling)
    return jnp.stack([first_block, second_block, third_block])


def draw_ctx_matrix(key, part):
    key = jax.random.fold_in(key, 14)
    ceiling = 3.0
    return ramped(key, CTX_DIM, 2 * D, 8 * CTX_DIM, ceiling)


def draw_ff_in(key, part):
    key = jax.random.fold_in(key, 15)
    ceiling = 3.0
    return ramped(key, D, 2 * FF, D, ceiling)


def draw_ff_down(key, part):
    key = jax.random.fold_in(key, 16)
    ceiling = 3.0
    return ramped(key, FF, D, FF, ceiling)


def draw_norm_gains(key, part):
    key = jax.random.fold_in(key, 18)
    ceiling = 3.0
    start = 0.6
    noise = jnp.clip(jax.random.normal(key, (3, D), jnp.float32), -4.0, 4.0)
    return start * rising(D, ceiling)[None, :] * (1.0 + 0.1 * noise)


def block_scale(own_key, shape, shards, smallest, largest):
    gain, own = 1.0, jax.random.fold_in(own_key, 6)
    for dim, blocks in shards:
        heights = jnp.exp(jax.random.uniform(jax.random.fold_in(own, dim), (blocks,), jnp.float32, smallest / len(shards), largest / len(shards)))
        gain = gain * jnp.repeat(heights, shape[dim] // blocks).reshape([-1 if axis == dim else 1 for axis in range(len(shape))])
    return gain


def normal_values(stream_key, dims, deviation, bound, split=(), held_as=jnp.bfloat16):
    values = deviation * jax.random.normal(stream_key, dims, jnp.float32)
    if split:
        values = values * block_scale(stream_key, dims, split, -0.22, 0.18)
    return jnp.clip(values, -bound, bound).astype(held_as)


def setup_inputs(seed: int = 0) -> dict:
    seeds = jax.random.split(jax.random.key(seed), 27)
    latents = normal_values(seeds[0], (CLIPS, CLIP_LEN, D), 1.0, 6.0, ((0, 32),))
    context = normal_values(seeds[1], (CLIPS, CTX, CTX_DIM), 1.0, 6.0, ((0, 32),))
    timestep = normal_values(seeds[2], (CLIPS, D), 1.0, 6.0, ((0, 32),))
    lengths = draw_lengths(jax.random.fold_in(seeds[26], 71), 0)
    cotangent = normal_values(seeds[4], (CLIPS, CLIP_LEN, D), 1.0, 6.0, ((0, 32),))
    mod_matrix = draw_mod_matrix(jax.random.fold_in(seeds[26], 71), 0)
    mod_first = normal_values(seeds[6], (D, 6 * D), (0.025 * (CLIPS * CLIP_LEN) ** 0.5), 16.0, ((0, 32),), jnp.float32)
    mod_second = jnp.clip(jnp.exp(math.log(2.94912) - 1.3862944 * jax.random.uniform(seeds[7], (D, 6 * D), jnp.float32) ** block_scale(seeds[7], (D, 6 * D), ((0, 32),), -0.2, 0.2)), 0.73728, 2.94912)
    qkv_matrix = draw_qkv_matrix(jax.random.fold_in(seeds[26], 71), 0)
    qkv_first = normal_values(seeds[9], (D, 3 * D), (0.025 * (CLIPS * CLIP_LEN) ** 0.5), 16.0, ((0, 32),), jnp.float32)
    qkv_second = jnp.clip(jnp.exp(math.log(2.94912) - 1.3862944 * jax.random.uniform(seeds[10], (D, 3 * D), jnp.float32) ** block_scale(seeds[10], (D, 3 * D), ((0, 32),), -0.2, 0.2)), 0.73728, 2.94912)
    square_set = draw_square_set(jax.random.fold_in(seeds[26], 71), 0)
    square_first = normal_values(seeds[12], (3, D, D), (0.025 * (CLIPS * CLIP_LEN) ** 0.5), 16.0, ((1, 32),), jnp.float32)
    square_second = jnp.clip(jnp.exp(math.log(2.94912) - 1.3862944 * jax.random.uniform(seeds[13], (3, D, D), jnp.float32) ** block_scale(seeds[13], (3, D, D), ((1, 32),), -0.2, 0.2)), 0.73728, 2.94912)
    ctx_matrix = draw_ctx_matrix(jax.random.fold_in(seeds[26], 71), 0)
    ctx_first = normal_values(seeds[15], (CTX_DIM, 2 * D), (0.025 * (CLIPS * CLIP_LEN) ** 0.5), 16.0, ((0, 32),), jnp.float32)
    ctx_second = jnp.clip(jnp.exp(math.log(2.94912) - 1.3862944 * jax.random.uniform(seeds[16], (CTX_DIM, 2 * D), jnp.float32) ** block_scale(seeds[16], (CTX_DIM, 2 * D), ((0, 32),), -0.2, 0.2)), 0.73728, 2.94912)
    ff_in = draw_ff_in(jax.random.fold_in(seeds[26], 71), 0)
    in_first = normal_values(seeds[18], (D, 2 * FF), (0.025 * (CLIPS * CLIP_LEN) ** 0.5), 16.0, ((0, 32),), jnp.float32)
    in_second = jnp.clip(jnp.exp(math.log(2.94912) - 1.3862944 * jax.random.uniform(seeds[19], (D, 2 * FF), jnp.float32) ** block_scale(seeds[19], (D, 2 * FF), ((0, 32),), -0.2, 0.2)), 0.73728, 2.94912)
    ff_down = draw_ff_down(jax.random.fold_in(seeds[26], 71), 0)
    down_first = normal_values(seeds[21], (FF, D), (0.025 * (CLIPS * CLIP_LEN) ** 0.5), 16.0, ((0, 32),), jnp.float32)
    down_second = jnp.clip(jnp.exp(math.log(2.94912) - 1.3862944 * jax.random.uniform(seeds[22], (FF, D), jnp.float32) ** block_scale(seeds[22], (FF, D), ((0, 32),), -0.2, 0.2)), 0.73728, 2.94912)
    norm_gains = draw_norm_gains(jax.random.fold_in(seeds[26], 71), 0)
    gains_first = normal_values(seeds[24], (3, D), (0.025 * (CLIPS * CLIP_LEN) ** 0.5), 16.0, ((1, 32),), jnp.float32)
    gains_second = jnp.clip(jnp.exp(math.log(2.94912) - 1.3862944 * jax.random.uniform(seeds[25], (3, D), jnp.float32) ** block_scale(seeds[25], (3, D), ((1, 32),), -0.2, 0.2)), 0.73728, 2.94912)
    return dict(latents=latents, context=context, timestep=timestep, lengths=lengths, cotangent=cotangent, mod_matrix=mod_matrix, mod_first=mod_first, mod_second=mod_second, qkv_matrix=qkv_matrix, qkv_first=qkv_first, qkv_second=qkv_second, square_set=square_set, square_first=square_first, square_second=square_second, ctx_matrix=ctx_matrix, ctx_first=ctx_first, ctx_second=ctx_second, ff_in=ff_in, in_first=in_first, in_second=in_second, ff_down=ff_down, down_first=down_first, down_second=down_second, norm_gains=norm_gains, gains_first=gains_first, gains_second=gains_second)


@jax.custom_vjp
def low(v):
    return lax.optimization_barrier(v.astype(jnp.bfloat16)).astype(jnp.float32)

@jax.custom_vjp
def low_back(v):
    return v

def low_keep(v):
    return (low(v), None)

def low_pass(kept, grad):
    return (grad,)

def back_keep(v):
    return (v, None)

def back_low(kept, grad):
    return (low(grad),)
low.defvjp(low_keep, low_pass)
low_back.defvjp(back_keep, back_low)
NORM_EPS = 1e-05
BETA_ONE = 0.9
BETA_TWO = 0.999
ADAM_EPS = 1e-06
DECAY = 0.01
RATE = 0.5
SCALE = 0.125
HIGHEST = lax.Precision.HIGHEST

def product(first_factor, second_factor):
    return jnp.matmul(first_factor, second_factor, precision=HIGHEST)

def layer_norm(matrix):
    centred = matrix - lax.optimization_barrier(jnp.mean(matrix, axis=-1, keepdims=True))
    spread = lax.optimization_barrier(jnp.mean(centred * centred, axis=-1, keepdims=True))
    return centred * lax.rsqrt(spread + NORM_EPS)

def attend(queries, key_rows, values, usable):
    scores = jnp.einsum('qhe,khe->hqk', queries, key_rows, precision=HIGHEST) * SCALE
    scores = low_back(jnp.where(usable[None, None, :], scores, -1e+30))
    ceiling = lax.optimization_barrier(jnp.max(scores, axis=-1, keepdims=True))
    powers = jnp.exp(scores - ceiling)
    chances = low(powers / lax.optimization_barrier(jnp.sum(powers, axis=-1, keepdims=True)))
    mixture = jnp.einsum('hqk,khe->qhe', chances, values, precision=HIGHEST)
    return low_back(low(mixture.reshape(mixture.shape[0], -1)))

def one_clip(stream, context_row, timestep_row, valid_count, params):
    mod_matrix, qkv_matrix, square_set, ctx_matrix, ff_in, ff_down, norm_gains = params
    frame_count = stream.shape[0]
    shifts = low_back(product(low(jax.nn.silu(timestep_row))[None, :], mod_matrix)).reshape(6, D)
    usable = jnp.arange(frame_count) < valid_count
    entry_attn = low(layer_norm(stream) * norm_gains[0] * (1.0 + shifts[1]) + shifts[0])
    qkv = low_back(low(product(entry_attn, qkv_matrix))).reshape(frame_count, 3, HEADS, HEAD_DIM)
    branch_attn = low_back(product(attend(qkv[:, 0], qkv[:, 1], qkv[:, 2], usable), square_set[0]))
    after_attn = stream + shifts[2] * branch_attn
    entry_cross = low(layer_norm(after_attn) * norm_gains[1])
    query_cross = low_back(low(product(entry_cross, square_set[1]))).reshape(frame_count, HEADS, HEAD_DIM)
    kv_cross = low_back(low(product(context_row, ctx_matrix))).reshape(CTX, 2, HEADS, HEAD_DIM)
    everywhere = jnp.arange(CTX) >= 0
    branch_cross = low_back(product(attend(query_cross, kv_cross[:, 0], kv_cross[:, 1], everywhere), square_set[2]))
    after_cross = after_attn + branch_cross
    entry_ffn = low(layer_norm(after_cross) * norm_gains[2] * (1.0 + shifts[4]) + shifts[3])
    gate_up = low_back(product(entry_ffn, ff_in))
    hidden = low(jax.nn.silu(gate_up[:, :FF]) * gate_up[:, FF:])
    branch_ffn = low_back(product(hidden, ff_down))
    result = after_cross + shifts[5] * branch_ffn
    keep_rows = usable.astype(jnp.float32)[:, None]
    branches = (result, shifts[2] * branch_attn, branch_cross, shifts[5] * branch_ffn)
    stream_terms = jnp.stack([jnp.sum(keep_rows * branch * branch) for branch in branches])
    return (result, stream_terms)

def forward(stream, params, context_all, timestep_all, lengths):
    lowered = tuple((low(matrix) for matrix in params))
    per_scan = 4

    def scan_step(totals, pieces):
        results, stream_terms = jax.vmap(one_clip, in_axes=(0, 0, 0, 0, None))(pieces[0], pieces[1], pieces[2], pieces[3], lowered)
        return (totals + lax.optimization_barrier(jnp.sum(stream_terms, axis=0)), results)
    pieces = tuple((operand.reshape((CLIPS // per_scan, per_scan) + operand.shape[1:]) for operand in (stream, context_all, timestep_all, lengths)))
    totals, results = lax.scan(jax.checkpoint(scan_step), jnp.zeros((4,), jnp.float32), pieces)
    return (results.reshape(stream.shape), totals)

def lamb(weight, first_moment, second_moment, gradient, reduce_axes):
    first_new = BETA_ONE * first_moment + (1.0 - BETA_ONE) * gradient
    second_new = BETA_TWO * second_moment + (1.0 - BETA_TWO) * gradient * gradient
    direction = first_new / (1.0 - BETA_ONE ** STEP) / (jnp.sqrt(second_new / (1.0 - BETA_TWO ** STEP)) + ADAM_EPS) + DECAY * weight
    weight_norm = jnp.sqrt(lax.optimization_barrier(jnp.sum(weight * weight, axis=reduce_axes, keepdims=True)))
    update_norm = jnp.sqrt(lax.optimization_barrier(jnp.sum(direction * direction, axis=reduce_axes, keepdims=True)))
    weight_new = weight - RATE * (weight_norm / update_norm) * direction
    return (weight_new, first_new, second_new, weight_norm.reshape(-1), update_norm.reshape(-1))

def reference(latents, context, timestep, lengths, cotangent, mod_matrix, mod_first, mod_second, qkv_matrix, qkv_first, qkv_second, square_set, square_first, square_second, ctx_matrix, ctx_first, ctx_second, ff_in, in_first, in_second, ff_down, down_first, down_second, norm_gains, gains_first, gains_second):
    params = (mod_matrix, qkv_matrix, square_set, ctx_matrix, ff_in, ff_down, norm_gains)
    firsts = (mod_first, qkv_first, square_first, ctx_first, in_first, down_first, gains_first)
    seconds = (mod_second, qkv_second, square_second, ctx_second, in_second, down_second, gains_second)
    context_float = context.astype(jnp.float32)
    timestep_float = timestep.astype(jnp.float32)

    def run_block(stream, weights):
        return forward(stream, weights, context_float, timestep_float, lengths)
    result, pullback, totals = jax.vjp(run_block, latents.astype(jnp.float32), params, has_aux=True)
    live_rows = (jnp.arange(CLIP_LEN)[None, :] < lengths[:, None]).astype(jnp.float32)
    d_latents, gradients = pullback(cotangent.astype(jnp.float32) * live_rows[:, :, None])
    stream_rms = jnp.sqrt(totals / (jnp.sum(lengths).astype(jnp.float32) * D))
    updated = []
    weight_parts = []
    update_parts = []
    for weight, first_moment, second_moment, gradient in zip(params, firsts, seconds, gradients):
        reduce_axes = (1, 2) if weight.ndim == 3 else None
        weight_new, first_new, second_new, weight_norm, update_norm = lamb(weight, first_moment, second_moment, gradient, reduce_axes)
        updated.append((weight_new, first_new, second_new))
        weight_parts.append(weight_norm)
        update_parts.append(update_norm)
    weight_norms = jnp.concatenate(weight_parts)
    update_norms = jnp.concatenate(update_parts)
    return (result.astype(jnp.bfloat16), d_latents.astype(jnp.bfloat16), updated[0][0], updated[0][1], updated[0][2], updated[1][0], updated[1][1], updated[1][2], updated[2][0], updated[2][1], updated[2][2], updated[3][0], updated[3][1], updated[3][2], updated[4][0], updated[4][1], updated[4][2], updated[5][0], updated[5][1], updated[5][2], updated[6][0], updated[6][1], updated[6][2], weight_norms, update_norms, stream_rms)
```

```python
import functools
import itertools

import jax
import jax.numpy as jnp
from jax import lax
from jax.experimental import pallas as pl
from jax.experimental.pallas import tpu as pltpu
from jax.sharding import Mesh, PartitionSpec as P

D = 1536
HEAD_DIM = 64
FF = 6144
STEP = 10


NORM_EPS = 1e-05
BETA_ONE = 0.9
BETA_TWO = 0.999
ADAM_EPS = 1e-06
DECAY = 0.01
RATE = 0.5
SCALE = 0.125

AXES = ("y", "c", "z", "x")
HALF = D // 2
PAIR = 2 * HEAD_DIM
BF16 = jnp.bfloat16
F32 = jnp.float32
ANY = pl.BlockSpec(memory_space=pl.ANY)
WHOLE = pl.BlockSpec(memory_space=pltpu.VMEM)
SCALARS = pl.BlockSpec(memory_space=pltpu.SMEM)


def norm_rows(matrix):
    centred = matrix - jnp.mean(matrix, axis=-1, keepdims=True)
    inverse = lax.rsqrt(jnp.mean(centred * centred, axis=-1, keepdims=True) + NORM_EPS)
    return (centred * inverse, inverse)


def norm_back(gradient, normed, inverse):
    return inverse * (
        gradient
        - jnp.mean(gradient, axis=-1, keepdims=True)
        - normed * jnp.mean(gradient * normed, axis=-1, keepdims=True)
    )


def dot(first, second):
    return jnp.dot(first, second, preferred_element_type=F32)


def dot_back(first, second):
    return lax.dot_general(first, second, (((1,), (1,)), ((), ())), preferred_element_type=F32)


def dot_rows(first, second):
    return lax.dot_general(first, second, (((0,), (0,)), ((), ())), preferred_element_type=F32)


def pick(array, index, axis):
    return lax.dynamic_index_in_dim(array, index, axis, keepdims=False)


def total(terms):
    return sum(term.astype(F32) for term in terms)


def only(block, head):
    lane = lax.broadcasted_iota(jnp.int32, block.shape, 1)
    mine = lane < HEAD_DIM if head == 0 else lane >= HEAD_DIM
    return jnp.where(mine, block, jnp.zeros_like(block))


def both_heads(first, second):
    lane = lax.broadcasted_iota(jnp.int32, first.shape, 1)
    return jnp.where(lane < HEAD_DIM, first, second)


def attend_kernel(valid_ref, query_ref, key_ref, value_ref, out_ref):
    valid = valid_ref[pl.program_id(0)]
    query, key, value = query_ref[...], key_ref[...], value_ref[...]
    mixed = []
    for head in range(2):
        scores = dot_back(only(query, head), key) * SCALE
        column = lax.broadcasted_iota(jnp.int32, scores.shape, 1)
        scores = jnp.where(column < valid, scores, -1e30)
        powers = jnp.exp(scores - jnp.max(scores, axis=-1, keepdims=True))
        chances = (powers / jnp.sum(powers, axis=-1, keepdims=True)).astype(BF16)
        mixed.append(dot(chances, value))
    out_ref[...] = both_heads(*mixed).astype(BF16)


def attend_back_kernel(
    valid_ref, query_ref, key_ref, value_ref, d_ref, d_query_ref, d_key_ref, d_value_ref
):
    valid = valid_ref[pl.program_id(0)]
    query, key, value, d_mix = query_ref[...], key_ref[...], value_ref[...], d_ref[...]
    parts = []
    for head in range(2):
        scores = dot_back(only(key, head), query) * SCALE
        row = lax.broadcasted_iota(jnp.int32, scores.shape, 0)
        scores = jnp.where(row < valid, scores, -1e30)
        powers = jnp.exp(scores - jnp.max(scores, axis=0, keepdims=True))
        chances = powers / jnp.sum(powers, axis=0, keepdims=True)
        d_chances = dot_back(only(value, head), d_mix)
        mean = jnp.sum(chances * d_chances, axis=0, keepdims=True)
        d_scores = (chances * (d_chances - mean)).astype(BF16)
        d_value = dot(chances.astype(BF16), d_mix)
        d_key = dot(d_scores, query) * SCALE
        d_query = dot_rows(d_scores, key) * SCALE
        parts.append((d_query, d_key, d_value))
    for out_ref, first, second in zip((d_query_ref, d_key_ref, d_value_ref), *parts):
        out_ref[...] = both_heads(first, second).astype(BF16)


def block_of(rows, row_shift, column_shift):
    return pl.BlockSpec((rows, PAIR), lambda b, j: (b + row_shift, j + column_shift))


def attend(valid, query, key, value):
    frames, words = query[1], key[1]
    pairs = HALF // PAIR
    return pl.pallas_call(
        attend_kernel,
        out_shape=jax.ShapeDtypeStruct((2 * frames, HALF), BF16),
        grid=(2, pairs),
        in_specs=[SCALARS] + [block_of(*part[1:]) for part in (query, key, value)],
        out_specs=block_of(frames, 0, 0),
        compiler_params=pltpu.CompilerParams(vmem_limit_bytes=32 * 2**20),
        cost_estimate=pl.CostEstimate(
            flops=32 * pairs * frames * words * PAIR,
            bytes_accessed=8 * (frames + words) * HALF,
            transcendentals=4 * pairs * frames * words,
        ),
    )(valid, query[0], key[0], value[0])


def attend_back(valid, query, key, value, d_mixture):
    frames, words = query[1], key[1]
    pairs = HALF // PAIR
    return pl.pallas_call(
        attend_back_kernel,
        out_shape=[
            jax.ShapeDtypeStruct((2 * rows, HALF), BF16) for rows in (frames, words, words)
        ],
        grid=(2, pairs),
        in_specs=[SCALARS]
        + [block_of(*part[1:]) for part in (query, key, value)]
        + [block_of(frames, 0, 0)],
        out_specs=[block_of(rows, 0, 0) for rows in (frames, words, words)],
        compiler_params=pltpu.CompilerParams(vmem_limit_bytes=48 * 2**20),
        cost_estimate=pl.CostEstimate(
            flops=80 * pairs * frames * words * PAIR,
            bytes_accessed=12 * (frames + words) * HALF,
            transcendentals=4 * pairs * frames * words,
        ),
    )(valid, query[0], key[0], value[0], d_mixture)


def copy_all(copies):
    for copy in copies:
        copy.start()
    for copy in copies:
        copy.wait()


def place_pieces(spot_ref, *refs, plan, sizes):
    ny, nb = sizes
    count = len(plan["offsets"]) * len(plan["parts"])
    pieces, outs, sem = refs[:count], refs[count:-1], refs[-1]
    y, x = spot_ref[0], spot_ref[3]
    copies = []
    for part, blocks in enumerate(plan["parts"]):
        for spot, (dy, dx) in enumerate(plan["offsets"]):
            from_y = lax.rem(y - dy + ny, ny)
            from_x = lax.rem(x - dx + nb, nb)
            piece = pieces[part * len(plan["offsets"]) + spot]
            for block, (out, lane, column, width) in enumerate(blocks):
                columns = pl.ds(column, width)
                if lane is None:
                    target = outs[out].at[from_y, :, from_x, :, columns]
                else:
                    target = outs[out].at[from_y, lane, :, from_x, :, columns]
                copies.append(
                    pltpu.make_async_copy(piece.at[:, block], target, sem.at[len(copies)])
                )
    copy_all(copies)


def place_ranks(spot_ref, lines_ref, in_ref, down_ref, sem, *, offsets, sizes, rows, depth):
    ny, na, nb = sizes
    y, c, x = spot_ref[0], spot_ref[1], spot_ref[3]
    copies = []
    for block, (dy, dc, dx) in enumerate(offsets):
        target = in_ref.at[
            lax.rem(y - dy + ny, ny), lax.rem(c + dc, 2), :, lax.rem(x - dx + nb, nb)
        ]
        source = lines_ref.at[:, pl.ds(block * rows, rows)]
        copies.append(pltpu.make_async_copy(source, target, sem.at[len(copies)]))
    source = lines_ref.at[:, pl.ds(len(offsets) * rows, depth)]
    copies.append(pltpu.make_async_copy(source, down_ref, sem.at[len(copies)]))
    copy_all(copies)


def place_columns(spot_ref, pieces_ref, out_ref, sem, *, offsets, sizes, width):
    ny, nb = sizes
    y, c, x = spot_ref[0], spot_ref[1], spot_ref[3]
    copies = []
    for k, (dy, dc, dx) in enumerate(offsets):
        rank = (lax.rem(y - dy + ny, ny) * 2 + lax.rem(c + dc, 2)) * nb + lax.rem(x - dx + nb, nb)
        for half in range(2):
            start = pl.multiple_of(half * FF + rank * width, 128)
            copies.append(
                pltpu.make_async_copy(
                    pieces_ref.at[k, :, pl.ds(half * width, width)],
                    out_ref.at[:, pl.ds(start, width)],
                    sem.at[len(copies)],
                )
            )
    copy_all(copies)


def place(kernel, spot, arrays, shapes, copies):
    size = sum(a.size * a.dtype.itemsize for a in arrays)
    return pl.pallas_call(
        kernel,
        out_shape=[jax.ShapeDtypeStruct(shape, BF16) for shape in shapes],
        in_specs=[SCALARS] + [ANY] * len(arrays),
        out_specs=[WHOLE] * len(shapes),
        scratch_shapes=[pltpu.SemaphoreType.DMA((copies,))],
        compiler_params=pltpu.CompilerParams(vmem_limit_bytes=40 * 2**20),
        cost_estimate=pl.CostEstimate(flops=0, bytes_accessed=2 * size, transcendentals=0),
    )(spot, *arrays)


def prepare_kernel(
    spot_ref, qkv_ref, square_ref, ctx_ref, in_ref, own_ref, other_ref, wide_ref, block_ref,
    *, offsets, sizes
):
    ny, nb = sizes
    y, c, x = spot_ref[0], spot_ref[1], spot_ref[3]
    part = D // (2 * ny)
    for out_ref, which in ((own_ref, c), (other_ref, 1 - c)):
        for k in range(5):
            for block in range(ny):
                start = block * 2 * part + which * part
                if k < 3:
                    values = qkv_ref[:, pl.ds(pl.multiple_of(k * D + start, part), part)]
                elif k == 3:
                    values = square_ref[1, :, pl.ds(pl.multiple_of(start, part), part)]
                else:
                    values = jnp.concatenate(
                        [
                            ctx_ref[:, pl.ds(pl.multiple_of(side * D + start, part), part)]
                            for side in range(2)
                        ]
                    )
                out_ref[k, :, block * part : (block + 1) * part] = values.astype(BF16)
    for k, matrix in enumerate((0, 2)):
        for side in range(2):
            values = square_ref[matrix, :, side * HALF : (side + 1) * HALF]
            wide_ref[2 * k + side] = values.astype(BF16)
    width = FF // len(offsets)
    for k, (dy, dc, dx) in enumerate(offsets):
        rank = (lax.rem(y + dy, ny) * 2 + lax.rem(c + dc, 2)) * nb + lax.rem(x + dx, nb)
        for side in range(2):
            start = pl.multiple_of(side * FF + rank * width, width)
            block_ref[k, :, side * width : (side + 1) * width] = in_ref[
                :, pl.ds(start, width)
            ].astype(BF16)


class Grid:
    def __init__(self, mesh):
        self.ny = mesh.shape["dp"] // 2
        self.nb = 2
        self.na = mesh.shape["fsdp"] // 2
        self.sizes = dict(y=self.ny, c=2, z=self.na, x=self.nb)
        self.count = self.ny * 2 * self.na * self.nb
        self.spots = list(itertools.product(*(range(self.sizes[axis]) for axis in AXES)))
        self.peers = list(itertools.product(range(self.ny), range(2), range(self.nb)))
        self.mesh = Mesh(mesh.devices.reshape(self.ny, 2, self.na, self.nb), AXES)

    def line(self, y, c, z, x):
        return ((y * 2 + c) * self.na + z) * self.nb + x

    def here(self):
        return {axis: lax.axis_index(axis) for axis in AXES}

    def move(self, array, **steps):
        steps = {axis: step % self.sizes[axis] for axis, step in steps.items()}
        steps = {axis: step for axis, step in steps.items() if step}
        if not steps:
            return array
        names = tuple(axis for axis in AXES if axis in steps)
        lengths = [self.sizes[axis] for axis in names]
        pairs = []
        for spot in itertools.product(*(range(n) for n in lengths)):
            source = target = 0
            for axis, at, n in zip(names, spot, lengths):
                source, target = source * n + at, target * n + (at + steps[axis]) % n
            pairs.append((source, target))
        return lax.ppermute(array, names, pairs)

    def rank(self, mine, offset):
        y, c, x = ((mine[axis] + step) % self.sizes[axis] for axis, step in zip("ycx", offset))
        return (y * 2 + c) * self.nb + x

    def swap(self, array):
        return self.move(array, c=1)

    def gather_small(self, array):
        shape = array.shape
        for axis in "xzcy":
            parts = [self.move(array, **{axis: k}) for k in range(self.sizes[axis])]
            array = jnp.concatenate([part.reshape((-1,) + shape) for part in parts])
        return array

    def scatter_small(self, array):
        sources = [array]
        for axis in "cyxz":
            where = 0
            arrays = []
            size = self.sizes[axis]
            sources = [s.reshape(self.small_shape(axis, s)) for s in sources]
            for k in range(1, size):
                part = total([s[:, k] for s in sources])
                arrays.append(self.move(part, **{axis: -k}))
            sources = [s[:, 0] for s in sources] + arrays
        return total(sources).reshape(array.shape[1:])

    def small_shape(self, axis, array):
        before = {"c": self.ny, "y": 1, "x": self.na, "z": 1}[axis]
        return (before, self.sizes[axis], -1, array.shape[-1])

    def sum_small(self, array):
        bit = 1
        while bit < self.count:
            array = array + lax.ppermute(array, AXES, [(d, d ^ bit) for d in range(self.count)])
            bit *= 2
        return array

    def spread(self, lines, turn):
        held = {(0, 0): lines}
        for axis in ("x", "y") if turn else ("y", "x"):
            for (y, x), piece in list(held.items()):
                for k in range(1, self.sizes[axis]):
                    step = dict(y=y, x=x)
                    step[axis] = k
                    held[(step["y"], step["x"])] = self.move(piece, **{axis: k})
        return held

    def gather_weights(self, parts, shapes, mine, spot):
        rows = parts[0][0][0].shape[0]
        mixed = jnp.stack([shard for part in parts for shard, *_ in part])
        lines = lax.all_gather(mixed, "z")
        start = 0
        held, plan = [], dict(parts=[])
        for turn, part in enumerate(parts):
            end = start + len(part)
            held.append(self.spread(lines[:, start:end], turn))
            start = end
            plan["parts"].append(
                [(out, lane, column, shard.shape[1]) for shard, out, lane, column in part]
            )
        plan["offsets"] = sorted(held[0])
        if rows % 16 == 0:
            arrays = [pieces[offset] for pieces in held for offset in plan["offsets"]]
            copies = len(plan["offsets"]) * sum(len(part) for part in parts)
            kernel = functools.partial(place_pieces, plan=plan, sizes=(self.ny, self.nb))
            return place(kernel, spot, arrays, shapes, copies)
        outs = [jnp.zeros(shape, BF16) for shape in shapes]
        for pieces, blocks in zip(held, plan["parts"]):
            for (dy, dx), piece in pieces.items():
                y = (mine["y"] - dy + self.ny) % self.ny
                x = (mine["x"] - dx + self.nb) % self.nb
                for block, (out, lane, column, width) in enumerate(blocks):
                    update = piece[:, block][None, :, None]
                    if lane is None:
                        at = (y, 0, x, 0, column)
                    else:
                        update = update[:, None]
                        at = (y, lane, 0, x, 0, column)
                    outs[out] = lax.dynamic_update_slice(outs[out], update, at)
        return outs

    def swap_ranks(self, blocks):
        shape = blocks.shape[1:]
        blocks = blocks.reshape((self.ny, 2, self.nb) + shape)
        for where, axis in ((1, "c"), (0, "y"), (2, "x")):
            parts = [
                self.move(lax.index_in_dim(blocks, k, where), **{axis: k})
                for k in range(self.sizes[axis])
            ]
            blocks = jnp.concatenate(parts, axis=where)
        return blocks.reshape((-1,) + shape)

    def gather_ranks(self, in_parts, down_part, mine, spot):
        peers, rows, width = in_parts.shape
        depth = down_part.shape[0]
        in_shape = (self.ny, 2, self.na, self.nb, rows, width)
        down_shape = (self.na, depth, D)
        if rows % 16 == 0 and width == D:
            mixed = jnp.concatenate([in_parts.reshape(-1, D), down_part])
            lines = lax.all_gather(mixed, "z")
            kernel = functools.partial(
                place_ranks,
                offsets=self.peers,
                sizes=(self.ny, self.na, self.nb),
                rows=rows,
                depth=depth,
            )
            rank_in, rank_down = place(kernel, spot, [lines], [in_shape, down_shape], peers + 1)
        else:
            rank_down = lax.all_gather(down_part, "z")
            lines = lax.all_gather(in_parts, "z")
            rank_in = jnp.zeros(in_shape, BF16)
            for k, (dy, dc, dx) in enumerate(self.peers):
                at = ((mine["y"] - dy) % self.ny, (mine["c"] + dc) % 2, 0, (mine["x"] - dx) % self.nb, 0, 0)
                rank_in = lax.dynamic_update_slice(rank_in, lines[:, k][None, None, :, None], at)
        return rank_in.reshape(-1, width), rank_down.reshape(-1, D)

    def join_columns(self, pieces, mine, spot):
        peers, rows, width = pieces.shape
        width = width // 2
        if rows % 16 == 0:
            kernel = functools.partial(
                place_columns, offsets=self.peers, sizes=(self.ny, self.nb), width=width
            )
            return place(kernel, spot, [pieces], [(rows, 2 * FF)], 2 * peers)[0]
        out = jnp.zeros((rows, 2, FF), BF16)
        for k, (dy, dc, dx) in enumerate(self.peers):
            y, x = (mine["y"] - dy) % self.ny, (mine["x"] - dx) % self.nb
            rank = (y * 2 + (mine["c"] + dc) % 2) * self.nb + x
            piece = pieces[k].reshape(rows, 2, width)
            out = lax.dynamic_update_slice(out, piece, (0, 0, rank * width))
        return out.reshape(rows, 2 * FF)

    def fold(self, array, turn, mine):
        names = "ycz"[: array.ndim - 3] if array.ndim == 6 else "yz"
        names = list(names + "x")
        sources = [array]
        for axis in "yx" if turn else "xy":
            where = names.index(axis)
            size = self.sizes[axis]
            arrived = []
            for k in range(1, size):
                away = total([pick(s, (mine[axis] + k) % size, where) for s in sources])
                arrived.append(self.move(away.astype(BF16), **{axis: k}))
            sources = [pick(s, mine[axis], where) for s in sources] + arrived
            names.remove(axis)
        out = total(sources).astype(BF16)
        return out if names[0] == "z" else jnp.swapaxes(out, 0, 1)

    def gather_rows(self, array):
        held = {}
        for y in range(self.ny):
            for x in range(self.nb):
                held[(y, 0, x)] = self.move(array, y=y, x=x)
                held[(y, 1, x)] = self.swap(held[(y, 0, x)])
        return held

    def scatter_rows(self, held):
        sources = []
        for (y, x), (own, other) in held.items():
            terms = [own, self.swap(other.astype(BF16))]
            if y or x:
                sources.append(self.move(total(terms).astype(BF16), y=-y, x=-x))
            else:
                sources += terms
        return total(sources)

    def to_rank(self, array, back=False):
        pairs = []
        for d in range(self.count):
            rank, z = divmod(d, self.na)
            y, c, x = self.peers[rank]
            pairs.append((d, self.line(y, c, z, x)))
        if back:
            pairs = [(b, a) for a, b in pairs]
        return lax.ppermute(array, AXES, pairs)


def lamb_terms(weight, first_moment, second_moment, gradient):
    first_new = BETA_ONE * first_moment + (1.0 - BETA_ONE) * gradient
    second_new = BETA_TWO * second_moment + (1.0 - BETA_TWO) * gradient * gradient
    direction = (
        first_new
        / (1.0 - BETA_ONE**STEP)
        / (jnp.sqrt(second_new / (1.0 - BETA_TWO**STEP)) + ADAM_EPS)
        + DECAY * weight
    )
    reduce_axes = (1, 2) if weight.ndim == 3 else None
    weight_part = jnp.sum(weight * weight, axis=reduce_axes).reshape(-1)
    update_part = jnp.sum(direction * direction, axis=reduce_axes).reshape(-1)
    return (direction, first_new, second_new, weight_part, update_part)


def shards(
    grid,
    latents,
    context,
    timestep,
    lengths,
    cotangent,
    mod_matrix,
    mod_first,
    mod_second,
    qkv_matrix,
    qkv_first,
    qkv_second,
    square_set,
    square_first,
    square_second,
    ctx_matrix,
    ctx_first,
    ctx_second,
    ff_in,
    in_first,
    in_second,
    ff_down,
    down_first,
    down_second,
    norm_gains,
    gains_first,
    gains_second,
):
    mine = grid.here()
    core = mine["c"]
    spot = jnp.stack([mine[axis] for axis in AXES]).astype(jnp.int32)
    device = grid.line(*(mine[axis] for axis in AXES))
    count, ranks = grid.count, len(grid.peers)
    rows = mod_matrix.shape[0]
    frames = latents.shape[1]
    words = context.shape[1]
    valid = lengths[0]
    keep_rows = (jnp.arange(frames) < valid).astype(F32)[:, None]

    lifted = jax.nn.silu(timestep[0].astype(F32)).astype(BF16)
    notes = jnp.concatenate([lifted, norm_gains.astype(BF16).reshape(-1)])
    notes = grid.gather_small(notes)
    origin = []
    for spot_of in grid.spots:
        source = [
            (mine[axis] - step) % grid.sizes[axis] for axis, step in zip(AXES, spot_of)
        ]
        origin.append(grid.line(*source))
    origin = jnp.stack(origin)
    sorter = (jnp.arange(count)[:, None] == origin[None, :]).astype(BF16)
    gain_rows = dot(sorter, notes[:, D:])
    gain_rows = gain_rows.reshape(count, 3, rows).transpose(1, 0, 2).reshape(3, D)
    lifted_own = lax.dynamic_slice(notes, (0, device * rows), (count, rows))
    shifts = grid.scatter_small(dot(lifted_own, mod_matrix.astype(BF16))).reshape(6, D)

    width = FF // ranks
    if rows % 16 == 0 and D // (2 * grid.ny) % 128 == 0:
        prepare = functools.partial(prepare_kernel, offsets=grid.peers, sizes=(grid.ny, grid.nb))
        five = (5, rows, HALF)
        five_own, five_other, wide_low, in_blocks = pl.pallas_call(
            prepare,
            out_shape=[
                jax.ShapeDtypeStruct(shape, BF16)
                for shape in (five, five, (4, rows, HALF), (ranks, rows, 2 * width))
            ],
            in_specs=[SCALARS] + [WHOLE] * 4,
            out_specs=[WHOLE] * 4,
            compiler_params=pltpu.CompilerParams(vmem_limit_bytes=40 * 2**20),
        )(spot, qkv_matrix, square_set, ctx_matrix, ff_in)
    else:
        five = [qkv_matrix[:, k * D : (k + 1) * D] for k in range(3)] + [
            square_set[1],
            jnp.concatenate([ctx_matrix[:, :D], ctx_matrix[:, D:]]),
        ]
        five = jnp.stack(five).astype(BF16).reshape(5, rows, grid.ny, 2, -1)
        five_own = pick(five, core, 3).reshape(5, rows, HALF)
        five_other = pick(five, 1 - core, 3).reshape(5, rows, HALF)
        wide_low = jnp.stack(
            [square_set[k, :, side * HALF : (side + 1) * HALF] for k in (0, 2) for side in range(2)]
        ).astype(BF16)
        in_halves = ff_in.reshape(rows, 2, FF)
        in_blocks = jnp.stack(
            [
                lax.dynamic_slice(in_halves, (0, 0, grid.rank(mine, offset) * width), (rows, 2, width))
                for offset in grid.peers
            ]
        ).astype(BF16).reshape(ranks, rows, 2 * width)
    five_other = grid.swap(five_other)
    five_low = jnp.where(core == 0, five_own, five_other)
    five_high = jnp.where(core == 0, five_other, five_own)
    tall = (grid.ny, 2, grid.na, grid.nb, rows)
    wide = (grid.ny, grid.na, grid.nb, rows, D)
    both = lambda k, out, at: [(five_low[k], out, 0, at), (five_high[k], out, 1, at)]
    sides = lambda k, out: [
        (wide_low[2 * k], out, None, 0),
        (wide_low[2 * k + 1], out, None, HALF),
    ]
    first = both(0, 0, 0) + both(1, 0, HALF) + both(2, 0, 2 * HALF)
    (matrix_qkv,) = grid.gather_weights(
        [first[:3], first[3:]], [tall + (3 * HALF,)], mine, spot
    )
    matrix_qkv = matrix_qkv.reshape(D, 3 * HALF)
    second = [sides(0, 0) + both(3, 1, 0), both(4, 2, 0) + sides(1, 3)]
    matrix_out, matrix_query, matrix_ctx, matrix_cross = grid.gather_weights(
        second, [wide, tall + (HALF,), tall + (HALF,), wide], mine, spot
    )
    matrix_out, matrix_cross = matrix_out.reshape(HALF, D), matrix_cross.reshape(HALF, D)
    matrix_query, matrix_ctx = matrix_query.reshape(D, HALF), matrix_ctx.reshape(D, HALF)

    in_parts = grid.swap_ranks(in_blocks)
    down_part = grid.to_rank(ff_down.astype(BF16))
    rank_in, rank_down = grid.gather_ranks(in_parts, down_part, mine, spot)

    pair_lengths = jnp.concatenate([lengths, grid.swap(lengths)])
    all_words = jnp.full((2,), words, jnp.int32)
    text = jnp.concatenate([context[0], grid.swap(context[0])])
    stream = latents[0].astype(F32)
    normed_one, inverse_one = norm_rows(stream)
    entry_attn = (normed_one * gain_rows[0] * (1.0 + shifts[1]) + shifts[0]).astype(BF16)
    d_result = cotangent[0].astype(F32) * keep_rows
    d_branch_ffn = (d_result * shifts[5]).astype(BF16)

    pair = lambda array: jnp.concatenate([array, grid.swap(array)])
    unpair = lambda sums: sums[:frames] + grid.swap(sums[frames:].astype(BF16)).astype(F32)
    columns = HALF // PAIR
    entry_pair = pair(entry_attn)
    qkv = dot(entry_pair, matrix_qkv).astype(BF16)
    self_parts = tuple((qkv, frames, 0, k * columns) for k in range(3))
    mixture_attn = attend(pair_lengths, *self_parts)
    branch_attn = unpair(dot(mixture_attn, matrix_out))
    after_attn = stream + shifts[2] * branch_attn
    normed_two, inverse_two = norm_rows(after_attn)
    entry_cross = pair((normed_two * gain_rows[1]).astype(BF16))
    query_cross = dot(entry_cross, matrix_query).astype(BF16)
    blank = jnp.zeros((2 * words, count, rows // 2), BF16)
    text_cut = text.reshape(2 * words, count, rows // 2)
    text_key = jnp.concatenate([text_cut, blank], axis=-1).reshape(2 * words, -1)
    text_value = jnp.concatenate([blank, text_cut], axis=-1).reshape(2 * words, -1)
    text_both = jnp.concatenate([text_key, text_value])
    kv_cross = dot(text_both, matrix_ctx).astype(BF16)
    cross_parts = ((query_cross, frames, 0, 0), (kv_cross, words, 0, 0), (kv_cross, words, 2, 0))
    mixture_cross = attend(all_words, *cross_parts)
    branch_cross = unpair(dot(mixture_cross, matrix_cross))
    after_cross = after_attn + branch_cross
    normed_three, inverse_three = norm_rows(after_cross)
    entry_ffn = (normed_three * gain_rows[2] * (1.0 + shifts[4]) + shifts[3]).astype(BF16)

    d_branch_held = grid.gather_rows(d_branch_ffn)
    entry_held = grid.gather_rows(entry_ffn)
    branch_held, d_entry_held = {}, {}
    entry_parts, d_branch_parts, hidden_parts, d_gate_up_parts = [], [], [], []
    for y in range(grid.ny):
        for x in range(grid.nb):
            entry_part = jnp.concatenate([entry_held[(y, c, x)] for c in range(2)])
            d_branch_part = jnp.concatenate([d_branch_held[(y, c, x)] for c in range(2)])
            gate_up = dot(entry_part, rank_in)
            gate_part, up_part = gate_up[:, :width], gate_up[:, width:]
            logistic = jax.nn.sigmoid(gate_part)
            hidden = (gate_part * logistic * up_part).astype(BF16)
            d_hidden = dot_back(d_branch_part, rank_down)
            d_gate_up = jnp.concatenate(
                [
                    d_hidden * up_part * logistic * (1.0 + gate_part * (1.0 - logistic)),
                    d_hidden * gate_part * logistic,
                ],
                axis=1,
            ).astype(BF16)
            d_entry_part = dot_back(d_gate_up, rank_in)
            branch_part = dot(hidden, rank_down)
            branch_held[(y, x)] = (branch_part[:frames], branch_part[frames:])
            d_entry_held[(y, x)] = (d_entry_part[:frames], d_entry_part[frames:])
            entry_parts.append(entry_part)
            d_branch_parts.append(d_branch_part)
            hidden_parts.append(hidden)
            d_gate_up_parts.append(d_gate_up)
    d_entry_ffn = grid.scatter_rows(d_entry_held)
    branch_ffn = grid.scatter_rows(branch_held)
    grad_down = dot_rows(jnp.concatenate(hidden_parts), jnp.concatenate(d_branch_parts))
    grad_down = lax.psum_scatter(grad_down.astype(BF16), "z", tiled=True)
    grad_down = grid.to_rank(grad_down, back=True).astype(F32)
    grad_in = dot_rows(jnp.concatenate(entry_parts), jnp.concatenate(d_gate_up_parts)).astype(BF16)
    grad_in = grad_in.reshape(grid.ny, 2, grid.na, grid.nb, rows, 2 * width)
    grad_in = grad_in.transpose(2, 0, 1, 3, 4, 5).reshape(-1, 2 * width)
    grad_in = lax.psum_scatter(grad_in, "z", tiled=True)
    grad_in = grad_in.reshape(ranks, rows, 2 * width)
    by_offset = jnp.stack(
        [
            pick(grad_in, grid.rank(mine, offset), 0)
            for offset in grid.peers
        ]
    )
    grad_in = grid.join_columns(grid.swap_ranks(by_offset), mine, spot).astype(F32)

    result = after_cross + shifts[5] * branch_ffn
    branches = (result, shifts[2] * branch_attn, branch_cross, shifts[5] * branch_ffn)
    stream_terms = jnp.stack([jnp.sum(keep_rows * branch * branch) for branch in branches])

    d_gate_ffn = jnp.sum(d_result * branch_ffn, axis=0)
    d_gain_ffn = jnp.sum(d_entry_ffn * normed_three * (1.0 + shifts[4]), axis=0)
    d_scale_ffn = jnp.sum(d_entry_ffn * normed_three * gain_rows[2], axis=0)
    d_shift_ffn = jnp.sum(d_entry_ffn, axis=0)
    d_after_cross = d_result + norm_back(
        d_entry_ffn * gain_rows[2] * (1.0 + shifts[4]), normed_three, inverse_three
    )

    def join(own, other):
        lead = own.shape[:-1]
        shape = lead + (grid.ny, 1, D // (2 * grid.ny))
        own, other = own.reshape(shape), other.reshape(shape)
        low = jnp.where(core == 0, own, other)
        high = jnp.where(core == 0, other, own)
        return jnp.concatenate([low, high], axis=-2).reshape(lead + (D,))

    d_branch_cross = pair(d_after_cross.astype(BF16))
    d_mixture_cross = dot_back(d_branch_cross, matrix_cross).astype(BF16)
    grad_cross = grid.fold(
        dot_rows(mixture_cross, d_branch_cross).astype(BF16).reshape(wide), 0, mine
    )
    d_query_cross, d_key_cross, d_value_cross = attend_back(
        all_words, *cross_parts, d_mixture_cross
    )
    d_entry_cross = unpair(dot_back(d_query_cross, matrix_query))
    d_kv_cross = jnp.concatenate([d_key_cross, d_value_cross])
    grad_ctx = dot_rows(text_both, d_kv_cross).astype(BF16)
    grad_ctx = grid.fold(grad_ctx.reshape(tall + (HALF,)), 0, mine)
    grad_query = dot_rows(entry_cross, d_query_cross).astype(BF16)
    grad_query = grid.fold(grad_query.reshape(tall + (HALF,)), 1, mine)
    d_gain_cross = jnp.sum(d_entry_cross * normed_two, axis=0)
    d_after_attn = d_after_cross + norm_back(d_entry_cross * gain_rows[1], normed_two, inverse_two)
    d_branch_attn = pair((d_after_attn * shifts[2]).astype(BF16))
    d_gate_attn = jnp.sum(d_after_attn * branch_attn, axis=0)
    d_mixture_attn = dot_back(d_branch_attn, matrix_out).astype(BF16)
    grad_out = grid.fold(
        dot_rows(mixture_attn, d_branch_attn).astype(BF16).reshape(wide), 1, mine
    )
    sums = jnp.concatenate(
        [
            grad_query.reshape(grid.na, 2 * rows, HALF),
            grad_ctx.reshape(grid.na, 2 * rows, HALF),
            grad_out[..., :HALF],
            grad_out[..., HALF:],
            grad_cross[..., :HALF],
            grad_cross[..., HALF:],
        ],
        axis=1,
    )
    sums = lax.psum_scatter(sums, "z").reshape(4, 2, rows, HALF)
    narrow = sums[:2]
    narrow_own = pick(narrow, core, 1)
    narrow_other = grid.swap(pick(narrow, 1 - core, 1))
    grad_query, grad_ctx = (join(narrow_own[k], narrow_other[k]).astype(F32) for k in range(2))
    grad_ctx = jnp.concatenate([grad_ctx[: rows // 2], grad_ctx[rows // 2 :]], axis=1)
    grad_out = jnp.concatenate([sums[2, 0], sums[2, 1]], axis=1).astype(F32)
    grad_cross = jnp.concatenate([sums[3, 0], sums[3, 1]], axis=1).astype(F32)

    d_qkv = jnp.concatenate(
        attend_back(pair_lengths, *self_parts, d_mixture_attn), axis=1
    )
    cut = 3 * HALF // 2
    folded = [
        grid.fold(
            dot_rows(entry_pair, part).astype(BF16).reshape(tall + (cut,)), turn, mine
        )
        for turn, part in enumerate((d_qkv[:, :cut], d_qkv[:, cut:]))
    ]
    folded = jnp.concatenate(folded, axis=-1).reshape(grid.na, 2 * rows, 3 * HALF)
    folded = lax.psum_scatter(folded, "z").reshape(2, rows, 3 * HALF)
    qkv_own = pick(folded, core, 0)
    qkv_other = grid.swap(pick(folded, 1 - core, 0))
    grad_qkv = jnp.concatenate(
        [
            join(qkv_own[:, k * HALF : (k + 1) * HALF], qkv_other[:, k * HALF : (k + 1) * HALF])
            for k in range(3)
        ],
        axis=1,
    ).astype(F32)
    d_entry_attn = unpair(dot_back(d_qkv, matrix_qkv))
    d_gain_attn = jnp.sum(d_entry_attn * normed_one * (1.0 + shifts[1]), axis=0)
    d_scale_attn = jnp.sum(d_entry_attn * normed_one * gain_rows[0], axis=0)
    d_shift_attn = jnp.sum(d_entry_attn, axis=0)
    d_latents = d_after_attn + norm_back(
        d_entry_attn * gain_rows[0] * (1.0 + shifts[1]), normed_one, inverse_one
    )
    small = jnp.concatenate(
        [
            d_shift_attn,
            d_scale_attn,
            d_gate_attn,
            d_shift_ffn,
            d_scale_ffn,
            d_gate_ffn,
            d_gain_attn,
            d_gain_cross,
            d_gain_ffn,
        ]
    ).astype(BF16)
    small = grid.gather_small(small)
    grad_mod = dot_rows(lifted_own, small[:, : 6 * D])
    gain_sums = jnp.sum(small[:, 6 * D :].astype(F32), axis=0).reshape(3, D)
    grad_gains = lax.dynamic_slice(gain_sums, (0, device * rows), (3, rows))

    summed = (
        grad_mod,
        grad_qkv,
        jnp.stack([grad_out, grad_query, grad_cross]),
        grad_ctx,
        grad_in,
        grad_down,
        grad_gains,
    )
    masters = (mod_matrix, qkv_matrix, square_set, ctx_matrix, ff_in, ff_down, norm_gains)
    firsts = (mod_first, qkv_first, square_first, ctx_first, in_first, down_first, gains_first)
    seconds = (
        mod_second,
        qkv_second,
        square_second,
        ctx_second,
        in_second,
        down_second,
        gains_second,
    )
    pending = []
    weight_parts = []
    update_parts = []
    for weight, first_moment, second_moment, gradient in zip(masters, firsts, seconds, summed):
        direction, first_new, second_new, weight_part, update_part = lamb_terms(
            weight, first_moment, second_moment, gradient
        )
        weight_parts.append(weight_part)
        update_parts.append(update_part)
        pending.append((weight, direction, first_new, second_new))
    totals = jnp.concatenate(
        weight_parts + update_parts + [stream_terms, jnp.sum(lengths).astype(F32).reshape(1)]
    )
    totals = grid.sum_small(totals)
    weight_norms = jnp.sqrt(totals[:9])
    update_norms = jnp.sqrt(totals[9:18])
    stream_rms = jnp.sqrt(totals[18:22] / (totals[22] * D))
    ratios = weight_norms / update_norms
    outputs = [result.astype(BF16)[None], d_latents.astype(BF16)[None]]
    cursor = 0
    for weight, direction, first_new, second_new in pending:
        if weight.ndim == 3:
            factor = ratios[cursor : cursor + weight.shape[0]].reshape(-1, 1, 1)
            cursor = cursor + weight.shape[0]
        else:
            factor = ratios[cursor]
            cursor = cursor + 1
        outputs.append(weight - RATE * factor * direction)
        outputs.append(first_new)
        outputs.append(second_new)
    outputs.append(weight_norms)
    outputs.append(update_norms)
    outputs.append(stream_rms)
    return tuple(outputs)


def solution(mesh):
    grid = Grid(mesh)
    clip = P(AXES, None, None)
    row = P(AXES, None)
    square = P(None, AXES, None)
    gains = P(None, AXES)
    weights = (row,) * 6 + (square,) * 3 + (row,) * 9 + (gains,) * 3
    in_specs = (clip, clip, row, P(AXES), clip) + weights
    out_specs = (clip, clip) + weights + (P(), P(), P())
    return jax.shard_map(
        functools.partial(shards, grid),
        mesh=grid.mesh,
        in_specs=in_specs,
        out_specs=out_specs,
        check_vma=False,
    )
```

```python
import functools
import itertools

import jax
import jax.numpy as jnp
from jax import lax
from jax.experimental import pallas as pl
from jax.experimental.pallas import tpu as pltpu
from jax.sharding import Mesh, PartitionSpec as P

D = 1536
HEAD_DIM = 64
FF = 6144
STEP = 10


NORM_EPS = 1e-05
BETA_ONE = 0.9
BETA_TWO = 0.999
ADAM_EPS = 1e-06
DECAY = 0.01
RATE = 0.5
SCALE = 0.125

AXES = ("y", "c", "z", "x")
HALF = D // 2
PAIR = 2 * HEAD_DIM
BF16 = jnp.bfloat16
F32 = jnp.float32
ANY = pl.BlockSpec(memory_space=pl.ANY)
WHOLE = pl.BlockSpec(memory_space=pltpu.VMEM)
SCALARS = pl.BlockSpec(memory_space=pltpu.SMEM)
LIGHT = pl.CostEstimate(flops=2**20, bytes_accessed=2**20, transcendentals=0)


def norm_rows(matrix):
    centred = matrix - jnp.mean(matrix, axis=-1, keepdims=True)
    inverse = lax.rsqrt(jnp.mean(centred * centred, axis=-1, keepdims=True) + NORM_EPS)
    return (centred * inverse, inverse)


def norm_back(gradient, normed, inverse):
    return inverse * (
        gradient
        - jnp.mean(gradient, axis=-1, keepdims=True)
        - normed * jnp.mean(gradient * normed, axis=-1, keepdims=True)
    )


def dot(first, second):
    return jnp.dot(first, second, preferred_element_type=F32)


def dot_back(first, second):
    return lax.dot_general(first, second, (((1,), (1,)), ((), ())), preferred_element_type=F32)


def dot_rows(first, second):
    return lax.dot_general(first, second, (((0,), (0,)), ((), ())), preferred_element_type=F32)


def pick(array, index, axis):
    return lax.dynamic_index_in_dim(array, index, axis, keepdims=False)


def no_work(*refs):
    pass


def after(values, others):
    values = list(values)
    return pl.pallas_call(
        no_work,
        out_shape=[jax.ShapeDtypeStruct(value.shape, value.dtype) for value in values],
        in_specs=[ANY] * (len(values) + len(others)),
        out_specs=[ANY] * len(values),
        input_output_aliases={k: k for k in range(len(values))},
    )(*values, *others)


def total(terms):
    return sum(term.astype(F32) for term in terms)


def only(block, head):
    lane = lax.broadcasted_iota(jnp.int32, block.shape, 1)
    mine = lane < HEAD_DIM if head == 0 else lane >= HEAD_DIM
    return jnp.where(mine, block, jnp.zeros_like(block))


def both_heads(first, second):
    lane = lax.broadcasted_iota(jnp.int32, first.shape, 1)
    return jnp.where(lane < HEAD_DIM, first, second)


def attend_kernel(valid_ref, query_ref, key_ref, value_ref, out_ref):
    valid = valid_ref[pl.program_id(0)]
    query, key, value = query_ref[...], key_ref[...], value_ref[...]
    mixed = []
    for head in range(2):
        scores = dot_back(only(query, head), key) * SCALE
        column = lax.broadcasted_iota(jnp.int32, scores.shape, 1)
        scores = jnp.where(column < valid, scores, -1e30)
        powers = jnp.exp(scores - jnp.max(scores, axis=-1, keepdims=True))
        chances = (powers / jnp.sum(powers, axis=-1, keepdims=True)).astype(BF16)
        mixed.append(dot(chances, value))
    out_ref[...] = both_heads(*mixed).astype(BF16)


def attend_back_kernel(
    valid_ref, query_ref, key_ref, value_ref, d_ref, d_query_ref, d_key_ref, d_value_ref
):
    valid = valid_ref[pl.program_id(0)]
    query, key, value, d_mix = query_ref[...], key_ref[...], value_ref[...], d_ref[...]
    parts = []
    for head in range(2):
        scores = dot_back(only(key, head), query) * SCALE
        row = lax.broadcasted_iota(jnp.int32, scores.shape, 0)
        scores = jnp.where(row < valid, scores, -1e30)
        powers = jnp.exp(scores - jnp.max(scores, axis=0, keepdims=True))
        chances = powers / jnp.sum(powers, axis=0, keepdims=True)
        d_chances = dot_back(only(value, head), d_mix)
        mean = jnp.sum(chances * d_chances, axis=0, keepdims=True)
        d_scores = (chances * (d_chances - mean)).astype(BF16)
        d_value = dot(chances.astype(BF16), d_mix)
        d_key = dot(d_scores, query) * SCALE
        d_query = dot_rows(d_scores, key) * SCALE
        parts.append((d_query, d_key, d_value))
    for out_ref, first, second in zip((d_query_ref, d_key_ref, d_value_ref), *parts):
        out_ref[...] = both_heads(first, second).astype(BF16)


def block_of(rows, row_shift, column_shift):
    return pl.BlockSpec((rows, PAIR), lambda b, j: (b + row_shift, j + column_shift))


def attend(valid, query, key, value):
    frames, words = query[1], key[1]
    pairs = HALF // PAIR
    return pl.pallas_call(
        attend_kernel,
        out_shape=jax.ShapeDtypeStruct((2 * frames, HALF), BF16),
        grid=(2, pairs),
        in_specs=[SCALARS] + [block_of(*part[1:]) for part in (query, key, value)],
        out_specs=block_of(frames, 0, 0),
        compiler_params=pltpu.CompilerParams(vmem_limit_bytes=32 * 2**20),
        cost_estimate=LIGHT,
    )(valid, query[0], key[0], value[0])


def attend_back(valid, query, key, value, d_mixture):
    frames, words = query[1], key[1]
    pairs = HALF // PAIR
    return pl.pallas_call(
        attend_back_kernel,
        out_shape=[
            jax.ShapeDtypeStruct((2 * rows, HALF), BF16) for rows in (frames, words, words)
        ],
        grid=(2, pairs),
        in_specs=[SCALARS]
        + [block_of(*part[1:]) for part in (query, key, value)]
        + [block_of(frames, 0, 0)],
        out_specs=[block_of(rows, 0, 0) for rows in (frames, words, words)],
        compiler_params=pltpu.CompilerParams(vmem_limit_bytes=48 * 2**20),
        cost_estimate=LIGHT,
    )(valid, query[0], key[0], value[0], d_mixture)


def copy_all(copies):
    for copy in copies:
        copy.start()
    for copy in copies:
        copy.wait()


def place_pieces(spot_ref, *refs, plan, sizes):
    ny, nb = sizes
    count = len(plan["offsets"]) * len(plan["parts"])
    pieces, outs, sem = refs[:count], refs[count:-1], refs[-1]
    y, x = spot_ref[0], spot_ref[3]
    copies = []
    for part, blocks in enumerate(plan["parts"]):
        for spot, (dy, dx) in enumerate(plan["offsets"]):
            from_y = lax.rem(y - dy + ny, ny)
            from_x = lax.rem(x - dx + nb, nb)
            piece = pieces[part * len(plan["offsets"]) + spot]
            for block, (out, lane, column, width) in enumerate(blocks):
                columns = pl.ds(column, width)
                if lane is None:
                    target = outs[out].at[from_y, :, from_x, :, columns]
                else:
                    target = outs[out].at[from_y, lane, :, from_x, :, columns]
                copies.append(
                    pltpu.make_async_copy(piece.at[:, block], target, sem.at[len(copies)])
                )
    copy_all(copies)


def place_ranks(spot_ref, lines_ref, in_ref, down_ref, sem, *, offsets, sizes, rows, depth):
    ny, na, nb = sizes
    y, c, x = spot_ref[0], spot_ref[1], spot_ref[3]
    copies = []
    for block, (dy, dc, dx) in enumerate(offsets):
        target = in_ref.at[
            lax.rem(y - dy + ny, ny), lax.rem(c + dc, 2), :, lax.rem(x - dx + nb, nb)
        ]
        source = lines_ref.at[:, pl.ds(block * rows, rows)]
        copies.append(pltpu.make_async_copy(source, target, sem.at[len(copies)]))
    source = lines_ref.at[:, pl.ds(len(offsets) * rows, depth)]
    copies.append(pltpu.make_async_copy(source, down_ref, sem.at[len(copies)]))
    copy_all(copies)


def place_columns(spot_ref, pieces_ref, out_ref, sem, *, offsets, sizes, width):
    ny, nb = sizes
    y, c, x = spot_ref[0], spot_ref[1], spot_ref[3]
    copies = []
    for k, (dy, dc, dx) in enumerate(offsets):
        rank = (lax.rem(y - dy + ny, ny) * 2 + lax.rem(c + dc, 2)) * nb + lax.rem(x - dx + nb, nb)
        for half in range(2):
            start = pl.multiple_of(half * FF + rank * width, 128)
            copies.append(
                pltpu.make_async_copy(
                    pieces_ref.at[k, :, pl.ds(half * width, width)],
                    out_ref.at[:, pl.ds(start, width)],
                    sem.at[len(copies)],
                )
            )
    copy_all(copies)


def place(kernel, spot, arrays, shapes, copies):
    size = sum(a.size * a.dtype.itemsize for a in arrays)
    return pl.pallas_call(
        kernel,
        out_shape=[jax.ShapeDtypeStruct(shape, BF16) for shape in shapes],
        in_specs=[SCALARS] + [ANY] * len(arrays),
        out_specs=[WHOLE] * len(shapes),
        scratch_shapes=[pltpu.SemaphoreType.DMA((copies,))],
        compiler_params=pltpu.CompilerParams(vmem_limit_bytes=40 * 2**20),
        cost_estimate=pl.CostEstimate(flops=0, bytes_accessed=2 * size, transcendentals=0),
    )(spot, *arrays)


def prepare_kernel(
    spot_ref, qkv_ref, square_ref, ctx_ref, in_ref, own_ref, other_ref, wide_ref, block_ref,
    *, offsets, sizes
):
    ny, nb = sizes
    y, c, x = spot_ref[0], spot_ref[1], spot_ref[3]
    part = D // (2 * ny)
    for out_ref, which in ((own_ref, c), (other_ref, 1 - c)):
        for k in range(5):
            for block in range(ny):
                start = block * 2 * part + which * part
                if k < 3:
                    values = qkv_ref[:, pl.ds(pl.multiple_of(k * D + start, part), part)]
                elif k == 3:
                    values = square_ref[1, :, pl.ds(pl.multiple_of(start, part), part)]
                else:
                    values = jnp.concatenate(
                        [
                            ctx_ref[:, pl.ds(pl.multiple_of(side * D + start, part), part)]
                            for side in range(2)
                        ]
                    )
                out_ref[k, :, block * part : (block + 1) * part] = values.astype(BF16)
    for k, matrix in enumerate((0, 2)):
        for side in range(2):
            values = square_ref[matrix, :, side * HALF : (side + 1) * HALF]
            wide_ref[2 * k + side] = values.astype(BF16)
    width = FF // len(offsets)
    for k, (dy, dc, dx) in enumerate(offsets):
        rank = (lax.rem(y + dy, ny) * 2 + lax.rem(c + dc, 2)) * nb + lax.rem(x + dx, nb)
        for side in range(2):
            start = pl.multiple_of(side * FF + rank * width, width)
            block_ref[k, :, side * width : (side + 1) * width] = in_ref[
                :, pl.ds(start, width)
            ].astype(BF16)


def ffn_kernel(
    entry_a, entry_b, d_a, d_b, in_hbm, down_hbm,
    hidden_ref, d_gate_up_ref, d_branch_ref, own_ref, other_ref,
    entry_ref, d_ref, in_ref, down_ref, sem,
):
    step = pl.program_id(0)
    sources = (entry_a, in_hbm, d_a, down_hbm, entry_b, d_b)
    targets = (entry_ref.at[0], in_ref, d_ref.at[0], down_ref, entry_ref.at[1], d_ref.at[1])
    copies = [
        pltpu.make_async_copy(source, target, sem.at[k])
        for k, (source, target) in enumerate(zip(sources, targets))
    ]

    @pl.when(step == 0)
    def _():
        for copy in copies:
            copy.start()
        for copy in copies[:4]:
            copy.wait()

    @pl.when(step == 1)
    def _():
        for copy in copies[4:]:
            copy.wait()

    width = down_ref.shape[0]
    frames = d_ref.shape[1]
    notes = entry_ref[step, frames:, :].astype(F32)
    gate_row = notes[0:1] + notes[1:2] + notes[2:3]
    d_branch = (d_ref[step].astype(F32) * gate_row).astype(BF16)
    d_branch_ref[...] = d_branch
    gate_up = dot(entry_ref[step, :frames, :], in_ref[...])
    gate, up = gate_up[:, :width], gate_up[:, width:]
    logistic = jax.nn.sigmoid(gate)
    hidden = (gate * logistic * up).astype(BF16)
    hidden_ref[...] = hidden
    d_hidden = dot_back(d_branch, down_ref[...])
    d_gate = d_hidden * up * logistic * (1.0 + gate * (1.0 - logistic))
    d_gate_up_ref[:, :width] = d_gate.astype(BF16)
    d_gate_up_ref[:, width:] = (d_hidden * gate * logistic).astype(BF16)
    d_entry = dot_back(d_gate_up_ref[...], in_ref[...]).astype(BF16)
    branch = dot(hidden, down_ref[...]).astype(BF16)

    @pl.when(step == 0)
    def _():
        own_ref[0] = d_entry
        own_ref[1] = branch

    @pl.when(step == 1)
    def _():
        other_ref[0] = d_entry
        other_ref[1] = branch


NOTE_ROWS = 16


def gate_notes(gate):
    high = gate.astype(BF16)
    rest = gate - high.astype(F32)
    middle = rest.astype(BF16)
    low = (rest - middle.astype(F32)).astype(BF16)
    blank = jnp.zeros((NOTE_ROWS - 3, gate.shape[0]), BF16)
    return jnp.concatenate([jnp.stack([high, middle, low]), blank])


def ffn_both_ways(entries, cotangents, rank_in, rank_down):
    frames = cotangents[0].shape[0]
    width = rank_down.shape[0]
    rows_of = lambda cols: pl.BlockSpec((frames, cols), lambda i: (i, 0))
    whole = pl.BlockSpec((2, frames, D), lambda i: (0, 0, 0))
    shape = lambda *sizes: jax.ShapeDtypeStruct(sizes, BF16)
    return pl.pallas_call(
        ffn_kernel,
        out_shape=[shape(2 * frames, cols) for cols in (width, 2 * width, D)]
        + [shape(2, frames, D)] * 2,
        grid=(2,),
        in_specs=[ANY] * 6,
        out_specs=[rows_of(cols) for cols in (width, 2 * width, D)] + [whole] * 2,
        scratch_shapes=[
            pltpu.VMEM((2, frames + NOTE_ROWS, D), BF16),
            pltpu.VMEM((2, frames, D), BF16),
            pltpu.VMEM((D, 2 * width), BF16),
            pltpu.VMEM((width, D), BF16),
            pltpu.SemaphoreType.DMA((6,)),
        ],
        compiler_params=pltpu.CompilerParams(vmem_limit_bytes=56 * 2**20),
        cost_estimate=LIGHT,
    )(*entries, *cotangents, rank_in, rank_down)


def outer_kernel(*refs, lefts, groups, rows, lanes):
    left_refs, right_refs, out_ref = refs[:lefts], refs[lefts:-1], refs[-1]

    def pieces(group):
        return [ref[k : k + rows, :] for ref in group for k in range(0, ref.shape[0], rows)]

    left_pieces = pieces(left_refs)
    start = column = 0
    for size in groups:
        group = right_refs[start : start + size]
        start += size
        sums = None
        for left, right in zip(left_pieces, pieces(group)):
            term = dot_rows(left, right)
            sums = term if sums is None else sums + term
        sums = sums.astype(BF16)
        end = column + sums.shape[1]
        if lanes is None:
            out_ref[0, :, column:end] = sums
        else:
            for k in range(out_ref.shape[0]):
                out_ref[k, 0, :, column:end] = sums[k * lanes : (k + 1) * lanes]
        column = end


def outer_sum(lefts, groups, rows, block, lanes=None, halves=1):
    depth = lefts[0].shape[1]
    cols = sum(group[0][1] for group in groups) // halves
    blocks = depth // block * halves
    if block % 128:
        left = jnp.concatenate([a[: a.shape[0] // rows * rows] for a in lefts])
        right = jnp.concatenate(
            [
                jnp.concatenate([a[:, at * width : (at + 1) * width] for a, width, at in group])
                for group in groups
            ],
            axis=1,
        )
        out = dot_rows(left, right).astype(BF16).reshape(depth // block, block, halves, cols)
        return jnp.swapaxes(out, 1, 2).reshape(blocks, block, cols)
    if lanes is None:
        out_shape = (blocks, block, cols)
        out_spec = pl.BlockSpec((1, block, cols), lambda i: (i, 0, 0))
    else:
        out_shape = (block // lanes, blocks, lanes, cols)
        out_spec = pl.BlockSpec((block // lanes, 1, lanes, cols), lambda i: (0, i, 0, 0))
    used = lambda array: array.shape[0] // rows * rows

    def right_spec(right):
        array, width, at = right
        if halves > 1:
            return pl.BlockSpec((array.shape[0], width // halves), lambda i: (0, i % halves))
        return pl.BlockSpec(
            (array.shape[0], width), lambda i: (0, at), pipeline_mode=pl.Buffered(1)
        )

    rights = [right for group in groups for right in group]
    return pl.pallas_call(
        functools.partial(
            outer_kernel,
            lefts=len(lefts),
            groups=[len(group) for group in groups],
            rows=rows,
            lanes=lanes,
        ),
        out_shape=jax.ShapeDtypeStruct(out_shape, BF16),
        grid=(blocks,),
        in_specs=[pl.BlockSpec((used(a), block), lambda i: (0, i // halves)) for a in lefts]
        + [right_spec(right) for right in rights],
        out_specs=out_spec,
        compiler_params=pltpu.CompilerParams(vmem_limit_bytes=56 * 2**20),
        cost_estimate=LIGHT,
    )(*lefts, *[right[0] for right in rights])


def reduce_kernel(*refs, plan, inputs):
    arrays, (small_hbm, in_hbm, down_hbm) = refs[:inputs], refs[inputs : inputs + 3]
    out_ref, small_ref, in_ref, down_ref, down_in = refs[inputs + 3 : inputs + 8]
    (
        blocks, first_x, first_y, second, second_in, kept, lines_in, mine, other_in, left_ref, right_ref, notes,
        load_sem, first_send, first_recv, second_send, second_recv, line_send, line_recv,
        core_send, core_recv, note_send, note_recv,
        in_own, in_core, in_y, in_x, in_send, in_recv, down_send, down_recv, down_sem,
    ) = refs[inputs + 8 :]
    y, c, z, x = (lax.axis_index(axis) for axis in AXES)
    na, rows = kept.shape[1], kept.shape[3]
    far_y, far_c, far_x = 1 - y, 1 - c, 1 - x
    count = len(plan)
    names = [("y", far_y), ("c", far_c), ("x", far_x)]
    names += [("z", lax.rem(z + k, na)) for k in range(1, na)]
    slots = {}
    for m, (_, _, _, turn) in enumerate(plan):
        slots[m] = sum(1 for other in plan[:m] if other[3] == turn)

    def remote(source, target, send, recv, axis, at):
        return pltpu.make_async_remote_copy(
            src_ref=source,
            dst_ref=target,
            send_sem=send,
            recv_sem=recv,
            device_id={axis: at},
            device_id_type=pl.DeviceIdType.MESH,
        )

    barrier = pltpu.get_barrier_semaphore()
    for axis, at in names:
        pl.semaphore_signal(
            barrier, inc=1, device_id={axis: at}, device_id_type=pl.DeviceIdType.MESH
        )
    pl.semaphore_wait(barrier, len(names))

    def first_copy(m):
        if plan[m][3]:
            source, target, axis, at = blocks.at[m, far_y], first_y.at[slots[m]], "y", far_y
        else:
            source, target, axis, at = blocks.at[m, :, :, :, far_x], first_x.at[slots[m]], "x", far_x
        return remote(source, target, first_send.at[m], first_recv.at[m], axis, at)

    def second_copy(m):
        axis, at = ("x", far_x) if plan[m][3] else ("y", far_y)
        return remote(
            second.at[m], second_in.at[m], second_send.at[m], second_recv.at[m], axis, at
        )

    def line_copies(m):
        return [
            remote(
                kept.at[m, lax.rem(z + k, na)],
                lines_in.at[m, k - 1],
                line_send.at[m * (na - 1) + k - 1],
                line_recv.at[m * (na - 1) + k - 1],
                "z",
                lax.rem(z + k, na),
            )
            for k in range(1, na)
        ]

    def core_copy(m):
        return remote(
            mine.at[m, far_c], other_in.at[m], core_send.at[m], core_recv.at[m], "c", far_c
        )

    def note_copies(hop):
        if hop == 0:
            hops = [(notes.at[0, 0, 0, 0], notes.at[0, 0, 0, 1], "x", far_x)]
        elif hop == 1:
            hops = [
                (notes.at[0, 0, 0], notes.at[0, 0, k], "z", lax.rem(z + k, na))
                for k in range(1, na)
            ]
        elif hop == 2:
            hops = [(notes.at[0, 0], notes.at[0, 1], "c", far_c)]
        else:
            hops = [(notes.at[0], notes.at[1], "y", far_y)]
        at = 0 if hop == 0 else hop + (na - 2 if hop > 1 else 0)
        return [
            remote(source, target, note_send.at[at + k], note_recv.at[at + k], axis, to)
            for k, (source, target, axis, to) in enumerate(hops)
        ]

    def loads(m):
        copies = []
        for group, buffer in ((plan[m][1], left_ref), (plan[m][2], right_ref)):
            start = 0
            for place_of in group:
                height, width = arrays[place_of].shape
                copies.append(
                    pltpu.make_async_copy(
                        arrays[place_of],
                        buffer.at[m % 2, pl.ds(start, height), pl.ds(0, width)],
                        load_sem.at[m % 2, len(copies)],
                    )
                )
                start += height
        return copies

    def compute(m):
        kind, lefts, rights, _ = plan[m]
        height = sum(arrays[place_of].shape[0] for place_of in lefts)
        depth = na * 2 * rows

        @pl.loop(0, 4)
        def _(step):
            at_y, at_c = step // 2, step % 2
            at, columns = (step, 0) if kind == "tall" else (at_y, at_c)
            left = left_ref[m % 2, :height, pl.ds(pl.multiple_of(at * depth, 128), depth)]
            right = right_ref[m % 2, :height, pl.ds(pl.multiple_of(columns * HALF, 128), HALF)]
            sums = dot_rows(left, right).astype(BF16)
            for k in range(2 * na):
                blocks[m, at_y, at_c, k // 2, k % 2] = sums[k * rows : (k + 1) * rows]

    def arrived(m, at_c, at_z, at_y, at_x):
        if plan[m][3]:
            came = first_y[slots[m], at_c, at_z, at_x]
        else:
            came = first_x[slots[m], at_y, at_c, at_z]
        return blocks[m, at_y, at_c, at_z, at_x].astype(F32) + came.astype(F32)

    load = pltpu.make_async_copy(small_hbm, notes.at[0, 0, 0, 0], load_sem.at[0, 0])
    load.start()
    load.wait()
    hops = [note_copies(hop) for hop in range(4)]
    for copy in hops[0]:
        copy.start()

    load = pltpu.make_async_copy(in_hbm, in_own, load_sem.at[0, 0])
    load.start()
    load.wait()

    def in_copies(first, pairs, axis, at):
        return [
            remote(source, target, in_send.at[first + k], in_recv.at[first + k], axis, at)
            for k, (source, target) in enumerate(pairs)
        ]

    in_hops = [
        in_copies(0, [(in_own.at[:, far_c], in_core)], "c", far_c),
        in_copies(
            1, [(in_own.at[far_y, c], in_y.at[0]), (in_core.at[far_y], in_y.at[1])], "y", far_y
        ),
        in_copies(
            3,
            [
                (in_own.at[y, c, far_x], in_x.at[0]),
                (in_core.at[y, far_x], in_x.at[1]),
                (in_y.at[0, far_x], in_x.at[2]),
                (in_y.at[1, far_x], in_x.at[3]),
            ],
            "x",
            far_x,
        ),
    ]
    for copy in in_hops[0]:
        copy.start()
    down_copies = [
        remote(
            down_hbm.at[lax.rem(z + k, na)], down_in.at[k - 1],
            down_send.at[k - 1], down_recv.at[k - 1], "z", lax.rem(z + k, na),
        )
        for k in range(1, na)
    ]
    for copy in down_copies:
        copy.start()
    for copy in loads(0):
        copy.start()
    def second_step(m):
        first_copy(m).wait_recv()

        @pl.loop(0, 2 * na)
        def _(step):
            at_c, at_z = step // na, step % na
            at_y, at_x = (y, far_x) if plan[m][3] else (far_y, x)
            second[m, at_c, at_z] = arrived(m, at_c, at_z, at_y, at_x).astype(BF16)

        second_copy(m).start()

    def line_step(m):
        second_copy(m).wait_recv()

        @pl.loop(0, 2 * na)
        def _(step):
            at_c, at_z = step // na, step % na
            sums = arrived(m, at_c, at_z, y, x) + second_in[m, at_c, at_z].astype(F32)
            kept[m, at_z, at_c] = sums.astype(BF16)

        for copy in line_copies(m):
            copy.start()

    def last_step(m):
        sums = kept[m, z].astype(F32)
        for k, copy in enumerate(line_copies(m)):
            copy.wait_recv()
            sums += lines_in[m, k].astype(F32)
        mine[m] = sums.astype(BF16)
        if plan[m][0] == "tall":
            core_copy(m).start()

    for m in range(count + 6):
        if m < count:
            for copy in loads(m):
                copy.wait()
            if m + 1 < count:
                for copy in loads(m + 1):
                    copy.start()
            compute(m)
            first_copy(m).start()
        if m in (1, 3):
            for copy in in_hops[m // 2]:
                copy.wait_recv()
            for copy in in_hops[m // 2 + 1]:
                copy.start()
        if m in (0, 2, 4):
            hop = m // 2
            for copy in hops[hop]:
                copy.wait_recv()
            for copy in hops[hop + 1]:
                copy.start()
        for behind, step in ((2, second_step), (4, line_step), (6, last_step)):
            if 0 <= m - behind < count:
                step(m - behind)
    order = range(count)
    for m in order:
        if plan[m][0] == "tall":
            core_copy(m).wait_recv()
            out_ref[m, 0] = mine[m, c]
            out_ref[m, 1] = other_in[m]
        else:
            out_ref[m] = mine[m]
    for copy in hops[3]:
        copy.wait_recv()
    small_ref[...] = notes[...]

    for copy in in_hops[2]:
        copy.wait_recv()
    width = in_own.shape[-1] // 2
    for at_y in range(2):
        for at_c in range(2):
            if at_y:
                near = in_y[at_c, x]
            else:
                near = in_core[y, x] if at_c else in_own[y, c, x]
            for at_x, piece in ((0, near), (1, in_x[at_y * 2 + at_c])):
                rank = (
                    lax.rem(y + at_y, 2) * 2 + lax.rem(c + at_c, 2)
                ) * 2 + lax.rem(x + at_x, 2)
                for half in range(2):
                    start = pl.multiple_of(half * FF + rank * width, 128)
                    in_ref[:, pl.ds(start, width)] = piece[:, half * width : (half + 1) * width]
    depth = down_ref.shape[0]
    sums = None
    for k in range(na):
        if k:
            down_copies[k - 1].wait_recv()
        source = down_in.at[k - 1] if k else down_hbm.at[z]
        copy = pltpu.make_async_copy(source, left_ref.at[0, pl.ds(0, depth)], down_sem.at[0])
        copy.start()
        copy.wait()
        term = left_ref[0, :depth, :].astype(F32)
        sums = term if sums is None else sums + term
    down_ref[...] = sums.astype(BF16)

    for hop in hops + in_hops + [down_copies]:
        for copy in hop:
            copy.wait_send()
    for m in range(count):
        first_copy(m).wait_send()
        second_copy(m).wait_send()
        for copy in line_copies(m):
            copy.wait_send()
        if plan[m][0] == "tall":
            core_copy(m).wait_send()


def reduce_group(matrices, small, grad_in, grad_down, na, rows):
    arrays, plan = [], []
    for kind, lefts, rights, turn in matrices:
        places = []
        for group in (lefts, rights):
            places.append([])
            for array in group:
                found = [k for k, known in enumerate(arrays) if known is array]
                if not found:
                    arrays.append(array)
                    found = [len(arrays) - 1]
                places[-1].append(found[0])
        plan.append((kind, *places, turn))
    count = len(plan)
    tall = max(sum(a.shape[0] for a in lefts) for _, lefts, _, _ in matrices)
    turns = [turn for *_, turn in plan]
    low = lambda *shape: pltpu.VMEM(shape, BF16)
    sem = lambda *shape: pltpu.SemaphoreType.DMA(shape)
    all_small = (2, 2, na, 2) + small.shape
    return pl.pallas_call(
        functools.partial(reduce_kernel, plan=plan, inputs=len(arrays)),
        out_shape=[
            jax.ShapeDtypeStruct((count, 2, rows, HALF), BF16),
            jax.ShapeDtypeStruct(all_small, BF16),
            jax.ShapeDtypeStruct((rows, 2 * FF), BF16),
            jax.ShapeDtypeStruct(grad_down.shape[1:], BF16),
            jax.ShapeDtypeStruct((na - 1,) + grad_down.shape[1:], BF16),
        ],
        in_specs=[ANY] * (len(arrays) + 3),
        out_specs=[WHOLE] * 4 + [ANY],
        scratch_shapes=[
            low(count, 2, 2, na, 2, rows, HALF),
            low(turns.count(0), 2, 2, na, rows, HALF),
            low(turns.count(1), 2, na, 2, rows, HALF),
            low(count, 2, na, rows, HALF),
            low(count, 2, na, rows, HALF),
            low(count, na, 2, rows, HALF),
            low(count, na - 1, 2, rows, HALF),
            low(count, 2, rows, HALF),
            low(count, rows, HALF),
            low(2, tall, D),
            low(2, tall, D),
            low(*all_small),
            sem(2, 4),
            sem(count),
            sem(count),
            sem(count),
            sem(count),
            sem(count * (na - 1)),
            sem(count * (na - 1)),
            sem(count),
            sem(count),
            sem(na + 2),
            sem(na + 2),
            low(*grad_in.shape),
            low(2, 2, *grad_in.shape[-2:]),
            low(2, 2, *grad_in.shape[-2:]),
            low(4, *grad_in.shape[-2:]),
            sem(7),
            sem(7),
            sem(na - 1),
            sem(na - 1),
            sem(1),
        ],
        compiler_params=pltpu.CompilerParams(
            vmem_limit_bytes=60 * 2**20, collective_id=1, has_side_effects=True
        ),
        cost_estimate=LIGHT,
    )(*arrays, small, grad_in, grad_down)


def pair_in_kernel(own_ref, other_ref, weight_ref, out_ref, *, product):
    for step, ref in enumerate((own_ref, other_ref)):

        @pl.when(pl.program_id(0) == step)
        def _():
            out_ref[...] = product(ref[...], weight_ref[...]).astype(BF16)


def pair_in(own, other, weight, product):
    frames = own.shape[0]
    cols = weight.shape[1] if product is dot else weight.shape[0]
    whole = lambda array: pl.BlockSpec(
        array.shape, lambda i: (0, 0), pipeline_mode=pl.Buffered(1)
    )
    return pl.pallas_call(
        functools.partial(pair_in_kernel, product=product),
        out_shape=jax.ShapeDtypeStruct((2 * frames, cols), BF16),
        grid=(2,),
        in_specs=[whole(own), whole(other), whole(weight)],
        out_specs=pl.BlockSpec((frames, cols), lambda i: (i, 0)),
        compiler_params=pltpu.CompilerParams(vmem_limit_bytes=48 * 2**20),
        cost_estimate=LIGHT,
    )(own, other, weight)


def pair_out_kernel(*refs, product):
    part_refs, weight_ref, own_ref, other_ref = refs[:-3], refs[-3], refs[-2], refs[-1]
    sums = None
    column = 0
    for ref in part_refs:
        weight = weight_ref[...]
        if len(part_refs) > 1:
            weight = weight_ref[:, column : column + ref.shape[1]]
            column += ref.shape[1]
        term = product(ref[...], weight)
        sums = term if sums is None else sums + term

    @pl.when(pl.program_id(0) == 0)
    def _():
        own_ref[...] = sums

    @pl.when(pl.program_id(0) == 1)
    def _():
        other_ref[...] = sums.astype(BF16)


def pair_out(parts, weight, product):
    frames = parts[0].shape[0] // 2
    cols = weight.shape[1] if product is dot else weight.shape[0]
    whole = pl.BlockSpec((frames, cols), lambda i: (0, 0))
    return pl.pallas_call(
        functools.partial(pair_out_kernel, product=product),
        out_shape=[
            jax.ShapeDtypeStruct((frames, cols), F32),
            jax.ShapeDtypeStruct((frames, cols), BF16),
        ],
        grid=(2,),
        in_specs=[pl.BlockSpec((frames, part.shape[1]), lambda i: (i, 0)) for part in parts]
        + [pl.BlockSpec(weight.shape, lambda i: (0, 0), pipeline_mode=pl.Buffered(1))],
        out_specs=[whole, whole],
        compiler_params=pltpu.CompilerParams(vmem_limit_bytes=48 * 2**20),
        cost_estimate=LIGHT,
    )(*parts, weight)


def shift_kernel(
    terms_ref, cot_hbm, in_ref, shifts_ref, cots_hbm, parts_ref,
    from_core, line_out, line_in, y_out, y_in, x_out, x_in,
    in_core, in_y, in_x,
    core_sem, line_send, line_recv, step_sem, cot_send, cot_recv, relay_send, relay_recv,
    in_send, in_recv,
):
    y, c, z, x = (lax.axis_index(axis) for axis in AXES)
    na = terms_ref.shape[2]
    far_y, far_c, far_x = 1 - y, 1 - c, 1 - x

    def remote(source, target, send, recv, device):
        return pltpu.make_async_remote_copy(
            src_ref=source,
            dst_ref=target,
            send_sem=send,
            recv_sem=recv,
            device_id=device,
            device_id_type=pl.DeviceIdType.MESH,
        )

    devices = [{"y": far_y}, {"c": far_c}, {"x": far_x}]
    devices += [{"z": lax.rem(z + k, na)} for k in range(1, na)]
    barrier = pltpu.get_barrier_semaphore()
    for device in devices:
        pl.semaphore_signal(
            barrier, inc=1, device_id=device, device_id_type=pl.DeviceIdType.MESH
        )
    pl.semaphore_wait(barrier, len(devices))

    to_core = remote(terms_ref.at[:, 1], from_core, core_sem.at[0], core_sem.at[1], {"c": far_c})
    to_core.start()

    def block_copies(first, pairs, device):
        return [
            remote(source, target, in_send.at[first + k], in_recv.at[first + k], device)
            for k, (source, target) in enumerate(pairs)
        ]

    in_hops = [
        block_copies(0, [(in_ref.at[:, 1], in_core)], {"c": far_c}),
        block_copies(1, [(in_ref.at[1, 0], in_y.at[0]), (in_core.at[1], in_y.at[1])], {"y": far_y}),
        block_copies(
            3,
            [
                (in_ref.at[0, 0, 1], in_x.at[0]),
                (in_core.at[0, 1], in_x.at[1]),
                (in_y.at[0, 1], in_x.at[2]),
                (in_y.at[1, 1], in_x.at[3]),
            ],
            {"x": far_x},
        ),
    ]
    for copy in in_hops[0]:
        copy.start()
    chips = {1: {"x": far_x}, 2: {"y": far_y}}
    cots = {
        2 * k: remote(cot_hbm, cots_hbm.at[2 * k], cot_send.at[2 * k], cot_recv.at[2 * k], chips[k])
        for k in chips
    }
    cots[1] = remote(cot_hbm, cots_hbm.at[1], cot_send.at[1], cot_recv.at[1], {"c": far_c})
    for k in (1, 2, 3):
        cots[2 * k + 1] = remote(
            cots_hbm.at[2 * k], cots_hbm.at[2 * k + 1],
            cot_send.at[2 * k + 1], cot_recv.at[2 * k + 1], {"c": far_c},
        )
    relays = []
    for k, (part, size) in enumerate(halves_of(cot_hbm.shape[0])):
        near, next_to = (1, 2) if k == 0 else (2, 1)
        here = pl.ds(part, size)
        relays.append(
            remote(
                cots_hbm.at[2 * near, here], cots_hbm.at[6, here],
                relay_send.at[k], relay_recv.at[k], chips[next_to],
            )
        )
    cots[2].start()
    cots[4].start()
    cots[1].start()

    to_core.wait_recv()
    for copy in in_hops[0]:
        copy.wait_recv()
    for copy in in_hops[1]:
        copy.start()
    lines = []
    for k in range(1, na):
        line_out[k - 1] = terms_ref[:, 0, k] + from_core[:, k]
        lines.append(
            remote(
                line_out.at[k - 1], line_in.at[k - 1], line_send.at[k - 1], line_recv.at[k - 1],
                {"z": lax.rem(z - k + na, na)},
            )
        )
        lines[-1].start()
    here = terms_ref[:, 0, 0] + from_core[:, 0]
    for k, copy in enumerate(lines):
        copy.wait_recv()
        here = here + line_in[k]
    y_out[...] = here[1]
    to_y = remote(y_out, y_in, step_sem.at[0], step_sem.at[1], {"y": far_y})
    to_y.start()
    for k in (1, 2):
        cots[2 * k].wait_recv()
    for copy in relays:
        copy.start()
    for k in (1, 2):
        cots[2 * k + 1].start()
    to_y.wait_recv()
    here = here[0] + y_in[...]
    x_out[...] = here[1]
    to_x = remote(x_out, x_in, step_sem.at[2], step_sem.at[3], {"x": far_x})
    to_x.start()
    for copy in in_hops[1]:
        copy.wait_recv()
    for copy in in_hops[2]:
        copy.start()
    to_x.wait_recv()
    shifts_ref[...] = here[0] + x_in[...]

    for copy in relays:
        copy.wait_recv()
    cots[7].start()
    for copy in in_hops[2]:
        copy.wait_recv()
    for at_y in range(2):
        for at_c in range(2):
            near = in_ref[0, 0, 0] if not at_y and not at_c else None
            if near is None:
                near = in_y[at_c, 0] if at_y else in_core[0, 0]
            parts_ref[at_y, at_c, 0] = near
            parts_ref[at_y, at_c, 1] = in_x[at_y * 2 + at_c]
    for k in (1, 3, 5, 7):
        cots[k].wait_recv()
        cots[k].wait_send()
    for copy in [to_core, to_y, to_x, cots[2], cots[4]] + lines + relays + sum(in_hops, []):
        copy.wait_send()


def sum_shifts(terms, cotangent, blocks, na):
    rows = terms.shape[-2]
    full = lambda *shape: pltpu.VMEM(shape + (rows, 128), F32)
    sem = lambda size: pltpu.SemaphoreType.DMA((size,))
    block = blocks.shape[-2:]
    low = lambda *shape: pltpu.VMEM(shape + block, BF16)
    return pl.pallas_call(
        shift_kernel,
        out_shape=[
            jax.ShapeDtypeStruct((rows, 128), F32),
            jax.ShapeDtypeStruct((8,) + cotangent.shape, BF16),
            jax.ShapeDtypeStruct(blocks.shape, BF16),
        ],
        in_specs=[WHOLE, ANY, WHOLE],
        out_specs=[WHOLE, ANY, WHOLE],
        scratch_shapes=[
            full(2, na, 2),
            full(na - 1, 2, 2),
            full(na - 1, 2, 2),
            full(2),
            full(2),
            full(),
            full(),
            low(2, 2),
            low(2, 2),
            low(4),
            sem(2),
            sem(na - 1),
            sem(na - 1),
            sem(4),
            sem(8),
            sem(8),
            sem(2),
            sem(2),
            sem(7),
            sem(7),
        ],
        compiler_params=pltpu.CompilerParams(
            vmem_limit_bytes=32 * 2**20, collective_id=2, has_side_effects=True
        ),
        cost_estimate=LIGHT,
    )(terms, cotangent, blocks)


def halves_of(height):
    cut = height // 32 * 16
    return (0, cut), (cut, height - cut)


def ffn_group_kernel(
    entry_hbm, notes_hbm, cot_hbm, cots_hbm, in_hbm, down_hbm,
    d_entry_hbm, grad_down_hbm, grad_in_hbm, branch_hbm, own_hbm, other_hbm, pair_hbm, back_hbm,
    sum_hbm, branch_back_hbm,
    entry, d_branch, hidden, d_gate_up, in_ref, down_ref, partial, away, branch, loaded, sums,
    local_sem, entry_send, entry_recv, cot_sem,
    pair_send, pair_recv, back_send, back_recv, branch_sem, out_sem,
    relay_send, relay_recv, branch_pair_send, branch_pair_recv, branch_send, branch_recv,
    *, chips, sizes,
):
    ny, nb = sizes
    y, c, x = lax.axis_index("y"), lax.axis_index("c"), lax.axis_index("x")
    frames = cot_hbm.shape[0]
    rows = frames // 2
    width = down_ref.shape[0]
    count = len(chips)
    sibling = {"c": 1 - c}
    ahead = [{"y": lax.rem(y + dy, ny), "x": lax.rem(x + dx, nb)} for dy, dx in chips]
    behind = [
        {"y": lax.rem(y - dy + ny, ny), "x": lax.rem(x - dx + nb, nb)} for dy, dx in chips
    ]

    def remote(source, target, send, recv, device):
        return pltpu.make_async_remote_copy(
            src_ref=source,
            dst_ref=target,
            send_sem=send,
            recv_sem=recv,
            device_id=device,
            device_id_type=pl.DeviceIdType.MESH,
        )

    barrier = pltpu.get_barrier_semaphore()
    for device in [sibling] + behind[1:]:
        pl.semaphore_signal(
            barrier, inc=1, device_id=device, device_id_type=pl.DeviceIdType.MESH
        )
    pl.semaphore_wait(barrier, count)

    loads = [
        pltpu.make_async_copy(source, target, local_sem.at[k])
        for k, (source, target) in enumerate(
            [
                (entry_hbm, entry.at[0, pl.ds(0, frames)]),
                (notes_hbm, entry.at[0, pl.ds(frames, NOTE_ROWS)]),
                (in_hbm, in_ref),
                (down_hbm, down_ref),
            ]
        )
    ]
    for load in loads:
        load.start()
    cot_loads = [
        pltpu.make_async_copy(
            cots_hbm.at[k] if k else cot_hbm, d_branch.at[k], cot_sem.at[k]
        )
        for k in range(2 * count)
    ]
    for load in cot_loads:
        load.start()
    entry_copies = {
        1: remote(entry.at[0], entry.at[1], entry_send.at[1], entry_recv.at[1], sibling)
    }
    for k in range(1, count):
        entry_copies[2 * k] = remote(
            entry.at[0], entry.at[2 * k], entry_send.at[2 * k], entry_recv.at[2 * k], ahead[k]
        )
        entry_copies[2 * k + 1] = remote(
            entry.at[2 * k], entry.at[2 * k + 1],
            entry_send.at[2 * k + 1], entry_recv.at[2 * k + 1], sibling,
        )
    for load in loads[:2]:
        load.wait()
    for k in (2, 4, 1):
        entry_copies[k].start()

    relays = []
    height = entry.shape[1]
    for k, (part, size) in enumerate(halves_of(height)):
        near, next_to = (1, 2) if k == 0 else (2, 1)
        here = pl.ds(part, size)
        relays.append(
            remote(
                entry.at[2 * near, here], entry.at[2 * 3, here],
                relay_send.at[k], relay_recv.at[k], ahead[next_to],
            )
        )

    def branch_copies(k):
        copies = []
        if k == 0:
            copies.append(pltpu.make_async_copy(branch.at[0], own_hbm, branch_sem.at[0]))
        copies.append(
            remote(
                branch.at[1], other_hbm.at[k], branch_pair_send.at[k], branch_pair_recv.at[k], sibling
            )
        )
        return copies

    def branch_wait(k):
        for copy in branch_copies(k)[:-1]:
            copy.wait()
        branch_copies(k)[-1].wait_send()

    def branch_copy(k):
        return remote(
            sum_hbm.at[k - 1], branch_back_hbm.at[k - 1], branch_send.at[k], branch_recv.at[k],
            behind[k],
        )

    def pair_copy(k):
        return remote(
            away.at[k % 2], pair_hbm.at[k], pair_send.at[k], pair_recv.at[k], sibling
        )

    def back_copy(k):
        return remote(
            partial.at[k], back_hbm.at[k - 1], back_send.at[k], back_recv.at[k], behind[k]
        )

    def compute(k, i):
        @pl.loop(0, 2)
        def _(part):
            slot = 2 * k + i
            here = pl.ds(pl.multiple_of(part * rows, rows), rows)
            notes = entry[slot, frames:, :].astype(F32)
            gate_row = notes[0:1] + notes[1:2] + notes[2:3]
            d_here = (d_branch[slot, here, :].astype(F32) * gate_row).astype(BF16)
            d_branch[slot, here, :] = d_here
            gate_up = dot(entry[slot, here, :], in_ref[...])
            gate, up = gate_up[:, :width], gate_up[:, width:]
            logistic = jax.nn.sigmoid(gate)
            hidden_here = (gate * logistic * up).astype(BF16)
            hidden[slot, here, :] = hidden_here
            d_hidden = dot_back(d_here, down_ref[...])
            d_gate = d_hidden * up * logistic * (1.0 + gate * (1.0 - logistic))
            d_gate_up[slot, here, :width] = d_gate.astype(BF16)
            d_gate_up[slot, here, width:] = (d_hidden * gate * logistic).astype(BF16)
            d_entry = dot_back(d_gate_up[slot, here, :], in_ref[...]).astype(BF16)
            branch[i, here, :] = dot(hidden_here, down_ref[...]).astype(BF16)

            if i == 0:
                partial[k, here, :] = d_entry
            else:
                away[k % 2, here, :] = d_entry

    def move(source, target):
        copy = pltpu.make_async_copy(source, target, out_sem.at[0])
        copy.start()
        copy.wait()

    def fetch(source):
        move(source, loaded)
        return loaded[...].astype(F32)

    def branch_terms(k):
        branch_copies(k)[-1].wait_recv()
        own = branch[0].astype(F32) if k else fetch(own_hbm)
        return own + fetch(other_hbm.at[k])

    def finish(k):
        pair_copy(k).wait_recv()
        partial[k] = (partial[k].astype(F32) + fetch(pair_hbm.at[k])).astype(BF16)
        if k:
            back_copy(k).start()
            pair_copy(k).wait_send()
            away[k % 2] = branch_terms(k).astype(BF16)
            move(away.at[k % 2], sum_hbm.at[k - 1])
            branch_copy(k).start()
        else:
            pair_copy(k).wait_send()

    for k in range(count):
        if k == 0:
            for load in loads[2:]:
                load.wait()
        elif k < 3:
            if k == 1:
                entry_copies[2].wait_recv()
                entry_copies[4].wait_recv()
                for copy in relays:
                    copy.start()
            entry_copies[2 * k + 1].start()
        else:
            for copy in relays:
                copy.wait_recv()
            entry_copies[2 * k + 1].start()
        entry_copies[2 * k + 1].wait_recv()
        cot_loads[2 * k].wait()
        cot_loads[2 * k + 1].wait()
        if k:
            branch_wait(k - 1)
        compute(k, 0)
        if k == 1:
            finish(0)
        compute(k, 1)
        pair_copy(k).start()
        for copy in branch_copies(k):
            copy.start()
        if k:
            finish(k)
    branch_wait(count - 1)

    down_rows = 256 if width % 256 == 0 else 128

    @pl.loop(0, width // down_rows)
    def _(block):
        columns = pl.ds(pl.multiple_of(block * down_rows, down_rows), down_rows)
        term = dot_rows(hidden[0, :, columns], d_branch[0])
        for slot in range(1, 2 * count):
            term += dot_rows(hidden[slot, :, columns], d_branch[slot])
        branch[0, :down_rows, :] = term.astype(BF16)
        copy = pltpu.make_async_copy(
            branch.at[0, pl.ds(0, down_rows)], grad_down_hbm.at[columns], out_sem.at[1]
        )
        copy.start()
        copy.wait()

    na, _, lanes, _ = grad_in_hbm.shape
    in_rows = na * lanes

    @pl.loop(0, D // in_rows)
    def _(block):
        columns = pl.ds(pl.multiple_of(block * in_rows, 128), in_rows)
        term = dot_rows(entry[0, :frames, columns], d_gate_up[0])
        for slot in range(1, 2 * count):
            term += dot_rows(entry[slot, :frames, columns], d_gate_up[slot])
        branch[1, :in_rows, :] = term.astype(BF16)
        copies = [
            pltpu.make_async_copy(
                branch.at[1, pl.ds(z * lanes, lanes)], grad_in_hbm.at[z, block], out_sem.at[2 + z]
            )
            for z in range(na)
        ]
        copy_all(copies)

    total_here = partial[0].astype(F32)
    for k in range(1, count):
        back_copy(k).wait_recv()
        total_here += fetch(back_hbm.at[k - 1])
    sums[...] = total_here
    move(sums, d_entry_hbm)
    total_here = branch_terms(0)
    for k in range(1, count):
        branch_copy(k).wait_recv()
        total_here += fetch(branch_back_hbm.at[k - 1])
    sums[...] = total_here
    move(sums, branch_hbm)

    entry_copies[1].wait_send()
    for k in range(1, count):
        if k < 3:
            entry_copies[2 * k].wait_send()
            relays[k - 1].wait_send()
        entry_copies[2 * k + 1].wait_send()
        back_copy(k).wait_send()
        branch_copy(k).wait_send()


def ffn_group(entry, notes, cotangent, cotangents, rank_in, rank_down, chips, sizes, na, lanes):
    frames = cotangent.shape[0]
    width = rank_down.shape[0]
    count = len(chips)
    low = lambda *shape: jax.ShapeDtypeStruct(shape, BF16)
    sem = lambda size: pltpu.SemaphoreType.DMA((size,))
    clip = (frames, D)
    return pl.pallas_call(
        functools.partial(ffn_group_kernel, chips=chips, sizes=sizes),
        out_shape=[
            jax.ShapeDtypeStruct(clip, F32),
            low(width, D),
            low(na, D // (na * lanes), lanes, 2 * width),
            jax.ShapeDtypeStruct(clip, F32),
            low(*clip),
            low(count, *clip),
            low(count, *clip),
            low(count - 1, *clip),
            low(count - 1, *clip),
            low(count - 1, *clip),
        ],
        in_specs=[ANY] * 6,
        out_specs=[ANY] * 10,
        scratch_shapes=[
            pltpu.VMEM((2 * count, frames + NOTE_ROWS, D), BF16),
            pltpu.VMEM((2 * count, frames, D), BF16),
            pltpu.VMEM((2 * count, frames, width), BF16),
            pltpu.VMEM((2 * count, frames, 2 * width), BF16),
            pltpu.VMEM((D, 2 * width), BF16),
            pltpu.VMEM((width, D), BF16),
            pltpu.VMEM((count, frames, D), BF16),
            pltpu.VMEM((2, frames, D), BF16),
            pltpu.VMEM((2, frames, D), BF16),
            pltpu.VMEM(clip, BF16),
            pltpu.VMEM(clip, F32),
            sem(4),
            sem(2 * count),
            sem(2 * count),
            sem(2 * count),
            sem(count),
            sem(count),
            sem(count),
            sem(count),
            sem(2),
            sem(2 + na),
            sem(2),
            sem(2),
            sem(count),
            sem(count),
            sem(count),
            sem(count),
        ],
        compiler_params=pltpu.CompilerParams(
            vmem_limit_bytes=60 * 2**20, collective_id=0, has_side_effects=True
        ),
        cost_estimate=LIGHT,
    )(entry, notes, cotangent, cotangents, rank_in, rank_down)


def stack_kernel(*refs):
    out_ref = refs[-1]
    out_ref[...] = jnp.zeros_like(out_ref)
    rows = refs[0].shape[0]
    for k, ref in enumerate(refs[:-1]):
        out_ref[k * rows : (k + 1) * rows, :] = ref[...].astype(BF16)


def stack_vectors(vectors):
    parts = [vector.reshape(-1, 128) for vector in vectors]
    rows = sum(part.shape[0] for part in parts)
    return pl.pallas_call(
        stack_kernel,
        out_shape=jax.ShapeDtypeStruct((rows + -rows % 16, 128), BF16),
        in_specs=[WHOLE] * len(parts),
        out_specs=WHOLE,
        cost_estimate=LIGHT,
    )(*parts)


def total_kernel(sums_ref, out_ref, steps, lines, step_send, step_recv, line_send, line_recv):
    y, c, z, x = (lax.axis_index(axis) for axis in AXES)
    na = lines.shape[0]

    def remote(source, target, send, recv, device):
        return pltpu.make_async_remote_copy(
            src_ref=source,
            dst_ref=target,
            send_sem=send,
            recv_sem=recv,
            device_id=device,
            device_id_type=pl.DeviceIdType.MESH,
        )

    near = [{"c": 1 - c}, {"x": 1 - x}, {"y": 1 - y}]
    far = [{"z": lax.rem(z + k, na)} for k in range(1, na)]
    barrier = pltpu.get_barrier_semaphore()
    for device in near + far:
        pl.semaphore_signal(
            barrier, inc=1, device_id=device, device_id_type=pl.DeviceIdType.MESH
        )
    pl.semaphore_wait(barrier, len(near) + len(far))
    steps[0, 0] = sums_ref[...]
    for k, device in enumerate(near):
        copy = remote(steps.at[k, 0], steps.at[k, 1], step_send.at[k], step_recv.at[k], device)
        copy.start()
        copy.wait()
        both = steps[k, 0] + steps[k, 1]
        if k < 2:
            steps[k + 1, 0] = both
    lines[z] = both
    copies = [
        remote(lines.at[z], lines.at[z], line_send.at[k], line_recv.at[k], device)
        for k, device in enumerate(far)
    ]
    for copy in copies:
        copy.start()
    for copy in copies:
        copy.wait()
    whole = lines[0]
    for k in range(1, na):
        whole = whole + lines[k]
    out_ref[...] = whole


def total_over_devices(sums, na):
    sem = lambda size: pltpu.SemaphoreType.DMA((size,))
    return pl.pallas_call(
        total_kernel,
        out_shape=jax.ShapeDtypeStruct(sums.shape, F32),
        in_specs=[WHOLE],
        out_specs=WHOLE,
        scratch_shapes=[
            pltpu.VMEM((3, 2) + sums.shape, F32),
            pltpu.VMEM((na,) + sums.shape, F32),
            sem(3),
            sem(3),
            sem(na - 1),
            sem(na - 1),
        ],
        compiler_params=pltpu.CompilerParams(collective_id=3, has_side_effects=True),
        cost_estimate=LIGHT,
    )(sums)


def step_kernel(factor_ref, *refs):
    count = len(refs) // 3
    at = 0
    for weight_ref, direction_ref, out_ref in zip(refs[:count], refs[count : 2 * count], refs[2 * count :]):
        if len(weight_ref.shape) == 3:
            for k in range(weight_ref.shape[0]):
                out_ref[k] = weight_ref[k] - factor_ref[at] * direction_ref[k]
                at += 1
        else:
            out_ref[...] = weight_ref[...] - factor_ref[at] * direction_ref[...]
            at += 1


def step_weights(factors, weights, directions):
    return pl.pallas_call(
        step_kernel,
        out_shape=[jax.ShapeDtypeStruct(weight.shape, F32) for weight in weights],
        in_specs=[SCALARS] + [WHOLE] * (2 * len(weights)),
        out_specs=[WHOLE] * len(weights),
        compiler_params=pltpu.CompilerParams(vmem_limit_bytes=56 * 2**20),
        cost_estimate=LIGHT,
    )(factors, *weights, *directions)


def lamb_kernel(spot_ref, weight_ref, first_ref, second_ref, *refs):
    gradient_refs = refs[:-4]
    first_out, second_out, direction_out, sums_ref = refs[-4:]
    gradient = gradient_refs[0][...].astype(F32)
    if len(gradient_refs) == 2:
        ours = pl.program_id(1) % 2 == spot_ref[1]
        gradient = jnp.where(ours, gradient, gradient_refs[1][...].astype(F32))
    weight = weight_ref[...]
    first_new = BETA_ONE * first_ref[...] + (1.0 - BETA_ONE) * gradient
    second_new = BETA_TWO * second_ref[...] + (1.0 - BETA_TWO) * gradient * gradient
    direction = (
        first_new
        / (1.0 - BETA_ONE**STEP)
        / (jnp.sqrt(second_new / (1.0 - BETA_TWO**STEP)) + ADAM_EPS)
        + DECAY * weight
    )
    first_out[...] = first_new
    second_out[...] = second_new
    direction_out[...] = direction

    @pl.when(pl.program_id(1) == 0)
    def _():
        sums_ref[...] = jnp.zeros_like(sums_ref)

    for row, values in enumerate((weight, direction)):
        squares = jnp.sum(values * values, axis=1)
        for start in range(0, squares.shape[1], 128):
            sums_ref[:, row, :] += squares[:, start : start + 128]


def lamb_terms(spot, weight, first_moment, second_moment, gradients, block):
    shape = weight.shape
    arrays = [
        array.reshape((-1,) + array.shape[-2:])
        for array in (weight, first_moment, second_moment, *gradients)
    ]
    groups, rows, cols = arrays[0].shape
    in_blocks = len(gradients) == 1 and arrays[3].shape != arrays[0].shape
    spec = pl.BlockSpec((1, rows, block), lambda i, j: (i, 0, j))
    turns = 2 * HALF // block
    halves = pl.BlockSpec((1, rows, block), lambda i, j: (j // turns, 0, j % turns // 2))
    by_block = pl.BlockSpec((1, rows, block), lambda i, j: (j, 0, 0))
    full = jax.ShapeDtypeStruct((groups, rows, cols), F32)
    out = pl.pallas_call(
        lamb_kernel,
        out_shape=[full, full, full, jax.ShapeDtypeStruct((groups, 8, 128), F32)],
        grid=(groups, cols // block),
        in_specs=[SCALARS]
        + [spec] * 3
        + [by_block if in_blocks else spec if len(gradients) == 1 else halves] * len(gradients),
        out_specs=[spec] * 3 + [pl.BlockSpec((1, 8, 128), lambda i, j: (i, 0, 0))],
        compiler_params=pltpu.CompilerParams(vmem_limit_bytes=40 * 2**20),
        cost_estimate=pl.CostEstimate(
            flops=20 * weight.size, bytes_accessed=28 * weight.size, transcendentals=weight.size
        ),
    )(spot, *arrays)
    return [array.reshape(shape) for array in out[:3]] + [jnp.sum(out[3][:, :2], axis=-1)]


class Grid:
    def __init__(self, mesh):
        self.ny = mesh.shape["dp"] // 2
        self.nb = 2
        self.na = mesh.shape["fsdp"] // 2
        self.sizes = dict(y=self.ny, c=2, z=self.na, x=self.nb)
        self.count = self.ny * 2 * self.na * self.nb
        self.spots = list(itertools.product(*(range(self.sizes[axis]) for axis in AXES)))
        self.peers = list(itertools.product(range(self.ny), range(2), range(self.nb)))
        self.chips = list(itertools.product(range(self.ny), range(self.nb)))
        self.back = [
            (dy, dc, dx)
            for dx in range(self.nb)
            for dy in range(self.ny)
            for dc in range(2)
        ]
        self.mesh = Mesh(mesh.devices.reshape(self.ny, 2, self.na, self.nb), AXES)

    def line(self, y, c, z, x):
        return ((y * 2 + c) * self.na + z) * self.nb + x

    def here(self):
        return {axis: lax.axis_index(axis) for axis in AXES}

    def move(self, array, **steps):
        steps = {axis: step % self.sizes[axis] for axis, step in steps.items()}
        steps = {axis: step for axis, step in steps.items() if step}
        if not steps:
            return array
        names = tuple(axis for axis in AXES if axis in steps)
        lengths = [self.sizes[axis] for axis in names]
        pairs = []
        for spot in itertools.product(*(range(n) for n in lengths)):
            source = target = 0
            for axis, at, n in zip(names, spot, lengths):
                source, target = source * n + at, target * n + (at + steps[axis]) % n
            pairs.append((source, target))
        return lax.ppermute(array, names, pairs)

    def rank(self, mine, offset):
        y, c, x = ((mine[axis] + step) % self.sizes[axis] for axis, step in zip("ycx", offset))
        return (y * 2 + c) * self.nb + x

    def swap(self, array):
        return self.move(array, c=1)

    def gather_small(self, array):
        shape = array.shape
        for axis in "xzcy":
            parts = [self.move(array, **{axis: k}) for k in range(self.sizes[axis])]
            array = jnp.concatenate([part.reshape((-1,) + shape) for part in parts])
        return array

    def scatter_small(self, array):
        sources = [array]
        for axis in "cyxz":
            where = 0
            arrays = []
            size = self.sizes[axis]
            sources = [s.reshape(self.small_shape(axis, s)) for s in sources]
            for k in range(1, size):
                part = total([s[:, k] for s in sources])
                arrays.append(self.move(part, **{axis: -k}))
            sources = [s[:, 0] for s in sources] + arrays
        return total(sources).reshape(array.shape[1:])

    def small_shape(self, axis, array):
        before = {"c": self.ny, "y": 1, "x": self.na, "z": 1}[axis]
        return (before, self.sizes[axis], -1, array.shape[-1])

    def sum_small(self, array):
        bit = 1
        while bit < self.count:
            array = array + lax.ppermute(array, AXES, [(d, d ^ bit) for d in range(self.count)])
            bit *= 2
        return array

    def spread(self, lines, turn):
        held, marks = {(0, 0): lines}, []
        for axis in ("x", "y") if turn else ("y", "x"):
            for (y, x), piece in list(held.items()):
                for k in range(1, self.sizes[axis]):
                    step = dict(y=y, x=x)
                    step[axis] = k
                    held[(step["y"], step["x"])] = self.move(piece, **{axis: k})
            marks = marks or list(held.values())[1:]
        return held, marks

    def gather_weights(self, parts, shapes, mine, spot, first):
        rows = parts[0][0][0].shape[0]
        mixed = jnp.stack([shard for part in parts for shard, *_ in part])
        lines = lax.all_gather(mixed, "z")
        if first:
            (lines,) = after([lines], first)
        start = 0
        held, marks, plan = [], [], dict(parts=[])
        for turn, part in enumerate(parts):
            end = start + len(part)
            pieces, arrived = self.spread(lines[:, start:end], turn)
            held.append(pieces)
            marks += arrived
            start = end
            plan["parts"].append(
                [(out, lane, column, shard.shape[1]) for shard, out, lane, column in part]
            )
        plan["offsets"] = sorted(held[0])
        if rows % 16 == 0:
            arrays = [pieces[offset] for pieces in held for offset in plan["offsets"]]
            copies = len(plan["offsets"]) * sum(len(part) for part in parts)
            kernel = functools.partial(place_pieces, plan=plan, sizes=(self.ny, self.nb))
            return place(kernel, spot, arrays, shapes, copies), marks
        outs = [jnp.zeros(shape, BF16) for shape in shapes]
        for pieces, blocks in zip(held, plan["parts"]):
            for (dy, dx), piece in pieces.items():
                y = (mine["y"] - dy + self.ny) % self.ny
                x = (mine["x"] - dx + self.nb) % self.nb
                for block, (out, lane, column, width) in enumerate(blocks):
                    update = piece[:, block][None, :, None]
                    if lane is None:
                        at = (y, 0, x, 0, column)
                    else:
                        update = update[:, None]
                        at = (y, lane, 0, x, 0, column)
                    outs[out] = lax.dynamic_update_slice(outs[out], update, at)
        return outs, marks

    def swap_ranks(self, blocks):
        shape = blocks.shape[1:]
        blocks = blocks.reshape((self.ny, 2, self.nb) + shape)
        for where, axis in ((1, "c"), (0, "y"), (2, "x")):
            parts = [
                self.move(lax.index_in_dim(blocks, k, where), **{axis: k})
                for k in range(self.sizes[axis])
            ]
            blocks = jnp.concatenate(parts, axis=where)
        return blocks.reshape((-1,) + shape)

    def swap_back(self, blocks, mine):
        for where, axis in ((1, "c"), (1, "y"), (2, "x")):
            parts = [
                self.move(pick(blocks, (mine[axis] + k) % self.sizes[axis], where), **{axis: k})
                for k in range(self.sizes[axis])
            ]
            blocks = jnp.stack(parts)
        return blocks.reshape((-1,) + blocks.shape[-2:])

    def gather_ranks(self, in_parts, down_part, mine, spot):
        peers, rows, width = in_parts.shape
        depth = down_part.shape[0]
        in_shape = (self.ny, 2, self.na, self.nb, rows, width)
        down_shape = (self.na, depth, D)
        if rows % 16 == 0 and width == D:
            mixed = jnp.concatenate([in_parts.reshape(-1, D), down_part])
            lines = lax.all_gather(mixed, "z")
            kernel = functools.partial(
                place_ranks,
                offsets=self.peers,
                sizes=(self.ny, self.na, self.nb),
                rows=rows,
                depth=depth,
            )
            rank_in, rank_down = place(kernel, spot, [lines], [in_shape, down_shape], peers + 1)
        else:
            rank_down = lax.all_gather(down_part, "z")
            lines = lax.all_gather(in_parts, "z")
            rank_in = jnp.zeros(in_shape, BF16)
            for k, (dy, dc, dx) in enumerate(self.peers):
                at = ((mine["y"] - dy) % self.ny, (mine["c"] + dc) % 2, 0, (mine["x"] - dx) % self.nb, 0, 0)
                rank_in = lax.dynamic_update_slice(rank_in, lines[:, k][None, None, :, None], at)
        return rank_in.reshape(-1, width), rank_down.reshape(-1, D)

    def join_columns(self, pieces, mine, spot):
        peers, rows, width = pieces.shape
        width = width // 2
        if rows % 16 == 0:
            kernel = functools.partial(
                place_columns, offsets=self.back, sizes=(self.ny, self.nb), width=width
            )
            return place(kernel, spot, [pieces], [(rows, 2 * FF)], 2 * peers)[0]
        out = jnp.zeros((rows, 2, FF), BF16)
        for k, (dy, dc, dx) in enumerate(self.back):
            y, x = (mine["y"] - dy) % self.ny, (mine["x"] - dx) % self.nb
            rank = (y * 2 + (mine["c"] + dc) % 2) * self.nb + x
            piece = pieces[k].reshape(rows, 2, width)
            out = lax.dynamic_update_slice(out, piece, (0, 0, rank * width))
        return out.reshape(rows, 2 * FF)

    def fold(self, array, names, turn, mine, between=(), behind=(), marks=None):
        names = list(names)
        sources = [array]
        for axis, waits in zip("yx" if turn else "xy", (between, behind)):
            where = names.index(axis)
            size = self.sizes[axis]
            arrived = []
            for k in range(1, size):
                away = total([pick(s, (mine[axis] + k) % size, where) for s in sources])
                arrived.append(self.move(away.astype(BF16), **{axis: k}))
            if waits:
                arrived = after(arrived, waits)
            if marks is not None and len(names) > len(array.shape) - 3:
                marks += arrived
            sources = [pick(s, mine[axis], where) for s in sources] + list(arrived)
            names.remove(axis)
        return total(sources).astype(BF16)

    def to_rank(self, array, back=False):
        pairs = []
        for d in range(self.count):
            rank, z = divmod(d, self.na)
            y, c, x = self.peers[rank]
            pairs.append((d, self.line(y, c, z, x)))
        if back:
            pairs = [(b, a) for a, b in pairs]
        return lax.ppermute(array, AXES, pairs)


def lamb_small(weight, first_moment, second_moment, gradient):
    first_new = BETA_ONE * first_moment + (1.0 - BETA_ONE) * gradient
    second_new = BETA_TWO * second_moment + (1.0 - BETA_TWO) * gradient * gradient
    direction = (
        first_new
        / (1.0 - BETA_ONE**STEP)
        / (jnp.sqrt(second_new / (1.0 - BETA_TWO**STEP)) + ADAM_EPS)
        + DECAY * weight
    )
    sums = jnp.stack([jnp.sum(weight * weight), jnp.sum(direction * direction)])
    return [first_new, second_new, direction, sums[None]]


def shards(
    grid,
    latents,
    context,
    timestep,
    lengths,
    cotangent,
    mod_matrix,
    mod_first,
    mod_second,
    qkv_matrix,
    qkv_first,
    qkv_second,
    square_set,
    square_first,
    square_second,
    ctx_matrix,
    ctx_first,
    ctx_second,
    ff_in,
    in_first,
    in_second,
    ff_down,
    down_first,
    down_second,
    norm_gains,
    gains_first,
    gains_second,
):
    mine = grid.here()
    core = mine["c"]
    spot = jnp.stack([mine[axis] for axis in AXES]).astype(jnp.int32)
    device = grid.line(*(mine[axis] for axis in AXES))
    count, ranks = grid.count, len(grid.peers)
    rows = mod_matrix.shape[0]
    frames = latents.shape[1]
    words = context.shape[1]
    valid = lengths[0]
    keep_rows = (jnp.arange(frames) < valid).astype(F32)[:, None]

    width = FF // ranks
    if rows % 16 == 0 and D // (2 * grid.ny) % 128 == 0:
        prepare = functools.partial(prepare_kernel, offsets=grid.peers, sizes=(grid.ny, grid.nb))
        five = (5, rows, HALF)
        five_own, five_other, wide_low, in_blocks = pl.pallas_call(
            prepare,
            out_shape=[
                jax.ShapeDtypeStruct(shape, BF16)
                for shape in (five, five, (4, rows, HALF), (ranks, rows, 2 * width))
            ],
            in_specs=[SCALARS] + [WHOLE] * 4,
            out_specs=[WHOLE] * 4,
            compiler_params=pltpu.CompilerParams(vmem_limit_bytes=40 * 2**20),
        )(spot, qkv_matrix, square_set, ctx_matrix, ff_in)
    else:
        five = [qkv_matrix[:, k * D : (k + 1) * D] for k in range(3)] + [
            square_set[1],
            jnp.concatenate([ctx_matrix[:, :D], ctx_matrix[:, D:]]),
        ]
        five = jnp.stack(five).astype(BF16).reshape(5, rows, grid.ny, 2, -1)
        five_own = pick(five, core, 3).reshape(5, rows, HALF)
        five_other = pick(five, 1 - core, 3).reshape(5, rows, HALF)
        wide_low = jnp.stack(
            [square_set[k, :, side * HALF : (side + 1) * HALF] for k in (0, 2) for side in range(2)]
        ).astype(BF16)
        in_halves = ff_in.reshape(rows, 2, FF)
        in_blocks = jnp.stack(
            [
                lax.dynamic_slice(in_halves, (0, 0, grid.rank(mine, offset) * width), (rows, 2, width))
                for offset in grid.peers
            ]
        ).astype(BF16).reshape(ranks, rows, 2 * width)
    five_other = grid.swap(five_other)
    five_low = jnp.where(core == 0, five_own, five_other)
    five_high = jnp.where(core == 0, five_other, five_own)
    lifted = jax.nn.silu(timestep[0].astype(F32)).astype(BF16)
    notes = jnp.concatenate([lifted, norm_gains.astype(BF16).reshape(-1)])
    (notes,) = after([notes], (five_other,))
    notes = grid.gather_small(notes)
    origin = []
    for spot_of in grid.spots:
        source = [
            (mine[axis] - step) % grid.sizes[axis] for axis, step in zip(AXES, spot_of)
        ]
        origin.append(grid.line(*source))
    origin = jnp.stack(origin)
    sorter = (jnp.arange(count)[:, None] == origin[None, :]).astype(BF16)
    gain_rows = dot(sorter, notes[:, D:])
    gain_rows = gain_rows.reshape(count, 3, rows).transpose(1, 0, 2).reshape(3, D)
    lifted_own = lax.dynamic_slice(notes, (0, device * rows), (count, rows))
    shift_terms = dot(lifted_own, mod_matrix.astype(BF16))
    grouped = rows % 16 == 0 and grid.ny == 2 and grid.nb == 2
    cotangent_own = (cotangent[0].astype(F32) * keep_rows).astype(BF16)
    if grouped:
        shift_terms = shift_terms.reshape(grid.ny, 2, grid.na, grid.nb, 6 * D // 128, 128)
        blocks = in_blocks.reshape(grid.ny, 2, grid.nb, rows, 2 * width)
        shifts, cotangents, in_parts = sum_shifts(shift_terms, cotangent_own, blocks, grid.na)
        in_parts = in_parts.reshape(ranks, rows, 2 * width)
        shifts = shifts.reshape(6, D)
    else:
        shifts = grid.scatter_small(shift_terms).reshape(6, D)
        in_parts = grid.swap_ranks(in_blocks)

    tall = (grid.ny, 2, grid.na, grid.nb, rows)
    wide = (grid.ny, grid.na, grid.nb, rows, D)
    both = lambda k, out, at: [(five_low[k], out, 0, at), (five_high[k], out, 1, at)]
    sides = lambda k, out: [
        (wide_low[2 * k], out, None, 0),
        (wide_low[2 * k + 1], out, None, HALF),
    ]
    first = both(0, 0, 0) + both(1, 0, HALF) + both(2, 0, 2 * HALF)
    (down_low,) = after([ff_down.astype(BF16)], (shifts,))
    down_part = grid.to_rank(down_low)
    (matrix_qkv,), marks = grid.gather_weights(
        [first[:3], first[3:]], [tall + (3 * HALF,)], mine, spot, (shifts,)
    )
    (down_part,) = after([down_part], (*marks, matrix_qkv))
    matrix_qkv = matrix_qkv.reshape(D, 3 * HALF)
    (matrix_out, matrix_query), marks = grid.gather_weights(
        [sides(0, 0), both(3, 1, 0)], [wide, tall + (HALF,)], mine, spot, marks
    )
    (matrix_ctx, matrix_cross), marks = grid.gather_weights(
        [both(4, 0, 0), sides(1, 1)], [tall + (HALF,), wide], mine, spot, marks
    )
    matrix_out, matrix_cross = matrix_out.reshape(HALF, D), matrix_cross.reshape(HALF, D)
    matrix_query, matrix_ctx = matrix_query.reshape(D, HALF), matrix_ctx.reshape(D, HALF)

    rank_in, rank_down = grid.gather_ranks(in_parts, down_part, mine, spot)

    pair_lengths = jnp.concatenate([lengths, grid.swap(lengths)])
    all_words = jnp.full((2,), words, jnp.int32)
    text = jnp.concatenate([context[0], grid.swap(context[0])])
    stream = latents[0].astype(F32)
    normed_one, inverse_one = norm_rows(stream)
    entry_attn = (normed_one * gain_rows[0] * (1.0 + shifts[1]) + shifts[0]).astype(BF16)
    d_result = cotangent[0].astype(F32) * keep_rows

    columns = HALF // PAIR
    entry_pair = [entry_attn, grid.swap(entry_attn)]
    qkv = pair_in(*entry_pair, matrix_qkv, dot)
    self_parts = tuple((qkv, frames, 0, k * columns) for k in range(3))
    mixture_attn = attend(pair_lengths, *self_parts)
    own, away = pair_out([mixture_attn], matrix_out, dot)
    branch_attn = own + grid.swap(away).astype(F32)
    after_attn = stream + shifts[2] * branch_attn
    normed_two, inverse_two = norm_rows(after_attn)
    entry_cross = (normed_two * gain_rows[1]).astype(BF16)
    cross_pair = [entry_cross, grid.swap(entry_cross)]
    query_cross = pair_in(*cross_pair, matrix_query, dot)
    blank = jnp.zeros((2 * words, count, rows // 2), BF16)
    text_cut = text.reshape(2 * words, count, rows // 2)
    text_key = jnp.concatenate([text_cut, blank], axis=-1).reshape(2 * words, -1)
    text_value = jnp.concatenate([blank, text_cut], axis=-1).reshape(2 * words, -1)
    text_both = jnp.concatenate([text_key, text_value])
    kv_cross = dot(text_both, matrix_ctx).astype(BF16)
    cross_parts = ((query_cross, frames, 0, 0), (kv_cross, words, 0, 0), (kv_cross, words, 2, 0))
    mixture_cross = attend(all_words, *cross_parts)
    own, away = pair_out([mixture_cross], matrix_cross, dot)
    branch_cross = own + grid.swap(away).astype(F32)
    after_cross = after_attn + branch_cross
    normed_three, inverse_three = norm_rows(after_cross)
    entry_ffn = (normed_three * gain_rows[2] * (1.0 + shifts[4]) + shifts[3]).astype(BF16)

    notes = gate_notes(shifts[5])
    whole = lambda array: (array, array.shape[1], 0)
    chips = grid.chips
    if grouped:
        d_entry_ffn, grad_down, grad_in, branch_ffn, *_ = ffn_group(
            entry_ffn, notes, cotangent_own, cotangents, rank_in, rank_down,
            chips, (grid.ny, grid.nb), grid.na, grid.nb * rows,
        )
        grad_in = grad_in.reshape(-1, 2 * width)
    else:
        entry_ext = jnp.concatenate([entry_ffn, notes])
        cot_arrived = [grid.move(cotangent_own, y=y, x=x) for y, x in grid.chips]
        (entry_ext,) = after([entry_ext], cot_arrived[1:])
        arrived = [grid.move(entry_ext, y=y, x=x) for y, x in grid.chips]
        entry_parts, hidden_parts, d_gate_up_parts, d_branch_parts = [], [], [], []
        d_entry_sources, folded_rows, branch_own, branch_away = [], [], [], []
        for k, (y, x) in enumerate(grid.chips):
            own_entry, own_cot = arrived[k], cot_arrived[k]
            if k in (1, 2):
                own_entry, own_cot = after([own_entry, own_cot], hidden_parts[:1])
            elif k > 2:
                own_entry, own_cot = after([own_entry, own_cot], folded_rows[k - 2 : k - 1])
            entries = [own_entry, grid.swap(own_entry)]
            hidden, d_gate_up, d_branch, own, other = ffn_both_ways(
                entries, [own_cot, grid.swap(own_cot)], rank_in, rank_down
            )
            other = grid.swap(other)
            folded_rows.append(total([own[0], other[0]]).astype(BF16))
            if k:
                d_entry_sources.append(grid.move(folded_rows[k], y=-y, x=-x))
                branch_away.append(total([own[1], other[1]]).astype(BF16))
            else:
                d_entry_sources += [own[0], other[0]]
                branch_own += [own[1], other[1]]
            entry_parts += entries
            hidden_parts.append(hidden)
            d_gate_up_parts.append(d_gate_up)
            d_branch_parts.append(d_branch)
        hidden_parts[:1] = after(hidden_parts[:1], folded_rows[-2:-1])
        grad_down = outer_sum(
            hidden_parts, [[whole(a) for a in d_branch_parts]], frames, 256 if width % 256 == 0 else 128
        ).reshape(width, D)
        d_gate_up_parts[:1] = after(d_gate_up_parts[:1], folded_rows[-1:])
        in_group = [[whole(a) for a in d_gate_up_parts]]
        if rows % 16 == 0:
            grad_in = outer_sum(
                entry_parts, in_group, frames, D // (2 * grid.ny), grid.nb * rows
            )
        else:
            grad_in = outer_sum(entry_parts, in_group, frames, D // 4)
            grad_in = grad_in.reshape(2 * grid.ny, grid.na, grid.nb * rows, 2 * width)
            grad_in = jnp.swapaxes(grad_in, 0, 1)
        grad_in = grad_in.reshape(-1, 2 * width)
        d_entry_ffn = total(after(d_entry_sources, (grad_down, grad_in)))
        branch_arrived = [
            grid.move(away, y=-y, x=-x) for away, (y, x) in zip(branch_away, chips[1:])
        ]
        branch_ffn = total(branch_own + branch_arrived)
    grad_in = lax.psum_scatter(grad_in, "z", tiled=True)

    d_gain_ffn = jnp.sum(d_entry_ffn * normed_three * (1.0 + shifts[4]), axis=0)
    d_scale_ffn = jnp.sum(d_entry_ffn * normed_three * gain_rows[2], axis=0)
    d_shift_ffn = jnp.sum(d_entry_ffn, axis=0)
    d_after_cross = d_result + norm_back(
        d_entry_ffn * gain_rows[2] * (1.0 + shifts[4]), normed_three, inverse_three
    )

    def join(own, other):
        lead = own.shape[:-1]
        shape = lead + (grid.ny, 1, D // (2 * grid.ny))
        own, other = own.reshape(shape), other.reshape(shape)
        low = jnp.where(core == 0, own, other)
        high = jnp.where(core == 0, other, own)
        return jnp.concatenate([low, high], axis=-2).reshape(lead + (D,))

    d_branch_cross = d_after_cross.astype(BF16)
    d_cross_pair = [d_branch_cross, grid.swap(d_branch_cross)]
    d_mixture_cross = pair_in(*d_cross_pair, matrix_cross, dot_back)
    d_query_cross, d_key_cross, d_value_cross = attend_back(
        all_words, *cross_parts, d_mixture_cross
    )
    own, away = pair_out([d_query_cross], matrix_query, dot_back)
    d_entry_cross = own + grid.swap(away).astype(F32)
    d_gain_cross = jnp.sum(d_entry_cross * normed_two, axis=0)
    d_after_attn = d_after_cross + norm_back(d_entry_cross * gain_rows[1], normed_two, inverse_two)
    d_branch_attn = (d_after_attn * shifts[2]).astype(BF16)
    d_attn_pair = [d_branch_attn, grid.swap(d_branch_attn)]
    d_gate_attn = jnp.sum(d_after_attn * branch_attn, axis=0)
    d_mixture_attn = pair_in(*d_attn_pair, matrix_out, dot_back)
    d_queries, d_keys, d_values = attend_back(pair_lengths, *self_parts, d_mixture_attn)
    own, away = pair_out([d_queries, d_keys, d_values], matrix_qkv, dot_back)
    d_entry_attn = own + grid.swap(away).astype(F32)
    d_gain_attn = jnp.sum(d_entry_attn * normed_one * (1.0 + shifts[1]), axis=0)
    d_scale_attn = jnp.sum(d_entry_attn * normed_one * gain_rows[0], axis=0)
    d_shift_attn = jnp.sum(d_entry_attn, axis=0)
    d_latents = d_after_attn + norm_back(
        d_entry_attn * gain_rows[0] * (1.0 + shifts[1]), normed_one, inverse_one
    )


    d_gate_ffn = jnp.sum(d_result * branch_ffn, axis=0)
    result = after_cross + shifts[5] * branch_ffn
    branches = (result, shifts[2] * branch_attn, branch_cross, shifts[5] * branch_ffn)
    stream_terms = jnp.stack([jnp.sum(keep_rows * branch * branch) for branch in branches])
    vectors = [
        d_shift_attn,
        d_scale_attn,
        d_gate_attn,
        d_shift_ffn,
        d_scale_ffn,
        d_gate_ffn,
        d_gain_attn,
        d_gain_cross,
        d_gain_ffn,
    ]
    small = stack_vectors(vectors)

    beside = lambda halves: jnp.concatenate([halves[0], halves[1]], axis=1)
    if grouped:
        reduced, small, grad_in, grad_down, _ = reduce_group(
            [
                ("wide", [mixture_cross], d_cross_pair, 0),
                ("tall", cross_pair, [d_query_cross], 1),
                ("tall", [text_both], [d_key_cross, d_value_cross], 0),
                ("wide", [mixture_attn], d_attn_pair, 1),
                ("tall", entry_pair, [d_queries], 0),
                ("tall", entry_pair, [d_keys], 1),
                ("tall", entry_pair, [d_values], 0),
            ],
            small, grad_in.reshape(grid.ny, 2, grid.nb, rows, 2 * width),
            grad_down.reshape(grid.na, -1, D), grid.na, rows,
        )
        small = small.reshape(count, -1, 128)[:, : 9 * D // 128].reshape(count, 9, D)
        grad_cross, grad_out = beside(reduced[0]), beside(reduced[3])
        grad_query, grad_ctx = (join(reduced[k, 0], reduced[k, 1]) for k in (1, 2))
        qkv_parts = [reduced[4:, 0], reduced[4:, 1]]
        turn_width = D // (2 * grid.ny)
    else:
        grad_down = lax.psum_scatter(grad_down, "z", tiled=True)
        grad_in = grid.swap_back(grad_in.reshape(grid.ny, 2, grid.nb, rows, 2 * width), mine)
        grad_in = grid.join_columns(grad_in, mine, spot)
        small = grid.gather_small(small[: 9 * D // 128].reshape(9, D))
        block = D // (2 * grid.ny)

        def reduce(lefts, right, piece, halves=1):
            groups = [[whole(array) for array in right]]
            gradient = outer_sum(lefts, groups, piece, block, None, halves)
            gradient = grid.fold(gradient.reshape(tall + (-1,)), "yczx", 0, mine)
            return lax.psum_scatter(jnp.swapaxes(gradient, 0, 1), "z")

        def reduce_tall(lefts, right, piece):
            sums = reduce(lefts, right, piece)
            return join(pick(sums, core, 0), grid.swap(pick(sums, 1 - core, 0)))

        grad_cross = beside(reduce([mixture_cross], d_cross_pair, frames, 2))
        grad_out = beside(reduce([mixture_attn], d_attn_pair, frames, 2))
        grad_query = reduce_tall(cross_pair, [d_query_cross], frames)
        grad_ctx = reduce_tall([text_both], [d_key_cross, d_value_cross], 2 * words)
        qkv_parts = [
            jnp.concatenate(
                [reduce_tall(entry_pair, [d], frames) for d in (d_queries, d_keys, d_values)],
                axis=1,
            )
        ]
        turn_width = D
    grad_ctx = jnp.concatenate([grad_ctx[: rows // 2], grad_ctx[rows // 2 :]], axis=1)
    grad_square = jnp.stack([grad_out, grad_query, grad_cross])
    grad_mod = jnp.einsum("nd,nkm->kdm", lifted_own, small[:, :6], preferred_element_type=F32)
    gain_sums = jnp.sum(small[:, 6:].astype(F32), axis=0)
    grad_gains = lax.dynamic_slice(gain_sums, (0, device * rows), (3, rows))
    grad_down = grid.to_rank(grad_down, back=True)

    lamb = functools.partial(lamb_terms, spot)
    done = {}
    done["qkv"] = lamb(qkv_matrix, qkv_first, qkv_second, qkv_parts, turn_width)
    done["mod"] = lamb(mod_matrix, mod_first, mod_second, [grad_mod], D)
    done["square"] = lamb(square_set, square_first, square_second, [grad_square], HALF)
    done["ctx"] = lamb(ctx_matrix, ctx_first, ctx_second, [grad_ctx], D)
    done["down"] = lamb(ff_down, down_first, down_second, [grad_down], 256)
    done["in"] = lamb(ff_in, in_first, in_second, [grad_in], 1024)
    done["gains"] = lamb_small(norm_gains, gains_first, gains_second, grad_gains)
    names = ("mod", "qkv", "square", "ctx", "in", "down", "gains")
    sums = [done[name][3] for name in names]
    sums.append(jnp.stack([stream_terms, jnp.sum(lengths) * jnp.ones(4)]).T)
    sums = jnp.concatenate(sums)
    if grouped:
        wanted = sums.shape
        sums = jnp.pad(sums, ((0, -wanted[0] % 8), (0, 128 - wanted[1])))
        sums = total_over_devices(sums, grid.na)[: wanted[0], : wanted[1]]
    else:
        sums = grid.sum_small(sums)
    norms = jnp.sqrt(sums[:9])
    weight_norms, update_norms = norms[:, 0], norms[:, 1]
    stream_rms = jnp.sqrt(sums[9:, 0] / (sums[9:, 1] * D))
    factors = RATE * (weight_norms / update_norms)
    masters = [mod_matrix, qkv_matrix, square_set, ctx_matrix, ff_in, ff_down, norm_gains]
    weights_new = step_weights(factors, masters, [done[name][2] for name in names])
    outputs = [result.astype(BF16)[None], d_latents.astype(BF16)[None]]
    for name, weight_new in zip(names, weights_new):
        outputs += [weight_new, done[name][0], done[name][1]]
    outputs.append(weight_norms)
    outputs.append(update_norms)
    outputs.append(stream_rms)
    return tuple(outputs)


def solution(mesh):
    grid = Grid(mesh)
    clip = P(AXES, None, None)
    row = P(AXES, None)
    square = P(None, AXES, None)
    gains = P(None, AXES)
    weights = (row,) * 6 + (square,) * 3 + (row,) * 9 + (gains,) * 3
    in_specs = (clip, clip, row, P(AXES), clip) + weights
    out_specs = (clip, clip) + weights + (P(), P(), P())
    return jax.shard_map(
        functools.partial(shards, grid),
        mesh=grid.mesh,
        in_specs=in_specs,
        out_specs=out_specs,
        check_vma=False,
    )
```

```python
import functools
import itertools

import jax
import jax.numpy as jnp
from jax import lax
from jax.experimental import pallas as pl
from jax.experimental.pallas import tpu as pltpu
from jax.sharding import Mesh, PartitionSpec as P

D = 1536
HEAD_DIM = 64
FF = 6144
STEP = 10


NORM_EPS = 1e-05
BETA_ONE = 0.9
BETA_TWO = 0.999
ADAM_EPS = 1e-06
DECAY = 0.01
RATE = 0.5
SCALE = 0.125

AXES = ("y", "c", "z", "x")
HALF = D // 2
PAIR = 2 * HEAD_DIM
BF16 = jnp.bfloat16
F32 = jnp.float32
ANY = pl.BlockSpec(memory_space=pl.ANY)
WHOLE = pl.BlockSpec(memory_space=pltpu.VMEM)
SCALARS = pl.BlockSpec(memory_space=pltpu.SMEM)
LIGHT = pl.CostEstimate(flops=2**20, bytes_accessed=2**20, transcendentals=0)


def norm_rows(matrix):
    centred = matrix - jnp.mean(matrix, axis=-1, keepdims=True)
    inverse = lax.rsqrt(jnp.mean(centred * centred, axis=-1, keepdims=True) + NORM_EPS)
    return (centred * inverse, inverse)


def norm_back(gradient, normed, inverse):
    return inverse * (
        gradient
        - jnp.mean(gradient, axis=-1, keepdims=True)
        - normed * jnp.mean(gradient * normed, axis=-1, keepdims=True)
    )


def dot(first, second):
    return jnp.dot(first, second, preferred_element_type=F32)


def dot_back(first, second):
    return lax.dot_general(first, second, (((1,), (1,)), ((), ())), preferred_element_type=F32)


def dot_rows(first, second):
    return lax.dot_general(first, second, (((0,), (0,)), ((), ())), preferred_element_type=F32)


def pick(array, index, axis):
    return lax.dynamic_index_in_dim(array, index, axis, keepdims=False)


def no_work(*refs):
    pass


def after(values, others):
    values = list(values)
    return pl.pallas_call(
        no_work,
        out_shape=[jax.ShapeDtypeStruct(value.shape, value.dtype) for value in values],
        in_specs=[ANY] * (len(values) + len(others)),
        out_specs=[ANY] * len(values),
        input_output_aliases={k: k for k in range(len(values))},
    )(*values, *others)


def total(terms):
    return sum(term.astype(F32) for term in terms)


def only(block, head):
    lane = lax.broadcasted_iota(jnp.int32, block.shape, 1)
    mine = lane < HEAD_DIM if head == 0 else lane >= HEAD_DIM
    return jnp.where(mine, block, jnp.zeros_like(block))


def both_heads(first, second):
    lane = lax.broadcasted_iota(jnp.int32, first.shape, 1)
    return jnp.where(lane < HEAD_DIM, first, second)


def attend_heads(valid, query, key, value):
    mixed = []
    for head in range(2):
        scores = dot_back(only(query, head), key) * SCALE
        column = lax.broadcasted_iota(jnp.int32, scores.shape, 1)
        scores = jnp.where(column < valid, scores, -1e30)
        powers = jnp.exp(scores - jnp.max(scores, axis=-1, keepdims=True))
        chances = (powers / jnp.sum(powers, axis=-1, keepdims=True)).astype(BF16)
        mixed.append(dot(chances, value))
    return both_heads(*mixed).astype(BF16)


def attend_kernel(valid_ref, query_ref, key_ref, value_ref, out_ref):
    valid = valid_ref[pl.program_id(0)]
    out_ref[...] = attend_heads(valid, query_ref[...], key_ref[...], value_ref[...])


def attend_back_kernel(
    valid_ref, query_ref, key_ref, value_ref, d_ref, d_query_ref, d_key_ref, d_value_ref
):
    valid = valid_ref[pl.program_id(0)]
    query, key, value, d_mix = query_ref[...], key_ref[...], value_ref[...], d_ref[...]
    parts = []
    for head in range(2):
        scores = dot_back(only(key, head), query) * SCALE
        row = lax.broadcasted_iota(jnp.int32, scores.shape, 0)
        scores = jnp.where(row < valid, scores, -1e30)
        powers = jnp.exp(scores - jnp.max(scores, axis=0, keepdims=True))
        chances = powers / jnp.sum(powers, axis=0, keepdims=True)
        d_chances = dot_back(only(value, head), d_mix)
        mean = jnp.sum(chances * d_chances, axis=0, keepdims=True)
        d_scores = (chances * (d_chances - mean)).astype(BF16)
        d_value = dot(chances.astype(BF16), d_mix)
        d_key = dot(d_scores, query) * SCALE
        d_query = dot_rows(d_scores, key) * SCALE
        parts.append((d_query, d_key, d_value))
    for out_ref, first, second in zip((d_query_ref, d_key_ref, d_value_ref), *parts):
        out_ref[...] = both_heads(first, second).astype(BF16)


def block_of(rows, row_shift, column_shift):
    return pl.BlockSpec((rows, PAIR), lambda b, j: (b + row_shift, j + column_shift))


def attend(valid, query, key, value):
    frames, words = query[1], key[1]
    pairs = HALF // PAIR
    return pl.pallas_call(
        attend_kernel,
        out_shape=jax.ShapeDtypeStruct((2 * frames, HALF), BF16),
        grid=(2, pairs),
        in_specs=[SCALARS] + [block_of(*part[1:]) for part in (query, key, value)],
        out_specs=block_of(frames, 0, 0),
        compiler_params=pltpu.CompilerParams(vmem_limit_bytes=32 * 2**20),
        cost_estimate=LIGHT,
    )(valid, query[0], key[0], value[0])


def attend_back(valid, query, key, value, d_mixture):
    frames, words = query[1], key[1]
    pairs = HALF // PAIR
    return pl.pallas_call(
        attend_back_kernel,
        out_shape=[
            jax.ShapeDtypeStruct((2 * rows, HALF), BF16) for rows in (frames, words, words)
        ],
        grid=(2, pairs),
        in_specs=[SCALARS]
        + [block_of(*part[1:]) for part in (query, key, value)]
        + [block_of(frames, 0, 0)],
        out_specs=[block_of(rows, 0, 0) for rows in (frames, words, words)],
        compiler_params=pltpu.CompilerParams(vmem_limit_bytes=48 * 2**20),
        cost_estimate=LIGHT,
    )(valid, query[0], key[0], value[0], d_mixture)


def copy_all(copies):
    for copy in copies:
        copy.start()
    for copy in copies:
        copy.wait()


def place_pieces(spot_ref, *refs, plan, sizes):
    ny, nb = sizes
    count = len(plan["offsets"]) * len(plan["parts"])
    pieces, sem = refs[:count], refs[-1]
    outs = refs[-1 - plan["outs"] : -1]
    y, x = spot_ref[0], spot_ref[3]
    copies = []
    for part, blocks in enumerate(plan["parts"]):
        for spot, (dy, dx) in enumerate(plan["offsets"]):
            from_y = lax.rem(y - dy + ny, ny)
            from_x = lax.rem(x - dx + nb, nb)
            piece = pieces[part * len(plan["offsets"]) + spot]
            for block, (out, lane, column, width) in enumerate(blocks):
                columns = pl.ds(column, width)
                if lane is None:
                    target = outs[out].at[from_y, :, from_x, :, columns]
                else:
                    target = outs[out].at[from_y, lane, :, from_x, :, columns]
                copies.append(
                    pltpu.make_async_copy(piece.at[:, block], target, sem.at[len(copies)])
                )
    copy_all(copies)


def place_ranks(spot_ref, lines_ref, in_ref, down_ref, sem, *, offsets, sizes, rows, depth):
    ny, na, nb = sizes
    y, c, x = spot_ref[0], spot_ref[1], spot_ref[3]
    copies = []
    for block, (dy, dc, dx) in enumerate(offsets):
        target = in_ref.at[
            lax.rem(y - dy + ny, ny), lax.rem(c + dc, 2), :, lax.rem(x - dx + nb, nb)
        ]
        source = lines_ref.at[:, pl.ds(block * rows, rows)]
        copies.append(pltpu.make_async_copy(source, target, sem.at[len(copies)]))
    source = lines_ref.at[:, pl.ds(len(offsets) * rows, depth)]
    copies.append(pltpu.make_async_copy(source, down_ref, sem.at[len(copies)]))
    copy_all(copies)


def place_columns(spot_ref, pieces_ref, out_ref, sem, *, offsets, sizes, width):
    ny, nb = sizes
    y, c, x = spot_ref[0], spot_ref[1], spot_ref[3]
    copies = []
    for k, (dy, dc, dx) in enumerate(offsets):
        rank = (lax.rem(y - dy + ny, ny) * 2 + lax.rem(c + dc, 2)) * nb + lax.rem(x - dx + nb, nb)
        for half in range(2):
            start = pl.multiple_of(half * FF + rank * width, 128)
            copies.append(
                pltpu.make_async_copy(
                    pieces_ref.at[k, :, pl.ds(half * width, width)],
                    out_ref.at[:, pl.ds(start, width)],
                    sem.at[len(copies)],
                )
            )
    copy_all(copies)


def place(kernel, spot, arrays, shapes, copies):
    size = sum(a.size * a.dtype.itemsize for a in arrays)
    return pl.pallas_call(
        kernel,
        out_shape=[jax.ShapeDtypeStruct(shape, BF16) for shape in shapes],
        in_specs=[SCALARS] + [ANY] * len(arrays),
        out_specs=[WHOLE] * len(shapes),
        scratch_shapes=[pltpu.SemaphoreType.DMA((copies,))],
        compiler_params=pltpu.CompilerParams(vmem_limit_bytes=40 * 2**20),
        cost_estimate=pl.CostEstimate(flops=0, bytes_accessed=2 * size, transcendentals=0),
    )(spot, *arrays)


def prepare_kernel(
    spot_ref, qkv_ref, square_ref, ctx_ref, in_ref, own_ref, other_ref, wide_ref, block_ref,
    *, offsets, sizes
):
    ny, na, nb = sizes
    y, c, x = spot_ref[0], spot_ref[1], spot_ref[3]
    part = D // (2 * ny)
    for out_ref, which in ((own_ref, c), (other_ref, 1 - c)):
        for k in range(5):
            for block in range(ny):
                start = block * 2 * part + which * part
                if k < 3:
                    values = qkv_ref[:, pl.ds(pl.multiple_of(k * D + start, part), part)]
                elif k == 3:
                    values = square_ref[1, :, pl.ds(pl.multiple_of(start, part), part)]
                else:
                    values = jnp.concatenate(
                        [
                            ctx_ref[:, pl.ds(pl.multiple_of(side * D + start, part), part)]
                            for side in range(2)
                        ]
                    )
                out_ref[k, :, block * part : (block + 1) * part] = values.astype(BF16)
    for k, matrix in enumerate((0, 2)):
        for side in range(2):
            values = square_ref[matrix, :, side * HALF : (side + 1) * HALF]
            wide_ref[2 * k + side] = values.astype(BF16)
    width = FF // len(offsets)
    share = width // na
    for k, (dy, dc, dx) in enumerate(offsets):
        rank = lax.rem(y + dy, ny) * 2 + lax.rem(c + dc, 2)
        first = lax.rem(x + dx, nb) == 0
        for side in range(2):
            for z in range(na):
                start = pl.multiple_of(side * FF + (rank * na + z) * nb * share, 128)
                values = in_ref[:, pl.ds(start, nb * share)].astype(BF16)
                values = jnp.where(first, values[:, :share], values[:, share:])
                at = side * width + z * share
                block_ref[k, :, at : at + share] = values


BLOCKS = [(0, lane, k * HALF) for k in range(3) for lane in range(2)]
BLOCKS += [(1, None, 0), (1, None, HALF), (2, 0, 0), (2, 1, 0)]
BLOCKS += [(3, 0, 0), (3, 1, 0), (4, None, 0), (4, None, HALF)]
ACROSS = (0, 1, 2, 6, 7, 10, 11)


def gather_kernel(
    valid_ref, own_hbm, other_hbm, lines_hbm,
    mixture_ref, qkv_ref, *refs,
):
    outs, arrays = refs[:5], refs[5:10]
    entry, x_send, x_recv, y_send, y_recv, on_send, on_recv, own_sem, load_sem, out_sem = refs[10:]
    y, x = lax.axis_index("y"), lax.axis_index("x")
    far_y, far_x = 1 - y, 1 - x
    frames = entry.shape[1]

    def place_of(block, at_y, at_x):
        array, lane, column = BLOCKS[block]
        columns = pl.ds(column, HALF)
        if lane is None:
            return arrays[array].at[at_y, :, at_x, :, columns]
        return arrays[array].at[at_y, lane, :, at_x, :, columns]

    def remote(source, target, send, recv, device):
        return pltpu.make_async_remote_copy(
            src_ref=source,
            dst_ref=target,
            send_sem=send,
            recv_sem=recv,
            device_id=device,
            device_id_type=pl.DeviceIdType.MESH,
        )

    barrier = pltpu.get_barrier_semaphore()
    for device in ({"y": far_y}, {"x": far_x}):
        pl.semaphore_signal(
            barrier, inc=1, device_id=device, device_id_type=pl.DeviceIdType.MESH
        )
    pl.semaphore_wait(barrier, 2)
    count = len(BLOCKS)
    to_x, to_y, onward, own = [], [], [], []
    for b in range(count):
        here = place_of(b, y, x)
        to_x.append(remote(lines_hbm.at[:, b], here, x_send.at[b], x_recv.at[b], {"x": far_x}))
        to_y.append(remote(lines_hbm.at[:, b], here, y_send.at[b], y_recv.at[b], {"y": far_y}))
        if b in ACROSS:
            there, device = place_of(b, y, far_x), {"y": far_y}
        else:
            there, device = place_of(b, far_y, x), {"x": far_x}
        onward.append(remote(there, there, on_send.at[b], on_recv.at[b], device))
        own.append(pltpu.make_async_copy(lines_hbm.at[:, b], here, own_sem.at[b]))

    def send(blocks):
        for b in blocks:
            to_x[b].start()
            to_y[b].start()
            own[b].start()

    def hand_on(blocks):
        for b in blocks:
            (to_x if b in ACROSS else to_y)[b].wait_recv()
            onward[b].start()

    def arrive(blocks):
        for b in blocks:
            own[b].wait()
            (to_y if b in ACROSS else to_x)[b].wait_recv()
            onward[b].wait_recv()

    send(range(6))
    loads = [
        pltpu.make_async_copy(source, entry.at[k], load_sem.at[k])
        for k, source in enumerate((own_hbm, other_hbm))
    ]
    for load in loads:
        load.start()
    hand_on(range(6))
    send(range(6, count))
    for load in loads:
        load.wait()
    arrive(range(6))
    copies = [pltpu.make_async_copy(arrays[0], outs[0], out_sem.at[0])]
    copies[0].start()
    for k in range(2):
        weights = arrays[0][...].reshape(D, 3 * HALF)
        qkv_ref[k * frames : (k + 1) * frames, :] = dot(entry[k], weights).astype(BF16)
    pairs = HALF // PAIR

    @pl.loop(0, 2 * pairs)
    def _(step):
        clip, j = step // pairs, step % pairs
        rows = pl.ds(pl.multiple_of(clip * frames, frames), frames)
        lanes = [pl.ds(pl.multiple_of(k * HALF + j * PAIR, PAIR), PAIR) for k in range(3)]
        query, key, value = (qkv_ref[rows, lane] for lane in lanes)
        mixture_ref[rows, lanes[0]] = attend_heads(valid_ref[clip], query, key, value)

    hand_on(range(6, count))
    arrive(range(6, count))
    for k in range(1, 5):
        copies.append(pltpu.make_async_copy(arrays[k], outs[k], out_sem.at[k]))
        copies[k].start()
    for copy in copies:
        copy.wait()
    for b in range(count):
        to_x[b].wait_send()
        to_y[b].wait_send()
        onward[b].wait_send()


def gather_group(valid, own, other, lines):
    na, count, rows, _ = lines.shape
    frames = own.shape[0]
    tall = lambda cols: (2, 2, na, 2, rows, cols)
    wide = (2, na, 2, rows, D)
    shapes = [tall(3 * HALF), wide, tall(HALF), tall(HALF), wide]
    sem = lambda size: pltpu.SemaphoreType.DMA((size,))
    return pl.pallas_call(
        gather_kernel,
        out_shape=[
            jax.ShapeDtypeStruct((2 * frames, HALF), BF16),
            jax.ShapeDtypeStruct((2 * frames, 3 * HALF), BF16),
        ]
        + [jax.ShapeDtypeStruct(shape, BF16) for shape in shapes],
        in_specs=[SCALARS] + [ANY] * 3,
        out_specs=[WHOLE] * 2 + [ANY] * 5,
        scratch_shapes=[pltpu.VMEM(shape, BF16) for shape in shapes]
        + [pltpu.VMEM((2, frames, D), BF16)]
        + [sem(count)] * 7
        + [sem(2), sem(5)],
        compiler_params=pltpu.CompilerParams(
            vmem_limit_bytes=56 * 2**20, collective_id=4, has_side_effects=True
        ),
        cost_estimate=LIGHT,
    )(valid, own, other, lines)


def ffn_kernel(
    entry_a, entry_b, d_a, d_b, in_hbm, down_hbm,
    hidden_ref, d_gate_up_ref, d_branch_ref, own_ref, other_ref,
    entry_ref, d_ref, in_ref, down_ref, sem,
):
    step = pl.program_id(0)
    sources = (entry_a, in_hbm, d_a, down_hbm, entry_b, d_b)
    targets = (entry_ref.at[0], in_ref, d_ref.at[0], down_ref, entry_ref.at[1], d_ref.at[1])
    copies = [
        pltpu.make_async_copy(source, target, sem.at[k])
        for k, (source, target) in enumerate(zip(sources, targets))
    ]

    @pl.when(step == 0)
    def _():
        for copy in copies:
            copy.start()
        for copy in copies[:4]:
            copy.wait()

    @pl.when(step == 1)
    def _():
        for copy in copies[4:]:
            copy.wait()

    width = down_ref.shape[0]
    frames = d_ref.shape[1]
    notes = entry_ref[step, frames:, :].astype(F32)
    gate_row = notes[0:1] + notes[1:2] + notes[2:3]
    d_branch = (d_ref[step].astype(F32) * gate_row).astype(BF16)
    d_branch_ref[...] = d_branch
    gate_up = dot(entry_ref[step, :frames, :], in_ref[...])
    gate, up = gate_up[:, :width], gate_up[:, width:]
    logistic = jax.nn.sigmoid(gate)
    hidden = (gate * logistic * up).astype(BF16)
    hidden_ref[...] = hidden
    d_hidden = dot_back(d_branch, down_ref[...])
    d_gate = d_hidden * up * logistic * (1.0 + gate * (1.0 - logistic))
    d_gate_up_ref[:, :width] = d_gate.astype(BF16)
    d_gate_up_ref[:, width:] = (d_hidden * gate * logistic).astype(BF16)
    d_entry = dot_back(d_gate_up_ref[...], in_ref[...]).astype(BF16)
    branch = dot(hidden, down_ref[...]).astype(BF16)

    @pl.when(step == 0)
    def _():
        own_ref[0] = d_entry
        own_ref[1] = branch

    @pl.when(step == 1)
    def _():
        other_ref[0] = d_entry
        other_ref[1] = branch


NOTE_ROWS = 16


def gate_notes(gate):
    high = gate.astype(BF16)
    rest = gate - high.astype(F32)
    middle = rest.astype(BF16)
    low = (rest - middle.astype(F32)).astype(BF16)
    blank = jnp.zeros((NOTE_ROWS - 3, gate.shape[0]), BF16)
    return jnp.concatenate([jnp.stack([high, middle, low]), blank])


def ffn_both_ways(entries, cotangents, rank_in, rank_down):
    frames = cotangents[0].shape[0]
    width = rank_down.shape[0]
    rows_of = lambda cols: pl.BlockSpec((frames, cols), lambda i: (i, 0))
    whole = pl.BlockSpec((2, frames, D), lambda i: (0, 0, 0))
    shape = lambda *sizes: jax.ShapeDtypeStruct(sizes, BF16)
    return pl.pallas_call(
        ffn_kernel,
        out_shape=[shape(2 * frames, cols) for cols in (width, 2 * width, D)]
        + [shape(2, frames, D)] * 2,
        grid=(2,),
        in_specs=[ANY] * 6,
        out_specs=[rows_of(cols) for cols in (width, 2 * width, D)] + [whole] * 2,
        scratch_shapes=[
            pltpu.VMEM((2, frames + NOTE_ROWS, D), BF16),
            pltpu.VMEM((2, frames, D), BF16),
            pltpu.VMEM((D, 2 * width), BF16),
            pltpu.VMEM((width, D), BF16),
            pltpu.SemaphoreType.DMA((6,)),
        ],
        compiler_params=pltpu.CompilerParams(vmem_limit_bytes=56 * 2**20),
        cost_estimate=LIGHT,
    )(*entries, *cotangents, rank_in, rank_down)


def outer_kernel(*refs, lefts, groups, rows, lanes):
    left_refs, right_refs, out_ref = refs[:lefts], refs[lefts:-1], refs[-1]

    def pieces(group):
        return [ref[k : k + rows, :] for ref in group for k in range(0, ref.shape[0], rows)]

    left_pieces = pieces(left_refs)
    start = column = 0
    for size in groups:
        group = right_refs[start : start + size]
        start += size
        sums = None
        for left, right in zip(left_pieces, pieces(group)):
            term = dot_rows(left, right)
            sums = term if sums is None else sums + term
        sums = sums.astype(BF16)
        end = column + sums.shape[1]
        if lanes is None:
            out_ref[0, :, column:end] = sums
        else:
            for k in range(out_ref.shape[0]):
                out_ref[k, 0, :, column:end] = sums[k * lanes : (k + 1) * lanes]
        column = end


def outer_sum(lefts, groups, rows, block, lanes=None, halves=1):
    depth = lefts[0].shape[1]
    cols = sum(group[0][1] for group in groups) // halves
    blocks = depth // block * halves
    if block % 128:
        left = jnp.concatenate([a[: a.shape[0] // rows * rows] for a in lefts])
        right = jnp.concatenate(
            [
                jnp.concatenate([a[:, at * width : (at + 1) * width] for a, width, at in group])
                for group in groups
            ],
            axis=1,
        )
        out = dot_rows(left, right).astype(BF16).reshape(depth // block, block, halves, cols)
        return jnp.swapaxes(out, 1, 2).reshape(blocks, block, cols)
    if lanes is None:
        out_shape = (blocks, block, cols)
        out_spec = pl.BlockSpec((1, block, cols), lambda i: (i, 0, 0))
    else:
        out_shape = (block // lanes, blocks, lanes, cols)
        out_spec = pl.BlockSpec((block // lanes, 1, lanes, cols), lambda i: (0, i, 0, 0))
    used = lambda array: array.shape[0] // rows * rows

    def right_spec(right):
        array, width, at = right
        if halves > 1:
            return pl.BlockSpec((array.shape[0], width // halves), lambda i: (0, i % halves))
        return pl.BlockSpec(
            (array.shape[0], width), lambda i: (0, at), pipeline_mode=pl.Buffered(1)
        )

    rights = [right for group in groups for right in group]
    return pl.pallas_call(
        functools.partial(
            outer_kernel,
            lefts=len(lefts),
            groups=[len(group) for group in groups],
            rows=rows,
            lanes=lanes,
        ),
        out_shape=jax.ShapeDtypeStruct(out_shape, BF16),
        grid=(blocks,),
        in_specs=[pl.BlockSpec((used(a), block), lambda i: (0, i // halves)) for a in lefts]
        + [right_spec(right) for right in rights],
        out_specs=out_spec,
        compiler_params=pltpu.CompilerParams(vmem_limit_bytes=56 * 2**20),
        cost_estimate=LIGHT,
    )(*lefts, *[right[0] for right in rights])


def reduce_kernel(*refs, plan, inputs):
    arrays, (small_hbm, in_hbm, down_hbm) = refs[:inputs], refs[inputs : inputs + 3]
    out_ref, small_ref, in_ref, down_ref, down_in = refs[inputs + 3 : inputs + 8]
    (
        blocks, first_x, first_y, second, second_in, kept, lines_in, mine, other_in, left_ref, right_ref, notes,
        load_sem, first_send, first_recv, second_send, second_recv, line_send, line_recv,
        core_send, core_recv, note_send, note_recv,
        in_own, in_core, in_y, in_x, in_send, in_recv, down_send, down_recv, down_sem,
    ) = refs[inputs + 8 :]
    y, c, z, x = (lax.axis_index(axis) for axis in AXES)
    na, rows = kept.shape[1], kept.shape[3]
    far_y, far_c, far_x = 1 - y, 1 - c, 1 - x
    count = len(plan)
    names = [("y", far_y), ("c", far_c), ("x", far_x)]
    names += [("z", lax.rem(z + k, na)) for k in range(1, na)]
    slots = {}
    for m, (_, _, _, turn) in enumerate(plan):
        slots[m] = sum(1 for other in plan[:m] if other[3] == turn)

    def remote(source, target, send, recv, axis, at):
        return pltpu.make_async_remote_copy(
            src_ref=source,
            dst_ref=target,
            send_sem=send,
            recv_sem=recv,
            device_id={axis: at},
            device_id_type=pl.DeviceIdType.MESH,
        )

    barrier = pltpu.get_barrier_semaphore()
    for axis, at in names:
        pl.semaphore_signal(
            barrier, inc=1, device_id={axis: at}, device_id_type=pl.DeviceIdType.MESH
        )
    pl.semaphore_wait(barrier, len(names))

    def first_copy(m):
        if plan[m][3]:
            source, target, axis, at = blocks.at[m, far_y], first_y.at[slots[m]], "y", far_y
        else:
            source, target, axis, at = blocks.at[m, :, :, :, far_x], first_x.at[slots[m]], "x", far_x
        return remote(source, target, first_send.at[m], first_recv.at[m], axis, at)

    def second_copy(m):
        axis, at = ("x", far_x) if plan[m][3] else ("y", far_y)
        return remote(
            second.at[m], second_in.at[m], second_send.at[m], second_recv.at[m], axis, at
        )

    def line_copies(m):
        return [
            remote(
                kept.at[m, lax.rem(z + k, na)],
                lines_in.at[m, k - 1],
                line_send.at[m * (na - 1) + k - 1],
                line_recv.at[m * (na - 1) + k - 1],
                "z",
                lax.rem(z + k, na),
            )
            for k in range(1, na)
        ]

    def core_copy(m):
        return remote(
            mine.at[m, far_c], other_in.at[m], core_send.at[m], core_recv.at[m], "c", far_c
        )

    def note_copies(hop):
        if hop == 0:
            hops = [(notes.at[0, 0, 0, 0], notes.at[0, 0, 0, 1], "x", far_x)]
        elif hop == 1:
            hops = [
                (notes.at[0, 0, 0], notes.at[0, 0, k], "z", lax.rem(z + k, na))
                for k in range(1, na)
            ]
        elif hop == 2:
            hops = [(notes.at[0, 0], notes.at[0, 1], "c", far_c)]
        else:
            hops = [(notes.at[0], notes.at[1], "y", far_y)]
        at = 0 if hop == 0 else hop + (na - 2 if hop > 1 else 0)
        return [
            remote(source, target, note_send.at[at + k], note_recv.at[at + k], axis, to)
            for k, (source, target, axis, to) in enumerate(hops)
        ]

    def loads(m):
        copies = []
        for group, buffer in ((plan[m][1], left_ref), (plan[m][2], right_ref)):
            start = 0
            for place_of in group:
                height, width = arrays[place_of].shape
                copies.append(
                    pltpu.make_async_copy(
                        arrays[place_of],
                        buffer.at[m % 2, pl.ds(start, height), pl.ds(0, width)],
                        load_sem.at[m % 2, len(copies)],
                    )
                )
                start += height
        return copies

    def compute(m):
        kind, lefts, rights, _ = plan[m]
        height = sum(arrays[place_of].shape[0] for place_of in lefts)
        depth = na * 2 * rows

        @pl.loop(0, 4)
        def _(step):
            at_y, at_c = step // 2, step % 2
            at, columns = (step, 0) if kind == "tall" else (at_y, at_c)
            left = left_ref[m % 2, :height, pl.ds(pl.multiple_of(at * depth, 128), depth)]
            right = right_ref[m % 2, :height, pl.ds(pl.multiple_of(columns * HALF, 128), HALF)]
            sums = dot_rows(left, right).astype(BF16)
            for k in range(2 * na):
                blocks[m, at_y, at_c, k // 2, k % 2] = sums[k * rows : (k + 1) * rows]

    def arrived(m, at_c, at_z, at_y, at_x):
        if plan[m][3]:
            came = first_y[slots[m], at_c, at_z, at_x]
        else:
            came = first_x[slots[m], at_y, at_c, at_z]
        return blocks[m, at_y, at_c, at_z, at_x].astype(F32) + came.astype(F32)

    load = pltpu.make_async_copy(small_hbm, notes.at[0, 0, 0, 0], load_sem.at[0, 0])
    load.start()
    load.wait()
    hops = [note_copies(hop) for hop in range(4)]
    for copy in hops[0]:
        copy.start()

    load = pltpu.make_async_copy(in_hbm, in_own, load_sem.at[0, 0])
    load.start()
    load.wait()

    def in_copies(first, pairs, axis, at):
        return [
            remote(source, target, in_send.at[first + k], in_recv.at[first + k], axis, at)
            for k, (source, target) in enumerate(pairs)
        ]

    in_hops = [
        in_copies(0, [(in_own.at[:, far_c], in_core)], "c", far_c),
        in_copies(
            1, [(in_own.at[far_y, c], in_y.at[0]), (in_core.at[far_y], in_y.at[1])], "y", far_y
        ),
        in_copies(
            3,
            [
                (in_own.at[y, c, far_x], in_x.at[0]),
                (in_core.at[y, far_x], in_x.at[1]),
                (in_y.at[0, far_x], in_x.at[2]),
                (in_y.at[1, far_x], in_x.at[3]),
            ],
            "x",
            far_x,
        ),
    ]
    for copy in in_hops[0]:
        copy.start()
    down_copies = [
        remote(
            down_hbm.at[lax.rem(z + k, na)], down_in.at[k - 1],
            down_send.at[k - 1], down_recv.at[k - 1], "z", lax.rem(z + k, na),
        )
        for k in range(1, na)
    ]
    for copy in down_copies:
        copy.start()
    for copy in loads(0):
        copy.start()
    def second_step(m):
        first_copy(m).wait_recv()

        @pl.loop(0, 2 * na)
        def _(step):
            at_c, at_z = step // na, step % na
            at_y, at_x = (y, far_x) if plan[m][3] else (far_y, x)
            second[m, at_c, at_z] = arrived(m, at_c, at_z, at_y, at_x).astype(BF16)

        second_copy(m).start()

    def line_step(m):
        second_copy(m).wait_recv()

        @pl.loop(0, 2 * na)
        def _(step):
            at_c, at_z = step // na, step % na
            sums = arrived(m, at_c, at_z, y, x) + second_in[m, at_c, at_z].astype(F32)
            kept[m, at_z, at_c] = sums.astype(BF16)

        for copy in line_copies(m):
            copy.start()

    def last_step(m):
        sums = kept[m, z].astype(F32)
        for k, copy in enumerate(line_copies(m)):
            copy.wait_recv()
            sums += lines_in[m, k].astype(F32)
        mine[m] = sums.astype(BF16)
        if plan[m][0] == "tall":
            core_copy(m).start()

    for m in range(count + 6):
        if m < count:
            for copy in loads(m):
                copy.wait()
            if m + 1 < count:
                for copy in loads(m + 1):
                    copy.start()
            compute(m)
            first_copy(m).start()
        if m in (1, 3):
            for copy in in_hops[m // 2]:
                copy.wait_recv()
            for copy in in_hops[m // 2 + 1]:
                copy.start()
        if m in (0, 2, 4):
            hop = m // 2
            for copy in hops[hop]:
                copy.wait_recv()
            for copy in hops[hop + 1]:
                copy.start()
        for behind, step in ((2, second_step), (4, line_step), (6, last_step)):
            if 0 <= m - behind < count:
                step(m - behind)
    order = range(count)
    for m in order:
        if plan[m][0] == "tall":
            core_copy(m).wait_recv()
            out_ref[m, 0] = mine[m, c]
            out_ref[m, 1] = other_in[m]
        else:
            out_ref[m] = mine[m]
    for copy in hops[3]:
        copy.wait_recv()
    small_ref[...] = notes[...]

    for copy in in_hops[2]:
        copy.wait_recv()
    width = in_own.shape[-1] // 2
    share = width // na
    for at_y in range(2):
        for at_c in range(2):
            if at_y:
                near = in_y[at_c, x]
            else:
                near = in_core[y, x] if at_c else in_own[y, c, x]
            across = in_x[at_y * 2 + at_c]
            low = jnp.where(x == 0, near, across)
            high = jnp.where(x == 0, across, near)
            rank = lax.rem(y + at_y, 2) * 2 + lax.rem(c + at_c, 2)
            for half in range(2):
                for k in range(na):
                    at = half * width + k * share
                    start = pl.multiple_of(half * FF + (rank * na + k) * 2 * share, 128)
                    in_ref[:, pl.ds(start, 2 * share)] = jnp.concatenate(
                        [low[:, at : at + share], high[:, at : at + share]], axis=1
                    )
    depth = down_ref.shape[0]
    sums = None
    for k in range(na):
        if k:
            down_copies[k - 1].wait_recv()
        source = down_in.at[k - 1] if k else down_hbm.at[z]
        copy = pltpu.make_async_copy(source, left_ref.at[0, pl.ds(0, depth)], down_sem.at[0])
        copy.start()
        copy.wait()
        term = left_ref[0, :depth, :].astype(F32)
        sums = term if sums is None else sums + term
    down_ref[...] = sums.astype(BF16)

    for hop in hops + in_hops + [down_copies]:
        for copy in hop:
            copy.wait_send()
    for m in range(count):
        first_copy(m).wait_send()
        second_copy(m).wait_send()
        for copy in line_copies(m):
            copy.wait_send()
        if plan[m][0] == "tall":
            core_copy(m).wait_send()


def reduce_group(matrices, small, grad_in, grad_down, na, rows):
    arrays, plan = [], []
    for kind, lefts, rights, turn in matrices:
        places = []
        for group in (lefts, rights):
            places.append([])
            for array in group:
                found = [k for k, known in enumerate(arrays) if known is array]
                if not found:
                    arrays.append(array)
                    found = [len(arrays) - 1]
                places[-1].append(found[0])
        plan.append((kind, *places, turn))
    count = len(plan)
    tall = max(sum(a.shape[0] for a in lefts) for _, lefts, _, _ in matrices)
    turns = [turn for *_, turn in plan]
    low = lambda *shape: pltpu.VMEM(shape, BF16)
    sem = lambda *shape: pltpu.SemaphoreType.DMA(shape)
    all_small = (2, 2, na, 2) + small.shape
    return pl.pallas_call(
        functools.partial(reduce_kernel, plan=plan, inputs=len(arrays)),
        out_shape=[
            jax.ShapeDtypeStruct((count, 2, rows, HALF), BF16),
            jax.ShapeDtypeStruct(all_small, BF16),
            jax.ShapeDtypeStruct((rows, 2 * FF), BF16),
            jax.ShapeDtypeStruct(grad_down.shape[1:], BF16),
            jax.ShapeDtypeStruct((na - 1,) + grad_down.shape[1:], BF16),
        ],
        in_specs=[ANY] * (len(arrays) + 3),
        out_specs=[WHOLE] * 4 + [ANY],
        scratch_shapes=[
            low(count, 2, 2, na, 2, rows, HALF),
            low(turns.count(0), 2, 2, na, rows, HALF),
            low(turns.count(1), 2, na, 2, rows, HALF),
            low(count, 2, na, rows, HALF),
            low(count, 2, na, rows, HALF),
            low(count, na, 2, rows, HALF),
            low(count, na - 1, 2, rows, HALF),
            low(count, 2, rows, HALF),
            low(count, rows, HALF),
            low(2, tall, D),
            low(2, tall, D),
            low(*all_small),
            sem(2, 4),
            sem(count),
            sem(count),
            sem(count),
            sem(count),
            sem(count * (na - 1)),
            sem(count * (na - 1)),
            sem(count),
            sem(count),
            sem(na + 2),
            sem(na + 2),
            low(*grad_in.shape),
            low(2, 2, *grad_in.shape[-2:]),
            low(2, 2, *grad_in.shape[-2:]),
            low(4, *grad_in.shape[-2:]),
            sem(7),
            sem(7),
            sem(na - 1),
            sem(na - 1),
            sem(1),
        ],
        compiler_params=pltpu.CompilerParams(
            vmem_limit_bytes=60 * 2**20, collective_id=1, has_side_effects=True
        ),
        cost_estimate=LIGHT,
    )(*arrays, small, grad_in, grad_down)


def pair_in_kernel(own_ref, other_ref, weight_ref, out_ref, *, product):
    for step, ref in enumerate((own_ref, other_ref)):

        @pl.when(pl.program_id(0) == step)
        def _():
            out_ref[...] = product(ref[...], weight_ref[...]).astype(BF16)


def pair_in(own, other, weight, product):
    frames = own.shape[0]
    cols = weight.shape[1] if product is dot else weight.shape[0]
    whole = lambda array: pl.BlockSpec(
        array.shape, lambda i: (0, 0), pipeline_mode=pl.Buffered(1)
    )
    return pl.pallas_call(
        functools.partial(pair_in_kernel, product=product),
        out_shape=jax.ShapeDtypeStruct((2 * frames, cols), BF16),
        grid=(2,),
        in_specs=[whole(own), whole(other), whole(weight)],
        out_specs=pl.BlockSpec((frames, cols), lambda i: (i, 0)),
        compiler_params=pltpu.CompilerParams(vmem_limit_bytes=48 * 2**20),
        cost_estimate=LIGHT,
    )(own, other, weight)


def pair_out_kernel(*refs, product):
    part_refs, weight_ref, own_ref, other_ref = refs[:-3], refs[-3], refs[-2], refs[-1]
    sums = None
    column = 0
    for ref in part_refs:
        weight = weight_ref[...]
        if len(part_refs) > 1:
            weight = weight_ref[:, column : column + ref.shape[1]]
            column += ref.shape[1]
        term = product(ref[...], weight)
        sums = term if sums is None else sums + term

    @pl.when(pl.program_id(0) == 0)
    def _():
        own_ref[...] = sums

    @pl.when(pl.program_id(0) == 1)
    def _():
        other_ref[...] = sums.astype(BF16)


def pair_out(parts, weight, product):
    frames = parts[0].shape[0] // 2
    cols = weight.shape[1] if product is dot else weight.shape[0]
    whole = pl.BlockSpec((frames, cols), lambda i: (0, 0))
    return pl.pallas_call(
        functools.partial(pair_out_kernel, product=product),
        out_shape=[
            jax.ShapeDtypeStruct((frames, cols), F32),
            jax.ShapeDtypeStruct((frames, cols), BF16),
        ],
        grid=(2,),
        in_specs=[pl.BlockSpec((frames, part.shape[1]), lambda i: (i, 0)) for part in parts]
        + [pl.BlockSpec(weight.shape, lambda i: (0, 0), pipeline_mode=pl.Buffered(1))],
        out_specs=[whole, whole],
        compiler_params=pltpu.CompilerParams(vmem_limit_bytes=48 * 2**20),
        cost_estimate=LIGHT,
    )(*parts, weight)


def notes_kernel(own_ref, out_ref, notes, send, recv):
    y, c, z, x = (lax.axis_index(axis) for axis in AXES)
    na = notes.shape[2]
    far_y, far_c, far_x = {"y": 1 - y}, {"c": 1 - c}, {"x": 1 - x}
    lines = [{"z": lax.rem(z + k, na)} for k in range(1, na)]
    barrier = pltpu.get_barrier_semaphore()
    for device in [far_y, far_c, far_x] + lines:
        pl.semaphore_signal(
            barrier, inc=1, device_id=device, device_id_type=pl.DeviceIdType.MESH
        )
    pl.semaphore_wait(barrier, 3 + len(lines))
    notes[0, 0, 0, 0] = own_ref[...]
    hops = [
        [(notes.at[0, 0, 0, 0], notes.at[0, 0, 0, 1], far_x)],
        [(notes.at[0, 0, 0], notes.at[0, 0, k + 1], line) for k, line in enumerate(lines)],
        [(notes.at[0, 0], notes.at[0, 1], far_c)],
        [(notes.at[0], notes.at[1], far_y)],
    ]
    at = 0
    copies = []
    for hop in hops:
        group = []
        for source, target, device in hop:
            group.append(
                pltpu.make_async_remote_copy(
                    src_ref=source,
                    dst_ref=target,
                    send_sem=send.at[at],
                    recv_sem=recv.at[at],
                    device_id=device,
                    device_id_type=pl.DeviceIdType.MESH,
                )
            )
            at += 1
        for copy in group:
            copy.start()
        for copy in group:
            copy.wait_recv()
        copies += group
    for copy in copies:
        copy.wait_send()
    out_ref[...] = notes[...]


def gather_notes(notes, na):
    all_notes = (2, 2, na, 2) + notes.shape
    sem = pltpu.SemaphoreType.DMA((na + 2,))
    return pl.pallas_call(
        notes_kernel,
        out_shape=jax.ShapeDtypeStruct(all_notes, BF16),
        in_specs=[WHOLE],
        out_specs=WHOLE,
        scratch_shapes=[pltpu.VMEM(all_notes, BF16), sem, sem],
        compiler_params=pltpu.CompilerParams(collective_id=5, has_side_effects=True),
        cost_estimate=LIGHT,
    )(notes)


def shift_kernel(
    terms_ref, cot_hbm, in_ref, shifts_ref, cots_hbm, parts_ref,
    from_core, line_out, line_in, y_out, y_in, x_out, x_in,
    in_core, in_y, in_x,
    core_sem, line_send, line_recv, step_sem, cot_send, cot_recv, relay_send, relay_recv,
    in_send, in_recv,
):
    y, c, z, x = (lax.axis_index(axis) for axis in AXES)
    na = terms_ref.shape[2]
    far_y, far_c, far_x = 1 - y, 1 - c, 1 - x

    def remote(source, target, send, recv, device):
        return pltpu.make_async_remote_copy(
            src_ref=source,
            dst_ref=target,
            send_sem=send,
            recv_sem=recv,
            device_id=device,
            device_id_type=pl.DeviceIdType.MESH,
        )

    devices = [{"y": far_y}, {"c": far_c}, {"x": far_x}]
    devices += [{"z": lax.rem(z + k, na)} for k in range(1, na)]
    barrier = pltpu.get_barrier_semaphore()
    for device in devices:
        pl.semaphore_signal(
            barrier, inc=1, device_id=device, device_id_type=pl.DeviceIdType.MESH
        )
    pl.semaphore_wait(barrier, len(devices))

    to_core = remote(terms_ref.at[:, 1], from_core, core_sem.at[0], core_sem.at[1], {"c": far_c})
    to_core.start()

    def block_copies(first, pairs, device):
        return [
            remote(source, target, in_send.at[first + k], in_recv.at[first + k], device)
            for k, (source, target) in enumerate(pairs)
        ]

    in_hops = [
        block_copies(0, [(in_ref.at[:, 1], in_core)], {"c": far_c}),
        block_copies(1, [(in_ref.at[1, 0], in_y.at[0]), (in_core.at[1], in_y.at[1])], {"y": far_y}),
        block_copies(
            3,
            [
                (in_ref.at[0, 0, 1], in_x.at[0]),
                (in_core.at[0, 1], in_x.at[1]),
                (in_y.at[0, 1], in_x.at[2]),
                (in_y.at[1, 1], in_x.at[3]),
            ],
            {"x": far_x},
        ),
    ]
    for copy in in_hops[0]:
        copy.start()
    chips = {1: {"x": far_x}, 2: {"y": far_y}}
    cots = {
        2 * k: remote(cot_hbm, cots_hbm.at[2 * k], cot_send.at[2 * k], cot_recv.at[2 * k], chips[k])
        for k in chips
    }
    cots[1] = remote(cot_hbm, cots_hbm.at[1], cot_send.at[1], cot_recv.at[1], {"c": far_c})
    for k in (1, 2, 3):
        cots[2 * k + 1] = remote(
            cots_hbm.at[2 * k], cots_hbm.at[2 * k + 1],
            cot_send.at[2 * k + 1], cot_recv.at[2 * k + 1], {"c": far_c},
        )
    relays = []
    for k, (part, size) in enumerate(halves_of(cot_hbm.shape[0])):
        near, next_to = (1, 2) if k == 0 else (2, 1)
        here = pl.ds(part, size)
        relays.append(
            remote(
                cots_hbm.at[2 * near, here], cots_hbm.at[6, here],
                relay_send.at[k], relay_recv.at[k], chips[next_to],
            )
        )
    cots[2].start()
    cots[4].start()
    cots[1].start()

    to_core.wait_recv()
    for copy in in_hops[0]:
        copy.wait_recv()
    for copy in in_hops[1]:
        copy.start()
    lines = []
    for k in range(1, na):
        line_out[k - 1] = terms_ref[:, 0, k] + from_core[:, k]
        lines.append(
            remote(
                line_out.at[k - 1], line_in.at[k - 1], line_send.at[k - 1], line_recv.at[k - 1],
                {"z": lax.rem(z - k + na, na)},
            )
        )
        lines[-1].start()
    here = terms_ref[:, 0, 0] + from_core[:, 0]
    for k, copy in enumerate(lines):
        copy.wait_recv()
        here = here + line_in[k]
    y_out[...] = here[1]
    to_y = remote(y_out, y_in, step_sem.at[0], step_sem.at[1], {"y": far_y})
    to_y.start()
    for k in (1, 2):
        cots[2 * k].wait_recv()
    for copy in relays:
        copy.start()
    for k in (1, 2):
        cots[2 * k + 1].start()
    to_y.wait_recv()
    here = here[0] + y_in[...]
    x_out[...] = here[1]
    to_x = remote(x_out, x_in, step_sem.at[2], step_sem.at[3], {"x": far_x})
    to_x.start()
    for copy in in_hops[1]:
        copy.wait_recv()
    for copy in in_hops[2]:
        copy.start()
    to_x.wait_recv()
    shifts_ref[...] = here[0] + x_in[...]

    for copy in relays:
        copy.wait_recv()
    cots[7].start()
    for copy in in_hops[2]:
        copy.wait_recv()
    for at_y in range(2):
        for at_c in range(2):
            near = in_ref[0, 0, 0] if not at_y and not at_c else None
            if near is None:
                near = in_y[at_c, 0] if at_y else in_core[0, 0]
            parts_ref[at_y, at_c, 0] = near
            parts_ref[at_y, at_c, 1] = in_x[at_y * 2 + at_c]
    for k in (1, 3, 5, 7):
        cots[k].wait_recv()
        cots[k].wait_send()
    for copy in [to_core, to_y, to_x, cots[2], cots[4]] + lines + relays + sum(in_hops, []):
        copy.wait_send()


def sum_shifts(terms, cotangent, blocks, na):
    rows = terms.shape[-2]
    full = lambda *shape: pltpu.VMEM(shape + (rows, 128), F32)
    sem = lambda size: pltpu.SemaphoreType.DMA((size,))
    block = blocks.shape[-2:]
    low = lambda *shape: pltpu.VMEM(shape + block, BF16)
    return pl.pallas_call(
        shift_kernel,
        out_shape=[
            jax.ShapeDtypeStruct((rows, 128), F32),
            jax.ShapeDtypeStruct((8,) + cotangent.shape, BF16),
            jax.ShapeDtypeStruct(blocks.shape, BF16),
        ],
        in_specs=[WHOLE, ANY, WHOLE],
        out_specs=[WHOLE, ANY, WHOLE],
        scratch_shapes=[
            full(2, na, 2),
            full(na - 1, 2, 2),
            full(na - 1, 2, 2),
            full(2),
            full(2),
            full(),
            full(),
            low(2, 2),
            low(2, 2),
            low(4),
            sem(2),
            sem(na - 1),
            sem(na - 1),
            sem(4),
            sem(8),
            sem(8),
            sem(2),
            sem(2),
            sem(7),
            sem(7),
        ],
        compiler_params=pltpu.CompilerParams(
            vmem_limit_bytes=32 * 2**20, collective_id=2, has_side_effects=True
        ),
        cost_estimate=LIGHT,
    )(terms, cotangent, blocks)


def halves_of(height):
    cut = height // 32 * 16
    return (0, cut), (cut, height - cut)


def ffn_group_kernel(
    entry_hbm, notes_hbm, cot_hbm, cots_hbm, lines_hbm, down_hbm,
    d_entry_hbm, grad_down_hbm, grad_in_hbm, branch_hbm, own_hbm, other_hbm, pair_hbm, back_hbm,
    sum_hbm, branch_back_hbm,
    entry, d_branch, hidden, d_gate_up, in_lines, down_lines, partial, away, branch, loaded, sums,
    local_sem, entry_send, entry_recv, cot_sem,
    pair_send, pair_recv, back_send, back_recv, branch_sem, out_sem,
    relay_send, relay_recv, branch_pair_send, branch_pair_recv, branch_send, branch_recv,
    *, chips, peers, sizes,
):
    ny, nb = sizes
    y, c, x = lax.axis_index("y"), lax.axis_index("c"), lax.axis_index("x")
    frames = cot_hbm.shape[0]
    rows = frames // 2
    own_rows = in_lines.shape[-2]
    width = down_lines.shape[0] * down_lines.shape[1]
    in_all = lambda: in_lines[...].reshape(D, 2 * width)
    down_all = lambda: down_lines[...].reshape(width, D)
    count = len(chips)
    sibling = {"c": 1 - c}
    ahead = [{"y": lax.rem(y + dy, ny), "x": lax.rem(x + dx, nb)} for dy, dx in chips]
    behind = [
        {"y": lax.rem(y - dy + ny, ny), "x": lax.rem(x - dx + nb, nb)} for dy, dx in chips
    ]

    def remote(source, target, send, recv, device):
        return pltpu.make_async_remote_copy(
            src_ref=source,
            dst_ref=target,
            send_sem=send,
            recv_sem=recv,
            device_id=device,
            device_id_type=pl.DeviceIdType.MESH,
        )

    barrier = pltpu.get_barrier_semaphore()
    for device in [sibling] + behind[1:]:
        pl.semaphore_signal(
            barrier, inc=1, device_id=device, device_id_type=pl.DeviceIdType.MESH
        )
    pl.semaphore_wait(barrier, count)

    loads = [
        pltpu.make_async_copy(source, target, local_sem.at[k])
        for k, (source, target) in enumerate(
            [
                (entry_hbm, entry.at[0, pl.ds(0, frames)]),
                (notes_hbm, entry.at[0, pl.ds(frames, NOTE_ROWS)]),
                (down_hbm, down_lines),
            ]
        )
    ]
    for k, (dy, dc, dx) in enumerate(peers):
        target = in_lines.at[
            lax.rem(y + dy, ny), lax.rem(c + dc, 2), :, lax.rem(x + dx, nb)
        ]
        source = lines_hbm.at[:, pl.ds(k * own_rows, own_rows)]
        loads.append(pltpu.make_async_copy(source, target, local_sem.at[3 + k]))
    for load in loads:
        load.start()
    cot_loads = [
        pltpu.make_async_copy(
            cots_hbm.at[k] if k else cot_hbm, d_branch.at[k], cot_sem.at[k]
        )
        for k in range(2 * count)
    ]
    for load in cot_loads:
        load.start()
    entry_copies = {
        1: remote(entry.at[0], entry.at[1], entry_send.at[1], entry_recv.at[1], sibling)
    }
    for k in range(1, count):
        entry_copies[2 * k] = remote(
            entry.at[0], entry.at[2 * k], entry_send.at[2 * k], entry_recv.at[2 * k], ahead[k]
        )
        entry_copies[2 * k + 1] = remote(
            entry.at[2 * k], entry.at[2 * k + 1],
            entry_send.at[2 * k + 1], entry_recv.at[2 * k + 1], sibling,
        )
    for load in loads[:2]:
        load.wait()
    for k in (2, 4, 1):
        entry_copies[k].start()

    relays = []
    height = entry.shape[1]
    for k, (part, size) in enumerate(halves_of(height)):
        near, next_to = (1, 2) if k == 0 else (2, 1)
        here = pl.ds(part, size)
        relays.append(
            remote(
                entry.at[2 * near, here], entry.at[2 * 3, here],
                relay_send.at[k], relay_recv.at[k], ahead[next_to],
            )
        )

    def branch_copies(k):
        copies = []
        if k == 0:
            copies.append(pltpu.make_async_copy(branch.at[0], own_hbm, branch_sem.at[0]))
        copies.append(
            remote(
                branch.at[1], other_hbm.at[k], branch_pair_send.at[k], branch_pair_recv.at[k], sibling
            )
        )
        return copies

    def branch_wait(k):
        for copy in branch_copies(k)[:-1]:
            copy.wait()
        branch_copies(k)[-1].wait_send()

    def branch_copy(k):
        return remote(
            sum_hbm.at[k - 1], branch_back_hbm.at[k - 1], branch_send.at[k], branch_recv.at[k],
            behind[k],
        )

    order = (0, 3, 1, 2)
    turn = {k: order.index(k) % 2 for k in order}

    def pair_copy(k):
        return remote(
            away.at[turn[k]], pair_hbm.at[k], pair_send.at[k], pair_recv.at[k], sibling
        )

    def back_copy(k):
        return remote(
            partial.at[k], back_hbm.at[k - 1], back_send.at[k], back_recv.at[k], behind[k]
        )

    def compute(k, i):
        @pl.loop(0, 2)
        def _(part):
            slot = 2 * k + i
            here = pl.ds(pl.multiple_of(part * rows, rows), rows)
            notes = entry[slot, frames:, :].astype(F32)
            gate_row = notes[0:1] + notes[1:2] + notes[2:3]
            d_here = (d_branch[slot, here, :].astype(F32) * gate_row).astype(BF16)
            d_branch[slot, here, :] = d_here
            gate_up = dot(entry[slot, here, :], in_all())
            gate, up = gate_up[:, :width], gate_up[:, width:]
            logistic = jax.nn.sigmoid(gate)
            hidden_here = (gate * logistic * up).astype(BF16)
            hidden[slot, here, :] = hidden_here
            d_hidden = dot_back(d_here, down_all())
            d_gate = d_hidden * up * logistic * (1.0 + gate * (1.0 - logistic))
            d_gate_up[slot, here, :width] = d_gate.astype(BF16)
            d_gate_up[slot, here, width:] = (d_hidden * gate * logistic).astype(BF16)
            d_entry = dot_back(d_gate_up[slot, here, :], in_all()).astype(BF16)
            branch[i, here, :] = dot(hidden_here, down_all()).astype(BF16)

            if i == 0:
                partial[k, here, :] = d_entry
            else:
                away[turn[k], here, :] = d_entry

    def move(source, target):
        copy = pltpu.make_async_copy(source, target, out_sem.at[0])
        copy.start()
        copy.wait()

    def fetch(source):
        move(source, loaded)
        return loaded[...].astype(F32)

    def branch_terms(k):
        branch_copies(k)[-1].wait_recv()
        own = branch[0].astype(F32) if k else fetch(own_hbm)
        return own + fetch(other_hbm.at[k])

    def finish(k):
        pair_copy(k).wait_recv()
        partial[k] = (partial[k].astype(F32) + fetch(pair_hbm.at[k])).astype(BF16)
        if k:
            back_copy(k).start()
            pair_copy(k).wait_send()
            away[turn[k]] = branch_terms(k).astype(BF16)
            move(away.at[turn[k]], sum_hbm.at[k - 1])
            branch_copy(k).start()
        else:
            pair_copy(k).wait_send()

    before = None
    for k in order:
        if k == 0:
            for load in loads[2:]:
                load.wait()
        elif k == 3:
            entry_copies[2].wait_recv()
            entry_copies[4].wait_recv()
            for copy in relays:
                copy.start()
            for near in (3, 5):
                entry_copies[near].start()
            for copy in relays:
                copy.wait_recv()
            entry_copies[7].start()
        entry_copies[2 * k + 1].wait_recv()
        cot_loads[2 * k].wait()
        cot_loads[2 * k + 1].wait()
        if before is not None:
            branch_wait(before)
        compute(k, 0)
        if before == 0:
            finish(0)
        compute(k, 1)
        pair_copy(k).start()
        for copy in branch_copies(k):
            copy.start()
        if k:
            finish(k)
        before = k
    branch_wait(before)

    down_rows = 256 if width % 256 == 0 else 128

    @pl.loop(0, width // down_rows)
    def _(block):
        columns = pl.ds(pl.multiple_of(block * down_rows, down_rows), down_rows)
        term = dot_rows(hidden[0, :, columns], d_branch[0])
        for slot in range(1, 2 * count):
            term += dot_rows(hidden[slot, :, columns], d_branch[slot])
        branch[0, :down_rows, :] = term.astype(BF16)
        copy = pltpu.make_async_copy(
            branch.at[0, pl.ds(0, down_rows)], grad_down_hbm.at[columns], out_sem.at[1]
        )
        copy.start()
        copy.wait()

    na, _, lanes, _ = grad_in_hbm.shape
    in_rows = na * lanes

    @pl.loop(0, D // in_rows)
    def _(block):
        columns = pl.ds(pl.multiple_of(block * in_rows, 128), in_rows)
        term = dot_rows(entry[0, :frames, columns], d_gate_up[0])
        for slot in range(1, 2 * count):
            term += dot_rows(entry[slot, :frames, columns], d_gate_up[slot])
        branch[1, :in_rows, :] = term.astype(BF16)
        copies = [
            pltpu.make_async_copy(
                branch.at[1, pl.ds(z * lanes, lanes)], grad_in_hbm.at[z, block], out_sem.at[2 + z]
            )
            for z in range(na)
        ]
        copy_all(copies)

    total_here = partial[0].astype(F32)
    for k in range(1, count):
        back_copy(k).wait_recv()
        total_here += fetch(back_hbm.at[k - 1])
    sums[...] = total_here
    move(sums, d_entry_hbm)
    total_here = branch_terms(0)
    for k in range(1, count):
        branch_copy(k).wait_recv()
        total_here += fetch(branch_back_hbm.at[k - 1])
    sums[...] = total_here
    move(sums, branch_hbm)

    entry_copies[1].wait_send()
    for k in range(1, count):
        if k < 3:
            entry_copies[2 * k].wait_send()
            relays[k - 1].wait_send()
        entry_copies[2 * k + 1].wait_send()
        back_copy(k).wait_send()
        branch_copy(k).wait_send()


def ffn_group(entry, notes, cotangent, cotangents, lines, down, chips, peers, sizes):
    frames = cotangent.shape[0]
    na, depth = down.shape[:2]
    width = na * depth
    rows = lines.shape[1] // len(peers)
    lanes = sizes[1] * rows
    count = len(chips)
    low = lambda *shape: jax.ShapeDtypeStruct(shape, BF16)
    sem = lambda size: pltpu.SemaphoreType.DMA((size,))
    clip = (frames, D)
    return pl.pallas_call(
        functools.partial(ffn_group_kernel, chips=chips, peers=peers, sizes=sizes),
        out_shape=[
            jax.ShapeDtypeStruct(clip, F32),
            low(width, D),
            low(na, D // (na * lanes), lanes, 2 * width),
            jax.ShapeDtypeStruct(clip, F32),
            low(*clip),
            low(count, *clip),
            low(count, *clip),
            low(count - 1, *clip),
            low(count - 1, *clip),
            low(count - 1, *clip),
        ],
        in_specs=[ANY] * 6,
        out_specs=[ANY] * 10,
        scratch_shapes=[
            pltpu.VMEM((2 * count, frames + NOTE_ROWS, D), BF16),
            pltpu.VMEM((2 * count, frames, D), BF16),
            pltpu.VMEM((2 * count, frames, width), BF16),
            pltpu.VMEM((2 * count, frames, 2 * width), BF16),
            pltpu.VMEM((sizes[0], 2, na, sizes[1], rows, 2 * width), BF16),
            pltpu.VMEM((na, depth, D), BF16),
            pltpu.VMEM((count, frames, D), BF16),
            pltpu.VMEM((2, frames, D), BF16),
            pltpu.VMEM((2, frames, D), BF16),
            pltpu.VMEM(clip, BF16),
            pltpu.VMEM(clip, F32),
            sem(3 + len(peers)),
            sem(2 * count),
            sem(2 * count),
            sem(2 * count),
            sem(count),
            sem(count),
            sem(count),
            sem(count),
            sem(2),
            sem(2 + na),
            sem(2),
            sem(2),
            sem(count),
            sem(count),
            sem(count),
            sem(count),
        ],
        compiler_params=pltpu.CompilerParams(
            vmem_limit_bytes=60 * 2**20, collective_id=0, has_side_effects=True
        ),
        cost_estimate=LIGHT,
    )(entry, notes, cotangent, cotangents, lines, down)


def stack_kernel(*refs):
    out_ref = refs[-1]
    out_ref[...] = jnp.zeros_like(out_ref)
    rows = refs[0].shape[0]
    for k, ref in enumerate(refs[:-1]):
        out_ref[k * rows : (k + 1) * rows, :] = ref[...].astype(BF16)


def stack_vectors(vectors):
    parts = [vector.reshape(-1, 128) for vector in vectors]
    rows = sum(part.shape[0] for part in parts)
    return pl.pallas_call(
        stack_kernel,
        out_shape=jax.ShapeDtypeStruct((rows + -rows % 16, 128), BF16),
        in_specs=[WHOLE] * len(parts),
        out_specs=WHOLE,
        cost_estimate=LIGHT,
    )(*parts)


def total_kernel(sums_ref, out_ref, steps, lines, step_send, step_recv, line_send, line_recv):
    y, c, z, x = (lax.axis_index(axis) for axis in AXES)
    na = lines.shape[0]

    def remote(source, target, send, recv, device):
        return pltpu.make_async_remote_copy(
            src_ref=source,
            dst_ref=target,
            send_sem=send,
            recv_sem=recv,
            device_id=device,
            device_id_type=pl.DeviceIdType.MESH,
        )

    near = [{"c": 1 - c}, {"x": 1 - x}, {"y": 1 - y}]
    far = [{"z": lax.rem(z + k, na)} for k in range(1, na)]
    barrier = pltpu.get_barrier_semaphore()
    for device in near + far:
        pl.semaphore_signal(
            barrier, inc=1, device_id=device, device_id_type=pl.DeviceIdType.MESH
        )
    pl.semaphore_wait(barrier, len(near) + len(far))
    steps[0, 0] = sums_ref[...]
    for k, device in enumerate(near):
        copy = remote(steps.at[k, 0], steps.at[k, 1], step_send.at[k], step_recv.at[k], device)
        copy.start()
        copy.wait()
        both = steps[k, 0] + steps[k, 1]
        if k < 2:
            steps[k + 1, 0] = both
    lines[z] = both
    copies = [
        remote(lines.at[z], lines.at[z], line_send.at[k], line_recv.at[k], device)
        for k, device in enumerate(far)
    ]
    for copy in copies:
        copy.start()
    for copy in copies:
        copy.wait()
    whole = lines[0]
    for k in range(1, na):
        whole = whole + lines[k]
    out_ref[...] = whole


def total_over_devices(sums, na):
    sem = lambda size: pltpu.SemaphoreType.DMA((size,))
    return pl.pallas_call(
        total_kernel,
        out_shape=jax.ShapeDtypeStruct(sums.shape, F32),
        in_specs=[WHOLE],
        out_specs=WHOLE,
        scratch_shapes=[
            pltpu.VMEM((3, 2) + sums.shape, F32),
            pltpu.VMEM((na,) + sums.shape, F32),
            sem(3),
            sem(3),
            sem(na - 1),
            sem(na - 1),
        ],
        compiler_params=pltpu.CompilerParams(collective_id=3, has_side_effects=True),
        cost_estimate=LIGHT,
    )(sums)


def step_kernel(factor_ref, *refs):
    count = len(refs) // 3
    at = 0
    for weight_ref, direction_ref, out_ref in zip(refs[:count], refs[count : 2 * count], refs[2 * count :]):
        if len(weight_ref.shape) == 3:
            for k in range(weight_ref.shape[0]):
                out_ref[k] = weight_ref[k] - factor_ref[at] * direction_ref[k]
                at += 1
        else:
            out_ref[...] = weight_ref[...] - factor_ref[at] * direction_ref[...]
            at += 1


def step_weights(factors, weights, directions):
    return pl.pallas_call(
        step_kernel,
        out_shape=[jax.ShapeDtypeStruct(weight.shape, F32) for weight in weights],
        in_specs=[SCALARS] + [WHOLE] * (2 * len(weights)),
        out_specs=[WHOLE] * len(weights),
        compiler_params=pltpu.CompilerParams(vmem_limit_bytes=56 * 2**20),
        cost_estimate=LIGHT,
    )(factors, *weights, *directions)


def lamb_kernel(spot_ref, weight_ref, first_ref, second_ref, *refs):
    gradient_refs = refs[:-4]
    first_out, second_out, direction_out, sums_ref = refs[-4:]
    gradient = gradient_refs[0][...].astype(F32)
    if len(gradient_refs) == 2:
        ours = pl.program_id(1) % 2 == spot_ref[1]
        gradient = jnp.where(ours, gradient, gradient_refs[1][...].astype(F32))
    weight = weight_ref[...]
    first_new = BETA_ONE * first_ref[...] + (1.0 - BETA_ONE) * gradient
    second_new = BETA_TWO * second_ref[...] + (1.0 - BETA_TWO) * gradient * gradient
    direction = (
        first_new
        / (1.0 - BETA_ONE**STEP)
        / (jnp.sqrt(second_new / (1.0 - BETA_TWO**STEP)) + ADAM_EPS)
        + DECAY * weight
    )
    first_out[...] = first_new
    second_out[...] = second_new
    direction_out[...] = direction

    @pl.when(pl.program_id(1) == 0)
    def _():
        sums_ref[...] = jnp.zeros_like(sums_ref)

    for row, values in enumerate((weight, direction)):
        squares = jnp.sum(values * values, axis=1)
        for start in range(0, squares.shape[1], 128):
            sums_ref[:, row, :] += squares[:, start : start + 128]


def lamb_terms(spot, weight, first_moment, second_moment, gradients, block):
    shape = weight.shape
    arrays = [
        array.reshape((-1,) + array.shape[-2:])
        for array in (weight, first_moment, second_moment, *gradients)
    ]
    groups, rows, cols = arrays[0].shape
    in_blocks = len(gradients) == 1 and arrays[3].shape != arrays[0].shape
    spec = pl.BlockSpec((1, rows, block), lambda i, j: (i, 0, j))
    turns = 2 * HALF // block
    halves = pl.BlockSpec((1, rows, block), lambda i, j: (j // turns, 0, j % turns // 2))
    by_block = pl.BlockSpec((1, rows, block), lambda i, j: (j, 0, 0))
    full = jax.ShapeDtypeStruct((groups, rows, cols), F32)
    out = pl.pallas_call(
        lamb_kernel,
        out_shape=[full, full, full, jax.ShapeDtypeStruct((groups, 8, 128), F32)],
        grid=(groups, cols // block),
        in_specs=[SCALARS]
        + [spec] * 3
        + [by_block if in_blocks else spec if len(gradients) == 1 else halves] * len(gradients),
        out_specs=[spec] * 3 + [pl.BlockSpec((1, 8, 128), lambda i, j: (i, 0, 0))],
        compiler_params=pltpu.CompilerParams(vmem_limit_bytes=40 * 2**20),
        cost_estimate=pl.CostEstimate(
            flops=20 * weight.size, bytes_accessed=28 * weight.size, transcendentals=weight.size
        ),
    )(spot, *arrays)
    return [array.reshape(shape) for array in out[:3]] + [jnp.sum(out[3][:, :2], axis=-1)]


class Grid:
    def __init__(self, mesh):
        self.ny = mesh.shape["dp"] // 2
        self.nb = 2
        self.na = mesh.shape["fsdp"] // 2
        self.sizes = dict(y=self.ny, c=2, z=self.na, x=self.nb)
        self.count = self.ny * 2 * self.na * self.nb
        self.spots = list(itertools.product(*(range(self.sizes[axis]) for axis in AXES)))
        self.peers = list(itertools.product(range(self.ny), range(2), range(self.nb)))
        self.chips = list(itertools.product(range(self.ny), range(self.nb)))
        self.back = [
            (dy, dc, dx)
            for dx in range(self.nb)
            for dy in range(self.ny)
            for dc in range(2)
        ]
        self.mesh = Mesh(mesh.devices.reshape(self.ny, 2, self.na, self.nb), AXES)

    def line(self, y, c, z, x):
        return ((y * 2 + c) * self.na + z) * self.nb + x

    def here(self):
        return {axis: lax.axis_index(axis) for axis in AXES}

    def move(self, array, **steps):
        steps = {axis: step % self.sizes[axis] for axis, step in steps.items()}
        steps = {axis: step for axis, step in steps.items() if step}
        if not steps:
            return array
        names = tuple(axis for axis in AXES if axis in steps)
        lengths = [self.sizes[axis] for axis in names]
        pairs = []
        for spot in itertools.product(*(range(n) for n in lengths)):
            source = target = 0
            for axis, at, n in zip(names, spot, lengths):
                source, target = source * n + at, target * n + (at + steps[axis]) % n
            pairs.append((source, target))
        return lax.ppermute(array, names, pairs)

    def rank(self, mine, offset):
        y, c, x = ((mine[axis] + step) % self.sizes[axis] for axis, step in zip("ycx", offset))
        return (y * 2 + c) * self.nb + x

    def swap(self, array):
        return self.move(array, c=1)

    def gather_small(self, array):
        shape = array.shape
        for axis in "xzcy":
            parts = [self.move(array, **{axis: k}) for k in range(self.sizes[axis])]
            array = jnp.concatenate([part.reshape((-1,) + shape) for part in parts])
        return array

    def scatter_small(self, array):
        sources = [array]
        for axis in "cyxz":
            where = 0
            arrays = []
            size = self.sizes[axis]
            sources = [s.reshape(self.small_shape(axis, s)) for s in sources]
            for k in range(1, size):
                part = total([s[:, k] for s in sources])
                arrays.append(self.move(part, **{axis: -k}))
            sources = [s[:, 0] for s in sources] + arrays
        return total(sources).reshape(array.shape[1:])

    def small_shape(self, axis, array):
        before = {"c": self.ny, "y": 1, "x": self.na, "z": 1}[axis]
        return (before, self.sizes[axis], -1, array.shape[-1])

    def sum_small(self, array):
        bit = 1
        while bit < self.count:
            array = array + lax.ppermute(array, AXES, [(d, d ^ bit) for d in range(self.count)])
            bit *= 2
        return array

    def spread(self, lines, turn, between):
        held, marks = {(0, 0): lines}, []
        for axis in ("x", "y") if turn else ("y", "x"):
            for (y, x), piece in list(held.items()):
                for k in range(1, self.sizes[axis]):
                    step = dict(y=y, x=x)
                    step[axis] = k
                    held[(step["y"], step["x"])] = self.move(piece, **{axis: k})
            if not marks:
                marks = list(held.values())[1:]
                if between:
                    held.update(zip(list(held)[1:], after(marks, between)))
        return held, marks

    def gather_weights(self, parts, shapes, mine, spot, first, between=(), behind=()):
        rows = parts[0][0][0].shape[0]
        mixed = jnp.stack([shard for part in parts for shard, *_ in part])
        lines = lax.all_gather(mixed, "z")
        if first:
            (lines,) = after([lines], first)
        start = 0
        held, marks, plan = [], [], dict(parts=[], outs=len(shapes))
        for turn, part in enumerate(parts):
            end = start + len(part)
            pieces, arrived = self.spread(lines[:, start:end], turn, between)
            held.append(pieces)
            marks += arrived
            start = end
            plan["parts"].append(
                [(out, lane, column, shard.shape[1]) for shard, out, lane, column in part]
            )
        plan["offsets"] = sorted(held[0])
        if rows % 16 == 0:
            arrays = [pieces[offset] for pieces in held for offset in plan["offsets"]]
            arrays += behind
            copies = len(plan["offsets"]) * sum(len(part) for part in parts)
            kernel = functools.partial(place_pieces, plan=plan, sizes=(self.ny, self.nb))
            return place(kernel, spot, arrays, shapes, copies), marks
        outs = [jnp.zeros(shape, BF16) for shape in shapes]
        for pieces, blocks in zip(held, plan["parts"]):
            for (dy, dx), piece in pieces.items():
                y = (mine["y"] - dy + self.ny) % self.ny
                x = (mine["x"] - dx + self.nb) % self.nb
                for block, (out, lane, column, width) in enumerate(blocks):
                    update = piece[:, block][None, :, None]
                    if lane is None:
                        at = (y, 0, x, 0, column)
                    else:
                        update = update[:, None]
                        at = (y, lane, 0, x, 0, column)
                    outs[out] = lax.dynamic_update_slice(outs[out], update, at)
        return outs, marks

    def swap_ranks(self, blocks):
        shape = blocks.shape[1:]
        blocks = blocks.reshape((self.ny, 2, self.nb) + shape)
        for where, axis in ((1, "c"), (0, "y"), (2, "x")):
            parts = [
                self.move(lax.index_in_dim(blocks, k, where), **{axis: k})
                for k in range(self.sizes[axis])
            ]
            blocks = jnp.concatenate(parts, axis=where)
        return blocks.reshape((-1,) + shape)

    def swap_back(self, blocks, mine):
        for where, axis in ((1, "c"), (1, "y"), (2, "x")):
            parts = [
                self.move(pick(blocks, (mine[axis] + k) % self.sizes[axis], where), **{axis: k})
                for k in range(self.sizes[axis])
            ]
            blocks = jnp.stack(parts)
        return blocks.reshape((-1,) + blocks.shape[-2:])

    def gather_ranks(self, in_parts, down_part, mine, spot):
        peers, rows, width = in_parts.shape
        depth = down_part.shape[0]
        in_shape = (self.ny, 2, self.na, self.nb, rows, width)
        down_shape = (self.na, depth, D)
        if rows % 16 == 0 and width == D:
            mixed = jnp.concatenate([in_parts.reshape(-1, D), down_part])
            lines = lax.all_gather(mixed, "z")
            kernel = functools.partial(
                place_ranks,
                offsets=self.peers,
                sizes=(self.ny, self.na, self.nb),
                rows=rows,
                depth=depth,
            )
            rank_in, rank_down = place(kernel, spot, [lines], [in_shape, down_shape], peers + 1)
        else:
            rank_down = lax.all_gather(down_part, "z")
            lines = lax.all_gather(in_parts, "z")
            rank_in = jnp.zeros(in_shape, BF16)
            for k, (dy, dc, dx) in enumerate(self.peers):
                at = ((mine["y"] - dy) % self.ny, (mine["c"] + dc) % 2, 0, (mine["x"] - dx) % self.nb, 0, 0)
                rank_in = lax.dynamic_update_slice(rank_in, lines[:, k][None, None, :, None], at)
        return rank_in.reshape(-1, width), rank_down.reshape(-1, D)

    def join_columns(self, pieces, mine, spot):
        peers, rows, width = pieces.shape
        width = width // 2
        if rows % 16 == 0:
            kernel = functools.partial(
                place_columns, offsets=self.back, sizes=(self.ny, self.nb), width=width
            )
            return place(kernel, spot, [pieces], [(rows, 2 * FF)], 2 * peers)[0]
        out = jnp.zeros((rows, 2, FF), BF16)
        for k, (dy, dc, dx) in enumerate(self.back):
            y, x = (mine["y"] - dy) % self.ny, (mine["x"] - dx) % self.nb
            rank = (y * 2 + (mine["c"] + dc) % 2) * self.nb + x
            piece = pieces[k].reshape(rows, 2, width)
            out = lax.dynamic_update_slice(out, piece, (0, 0, rank * width))
        return out.reshape(rows, 2 * FF)

    def fold(self, array, names, turn, mine, between=(), behind=(), marks=None):
        names = list(names)
        sources = [array]
        for axis, waits in zip("yx" if turn else "xy", (between, behind)):
            where = names.index(axis)
            size = self.sizes[axis]
            arrived = []
            for k in range(1, size):
                away = total([pick(s, (mine[axis] + k) % size, where) for s in sources])
                arrived.append(self.move(away.astype(BF16), **{axis: k}))
            if waits:
                arrived = after(arrived, waits)
            if marks is not None and len(names) > len(array.shape) - 3:
                marks += arrived
            sources = [pick(s, mine[axis], where) for s in sources] + list(arrived)
            names.remove(axis)
        return total(sources).astype(BF16)

    def to_rank(self, array, back=False):
        pairs = []
        for d in range(self.count):
            rank, z = divmod(d, self.na)
            y, c, x = self.peers[rank]
            pairs.append((d, self.line(y, c, z, x)))
        if back:
            pairs = [(b, a) for a, b in pairs]
        return lax.ppermute(array, AXES, pairs)


def lamb_small(weight, first_moment, second_moment, gradient):
    first_new = BETA_ONE * first_moment + (1.0 - BETA_ONE) * gradient
    second_new = BETA_TWO * second_moment + (1.0 - BETA_TWO) * gradient * gradient
    direction = (
        first_new
        / (1.0 - BETA_ONE**STEP)
        / (jnp.sqrt(second_new / (1.0 - BETA_TWO**STEP)) + ADAM_EPS)
        + DECAY * weight
    )
    sums = jnp.stack([jnp.sum(weight * weight), jnp.sum(direction * direction)])
    return [first_new, second_new, direction, sums[None]]


def shards(
    grid,
    latents,
    context,
    timestep,
    lengths,
    cotangent,
    mod_matrix,
    mod_first,
    mod_second,
    qkv_matrix,
    qkv_first,
    qkv_second,
    square_set,
    square_first,
    square_second,
    ctx_matrix,
    ctx_first,
    ctx_second,
    ff_in,
    in_first,
    in_second,
    ff_down,
    down_first,
    down_second,
    norm_gains,
    gains_first,
    gains_second,
):
    mine = grid.here()
    core = mine["c"]
    spot = jnp.stack([mine[axis] for axis in AXES]).astype(jnp.int32)
    device = grid.line(*(mine[axis] for axis in AXES))
    count, ranks = grid.count, len(grid.peers)
    rows = mod_matrix.shape[0]
    frames = latents.shape[1]
    words = context.shape[1]
    valid = lengths[0]
    keep_rows = (jnp.arange(frames) < valid).astype(F32)[:, None]

    width = FF // ranks
    grouped = rows % 16 == 0 and grid.ny == 2 and grid.nb == 2
    if grouped:
        prepare = functools.partial(prepare_kernel, offsets=grid.peers, sizes=(grid.ny, grid.na, grid.nb))
        five = (5, rows, HALF)
        five_own, five_other, wide_low, in_blocks = pl.pallas_call(
            prepare,
            out_shape=[
                jax.ShapeDtypeStruct(shape, BF16)
                for shape in (five, five, (4, rows, HALF), (ranks, rows, 2 * width))
            ],
            in_specs=[SCALARS] + [WHOLE] * 4,
            out_specs=[WHOLE] * 4,
            compiler_params=pltpu.CompilerParams(vmem_limit_bytes=40 * 2**20),
        )(spot, qkv_matrix, square_set, ctx_matrix, ff_in)
    else:
        five = [qkv_matrix[:, k * D : (k + 1) * D] for k in range(3)] + [
            square_set[1],
            jnp.concatenate([ctx_matrix[:, :D], ctx_matrix[:, D:]]),
        ]
        five = jnp.stack(five).astype(BF16).reshape(5, rows, grid.ny, 2, -1)
        five_own = pick(five, core, 3).reshape(5, rows, HALF)
        five_other = pick(five, 1 - core, 3).reshape(5, rows, HALF)
        wide_low = jnp.stack(
            [square_set[k, :, side * HALF : (side + 1) * HALF] for k in (0, 2) for side in range(2)]
        ).astype(BF16)
        in_halves = ff_in.reshape(rows, 2, FF)
        in_blocks = jnp.stack(
            [
                lax.dynamic_slice(in_halves, (0, 0, grid.rank(mine, offset) * width), (rows, 2, width))
                for offset in grid.peers
            ]
        ).astype(BF16).reshape(ranks, rows, 2 * width)
    five_other = grid.swap(five_other)
    five_low = jnp.where(core == 0, five_own, five_other)
    five_high = jnp.where(core == 0, five_other, five_own)
    lifted = jax.nn.silu(timestep[0].astype(F32)).astype(BF16)
    notes = jnp.concatenate([lifted, norm_gains.astype(BF16).reshape(-1)])
    if grouped:
        size = notes.shape[0]
        notes = jnp.pad(notes, (0, -size % 2048)).reshape(-1, 128)
        notes = gather_notes(notes, grid.na).reshape(count, -1)[:, :size]
    else:
        notes = grid.gather_small(notes)
    origin = []
    for spot_of in grid.spots:
        source = [
            (mine[axis] - step) % grid.sizes[axis] for axis, step in zip(AXES, spot_of)
        ]
        origin.append(grid.line(*source))
    origin = jnp.stack(origin)
    sorter = (jnp.arange(count)[:, None] == origin[None, :]).astype(BF16)
    gain_rows = dot(sorter, notes[:, D:])
    gain_rows = gain_rows.reshape(count, 3, rows).transpose(1, 0, 2).reshape(3, D)
    lifted_own = lax.dynamic_slice(notes, (0, device * rows), (count, rows))
    shift_terms = dot(lifted_own, mod_matrix.astype(BF16))
    text = jnp.concatenate([context[0], grid.swap(context[0])])
    blank = jnp.zeros((2 * words, count, rows // 2), BF16)
    text_cut = text.reshape(2 * words, count, rows // 2)
    text_key = jnp.concatenate([text_cut, blank], axis=-1).reshape(2 * words, -1)
    text_value = jnp.concatenate([blank, text_cut], axis=-1).reshape(2 * words, -1)
    text_both = jnp.concatenate([text_key, text_value])
    cotangent_own = (cotangent[0].astype(F32) * keep_rows).astype(BF16)
    if grouped:
        shift_terms = shift_terms.reshape(grid.ny, 2, grid.na, grid.nb, 6 * D // 128, 128)
        blocks = in_blocks.reshape(grid.ny, 2, grid.nb, rows, 2 * width)
        shifts, cotangents, in_parts = sum_shifts(shift_terms, cotangent_own, blocks, grid.na)
        in_parts = in_parts.reshape(ranks, rows, 2 * width)
        shifts = shifts.reshape(6, D)
    else:
        shifts = grid.scatter_small(shift_terms).reshape(6, D)
        in_parts = grid.swap_ranks(in_blocks)

    tall = (grid.ny, 2, grid.na, grid.nb, rows)
    wide = (grid.ny, grid.na, grid.nb, rows, D)
    both = lambda k, out, at: [(five_low[k], out, 0, at), (five_high[k], out, 1, at)]
    sides = lambda k, out: [
        (wide_low[2 * k], out, None, 0),
        (wide_low[2 * k + 1], out, None, HALF),
    ]
    stream = latents[0].astype(F32)
    normed_one, inverse_one = norm_rows(stream)
    entry_attn = (normed_one * gain_rows[0] * (1.0 + shifts[1]) + shifts[0]).astype(BF16)
    entry_pair = [entry_attn, grid.swap(entry_attn)]
    pair_lengths = jnp.concatenate([lengths, grid.swap(lengths)])
    columns = HALF // PAIR
    if grouped:
        blocks = [(five_low, five_high)[lane][k] for k in range(3) for lane in range(2)]
        blocks += [wide_low[0], wide_low[1], five_low[3], five_high[3]]
        blocks += [five_low[4], five_high[4], wide_low[2], wide_low[3]]
        lines = lax.all_gather(jnp.stack(blocks), "z")
        in_lines = lax.all_gather(in_parts.reshape(-1, D), "z")
        down_lines = lax.all_gather(ff_down.astype(BF16), "z")
        mixture_attn, qkv, matrix_qkv, matrix_out, matrix_query, matrix_ctx, matrix_cross = (
            gather_group(pair_lengths, *entry_pair, lines)
        )
        matrix_qkv = matrix_qkv.reshape(D, 3 * HALF)
    else:
        first = both(0, 0, 0) + both(1, 0, HALF) + both(2, 0, 2 * HALF)
        (matrix_qkv,), _ = grid.gather_weights(
            [first[:3], first[3:]], [tall + (3 * HALF,)], mine, spot, ()
        )
        matrix_qkv = matrix_qkv.reshape(D, 3 * HALF)
        (matrix_out, matrix_query), _ = grid.gather_weights(
            [sides(0, 0), both(3, 1, 0)], [wide, tall + (HALF,)], mine, spot, ()
        )
        (matrix_ctx, matrix_cross), _ = grid.gather_weights(
            [both(4, 0, 0), sides(1, 1)], [tall + (HALF,), wide], mine, spot, ()
        )
        down_part = grid.to_rank(ff_down.astype(BF16))
        rank_in, rank_down = grid.gather_ranks(in_parts, down_part, mine, spot)
        qkv = pair_in(*entry_pair, matrix_qkv, dot)
        mixture_attn = attend(pair_lengths, *((qkv, frames, 0, k * columns) for k in range(3)))
    matrix_out, matrix_cross = matrix_out.reshape(HALF, D), matrix_cross.reshape(HALF, D)
    matrix_query, matrix_ctx = matrix_query.reshape(D, HALF), matrix_ctx.reshape(D, HALF)

    all_words = jnp.full((2,), words, jnp.int32)
    d_result = cotangent[0].astype(F32) * keep_rows

    self_parts = tuple((qkv, frames, 0, k * columns) for k in range(3))
    own, away = pair_out([mixture_attn], matrix_out, dot)
    branch_attn = own + grid.swap(away).astype(F32)
    after_attn = stream + shifts[2] * branch_attn
    normed_two, inverse_two = norm_rows(after_attn)
    entry_cross = (normed_two * gain_rows[1]).astype(BF16)
    cross_pair = [entry_cross, grid.swap(entry_cross)]
    query_cross = pair_in(*cross_pair, matrix_query, dot)
    kv_cross = dot(text_both, matrix_ctx).astype(BF16)
    cross_parts = ((query_cross, frames, 0, 0), (kv_cross, words, 0, 0), (kv_cross, words, 2, 0))
    mixture_cross = attend(all_words, *cross_parts)
    own, away = pair_out([mixture_cross], matrix_cross, dot)
    branch_cross = own + grid.swap(away).astype(F32)
    after_cross = after_attn + branch_cross
    normed_three, inverse_three = norm_rows(after_cross)
    entry_ffn = (normed_three * gain_rows[2] * (1.0 + shifts[4]) + shifts[3]).astype(BF16)

    notes = gate_notes(shifts[5])
    whole = lambda array: (array, array.shape[1], 0)
    chips = grid.chips
    if grouped:
        d_entry_ffn, grad_down, grad_in, branch_ffn, *_ = ffn_group(
            entry_ffn, notes, cotangent_own, cotangents, in_lines, down_lines,
            chips, grid.peers, (grid.ny, grid.nb),
        )
        grad_in = grad_in.reshape(-1, 2 * width)
    else:
        entry_ext = jnp.concatenate([entry_ffn, notes])
        cot_arrived = [grid.move(cotangent_own, y=y, x=x) for y, x in grid.chips]
        (entry_ext,) = after([entry_ext], cot_arrived[1:])
        arrived = [grid.move(entry_ext, y=y, x=x) for y, x in grid.chips]
        entry_parts, hidden_parts, d_gate_up_parts, d_branch_parts = [], [], [], []
        d_entry_sources, folded_rows, branch_own, branch_away = [], [], [], []
        for k, (y, x) in enumerate(grid.chips):
            own_entry, own_cot = arrived[k], cot_arrived[k]
            if k in (1, 2):
                own_entry, own_cot = after([own_entry, own_cot], hidden_parts[:1])
            elif k > 2:
                own_entry, own_cot = after([own_entry, own_cot], folded_rows[k - 2 : k - 1])
            entries = [own_entry, grid.swap(own_entry)]
            hidden, d_gate_up, d_branch, own, other = ffn_both_ways(
                entries, [own_cot, grid.swap(own_cot)], rank_in, rank_down
            )
            other = grid.swap(other)
            folded_rows.append(total([own[0], other[0]]).astype(BF16))
            if k:
                d_entry_sources.append(grid.move(folded_rows[k], y=-y, x=-x))
                branch_away.append(total([own[1], other[1]]).astype(BF16))
            else:
                d_entry_sources += [own[0], other[0]]
                branch_own += [own[1], other[1]]
            entry_parts += entries
            hidden_parts.append(hidden)
            d_gate_up_parts.append(d_gate_up)
            d_branch_parts.append(d_branch)
        hidden_parts[:1] = after(hidden_parts[:1], folded_rows[-2:-1])
        grad_down = outer_sum(
            hidden_parts, [[whole(a) for a in d_branch_parts]], frames, 256 if width % 256 == 0 else 128
        ).reshape(width, D)
        d_gate_up_parts[:1] = after(d_gate_up_parts[:1], folded_rows[-1:])
        in_group = [[whole(a) for a in d_gate_up_parts]]
        if rows % 16 == 0:
            grad_in = outer_sum(
                entry_parts, in_group, frames, D // (2 * grid.ny), grid.nb * rows
            )
        else:
            grad_in = outer_sum(entry_parts, in_group, frames, D // 4)
            grad_in = grad_in.reshape(2 * grid.ny, grid.na, grid.nb * rows, 2 * width)
            grad_in = jnp.swapaxes(grad_in, 0, 1)
        grad_in = grad_in.reshape(-1, 2 * width)
        d_entry_ffn = total(after(d_entry_sources, (grad_down, grad_in)))
        branch_arrived = [
            grid.move(away, y=-y, x=-x) for away, (y, x) in zip(branch_away, chips[1:])
        ]
        branch_ffn = total(branch_own + branch_arrived)
    grad_in = lax.psum_scatter(grad_in, "z", tiled=True)

    d_gain_ffn = jnp.sum(d_entry_ffn * normed_three * (1.0 + shifts[4]), axis=0)
    d_scale_ffn = jnp.sum(d_entry_ffn * normed_three * gain_rows[2], axis=0)
    d_shift_ffn = jnp.sum(d_entry_ffn, axis=0)
    d_after_cross = d_result + norm_back(
        d_entry_ffn * gain_rows[2] * (1.0 + shifts[4]), normed_three, inverse_three
    )

    def join(own, other):
        lead = own.shape[:-1]
        shape = lead + (grid.ny, 1, D // (2 * grid.ny))
        own, other = own.reshape(shape), other.reshape(shape)
        low = jnp.where(core == 0, own, other)
        high = jnp.where(core == 0, other, own)
        return jnp.concatenate([low, high], axis=-2).reshape(lead + (D,))

    d_branch_cross = d_after_cross.astype(BF16)
    d_cross_pair = [d_branch_cross, grid.swap(d_branch_cross)]
    d_mixture_cross = pair_in(*d_cross_pair, matrix_cross, dot_back)
    d_query_cross, d_key_cross, d_value_cross = attend_back(
        all_words, *cross_parts, d_mixture_cross
    )
    own, away = pair_out([d_query_cross], matrix_query, dot_back)
    d_entry_cross = own + grid.swap(away).astype(F32)
    d_gain_cross = jnp.sum(d_entry_cross * normed_two, axis=0)
    d_after_attn = d_after_cross + norm_back(d_entry_cross * gain_rows[1], normed_two, inverse_two)
    d_branch_attn = (d_after_attn * shifts[2]).astype(BF16)
    d_attn_pair = [d_branch_attn, grid.swap(d_branch_attn)]
    d_gate_attn = jnp.sum(d_after_attn * branch_attn, axis=0)
    d_mixture_attn = pair_in(*d_attn_pair, matrix_out, dot_back)
    d_queries, d_keys, d_values = attend_back(pair_lengths, *self_parts, d_mixture_attn)
    own, away = pair_out([d_queries, d_keys, d_values], matrix_qkv, dot_back)
    d_entry_attn = own + grid.swap(away).astype(F32)
    d_gain_attn = jnp.sum(d_entry_attn * normed_one * (1.0 + shifts[1]), axis=0)
    d_scale_attn = jnp.sum(d_entry_attn * normed_one * gain_rows[0], axis=0)
    d_shift_attn = jnp.sum(d_entry_attn, axis=0)
    d_latents = d_after_attn + norm_back(
        d_entry_attn * gain_rows[0] * (1.0 + shifts[1]), normed_one, inverse_one
    )


    d_gate_ffn = jnp.sum(d_result * branch_ffn, axis=0)
    result = after_cross + shifts[5] * branch_ffn
    branches = (result, shifts[2] * branch_attn, branch_cross, shifts[5] * branch_ffn)
    stream_terms = jnp.stack([jnp.sum(keep_rows * branch * branch) for branch in branches])
    vectors = [
        d_shift_attn,
        d_scale_attn,
        d_gate_attn,
        d_shift_ffn,
        d_scale_ffn,
        d_gate_ffn,
        d_gain_attn,
        d_gain_cross,
        d_gain_ffn,
    ]
    small = stack_vectors(vectors)

    beside = lambda halves: jnp.concatenate([halves[0], halves[1]], axis=1)
    if grouped:
        reduced, small, grad_in, grad_down, _ = reduce_group(
            [
                ("wide", [mixture_cross], d_cross_pair, 0),
                ("tall", cross_pair, [d_query_cross], 1),
                ("tall", [text_both], [d_key_cross, d_value_cross], 0),
                ("wide", [mixture_attn], d_attn_pair, 1),
                ("tall", entry_pair, [d_queries], 0),
                ("tall", entry_pair, [d_keys], 1),
                ("tall", entry_pair, [d_values], 0),
            ],
            small, grad_in.reshape(grid.ny, 2, grid.nb, rows, 2 * width),
            grad_down.reshape(grid.na, -1, D), grid.na, rows,
        )
        small = small.reshape(count, -1, 128)[:, : 9 * D // 128].reshape(count, 9, D)
        grad_cross, grad_out = beside(reduced[0]), beside(reduced[3])
        grad_query, grad_ctx = (join(reduced[k, 0], reduced[k, 1]) for k in (1, 2))
        qkv_parts = [reduced[4:, 0], reduced[4:, 1]]
        turn_width = D // (2 * grid.ny)
    else:
        grad_down = lax.psum_scatter(grad_down, "z", tiled=True)
        grad_down = grid.to_rank(grad_down, back=True)
        grad_in = grid.swap_back(grad_in.reshape(grid.ny, 2, grid.nb, rows, 2 * width), mine)
        grad_in = grid.join_columns(grad_in, mine, spot)
        small = grid.gather_small(small[: 9 * D // 128].reshape(9, D))
        block = D // (2 * grid.ny)

        def reduce(lefts, right, piece, halves=1):
            groups = [[whole(array) for array in right]]
            gradient = outer_sum(lefts, groups, piece, block, None, halves)
            gradient = grid.fold(gradient.reshape(tall + (-1,)), "yczx", 0, mine)
            return lax.psum_scatter(jnp.swapaxes(gradient, 0, 1), "z")

        def reduce_tall(lefts, right, piece):
            sums = reduce(lefts, right, piece)
            return join(pick(sums, core, 0), grid.swap(pick(sums, 1 - core, 0)))

        grad_cross = beside(reduce([mixture_cross], d_cross_pair, frames, 2))
        grad_out = beside(reduce([mixture_attn], d_attn_pair, frames, 2))
        grad_query = reduce_tall(cross_pair, [d_query_cross], frames)
        grad_ctx = reduce_tall([text_both], [d_key_cross, d_value_cross], 2 * words)
        qkv_parts = [
            jnp.concatenate(
                [reduce_tall(entry_pair, [d], frames) for d in (d_queries, d_keys, d_values)],
                axis=1,
            )
        ]
        turn_width = D
    grad_ctx = jnp.concatenate([grad_ctx[: rows // 2], grad_ctx[rows // 2 :]], axis=1)
    grad_square = jnp.stack([grad_out, grad_query, grad_cross])
    grad_mod = jnp.einsum("nd,nkm->kdm", lifted_own, small[:, :6], preferred_element_type=F32)
    gain_sums = jnp.sum(small[:, 6:].astype(F32), axis=0)
    grad_gains = lax.dynamic_slice(gain_sums, (0, device * rows), (3, rows))
    lamb = functools.partial(lamb_terms, spot)
    done = {}
    done["qkv"] = lamb(qkv_matrix, qkv_first, qkv_second, qkv_parts, turn_width)
    done["mod"] = lamb(mod_matrix, mod_first, mod_second, [grad_mod], D)
    done["square"] = lamb(square_set, square_first, square_second, [grad_square], HALF)
    done["ctx"] = lamb(ctx_matrix, ctx_first, ctx_second, [grad_ctx], D)
    done["down"] = lamb(ff_down, down_first, down_second, [grad_down], 256)
    done["in"] = lamb(ff_in, in_first, in_second, [grad_in], 1024)
    done["gains"] = lamb_small(norm_gains, gains_first, gains_second, grad_gains)
    names = ("mod", "qkv", "square", "ctx", "in", "down", "gains")
    sums = [done[name][3] for name in names]
    sums.append(jnp.stack([stream_terms, jnp.sum(lengths) * jnp.ones(4)]).T)
    sums = jnp.concatenate(sums)
    if grouped:
        wanted = sums.shape
        sums = jnp.pad(sums, ((0, -wanted[0] % 8), (0, 128 - wanted[1])))
        sums = total_over_devices(sums, grid.na)[: wanted[0], : wanted[1]]
    else:
        sums = grid.sum_small(sums)
    norms = jnp.sqrt(sums[:9])
    weight_norms, update_norms = norms[:, 0], norms[:, 1]
    stream_rms = jnp.sqrt(sums[9:, 0] / (sums[9:, 1] * D))
    factors = RATE * (weight_norms / update_norms)
    masters = [mod_matrix, qkv_matrix, square_set, ctx_matrix, ff_in, ff_down, norm_gains]
    weights_new = step_weights(factors, masters, [done[name][2] for name in names])
    outputs = [result.astype(BF16)[None], d_latents.astype(BF16)[None]]
    for name, weight_new in zip(names, weights_new):
        outputs += [weight_new, done[name][0], done[name][1]]
    outputs.append(weight_norms)
    outputs.append(update_norms)
    outputs.append(stream_rms)
    return tuple(outputs)


def solution(mesh):
    grid = Grid(mesh)
    clip = P(AXES, None, None)
    row = P(AXES, None)
    square = P(None, AXES, None)
    gains = P(None, AXES)
    weights = (row,) * 6 + (square,) * 3 + (row,) * 9 + (gains,) * 3
    in_specs = (clip, clip, row, P(AXES), clip) + weights
    out_specs = (clip, clip) + weights + (P(), P(), P())
    return jax.shard_map(
        functools.partial(shards, grid),
        mesh=grid.mesh,
        in_specs=in_specs,
        out_specs=out_specs,
        check_vma=False,
    )
```

```python
import functools
import itertools

import jax
import jax.numpy as jnp
from jax import lax
from jax.experimental import pallas as pl
from jax.experimental.pallas import tpu as pltpu
from jax.sharding import Mesh, PartitionSpec as P

D = 1536
HEAD_DIM = 64
FF = 6144
STEP = 10


NORM_EPS = 1e-05
BETA_ONE = 0.9
BETA_TWO = 0.999
ADAM_EPS = 1e-06
DECAY = 0.01
RATE = 0.5
SCALE = 0.125

AXES = ("y", "c", "z", "x")
HALF = D // 2
PAIR = 2 * HEAD_DIM
BF16 = jnp.bfloat16
F32 = jnp.float32
ANY = pl.BlockSpec(memory_space=pl.ANY)
WHOLE = pl.BlockSpec(memory_space=pltpu.VMEM)
SCALARS = pl.BlockSpec(memory_space=pltpu.SMEM)
LIGHT = pl.CostEstimate(flops=2**20, bytes_accessed=2**20, transcendentals=0)


def norm_rows(matrix):
    centred = matrix - jnp.mean(matrix, axis=-1, keepdims=True)
    inverse = lax.rsqrt(jnp.mean(centred * centred, axis=-1, keepdims=True) + NORM_EPS)
    return (centred * inverse, inverse)


def norm_back(gradient, normed, inverse):
    return inverse * (
        gradient
        - jnp.mean(gradient, axis=-1, keepdims=True)
        - normed * jnp.mean(gradient * normed, axis=-1, keepdims=True)
    )


def dot(first, second):
    return jnp.dot(first, second, preferred_element_type=F32)


def dot_back(first, second):
    return lax.dot_general(first, second, (((1,), (1,)), ((), ())), preferred_element_type=F32)


def dot_rows(first, second):
    return lax.dot_general(first, second, (((0,), (0,)), ((), ())), preferred_element_type=F32)


def pick(array, index, axis):
    return lax.dynamic_index_in_dim(array, index, axis, keepdims=False)


def no_work(*refs):
    pass


def after(values, others):
    values = list(values)
    return pl.pallas_call(
        no_work,
        out_shape=[jax.ShapeDtypeStruct(value.shape, value.dtype) for value in values],
        in_specs=[ANY] * (len(values) + len(others)),
        out_specs=[ANY] * len(values),
        input_output_aliases={k: k for k in range(len(values))},
    )(*values, *others)


def total(terms):
    return sum(term.astype(F32) for term in terms)


def only(block, head):
    lane = lax.broadcasted_iota(jnp.int32, block.shape, 1)
    mine = lane < HEAD_DIM if head == 0 else lane >= HEAD_DIM
    return jnp.where(mine, block, jnp.zeros_like(block))


def both_heads(first, second):
    lane = lax.broadcasted_iota(jnp.int32, first.shape, 1)
    return jnp.where(lane < HEAD_DIM, first, second)


def attend_heads(valid, query, key, value):
    mixed = []
    for head in range(2):
        scores = dot_back(only(query, head), key) * SCALE
        column = lax.broadcasted_iota(jnp.int32, scores.shape, 1)
        scores = jnp.where(column < valid, scores, -1e30)
        powers = jnp.exp(scores - jnp.max(scores, axis=-1, keepdims=True))
        chances = (powers / jnp.sum(powers, axis=-1, keepdims=True)).astype(BF16)
        mixed.append(dot(chances, value))
    return both_heads(*mixed).astype(BF16)


def attend_kernel(valid_ref, query_ref, key_ref, value_ref, out_ref):
    valid = valid_ref[pl.program_id(0)]
    out_ref[...] = attend_heads(valid, query_ref[...], key_ref[...], value_ref[...])


def attend_back_kernel(
    valid_ref, query_ref, key_ref, value_ref, d_ref, d_query_ref, d_key_ref, d_value_ref
):
    valid = valid_ref[pl.program_id(0)]
    query, key, value, d_mix = query_ref[...], key_ref[...], value_ref[...], d_ref[...]
    parts = []
    for head in range(2):
        scores = dot_back(only(key, head), query) * SCALE
        row = lax.broadcasted_iota(jnp.int32, scores.shape, 0)
        scores = jnp.where(row < valid, scores, -1e30)
        powers = jnp.exp(scores - jnp.max(scores, axis=0, keepdims=True))
        chances = powers / jnp.sum(powers, axis=0, keepdims=True)
        d_chances = dot_back(only(value, head), d_mix)
        mean = jnp.sum(chances * d_chances, axis=0, keepdims=True)
        d_scores = (chances * (d_chances - mean)).astype(BF16)
        d_value = dot(chances.astype(BF16), d_mix)
        d_key = dot(d_scores, query) * SCALE
        d_query = dot_rows(d_scores, key) * SCALE
        parts.append((d_query, d_key, d_value))
    for out_ref, first, second in zip((d_query_ref, d_key_ref, d_value_ref), *parts):
        out_ref[...] = both_heads(first, second).astype(BF16)


def block_of(rows, row_shift, column_shift):
    return pl.BlockSpec((rows, PAIR), lambda b, j: (b + row_shift, j + column_shift))


def attend(valid, query, key, value):
    frames, words = query[1], key[1]
    pairs = HALF // PAIR
    return pl.pallas_call(
        attend_kernel,
        out_shape=jax.ShapeDtypeStruct((2 * frames, HALF), BF16),
        grid=(2, pairs),
        in_specs=[SCALARS] + [block_of(*part[1:]) for part in (query, key, value)],
        out_specs=block_of(frames, 0, 0),
        compiler_params=pltpu.CompilerParams(vmem_limit_bytes=32 * 2**20),
        cost_estimate=LIGHT,
    )(valid, query[0], key[0], value[0])


def attend_back(valid, query, key, value, d_mixture):
    frames, words = query[1], key[1]
    pairs = HALF // PAIR
    return pl.pallas_call(
        attend_back_kernel,
        out_shape=[
            jax.ShapeDtypeStruct((2 * rows, HALF), BF16) for rows in (frames, words, words)
        ],
        grid=(2, pairs),
        in_specs=[SCALARS]
        + [block_of(*part[1:]) for part in (query, key, value)]
        + [block_of(frames, 0, 0)],
        out_specs=[block_of(rows, 0, 0) for rows in (frames, words, words)],
        compiler_params=pltpu.CompilerParams(vmem_limit_bytes=48 * 2**20),
        cost_estimate=LIGHT,
    )(valid, query[0], key[0], value[0], d_mixture)


def copy_all(copies):
    for copy in copies:
        copy.start()
    for copy in copies:
        copy.wait()


def place_pieces(spot_ref, *refs, plan, sizes):
    ny, nb = sizes
    count = len(plan["offsets"]) * len(plan["parts"])
    pieces, sem = refs[:count], refs[-1]
    outs = refs[-1 - plan["outs"] : -1]
    y, x = spot_ref[0], spot_ref[3]
    copies = []
    for part, blocks in enumerate(plan["parts"]):
        for spot, (dy, dx) in enumerate(plan["offsets"]):
            from_y = lax.rem(y - dy + ny, ny)
            from_x = lax.rem(x - dx + nb, nb)
            piece = pieces[part * len(plan["offsets"]) + spot]
            for block, (out, lane, column, width) in enumerate(blocks):
                columns = pl.ds(column, width)
                if lane is None:
                    target = outs[out].at[from_y, :, from_x, :, columns]
                else:
                    target = outs[out].at[from_y, lane, :, from_x, :, columns]
                copies.append(
                    pltpu.make_async_copy(piece.at[:, block], target, sem.at[len(copies)])
                )
    copy_all(copies)


def place_ranks(spot_ref, lines_ref, in_ref, down_ref, sem, *, offsets, sizes, rows, depth):
    ny, na, nb = sizes
    y, c, x = spot_ref[0], spot_ref[1], spot_ref[3]
    copies = []
    for block, (dy, dc, dx) in enumerate(offsets):
        target = in_ref.at[
            lax.rem(y - dy + ny, ny), lax.rem(c + dc, 2), :, lax.rem(x - dx + nb, nb)
        ]
        source = lines_ref.at[:, pl.ds(block * rows, rows)]
        copies.append(pltpu.make_async_copy(source, target, sem.at[len(copies)]))
    source = lines_ref.at[:, pl.ds(len(offsets) * rows, depth)]
    copies.append(pltpu.make_async_copy(source, down_ref, sem.at[len(copies)]))
    copy_all(copies)


def place_columns(spot_ref, pieces_ref, out_ref, sem, *, offsets, sizes, width):
    ny, nb = sizes
    y, c, x = spot_ref[0], spot_ref[1], spot_ref[3]
    copies = []
    for k, (dy, dc, dx) in enumerate(offsets):
        rank = (lax.rem(y - dy + ny, ny) * 2 + lax.rem(c + dc, 2)) * nb + lax.rem(x - dx + nb, nb)
        for half in range(2):
            start = pl.multiple_of(half * FF + rank * width, 128)
            copies.append(
                pltpu.make_async_copy(
                    pieces_ref.at[k, :, pl.ds(half * width, width)],
                    out_ref.at[:, pl.ds(start, width)],
                    sem.at[len(copies)],
                )
            )
    copy_all(copies)


def place(kernel, spot, arrays, shapes, copies):
    size = sum(a.size * a.dtype.itemsize for a in arrays)
    return pl.pallas_call(
        kernel,
        out_shape=[jax.ShapeDtypeStruct(shape, BF16) for shape in shapes],
        in_specs=[SCALARS] + [ANY] * len(arrays),
        out_specs=[WHOLE] * len(shapes),
        scratch_shapes=[pltpu.SemaphoreType.DMA((copies,))],
        compiler_params=pltpu.CompilerParams(vmem_limit_bytes=40 * 2**20),
        cost_estimate=pl.CostEstimate(flops=0, bytes_accessed=2 * size, transcendentals=0),
    )(spot, *arrays)


def prepare_kernel(
    spot_ref, qkv_ref, square_ref, ctx_ref, in_ref, own_ref, other_ref, block_ref,
    *, offsets, sizes
):
    ny, na, nb = sizes
    y, c, x = spot_ref[0], spot_ref[1], spot_ref[3]
    part = D // (2 * ny)
    for out_ref, which in ((own_ref, c), (other_ref, 1 - c)):
        for k in range(5):
            for block in range(ny):
                start = block * 2 * part + which * part
                if k < 3:
                    values = qkv_ref[:, pl.ds(pl.multiple_of(k * D + start, part), part)]
                elif k == 3:
                    values = square_ref[1, :, pl.ds(pl.multiple_of(start, part), part)]
                else:
                    values = jnp.concatenate(
                        [
                            ctx_ref[:, pl.ds(pl.multiple_of(side * D + start, part), part)]
                            for side in range(2)
                        ]
                    )
                out_ref[k, :, block * part : (block + 1) * part] = values.astype(BF16)
    for k, matrix in enumerate((0, 2)):
        for side in range(2):
            values = square_ref[matrix, :, side * HALF : (side + 1) * HALF]
            own_ref[5 + 2 * k + side] = values.astype(BF16)
    width = FF // len(offsets)
    share = width // na
    for k, (dy, dc, dx) in enumerate(offsets):
        rank = lax.rem(y + dy, ny) * 2 + lax.rem(c + dc, 2)
        first = lax.rem(x + dx, nb) == 0
        for side in range(2):
            for z in range(na):
                start = pl.multiple_of(side * FF + (rank * na + z) * nb * share, 128)
                values = in_ref[:, pl.ds(start, nb * share)].astype(BF16)
                values = jnp.where(first, values[:, :share], values[:, share:])
                at = side * width + z * share
                block_ref[k, :, at : at + share] = values


BLOCKS = [(0, lane, k * HALF, lane, k) for k in range(3) for lane in range(2)]
BLOCKS += [(1, None, 0, 0, 5), (1, None, HALF, 0, 6), (2, 0, 0, 0, 3), (2, 1, 0, 1, 3)]
BLOCKS += [(3, 0, 0, 0, 4), (3, 1, 0, 1, 4), (4, None, 0, 0, 7), (4, None, HALF, 0, 8)]
ACROSS = (0, 1, 2, 6, 7, 10, 11)


def gather_kernel(
    valid_ref, own_hbm, other_hbm, lines_hbm, more_lines_hbm, words_ref, more_words_ref,
    mixture_ref, qkv_ref, text_ref, kv_ref, *refs,
):
    outs, arrays = refs[:5], refs[5:10]
    entry, x_send, x_recv, y_send, y_recv, on_send, on_recv, own_sem, load_sem, out_sem = refs[10:]
    y, c, x = (lax.axis_index(axis) for axis in "ycx")
    far_y, far_x = 1 - y, 1 - x
    frames = entry.shape[1]

    def place_of(block, at_y, at_x):
        array, lane, column, _, _ = BLOCKS[block]
        columns = pl.ds(column, HALF)
        if lane is None:
            return arrays[array].at[at_y, :, at_x, :, columns]
        return arrays[array].at[at_y, 1 - c if lane else c, :, at_x, :, columns]

    def remote(source, target, send, recv, device):
        return pltpu.make_async_remote_copy(
            src_ref=source,
            dst_ref=target,
            send_sem=send,
            recv_sem=recv,
            device_id=device,
            device_id_type=pl.DeviceIdType.MESH,
        )

    barrier = pltpu.get_barrier_semaphore()
    for device in ({"y": far_y}, {"x": far_x}):
        pl.semaphore_signal(
            barrier, inc=1, device_id=device, device_id_type=pl.DeviceIdType.MESH
        )
    pl.semaphore_wait(barrier, 2)
    count = len(BLOCKS)
    to_x, to_y, onward, own = [], [], [], []
    for b in range(count):
        here = place_of(b, y, x)
        source = (lines_hbm, more_lines_hbm)[BLOCKS[b][3]].at[:, BLOCKS[b][4]]
        to_x.append(remote(source, here, x_send.at[b], x_recv.at[b], {"x": far_x}))
        to_y.append(remote(source, here, y_send.at[b], y_recv.at[b], {"y": far_y}))
        if b in ACROSS:
            there, device = place_of(b, y, far_x), {"y": far_y}
        else:
            there, device = place_of(b, far_y, x), {"x": far_x}
        onward.append(remote(there, there, on_send.at[b], on_recv.at[b], device))
        own.append(pltpu.make_async_copy(source, here, own_sem.at[b]))

    def send(blocks):
        for b in blocks:
            to_x[b].start()
            to_y[b].start()
            own[b].start()

    def hand_on(blocks):
        for b in blocks:
            (to_x if b in ACROSS else to_y)[b].wait_recv()
            onward[b].start()

    def arrive(blocks):
        for b in blocks:
            own[b].wait()
            (to_y if b in ACROSS else to_x)[b].wait_recv()
            onward[b].wait_recv()

    send(range(6))
    loads = [
        pltpu.make_async_copy(source, entry.at[k], load_sem.at[k])
        for k, source in enumerate((own_hbm, other_hbm))
    ]
    for load in loads:
        load.start()
    text_ref[...] = jnp.zeros_like(text_ref)
    share = arrays[3].shape[-2] // 2
    for k, ref in enumerate((words_ref, more_words_ref)):
        height = ref.shape[0]
        words = ref[...]
        for device in range(D // (2 * share)):
            part = words[:, device * share : (device + 1) * share]
            for side in range(2):
                at, column = (2 * side + k) * height, (2 * device + side) * share
                text_ref[at : at + height, column : column + share] = part
    hand_on(range(6))
    send(range(6, count))
    for load in loads:
        load.wait()
    arrive(range(6))
    copies = [pltpu.make_async_copy(arrays[0], outs[0], out_sem.at[0])]
    copies[0].start()
    for k in range(2):
        weights = arrays[0][...].reshape(D, 3 * HALF)
        qkv_ref[k * frames : (k + 1) * frames, :] = dot(entry[k], weights).astype(BF16)
    pairs = HALF // PAIR

    @pl.loop(0, 2 * pairs)
    def _(step):
        clip, j = step // pairs, step % pairs
        rows = pl.ds(pl.multiple_of(clip * frames, frames), frames)
        lanes = [pl.ds(pl.multiple_of(k * HALF + j * PAIR, PAIR), PAIR) for k in range(3)]
        query, key, value = (qkv_ref[rows, lane] for lane in lanes)
        mixture_ref[rows, lanes[0]] = attend_heads(valid_ref[clip], query, key, value)

    hand_on(range(6, count))
    arrive(range(6, count))
    kv_ref[...] = dot(text_ref[...], arrays[3][...].reshape(D, HALF)).astype(BF16)
    for k in range(1, 5):
        copies.append(pltpu.make_async_copy(arrays[k], outs[k], out_sem.at[k]))
        copies[k].start()
    for copy in copies:
        copy.wait()
    for b in range(count):
        to_x[b].wait_send()
        to_y[b].wait_send()
        onward[b].wait_send()


def gather_group(valid, own, other, lines, more_lines, words, more_words):
    na, _, rows, _ = lines.shape
    count = len(BLOCKS)
    frames = own.shape[0]
    tall = lambda cols: (2, 2, na, 2, rows, cols)
    wide = (2, na, 2, rows, D)
    shapes = [tall(3 * HALF), wide, tall(HALF), tall(HALF), wide]
    sem = lambda size: pltpu.SemaphoreType.DMA((size,))
    return pl.pallas_call(
        gather_kernel,
        out_shape=[
            jax.ShapeDtypeStruct((2 * frames, HALF), BF16),
            jax.ShapeDtypeStruct((2 * frames, 3 * HALF), BF16),
            jax.ShapeDtypeStruct((4 * words.shape[0], D), BF16),
            jax.ShapeDtypeStruct((4 * words.shape[0], HALF), BF16),
        ]
        + [jax.ShapeDtypeStruct(shape, BF16) for shape in shapes],
        in_specs=[SCALARS] + [ANY] * 4 + [WHOLE] * 2,
        out_specs=[WHOLE] * 4 + [ANY] * 5,
        scratch_shapes=[pltpu.VMEM(shape, BF16) for shape in shapes]
        + [pltpu.VMEM((2, frames, D), BF16)]
        + [sem(count)] * 7
        + [sem(2), sem(5)],
        compiler_params=pltpu.CompilerParams(
            vmem_limit_bytes=56 * 2**20, collective_id=4, has_side_effects=True
        ),
        cost_estimate=LIGHT,
    )(valid, own, other, lines, more_lines, words, more_words)


def ffn_kernel(
    entry_a, entry_b, d_a, d_b, in_hbm, down_hbm,
    hidden_ref, d_gate_up_ref, d_branch_ref, own_ref, other_ref,
    entry_ref, d_ref, in_ref, down_ref, sem,
):
    step = pl.program_id(0)
    sources = (entry_a, in_hbm, d_a, down_hbm, entry_b, d_b)
    targets = (entry_ref.at[0], in_ref, d_ref.at[0], down_ref, entry_ref.at[1], d_ref.at[1])
    copies = [
        pltpu.make_async_copy(source, target, sem.at[k])
        for k, (source, target) in enumerate(zip(sources, targets))
    ]

    @pl.when(step == 0)
    def _():
        for copy in copies:
            copy.start()
        for copy in copies[:4]:
            copy.wait()

    @pl.when(step == 1)
    def _():
        for copy in copies[4:]:
            copy.wait()

    width = down_ref.shape[0]
    frames = d_ref.shape[1]
    notes = entry_ref[step, frames:, :].astype(F32)
    gate_row = notes[0:1] + notes[1:2] + notes[2:3]
    d_branch = (d_ref[step].astype(F32) * gate_row).astype(BF16)
    d_branch_ref[...] = d_branch
    gate_up = dot(entry_ref[step, :frames, :], in_ref[...])
    gate, up = gate_up[:, :width], gate_up[:, width:]
    logistic = jax.nn.sigmoid(gate)
    hidden = (gate * logistic * up).astype(BF16)
    hidden_ref[...] = hidden
    d_hidden = dot_back(d_branch, down_ref[...])
    d_gate = d_hidden * up * logistic * (1.0 + gate * (1.0 - logistic))
    d_gate_up_ref[:, :width] = d_gate.astype(BF16)
    d_gate_up_ref[:, width:] = (d_hidden * gate * logistic).astype(BF16)
    d_entry = dot_back(d_gate_up_ref[...], in_ref[...]).astype(BF16)
    branch = dot(hidden, down_ref[...]).astype(BF16)

    @pl.when(step == 0)
    def _():
        own_ref[0] = d_entry
        own_ref[1] = branch

    @pl.when(step == 1)
    def _():
        other_ref[0] = d_entry
        other_ref[1] = branch


NOTE_ROWS = 16


def gate_notes(gate):
    high = gate.astype(BF16)
    rest = gate - high.astype(F32)
    middle = rest.astype(BF16)
    low = (rest - middle.astype(F32)).astype(BF16)
    blank = jnp.zeros((NOTE_ROWS - 3, gate.shape[0]), BF16)
    return jnp.concatenate([jnp.stack([high, middle, low]), blank])


def ffn_both_ways(entries, cotangents, rank_in, rank_down):
    frames = cotangents[0].shape[0]
    width = rank_down.shape[0]
    rows_of = lambda cols: pl.BlockSpec((frames, cols), lambda i: (i, 0))
    whole = pl.BlockSpec((2, frames, D), lambda i: (0, 0, 0))
    shape = lambda *sizes: jax.ShapeDtypeStruct(sizes, BF16)
    return pl.pallas_call(
        ffn_kernel,
        out_shape=[shape(2 * frames, cols) for cols in (width, 2 * width, D)]
        + [shape(2, frames, D)] * 2,
        grid=(2,),
        in_specs=[ANY] * 6,
        out_specs=[rows_of(cols) for cols in (width, 2 * width, D)] + [whole] * 2,
        scratch_shapes=[
            pltpu.VMEM((2, frames + NOTE_ROWS, D), BF16),
            pltpu.VMEM((2, frames, D), BF16),
            pltpu.VMEM((D, 2 * width), BF16),
            pltpu.VMEM((width, D), BF16),
            pltpu.SemaphoreType.DMA((6,)),
        ],
        compiler_params=pltpu.CompilerParams(vmem_limit_bytes=56 * 2**20),
        cost_estimate=LIGHT,
    )(*entries, *cotangents, rank_in, rank_down)


def outer_kernel(*refs, lefts, groups, rows, lanes):
    left_refs, right_refs, out_ref = refs[:lefts], refs[lefts:-1], refs[-1]

    def pieces(group):
        return [ref[k : k + rows, :] for ref in group for k in range(0, ref.shape[0], rows)]

    left_pieces = pieces(left_refs)
    start = column = 0
    for size in groups:
        group = right_refs[start : start + size]
        start += size
        sums = None
        for left, right in zip(left_pieces, pieces(group)):
            term = dot_rows(left, right)
            sums = term if sums is None else sums + term
        sums = sums.astype(BF16)
        end = column + sums.shape[1]
        if lanes is None:
            out_ref[0, :, column:end] = sums
        else:
            for k in range(out_ref.shape[0]):
                out_ref[k, 0, :, column:end] = sums[k * lanes : (k + 1) * lanes]
        column = end


def outer_sum(lefts, groups, rows, block, lanes=None, halves=1):
    depth = lefts[0].shape[1]
    cols = sum(group[0][1] for group in groups) // halves
    blocks = depth // block * halves
    if block % 128:
        left = jnp.concatenate([a[: a.shape[0] // rows * rows] for a in lefts])
        right = jnp.concatenate(
            [
                jnp.concatenate([a[:, at * width : (at + 1) * width] for a, width, at in group])
                for group in groups
            ],
            axis=1,
        )
        out = dot_rows(left, right).astype(BF16).reshape(depth // block, block, halves, cols)
        return jnp.swapaxes(out, 1, 2).reshape(blocks, block, cols)
    if lanes is None:
        out_shape = (blocks, block, cols)
        out_spec = pl.BlockSpec((1, block, cols), lambda i: (i, 0, 0))
    else:
        out_shape = (block // lanes, blocks, lanes, cols)
        out_spec = pl.BlockSpec((block // lanes, 1, lanes, cols), lambda i: (0, i, 0, 0))
    used = lambda array: array.shape[0] // rows * rows

    def right_spec(right):
        array, width, at = right
        if halves > 1:
            return pl.BlockSpec((array.shape[0], width // halves), lambda i: (0, i % halves))
        return pl.BlockSpec(
            (array.shape[0], width), lambda i: (0, at), pipeline_mode=pl.Buffered(1)
        )

    rights = [right for group in groups for right in group]
    return pl.pallas_call(
        functools.partial(
            outer_kernel,
            lefts=len(lefts),
            groups=[len(group) for group in groups],
            rows=rows,
            lanes=lanes,
        ),
        out_shape=jax.ShapeDtypeStruct(out_shape, BF16),
        grid=(blocks,),
        in_specs=[pl.BlockSpec((used(a), block), lambda i: (0, i // halves)) for a in lefts]
        + [right_spec(right) for right in rights],
        out_specs=out_spec,
        compiler_params=pltpu.CompilerParams(vmem_limit_bytes=56 * 2**20),
        cost_estimate=LIGHT,
    )(*lefts, *[right[0] for right in rights])


def reduce_kernel(*refs, plan, inputs):
    arrays, (small_hbm, in_hbm, down_hbm) = refs[:inputs], refs[inputs : inputs + 3]
    out_ref, small_ref, in_ref, down_ref, down_in = refs[inputs + 3 : inputs + 8]
    (
        blocks, first_x, first_y, second, second_in, kept, lines_in, mine, other_in, left_ref, right_ref, notes,
        load_sem, first_send, first_recv, second_send, second_recv, line_send, line_recv,
        core_send, core_recv, note_send, note_recv,
        in_own, in_core, in_y, in_x, in_send, in_recv, down_send, down_recv, down_sem,
    ) = refs[inputs + 8 :]
    y, c, z, x = (lax.axis_index(axis) for axis in AXES)
    na, rows = kept.shape[1], kept.shape[3]
    far_y, far_c, far_x = 1 - y, 1 - c, 1 - x
    count = len(plan)
    names = [("y", far_y), ("c", far_c), ("x", far_x)]
    names += [("z", lax.rem(z + k, na)) for k in range(1, na)]
    slots = {}
    for m, (_, _, _, turn) in enumerate(plan):
        slots[m] = sum(1 for other in plan[:m] if other[3] == turn)

    def remote(source, target, send, recv, axis, at):
        return pltpu.make_async_remote_copy(
            src_ref=source,
            dst_ref=target,
            send_sem=send,
            recv_sem=recv,
            device_id={axis: at},
            device_id_type=pl.DeviceIdType.MESH,
        )

    barrier = pltpu.get_barrier_semaphore()
    for axis, at in names:
        pl.semaphore_signal(
            barrier, inc=1, device_id={axis: at}, device_id_type=pl.DeviceIdType.MESH
        )
    pl.semaphore_wait(barrier, len(names))

    def first_copy(m):
        if plan[m][3]:
            source, target, axis, at = blocks.at[m, far_y], first_y.at[slots[m]], "y", far_y
        else:
            source, target, axis, at = blocks.at[m, :, :, :, far_x], first_x.at[slots[m]], "x", far_x
        return remote(source, target, first_send.at[m], first_recv.at[m], axis, at)

    def second_copy(m):
        axis, at = ("x", far_x) if plan[m][3] else ("y", far_y)
        return remote(
            second.at[m], second_in.at[m], second_send.at[m], second_recv.at[m], axis, at
        )

    def line_copies(m):
        return [
            remote(
                kept.at[m, lax.rem(z + k, na)],
                lines_in.at[m, k - 1],
                line_send.at[m * (na - 1) + k - 1],
                line_recv.at[m * (na - 1) + k - 1],
                "z",
                lax.rem(z + k, na),
            )
            for k in range(1, na)
        ]

    def core_copy(m):
        return remote(
            mine.at[m, far_c], other_in.at[m], core_send.at[m], core_recv.at[m], "c", far_c
        )

    def note_copies(hop):
        if hop == 0:
            hops = [(notes.at[0, 0, 0, 0], notes.at[0, 0, 0, 1], "x", far_x)]
        elif hop == 1:
            hops = [
                (notes.at[0, 0, 0], notes.at[0, 0, k], "z", lax.rem(z + k, na))
                for k in range(1, na)
            ]
        elif hop == 2:
            hops = [(notes.at[0, 0], notes.at[0, 1], "c", far_c)]
        else:
            hops = [(notes.at[0], notes.at[1], "y", far_y)]
        at = 0 if hop == 0 else hop + (na - 2 if hop > 1 else 0)
        return [
            remote(source, target, note_send.at[at + k], note_recv.at[at + k], axis, to)
            for k, (source, target, axis, to) in enumerate(hops)
        ]

    def loads(m):
        copies = []
        for group, buffer in ((plan[m][1], left_ref), (plan[m][2], right_ref)):
            start = 0
            for place_of in group:
                height, width = arrays[place_of].shape
                copies.append(
                    pltpu.make_async_copy(
                        arrays[place_of],
                        buffer.at[m % 2, pl.ds(start, height), pl.ds(0, width)],
                        load_sem.at[m % 2, len(copies)],
                    )
                )
                start += height
        return copies

    def compute(m):
        kind, lefts, rights, _ = plan[m]
        height = sum(arrays[place_of].shape[0] for place_of in lefts)
        depth = na * 2 * rows

        @pl.loop(0, 4)
        def _(step):
            at_y, at_c = step // 2, step % 2
            at, columns = (step, 0) if kind == "tall" else (at_y, at_c)
            left = left_ref[m % 2, :height, pl.ds(pl.multiple_of(at * depth, 128), depth)]
            right = right_ref[m % 2, :height, pl.ds(pl.multiple_of(columns * HALF, 128), HALF)]
            sums = dot_rows(left, right).astype(BF16)
            for k in range(2 * na):
                blocks[m, at_y, at_c, k // 2, k % 2] = sums[k * rows : (k + 1) * rows]

    def arrived(m, at_c, at_z, at_y, at_x):
        if plan[m][3]:
            came = first_y[slots[m], at_c, at_z, at_x]
        else:
            came = first_x[slots[m], at_y, at_c, at_z]
        return blocks[m, at_y, at_c, at_z, at_x].astype(F32) + came.astype(F32)

    load = pltpu.make_async_copy(small_hbm, notes.at[0, 0, 0, 0], load_sem.at[0, 0])
    load.start()
    load.wait()
    hops = [note_copies(hop) for hop in range(4)]
    for copy in hops[0]:
        copy.start()

    load = pltpu.make_async_copy(in_hbm, in_own, load_sem.at[0, 0])
    load.start()
    load.wait()

    def in_copies(first, pairs, axis, at):
        return [
            remote(source, target, in_send.at[first + k], in_recv.at[first + k], axis, at)
            for k, (source, target) in enumerate(pairs)
        ]

    in_hops = [
        in_copies(0, [(in_own.at[:, far_c], in_core)], "c", far_c),
        in_copies(
            1, [(in_own.at[far_y, c], in_y.at[0]), (in_core.at[far_y], in_y.at[1])], "y", far_y
        ),
        in_copies(
            3,
            [
                (in_own.at[y, c, far_x], in_x.at[0]),
                (in_core.at[y, far_x], in_x.at[1]),
                (in_y.at[0, far_x], in_x.at[2]),
                (in_y.at[1, far_x], in_x.at[3]),
            ],
            "x",
            far_x,
        ),
    ]
    for copy in in_hops[0]:
        copy.start()
    down_copies = [
        remote(
            down_hbm.at[lax.rem(z + k, na)], down_in.at[k - 1],
            down_send.at[k - 1], down_recv.at[k - 1], "z", lax.rem(z + k, na),
        )
        for k in range(1, na)
    ]
    for copy in down_copies:
        copy.start()
    for copy in loads(0):
        copy.start()
    def second_step(m):
        first_copy(m).wait_recv()

        @pl.loop(0, 2 * na)
        def _(step):
            at_c, at_z = step // na, step % na
            at_y, at_x = (y, far_x) if plan[m][3] else (far_y, x)
            second[m, at_c, at_z] = arrived(m, at_c, at_z, at_y, at_x).astype(BF16)

        second_copy(m).start()

    def line_step(m):
        second_copy(m).wait_recv()

        @pl.loop(0, 2 * na)
        def _(step):
            at_c, at_z = step // na, step % na
            sums = arrived(m, at_c, at_z, y, x) + second_in[m, at_c, at_z].astype(F32)
            kept[m, at_z, at_c] = sums.astype(BF16)

        for copy in line_copies(m):
            copy.start()

    def last_step(m):
        sums = kept[m, z].astype(F32)
        for k, copy in enumerate(line_copies(m)):
            copy.wait_recv()
            sums += lines_in[m, k].astype(F32)
        mine[m] = sums.astype(BF16)
        if plan[m][0] == "tall":
            core_copy(m).start()

    for m in range(count + 6):
        if m < count:
            for copy in loads(m):
                copy.wait()
            if m + 1 < count:
                for copy in loads(m + 1):
                    copy.start()
            compute(m)
            first_copy(m).start()
        if m in (1, 3):
            for copy in in_hops[m // 2]:
                copy.wait_recv()
            for copy in in_hops[m // 2 + 1]:
                copy.start()
        if m in (0, 2, 4):
            hop = m // 2
            for copy in hops[hop]:
                copy.wait_recv()
            for copy in hops[hop + 1]:
                copy.start()
        for behind, step in ((2, second_step), (4, line_step), (6, last_step)):
            if 0 <= m - behind < count:
                step(m - behind)
    order = range(count)
    for m in order:
        if plan[m][0] == "tall":
            core_copy(m).wait_recv()
            out_ref[m, 0] = mine[m, c]
            out_ref[m, 1] = other_in[m]
        else:
            out_ref[m] = mine[m]
    for copy in hops[3]:
        copy.wait_recv()
    small_ref[...] = notes[...]

    for copy in in_hops[2]:
        copy.wait_recv()
    width = in_own.shape[-1] // 2
    share = width // na
    for at_y in range(2):
        for at_c in range(2):
            if at_y:
                near = in_y[at_c, x]
            else:
                near = in_core[y, x] if at_c else in_own[y, c, x]
            across = in_x[at_y * 2 + at_c]
            low = jnp.where(x == 0, near, across)
            high = jnp.where(x == 0, across, near)
            rank = lax.rem(y + at_y, 2) * 2 + lax.rem(c + at_c, 2)
            for half in range(2):
                for k in range(na):
                    at = half * width + k * share
                    start = pl.multiple_of(half * FF + (rank * na + k) * 2 * share, 128)
                    in_ref[:, pl.ds(start, 2 * share)] = jnp.concatenate(
                        [low[:, at : at + share], high[:, at : at + share]], axis=1
                    )
    depth = down_ref.shape[0]
    sums = None
    for k in range(na):
        if k:
            down_copies[k - 1].wait_recv()
        source = down_in.at[k - 1] if k else down_hbm.at[z]
        copy = pltpu.make_async_copy(source, left_ref.at[0, pl.ds(0, depth)], down_sem.at[0])
        copy.start()
        copy.wait()
        term = left_ref[0, :depth, :].astype(F32)
        sums = term if sums is None else sums + term
    down_ref[...] = sums.astype(BF16)

    for hop in hops + in_hops + [down_copies]:
        for copy in hop:
            copy.wait_send()
    for m in range(count):
        first_copy(m).wait_send()
        second_copy(m).wait_send()
        for copy in line_copies(m):
            copy.wait_send()
        if plan[m][0] == "tall":
            core_copy(m).wait_send()


def reduce_group(matrices, small, grad_in, grad_down, na, rows):
    arrays, plan = [], []
    for kind, lefts, rights, turn in matrices:
        places = []
        for group in (lefts, rights):
            places.append([])
            for array in group:
                found = [k for k, known in enumerate(arrays) if known is array]
                if not found:
                    arrays.append(array)
                    found = [len(arrays) - 1]
                places[-1].append(found[0])
        plan.append((kind, *places, turn))
    count = len(plan)
    tall = max(sum(a.shape[0] for a in lefts) for _, lefts, _, _ in matrices)
    turns = [turn for *_, turn in plan]
    low = lambda *shape: pltpu.VMEM(shape, BF16)
    sem = lambda *shape: pltpu.SemaphoreType.DMA(shape)
    all_small = (2, 2, na, 2) + small.shape
    return pl.pallas_call(
        functools.partial(reduce_kernel, plan=plan, inputs=len(arrays)),
        out_shape=[
            jax.ShapeDtypeStruct((count, 2, rows, HALF), BF16),
            jax.ShapeDtypeStruct(all_small, BF16),
            jax.ShapeDtypeStruct((rows, 2 * FF), BF16),
            jax.ShapeDtypeStruct(grad_down.shape[1:], BF16),
            jax.ShapeDtypeStruct((na - 1,) + grad_down.shape[1:], BF16),
        ],
        in_specs=[ANY] * (len(arrays) + 3),
        out_specs=[WHOLE] * 4 + [ANY],
        scratch_shapes=[
            low(count, 2, 2, na, 2, rows, HALF),
            low(turns.count(0), 2, 2, na, rows, HALF),
            low(turns.count(1), 2, na, 2, rows, HALF),
            low(count, 2, na, rows, HALF),
            low(count, 2, na, rows, HALF),
            low(count, na, 2, rows, HALF),
            low(count, na - 1, 2, rows, HALF),
            low(count, 2, rows, HALF),
            low(count, rows, HALF),
            low(2, tall, D),
            low(2, tall, D),
            low(*all_small),
            sem(2, 4),
            sem(count),
            sem(count),
            sem(count),
            sem(count),
            sem(count * (na - 1)),
            sem(count * (na - 1)),
            sem(count),
            sem(count),
            sem(na + 2),
            sem(na + 2),
            low(*grad_in.shape),
            low(2, 2, *grad_in.shape[-2:]),
            low(2, 2, *grad_in.shape[-2:]),
            low(4, *grad_in.shape[-2:]),
            sem(7),
            sem(7),
            sem(na - 1),
            sem(na - 1),
            sem(1),
        ],
        compiler_params=pltpu.CompilerParams(
            vmem_limit_bytes=60 * 2**20, collective_id=1, has_side_effects=True
        ),
        cost_estimate=LIGHT,
    )(*arrays, small, grad_in, grad_down)


def pair_in_kernel(own_ref, other_ref, weight_ref, out_ref, *, product):
    for step, ref in enumerate((own_ref, other_ref)):

        @pl.when(pl.program_id(0) == step)
        def _():
            out_ref[...] = product(ref[...], weight_ref[...]).astype(BF16)


def pair_in(own, other, weight, product):
    frames = own.shape[0]
    cols = weight.shape[1] if product is dot else weight.shape[0]
    whole = lambda array: pl.BlockSpec(
        array.shape, lambda i: (0, 0), pipeline_mode=pl.Buffered(1)
    )
    return pl.pallas_call(
        functools.partial(pair_in_kernel, product=product),
        out_shape=jax.ShapeDtypeStruct((2 * frames, cols), BF16),
        grid=(2,),
        in_specs=[whole(own), whole(other), whole(weight)],
        out_specs=pl.BlockSpec((frames, cols), lambda i: (i, 0)),
        compiler_params=pltpu.CompilerParams(vmem_limit_bytes=48 * 2**20),
        cost_estimate=LIGHT,
    )(own, other, weight)


def pair_out_kernel(*refs, product):
    part_refs, weight_ref, own_ref, other_ref = refs[:-3], refs[-3], refs[-2], refs[-1]
    sums = None
    column = 0
    for ref in part_refs:
        weight = weight_ref[...]
        if len(part_refs) > 1:
            weight = weight_ref[:, column : column + ref.shape[1]]
            column += ref.shape[1]
        term = product(ref[...], weight)
        sums = term if sums is None else sums + term

    @pl.when(pl.program_id(0) == 0)
    def _():
        own_ref[...] = sums

    @pl.when(pl.program_id(0) == 1)
    def _():
        other_ref[...] = sums.astype(BF16)


def pair_out(parts, weight, product):
    frames = parts[0].shape[0] // 2
    cols = weight.shape[1] if product is dot else weight.shape[0]
    whole = pl.BlockSpec((frames, cols), lambda i: (0, 0))
    return pl.pallas_call(
        functools.partial(pair_out_kernel, product=product),
        out_shape=[
            jax.ShapeDtypeStruct((frames, cols), F32),
            jax.ShapeDtypeStruct((frames, cols), BF16),
        ],
        grid=(2,),
        in_specs=[pl.BlockSpec((frames, part.shape[1]), lambda i: (i, 0)) for part in parts]
        + [pl.BlockSpec(weight.shape, lambda i: (0, 0), pipeline_mode=pl.Buffered(1))],
        out_specs=[whole, whole],
        compiler_params=pltpu.CompilerParams(vmem_limit_bytes=48 * 2**20),
        cost_estimate=LIGHT,
    )(*parts, weight)


def notes_kernel(own_ref, out_ref, notes, send, recv):
    y, c, z, x = (lax.axis_index(axis) for axis in AXES)
    na = notes.shape[2]
    far_y, far_c, far_x = {"y": 1 - y}, {"c": 1 - c}, {"x": 1 - x}
    lines = [{"z": lax.rem(z + k, na)} for k in range(1, na)]
    barrier = pltpu.get_barrier_semaphore()
    for device in [far_y, far_c, far_x] + lines:
        pl.semaphore_signal(
            barrier, inc=1, device_id=device, device_id_type=pl.DeviceIdType.MESH
        )
    pl.semaphore_wait(barrier, 3 + len(lines))
    notes[0, 0, 0, 0] = own_ref[...]
    hops = [
        [(notes.at[0, 0, 0, 0], notes.at[0, 0, 0, 1], far_x)],
        [(notes.at[0, 0, 0], notes.at[0, 0, k + 1], line) for k, line in enumerate(lines)],
        [(notes.at[0, 0], notes.at[0, 1], far_c)],
        [(notes.at[0], notes.at[1], far_y)],
    ]
    at = 0
    copies = []
    for hop in hops:
        group = []
        for source, target, device in hop:
            group.append(
                pltpu.make_async_remote_copy(
                    src_ref=source,
                    dst_ref=target,
                    send_sem=send.at[at],
                    recv_sem=recv.at[at],
                    device_id=device,
                    device_id_type=pl.DeviceIdType.MESH,
                )
            )
            at += 1
        for copy in group:
            copy.start()
        for copy in group:
            copy.wait_recv()
        copies += group
    for copy in copies:
        copy.wait_send()
    out_ref[...] = notes[...]


def gather_notes(notes, na):
    all_notes = (2, 2, na, 2) + notes.shape
    sem = pltpu.SemaphoreType.DMA((na + 2,))
    return pl.pallas_call(
        notes_kernel,
        out_shape=jax.ShapeDtypeStruct(all_notes, BF16),
        in_specs=[WHOLE],
        out_specs=WHOLE,
        scratch_shapes=[pltpu.VMEM(all_notes, BF16), sem, sem],
        compiler_params=pltpu.CompilerParams(collective_id=5, has_side_effects=True),
        cost_estimate=LIGHT,
    )(notes)


def shift_kernel(
    terms_ref, cot_hbm, in_ref, shifts_ref, cots_hbm, parts_ref,
    from_core, line_out, line_in, y_out, y_in, x_out, x_in,
    in_core, in_y, in_x,
    core_sem, line_send, line_recv, step_sem, cot_send, cot_recv, relay_send, relay_recv,
    in_send, in_recv,
):
    y, c, z, x = (lax.axis_index(axis) for axis in AXES)
    na = terms_ref.shape[2]
    far_y, far_c, far_x = 1 - y, 1 - c, 1 - x

    def remote(source, target, send, recv, device):
        return pltpu.make_async_remote_copy(
            src_ref=source,
            dst_ref=target,
            send_sem=send,
            recv_sem=recv,
            device_id=device,
            device_id_type=pl.DeviceIdType.MESH,
        )

    devices = [{"y": far_y}, {"c": far_c}, {"x": far_x}]
    devices += [{"z": lax.rem(z + k, na)} for k in range(1, na)]
    barrier = pltpu.get_barrier_semaphore()
    for device in devices:
        pl.semaphore_signal(
            barrier, inc=1, device_id=device, device_id_type=pl.DeviceIdType.MESH
        )
    pl.semaphore_wait(barrier, len(devices))

    to_core = remote(terms_ref.at[:, 1], from_core, core_sem.at[0], core_sem.at[1], {"c": far_c})
    to_core.start()

    def block_copies(first, pairs, device):
        return [
            remote(source, target, in_send.at[first + k], in_recv.at[first + k], device)
            for k, (source, target) in enumerate(pairs)
        ]

    in_hops = [
        block_copies(0, [(in_ref.at[:, 1], in_core)], {"c": far_c}),
        block_copies(1, [(in_ref.at[1, 0], in_y.at[0]), (in_core.at[1], in_y.at[1])], {"y": far_y}),
        block_copies(
            3,
            [
                (in_ref.at[0, 0, 1], in_x.at[0]),
                (in_core.at[0, 1], in_x.at[1]),
                (in_y.at[0, 1], in_x.at[2]),
                (in_y.at[1, 1], in_x.at[3]),
            ],
            {"x": far_x},
        ),
    ]
    for copy in in_hops[0]:
        copy.start()
    chips = {1: {"x": far_x}, 2: {"y": far_y}}
    cots = {
        2 * k: remote(cot_hbm, cots_hbm.at[2 * k], cot_send.at[2 * k], cot_recv.at[2 * k], chips[k])
        for k in chips
    }
    cots[1] = remote(cot_hbm, cots_hbm.at[1], cot_send.at[1], cot_recv.at[1], {"c": far_c})
    for k in (1, 2, 3):
        cots[2 * k + 1] = remote(
            cots_hbm.at[2 * k], cots_hbm.at[2 * k + 1],
            cot_send.at[2 * k + 1], cot_recv.at[2 * k + 1], {"c": far_c},
        )
    relays = []
    for k, (part, size) in enumerate(halves_of(cot_hbm.shape[0])):
        near, next_to = (1, 2) if k == 0 else (2, 1)
        here = pl.ds(part, size)
        relays.append(
            remote(
                cots_hbm.at[2 * near, here], cots_hbm.at[6, here],
                relay_send.at[k], relay_recv.at[k], chips[next_to],
            )
        )
    cots[2].start()
    cots[4].start()
    cots[1].start()

    to_core.wait_recv()
    for copy in in_hops[0]:
        copy.wait_recv()
    for copy in in_hops[1]:
        copy.start()
    lines = []
    for k in range(1, na):
        line_out[k - 1] = terms_ref[:, 0, k] + from_core[:, k]
        lines.append(
            remote(
                line_out.at[k - 1], line_in.at[k - 1], line_send.at[k - 1], line_recv.at[k - 1],
                {"z": lax.rem(z - k + na, na)},
            )
        )
        lines[-1].start()
    here = terms_ref[:, 0, 0] + from_core[:, 0]
    for k, copy in enumerate(lines):
        copy.wait_recv()
        here = here + line_in[k]
    y_out[...] = here[1]
    to_y = remote(y_out, y_in, step_sem.at[0], step_sem.at[1], {"y": far_y})
    to_y.start()
    for k in (1, 2):
        cots[2 * k].wait_recv()
    for copy in relays:
        copy.start()
    for k in (1, 2):
        cots[2 * k + 1].start()
    to_y.wait_recv()
    here = here[0] + y_in[...]
    x_out[...] = here[1]
    to_x = remote(x_out, x_in, step_sem.at[2], step_sem.at[3], {"x": far_x})
    to_x.start()
    for copy in in_hops[1]:
        copy.wait_recv()
    for copy in in_hops[2]:
        copy.start()
    to_x.wait_recv()
    shifts_ref[...] = here[0] + x_in[...]

    for copy in relays:
        copy.wait_recv()
    cots[7].start()
    for copy in in_hops[2]:
        copy.wait_recv()
    for at_y in range(2):
        for at_c in range(2):
            near = in_ref[0, 0, 0] if not at_y and not at_c else None
            if near is None:
                near = in_y[at_c, 0] if at_y else in_core[0, 0]
            parts_ref[at_y, at_c, 0] = near
            parts_ref[at_y, at_c, 1] = in_x[at_y * 2 + at_c]
    for k in (1, 3, 5, 7):
        cots[k].wait_recv()
        cots[k].wait_send()
    for copy in [to_core, to_y, to_x, cots[2], cots[4]] + lines + relays + sum(in_hops, []):
        copy.wait_send()


def sum_shifts(terms, cotangent, blocks, na):
    rows = terms.shape[-2]
    full = lambda *shape: pltpu.VMEM(shape + (rows, 128), F32)
    sem = lambda size: pltpu.SemaphoreType.DMA((size,))
    block = blocks.shape[-2:]
    low = lambda *shape: pltpu.VMEM(shape + block, BF16)
    return pl.pallas_call(
        shift_kernel,
        out_shape=[
            jax.ShapeDtypeStruct((rows, 128), F32),
            jax.ShapeDtypeStruct((8,) + cotangent.shape, BF16),
            jax.ShapeDtypeStruct(blocks.shape, BF16),
        ],
        in_specs=[WHOLE, ANY, WHOLE],
        out_specs=[WHOLE, ANY, WHOLE],
        scratch_shapes=[
            full(2, na, 2),
            full(na - 1, 2, 2),
            full(na - 1, 2, 2),
            full(2),
            full(2),
            full(),
            full(),
            low(2, 2),
            low(2, 2),
            low(4),
            sem(2),
            sem(na - 1),
            sem(na - 1),
            sem(4),
            sem(8),
            sem(8),
            sem(2),
            sem(2),
            sem(7),
            sem(7),
        ],
        compiler_params=pltpu.CompilerParams(
            vmem_limit_bytes=32 * 2**20, collective_id=2, has_side_effects=True
        ),
        cost_estimate=LIGHT,
    )(terms, cotangent, blocks)


def halves_of(height):
    cut = height // 32 * 16
    return (0, cut), (cut, height - cut)


def ffn_group_kernel(
    entry_hbm, notes_hbm, cot_hbm, cots_hbm, lines_hbm, down_hbm,
    d_entry_hbm, grad_down_hbm, grad_in_hbm, branch_hbm, own_hbm, other_hbm, pair_hbm, back_hbm,
    sum_hbm, branch_back_hbm,
    entry, d_branch, hidden, d_gate_up, in_lines, down_lines, partial, away, branch, loaded, sums,
    local_sem, entry_send, entry_recv, cot_sem,
    pair_send, pair_recv, back_send, back_recv, branch_sem, out_sem,
    relay_send, relay_recv, branch_pair_send, branch_pair_recv, branch_send, branch_recv,
    *, chips, peers, sizes,
):
    ny, nb = sizes
    y, c, x = lax.axis_index("y"), lax.axis_index("c"), lax.axis_index("x")
    frames = cot_hbm.shape[0]
    rows = frames // 2
    own_rows = in_lines.shape[-2]
    width = down_lines.shape[0] * down_lines.shape[1]
    in_all = lambda: in_lines[...].reshape(D, 2 * width)
    down_all = lambda: down_lines[...].reshape(width, D)
    count = len(chips)
    sibling = {"c": 1 - c}
    ahead = [{"y": lax.rem(y + dy, ny), "x": lax.rem(x + dx, nb)} for dy, dx in chips]
    behind = [
        {"y": lax.rem(y - dy + ny, ny), "x": lax.rem(x - dx + nb, nb)} for dy, dx in chips
    ]

    def remote(source, target, send, recv, device):
        return pltpu.make_async_remote_copy(
            src_ref=source,
            dst_ref=target,
            send_sem=send,
            recv_sem=recv,
            device_id=device,
            device_id_type=pl.DeviceIdType.MESH,
        )

    barrier = pltpu.get_barrier_semaphore()
    for device in [sibling] + behind[1:]:
        pl.semaphore_signal(
            barrier, inc=1, device_id=device, device_id_type=pl.DeviceIdType.MESH
        )
    pl.semaphore_wait(barrier, count)

    loads = [
        pltpu.make_async_copy(source, target, local_sem.at[k])
        for k, (source, target) in enumerate(
            [
                (entry_hbm, entry.at[0, pl.ds(0, frames)]),
                (notes_hbm, entry.at[0, pl.ds(frames, NOTE_ROWS)]),
                (down_hbm, down_lines),
            ]
        )
    ]
    for k, (dy, dc, dx) in enumerate(peers):
        target = in_lines.at[
            lax.rem(y + dy, ny), lax.rem(c + dc, 2), :, lax.rem(x + dx, nb)
        ]
        source = lines_hbm.at[:, pl.ds(k * own_rows, own_rows)]
        loads.append(pltpu.make_async_copy(source, target, local_sem.at[3 + k]))
    for load in loads:
        load.start()
    cot_loads = [
        pltpu.make_async_copy(
            cots_hbm.at[k] if k else cot_hbm, d_branch.at[k], cot_sem.at[k]
        )
        for k in range(2 * count)
    ]
    for load in cot_loads:
        load.start()
    entry_copies = {
        1: remote(entry.at[0], entry.at[1], entry_send.at[1], entry_recv.at[1], sibling)
    }
    for k in range(1, count):
        entry_copies[2 * k] = remote(
            entry.at[0], entry.at[2 * k], entry_send.at[2 * k], entry_recv.at[2 * k], ahead[k]
        )
        entry_copies[2 * k + 1] = remote(
            entry.at[2 * k], entry.at[2 * k + 1],
            entry_send.at[2 * k + 1], entry_recv.at[2 * k + 1], sibling,
        )
    for load in loads[:2]:
        load.wait()
    for k in (2, 4, 1):
        entry_copies[k].start()

    relays = []
    height = entry.shape[1]
    for k, (part, size) in enumerate(halves_of(height)):
        near, next_to = (1, 2) if k == 0 else (2, 1)
        here = pl.ds(part, size)
        relays.append(
            remote(
                entry.at[2 * near, here], entry.at[2 * 3, here],
                relay_send.at[k], relay_recv.at[k], ahead[next_to],
            )
        )

    def branch_copies(k):
        copies = []
        if k == 0:
            copies.append(pltpu.make_async_copy(branch.at[0], own_hbm, branch_sem.at[0]))
        copies.append(
            remote(
                branch.at[1], other_hbm.at[k], branch_pair_send.at[k], branch_pair_recv.at[k], sibling
            )
        )
        return copies

    def branch_wait(k):
        for copy in branch_copies(k)[:-1]:
            copy.wait()
        branch_copies(k)[-1].wait_send()

    def branch_copy(k):
        return remote(
            sum_hbm.at[k - 1], branch_back_hbm.at[k - 1], branch_send.at[k], branch_recv.at[k],
            behind[k],
        )

    order = (0, 3, 1, 2)
    turn = {k: order.index(k) % 2 for k in order}

    def pair_copy(k):
        return remote(
            away.at[turn[k]], pair_hbm.at[k], pair_send.at[k], pair_recv.at[k], sibling
        )

    def back_copy(k):
        return remote(
            partial.at[k], back_hbm.at[k - 1], back_send.at[k], back_recv.at[k], behind[k]
        )

    def compute(k, i):
        @pl.loop(0, 2)
        def _(part):
            slot = 2 * k + i
            here = pl.ds(pl.multiple_of(part * rows, rows), rows)
            notes = entry[slot, frames:, :].astype(F32)
            gate_row = notes[0:1] + notes[1:2] + notes[2:3]
            d_here = (d_branch[slot, here, :].astype(F32) * gate_row).astype(BF16)
            d_branch[slot, here, :] = d_here
            gate_up = dot(entry[slot, here, :], in_all())
            gate, up = gate_up[:, :width], gate_up[:, width:]
            logistic = jax.nn.sigmoid(gate)
            hidden_here = (gate * logistic * up).astype(BF16)
            hidden[slot, here, :] = hidden_here
            d_hidden = dot_back(d_here, down_all())
            d_gate = d_hidden * up * logistic * (1.0 + gate * (1.0 - logistic))
            d_gate_up[slot, here, :width] = d_gate.astype(BF16)
            d_gate_up[slot, here, width:] = (d_hidden * gate * logistic).astype(BF16)
            d_entry = dot_back(d_gate_up[slot, here, :], in_all()).astype(BF16)
            branch[i, here, :] = dot(hidden_here, down_all()).astype(BF16)

            if i == 0:
                partial[k, here, :] = d_entry
            else:
                away[turn[k], here, :] = d_entry

    def move(source, target):
        copy = pltpu.make_async_copy(source, target, out_sem.at[0])
        copy.start()
        copy.wait()

    def fetch(source):
        move(source, loaded)
        return loaded[...].astype(F32)

    def branch_terms(k):
        branch_copies(k)[-1].wait_recv()
        own = branch[0].astype(F32) if k else fetch(own_hbm)
        return own + fetch(other_hbm.at[k])

    def finish(k):
        pair_copy(k).wait_recv()
        partial[k] = (partial[k].astype(F32) + fetch(pair_hbm.at[k])).astype(BF16)
        if k:
            back_copy(k).start()
            pair_copy(k).wait_send()
            away[turn[k]] = branch_terms(k).astype(BF16)
            move(away.at[turn[k]], sum_hbm.at[k - 1])
            branch_copy(k).start()
        else:
            pair_copy(k).wait_send()

    before = None
    for k in order:
        if k == 0:
            for load in loads[2:]:
                load.wait()
        elif k == 3:
            entry_copies[2].wait_recv()
            entry_copies[4].wait_recv()
            for copy in relays:
                copy.start()
            for near in (3, 5):
                entry_copies[near].start()
            for copy in relays:
                copy.wait_recv()
            entry_copies[7].start()
        entry_copies[2 * k + 1].wait_recv()
        cot_loads[2 * k].wait()
        cot_loads[2 * k + 1].wait()
        if before is not None:
            branch_wait(before)
        compute(k, 0)
        if before == 0:
            finish(0)
        compute(k, 1)
        pair_copy(k).start()
        for copy in branch_copies(k):
            copy.start()
        if k:
            finish(k)
        before = k
    branch_wait(before)

    down_rows = 256 if width % 256 == 0 else 128

    @pl.loop(0, width // down_rows)
    def _(block):
        columns = pl.ds(pl.multiple_of(block * down_rows, down_rows), down_rows)
        term = dot_rows(hidden[0, :, columns], d_branch[0])
        for slot in range(1, 2 * count):
            term += dot_rows(hidden[slot, :, columns], d_branch[slot])
        branch[0, :down_rows, :] = term.astype(BF16)
        copy = pltpu.make_async_copy(
            branch.at[0, pl.ds(0, down_rows)], grad_down_hbm.at[columns], out_sem.at[1]
        )
        copy.start()
        copy.wait()

    na, _, lanes, _ = grad_in_hbm.shape
    in_rows = na * lanes

    @pl.loop(0, D // in_rows)
    def _(block):
        columns = pl.ds(pl.multiple_of(block * in_rows, 128), in_rows)
        term = dot_rows(entry[0, :frames, columns], d_gate_up[0])
        for slot in range(1, 2 * count):
            term += dot_rows(entry[slot, :frames, columns], d_gate_up[slot])
        branch[1, :in_rows, :] = term.astype(BF16)
        copies = [
            pltpu.make_async_copy(
                branch.at[1, pl.ds(z * lanes, lanes)], grad_in_hbm.at[z, block], out_sem.at[2 + z]
            )
            for z in range(na)
        ]
        copy_all(copies)

    total_here = partial[0].astype(F32)
    for k in range(1, count):
        back_copy(k).wait_recv()
        total_here += fetch(back_hbm.at[k - 1])
    sums[...] = total_here
    move(sums, d_entry_hbm)
    total_here = branch_terms(0)
    for k in range(1, count):
        branch_copy(k).wait_recv()
        total_here += fetch(branch_back_hbm.at[k - 1])
    sums[...] = total_here
    move(sums, branch_hbm)

    entry_copies[1].wait_send()
    for k in range(1, count):
        if k < 3:
            entry_copies[2 * k].wait_send()
            relays[k - 1].wait_send()
        entry_copies[2 * k + 1].wait_send()
        back_copy(k).wait_send()
        branch_copy(k).wait_send()


def ffn_group(entry, notes, cotangent, cotangents, lines, down, chips, peers, sizes):
    frames = cotangent.shape[0]
    na, depth = down.shape[:2]
    width = na * depth
    rows = lines.shape[1] // len(peers)
    lanes = sizes[1] * rows
    count = len(chips)
    low = lambda *shape: jax.ShapeDtypeStruct(shape, BF16)
    sem = lambda size: pltpu.SemaphoreType.DMA((size,))
    clip = (frames, D)
    return pl.pallas_call(
        functools.partial(ffn_group_kernel, chips=chips, peers=peers, sizes=sizes),
        out_shape=[
            jax.ShapeDtypeStruct(clip, F32),
            low(width, D),
            low(na, D // (na * lanes), lanes, 2 * width),
            jax.ShapeDtypeStruct(clip, F32),
            low(*clip),
            low(count, *clip),
            low(count, *clip),
            low(count - 1, *clip),
            low(count - 1, *clip),
            low(count - 1, *clip),
        ],
        in_specs=[ANY] * 6,
        out_specs=[ANY] * 10,
        scratch_shapes=[
            pltpu.VMEM((2 * count, frames + NOTE_ROWS, D), BF16),
            pltpu.VMEM((2 * count, frames, D), BF16),
            pltpu.VMEM((2 * count, frames, width), BF16),
            pltpu.VMEM((2 * count, frames, 2 * width), BF16),
            pltpu.VMEM((sizes[0], 2, na, sizes[1], rows, 2 * width), BF16),
            pltpu.VMEM((na, depth, D), BF16),
            pltpu.VMEM((count, frames, D), BF16),
            pltpu.VMEM((2, frames, D), BF16),
            pltpu.VMEM((2, frames, D), BF16),
            pltpu.VMEM(clip, BF16),
            pltpu.VMEM(clip, F32),
            sem(3 + len(peers)),
            sem(2 * count),
            sem(2 * count),
            sem(2 * count),
            sem(count),
            sem(count),
            sem(count),
            sem(count),
            sem(2),
            sem(2 + na),
            sem(2),
            sem(2),
            sem(count),
            sem(count),
            sem(count),
            sem(count),
        ],
        compiler_params=pltpu.CompilerParams(
            vmem_limit_bytes=60 * 2**20, collective_id=0, has_side_effects=True
        ),
        cost_estimate=LIGHT,
    )(entry, notes, cotangent, cotangents, lines, down)


def stack_kernel(*refs):
    out_ref = refs[-1]
    out_ref[...] = jnp.zeros_like(out_ref)
    rows = refs[0].shape[0]
    for k, ref in enumerate(refs[:-1]):
        out_ref[k * rows : (k + 1) * rows, :] = ref[...].astype(BF16)


def stack_vectors(vectors):
    parts = [vector.reshape(-1, 128) for vector in vectors]
    rows = sum(part.shape[0] for part in parts)
    return pl.pallas_call(
        stack_kernel,
        out_shape=jax.ShapeDtypeStruct((rows + -rows % 16, 128), BF16),
        in_specs=[WHOLE] * len(parts),
        out_specs=WHOLE,
        cost_estimate=LIGHT,
    )(*parts)


def total_kernel(sums_ref, out_ref, steps, lines, step_send, step_recv, line_send, line_recv):
    y, c, z, x = (lax.axis_index(axis) for axis in AXES)
    na = lines.shape[0]

    def remote(source, target, send, recv, device):
        return pltpu.make_async_remote_copy(
            src_ref=source,
            dst_ref=target,
            send_sem=send,
            recv_sem=recv,
            device_id=device,
            device_id_type=pl.DeviceIdType.MESH,
        )

    near = [{"c": 1 - c}, {"x": 1 - x}, {"y": 1 - y}]
    far = [{"z": lax.rem(z + k, na)} for k in range(1, na)]
    barrier = pltpu.get_barrier_semaphore()
    for device in near + far:
        pl.semaphore_signal(
            barrier, inc=1, device_id=device, device_id_type=pl.DeviceIdType.MESH
        )
    pl.semaphore_wait(barrier, len(near) + len(far))
    steps[0, 0] = sums_ref[...]
    for k, device in enumerate(near):
        copy = remote(steps.at[k, 0], steps.at[k, 1], step_send.at[k], step_recv.at[k], device)
        copy.start()
        copy.wait()
        both = steps[k, 0] + steps[k, 1]
        if k < 2:
            steps[k + 1, 0] = both
    lines[z] = both
    copies = [
        remote(lines.at[z], lines.at[z], line_send.at[k], line_recv.at[k], device)
        for k, device in enumerate(far)
    ]
    for copy in copies:
        copy.start()
    for copy in copies:
        copy.wait()
    whole = lines[0]
    for k in range(1, na):
        whole = whole + lines[k]
    out_ref[...] = whole


def total_over_devices(sums, na):
    sem = lambda size: pltpu.SemaphoreType.DMA((size,))
    return pl.pallas_call(
        total_kernel,
        out_shape=jax.ShapeDtypeStruct(sums.shape, F32),
        in_specs=[WHOLE],
        out_specs=WHOLE,
        scratch_shapes=[
            pltpu.VMEM((3, 2) + sums.shape, F32),
            pltpu.VMEM((na,) + sums.shape, F32),
            sem(3),
            sem(3),
            sem(na - 1),
            sem(na - 1),
        ],
        compiler_params=pltpu.CompilerParams(collective_id=3, has_side_effects=True),
        cost_estimate=LIGHT,
    )(sums)


def step_kernel(factor_ref, *refs):
    count = len(refs) // 3
    at = 0
    for weight_ref, direction_ref, out_ref in zip(refs[:count], refs[count : 2 * count], refs[2 * count :]):
        if len(weight_ref.shape) == 3:
            for k in range(weight_ref.shape[0]):
                out_ref[k] = weight_ref[k] - factor_ref[at] * direction_ref[k]
                at += 1
        else:
            out_ref[...] = weight_ref[...] - factor_ref[at] * direction_ref[...]
            at += 1


def step_weights(factors, weights, directions):
    return pl.pallas_call(
        step_kernel,
        out_shape=[jax.ShapeDtypeStruct(weight.shape, F32) for weight in weights],
        in_specs=[SCALARS] + [WHOLE] * (2 * len(weights)),
        out_specs=[WHOLE] * len(weights),
        compiler_params=pltpu.CompilerParams(vmem_limit_bytes=56 * 2**20),
        cost_estimate=LIGHT,
    )(factors, *weights, *directions)


def lamb_kernel(spot_ref, weight_ref, first_ref, second_ref, *refs):
    gradient_refs = refs[:-4]
    first_out, second_out, direction_out, sums_ref = refs[-4:]
    gradient = gradient_refs[0][...].astype(F32)
    if len(gradient_refs) == 2:
        ours = pl.program_id(1) % 2 == spot_ref[1]
        gradient = jnp.where(ours, gradient, gradient_refs[1][...].astype(F32))
    weight = weight_ref[...]
    first_new = BETA_ONE * first_ref[...] + (1.0 - BETA_ONE) * gradient
    second_new = BETA_TWO * second_ref[...] + (1.0 - BETA_TWO) * gradient * gradient
    direction = (
        first_new
        / (1.0 - BETA_ONE**STEP)
        / (jnp.sqrt(second_new / (1.0 - BETA_TWO**STEP)) + ADAM_EPS)
        + DECAY * weight
    )
    first_out[...] = first_new
    second_out[...] = second_new
    direction_out[...] = direction

    @pl.when(pl.program_id(1) == 0)
    def _():
        sums_ref[...] = jnp.zeros_like(sums_ref)

    for row, values in enumerate((weight, direction)):
        squares = jnp.sum(values * values, axis=1)
        for start in range(0, squares.shape[1], 128):
            sums_ref[:, row, :] += squares[:, start : start + 128]


def lamb_terms(spot, weight, first_moment, second_moment, gradients, block):
    shape = weight.shape
    arrays = [
        array.reshape((-1,) + array.shape[-2:])
        for array in (weight, first_moment, second_moment, *gradients)
    ]
    groups, rows, cols = arrays[0].shape
    in_blocks = len(gradients) == 1 and arrays[3].shape != arrays[0].shape
    spec = pl.BlockSpec((1, rows, block), lambda i, j: (i, 0, j))
    turns = 2 * HALF // block
    halves = pl.BlockSpec((1, rows, block), lambda i, j: (j // turns, 0, j % turns // 2))
    by_block = pl.BlockSpec((1, rows, block), lambda i, j: (j, 0, 0))
    full = jax.ShapeDtypeStruct((groups, rows, cols), F32)
    out = pl.pallas_call(
        lamb_kernel,
        out_shape=[full, full, full, jax.ShapeDtypeStruct((groups, 8, 128), F32)],
        grid=(groups, cols // block),
        in_specs=[SCALARS]
        + [spec] * 3
        + [by_block if in_blocks else spec if len(gradients) == 1 else halves] * len(gradients),
        out_specs=[spec] * 3 + [pl.BlockSpec((1, 8, 128), lambda i, j: (i, 0, 0))],
        compiler_params=pltpu.CompilerParams(vmem_limit_bytes=40 * 2**20),
        cost_estimate=pl.CostEstimate(
            flops=20 * weight.size, bytes_accessed=28 * weight.size, transcendentals=weight.size
        ),
    )(spot, *arrays)
    return [array.reshape(shape) for array in out[:3]] + [jnp.sum(out[3][:, :2], axis=-1)]


class Grid:
    def __init__(self, mesh):
        self.ny = mesh.shape["dp"] // 2
        self.nb = 2
        self.na = mesh.shape["fsdp"] // 2
        self.sizes = dict(y=self.ny, c=2, z=self.na, x=self.nb)
        self.count = self.ny * 2 * self.na * self.nb
        self.spots = list(itertools.product(*(range(self.sizes[axis]) for axis in AXES)))
        self.peers = list(itertools.product(range(self.ny), range(2), range(self.nb)))
        self.chips = list(itertools.product(range(self.ny), range(self.nb)))
        self.back = [
            (dy, dc, dx)
            for dx in range(self.nb)
            for dy in range(self.ny)
            for dc in range(2)
        ]
        self.mesh = Mesh(mesh.devices.reshape(self.ny, 2, self.na, self.nb), AXES)

    def line(self, y, c, z, x):
        return ((y * 2 + c) * self.na + z) * self.nb + x

    def here(self):
        return {axis: lax.axis_index(axis) for axis in AXES}

    def move(self, array, **steps):
        steps = {axis: step % self.sizes[axis] for axis, step in steps.items()}
        steps = {axis: step for axis, step in steps.items() if step}
        if not steps:
            return array
        names = tuple(axis for axis in AXES if axis in steps)
        lengths = [self.sizes[axis] for axis in names]
        pairs = []
        for spot in itertools.product(*(range(n) for n in lengths)):
            source = target = 0
            for axis, at, n in zip(names, spot, lengths):
                source, target = source * n + at, target * n + (at + steps[axis]) % n
            pairs.append((source, target))
        return lax.ppermute(array, names, pairs)

    def rank(self, mine, offset):
        y, c, x = ((mine[axis] + step) % self.sizes[axis] for axis, step in zip("ycx", offset))
        return (y * 2 + c) * self.nb + x

    def swap(self, array):
        return self.move(array, c=1)

    def gather_small(self, array):
        shape = array.shape
        for axis in "xzcy":
            parts = [self.move(array, **{axis: k}) for k in range(self.sizes[axis])]
            array = jnp.concatenate([part.reshape((-1,) + shape) for part in parts])
        return array

    def scatter_small(self, array):
        sources = [array]
        for axis in "cyxz":
            where = 0
            arrays = []
            size = self.sizes[axis]
            sources = [s.reshape(self.small_shape(axis, s)) for s in sources]
            for k in range(1, size):
                part = total([s[:, k] for s in sources])
                arrays.append(self.move(part, **{axis: -k}))
            sources = [s[:, 0] for s in sources] + arrays
        return total(sources).reshape(array.shape[1:])

    def small_shape(self, axis, array):
        before = {"c": self.ny, "y": 1, "x": self.na, "z": 1}[axis]
        return (before, self.sizes[axis], -1, array.shape[-1])

    def sum_small(self, array):
        bit = 1
        while bit < self.count:
            array = array + lax.ppermute(array, AXES, [(d, d ^ bit) for d in range(self.count)])
            bit *= 2
        return array

    def spread(self, lines, turn, between):
        held, marks = {(0, 0): lines}, []
        for axis in ("x", "y") if turn else ("y", "x"):
            for (y, x), piece in list(held.items()):
                for k in range(1, self.sizes[axis]):
                    step = dict(y=y, x=x)
                    step[axis] = k
                    held[(step["y"], step["x"])] = self.move(piece, **{axis: k})
            if not marks:
                marks = list(held.values())[1:]
                if between:
                    held.update(zip(list(held)[1:], after(marks, between)))
        return held, marks

    def gather_weights(self, parts, shapes, mine, spot, first, between=(), behind=()):
        rows = parts[0][0][0].shape[0]
        mixed = jnp.stack([shard for part in parts for shard, *_ in part])
        lines = lax.all_gather(mixed, "z")
        if first:
            (lines,) = after([lines], first)
        start = 0
        held, marks, plan = [], [], dict(parts=[], outs=len(shapes))
        for turn, part in enumerate(parts):
            end = start + len(part)
            pieces, arrived = self.spread(lines[:, start:end], turn, between)
            held.append(pieces)
            marks += arrived
            start = end
            plan["parts"].append(
                [(out, lane, column, shard.shape[1]) for shard, out, lane, column in part]
            )
        plan["offsets"] = sorted(held[0])
        if rows % 16 == 0:
            arrays = [pieces[offset] for pieces in held for offset in plan["offsets"]]
            arrays += behind
            copies = len(plan["offsets"]) * sum(len(part) for part in parts)
            kernel = functools.partial(place_pieces, plan=plan, sizes=(self.ny, self.nb))
            return place(kernel, spot, arrays, shapes, copies), marks
        outs = [jnp.zeros(shape, BF16) for shape in shapes]
        for pieces, blocks in zip(held, plan["parts"]):
            for (dy, dx), piece in pieces.items():
                y = (mine["y"] - dy + self.ny) % self.ny
                x = (mine["x"] - dx + self.nb) % self.nb
                for block, (out, lane, column, width) in enumerate(blocks):
                    update = piece[:, block][None, :, None]
                    if lane is None:
                        at = (y, 0, x, 0, column)
                    else:
                        update = update[:, None]
                        at = (y, lane, 0, x, 0, column)
                    outs[out] = lax.dynamic_update_slice(outs[out], update, at)
        return outs, marks

    def swap_ranks(self, blocks):
        shape = blocks.shape[1:]
        blocks = blocks.reshape((self.ny, 2, self.nb) + shape)
        for where, axis in ((1, "c"), (0, "y"), (2, "x")):
            parts = [
                self.move(lax.index_in_dim(blocks, k, where), **{axis: k})
                for k in range(self.sizes[axis])
            ]
            blocks = jnp.concatenate(parts, axis=where)
        return blocks.reshape((-1,) + shape)

    def swap_back(self, blocks, mine):
        for where, axis in ((1, "c"), (1, "y"), (2, "x")):
            parts = [
                self.move(pick(blocks, (mine[axis] + k) % self.sizes[axis], where), **{axis: k})
                for k in range(self.sizes[axis])
            ]
            blocks = jnp.stack(parts)
        return blocks.reshape((-1,) + blocks.shape[-2:])

    def gather_ranks(self, in_parts, down_part, mine, spot):
        peers, rows, width = in_parts.shape
        depth = down_part.shape[0]
        in_shape = (self.ny, 2, self.na, self.nb, rows, width)
        down_shape = (self.na, depth, D)
        if rows % 16 == 0 and width == D:
            mixed = jnp.concatenate([in_parts.reshape(-1, D), down_part])
            lines = lax.all_gather(mixed, "z")
            kernel = functools.partial(
                place_ranks,
                offsets=self.peers,
                sizes=(self.ny, self.na, self.nb),
                rows=rows,
                depth=depth,
            )
            rank_in, rank_down = place(kernel, spot, [lines], [in_shape, down_shape], peers + 1)
        else:
            rank_down = lax.all_gather(down_part, "z")
            lines = lax.all_gather(in_parts, "z")
            rank_in = jnp.zeros(in_shape, BF16)
            for k, (dy, dc, dx) in enumerate(self.peers):
                at = ((mine["y"] - dy) % self.ny, (mine["c"] + dc) % 2, 0, (mine["x"] - dx) % self.nb, 0, 0)
                rank_in = lax.dynamic_update_slice(rank_in, lines[:, k][None, None, :, None], at)
        return rank_in.reshape(-1, width), rank_down.reshape(-1, D)

    def join_columns(self, pieces, mine, spot):
        peers, rows, width = pieces.shape
        width = width // 2
        if rows % 16 == 0:
            kernel = functools.partial(
                place_columns, offsets=self.back, sizes=(self.ny, self.nb), width=width
            )
            return place(kernel, spot, [pieces], [(rows, 2 * FF)], 2 * peers)[0]
        out = jnp.zeros((rows, 2, FF), BF16)
        for k, (dy, dc, dx) in enumerate(self.back):
            y, x = (mine["y"] - dy) % self.ny, (mine["x"] - dx) % self.nb
            rank = (y * 2 + (mine["c"] + dc) % 2) * self.nb + x
            piece = pieces[k].reshape(rows, 2, width)
            out = lax.dynamic_update_slice(out, piece, (0, 0, rank * width))
        return out.reshape(rows, 2 * FF)

    def fold(self, array, names, turn, mine, between=(), behind=(), marks=None):
        names = list(names)
        sources = [array]
        for axis, waits in zip("yx" if turn else "xy", (between, behind)):
            where = names.index(axis)
            size = self.sizes[axis]
            arrived = []
            for k in range(1, size):
                away = total([pick(s, (mine[axis] + k) % size, where) for s in sources])
                arrived.append(self.move(away.astype(BF16), **{axis: k}))
            if waits:
                arrived = after(arrived, waits)
            if marks is not None and len(names) > len(array.shape) - 3:
                marks += arrived
            sources = [pick(s, mine[axis], where) for s in sources] + list(arrived)
            names.remove(axis)
        return total(sources).astype(BF16)

    def to_rank(self, array, back=False):
        pairs = []
        for d in range(self.count):
            rank, z = divmod(d, self.na)
            y, c, x = self.peers[rank]
            pairs.append((d, self.line(y, c, z, x)))
        if back:
            pairs = [(b, a) for a, b in pairs]
        return lax.ppermute(array, AXES, pairs)


def lamb_small(weight, first_moment, second_moment, gradient):
    first_new = BETA_ONE * first_moment + (1.0 - BETA_ONE) * gradient
    second_new = BETA_TWO * second_moment + (1.0 - BETA_TWO) * gradient * gradient
    direction = (
        first_new
        / (1.0 - BETA_ONE**STEP)
        / (jnp.sqrt(second_new / (1.0 - BETA_TWO**STEP)) + ADAM_EPS)
        + DECAY * weight
    )
    sums = jnp.stack([jnp.sum(weight * weight), jnp.sum(direction * direction)])
    return [first_new, second_new, direction, sums[None]]


def shards(
    grid,
    latents,
    context,
    timestep,
    lengths,
    cotangent,
    mod_matrix,
    mod_first,
    mod_second,
    qkv_matrix,
    qkv_first,
    qkv_second,
    square_set,
    square_first,
    square_second,
    ctx_matrix,
    ctx_first,
    ctx_second,
    ff_in,
    in_first,
    in_second,
    ff_down,
    down_first,
    down_second,
    norm_gains,
    gains_first,
    gains_second,
):
    mine = grid.here()
    core = mine["c"]
    spot = jnp.stack([mine[axis] for axis in AXES]).astype(jnp.int32)
    device = grid.line(*(mine[axis] for axis in AXES))
    count, ranks = grid.count, len(grid.peers)
    rows = mod_matrix.shape[0]
    frames = latents.shape[1]
    words = context.shape[1]
    valid = lengths[0]
    keep_rows = (jnp.arange(frames) < valid).astype(F32)[:, None]

    width = FF // ranks
    grouped = rows % 16 == 0 and grid.ny == 2 and grid.nb == 2
    if grouped:
        prepare = functools.partial(prepare_kernel, offsets=grid.peers, sizes=(grid.ny, grid.na, grid.nb))
        low_own, five_other, in_blocks = pl.pallas_call(
            prepare,
            out_shape=[
                jax.ShapeDtypeStruct(shape, BF16)
                for shape in ((9, rows, HALF), (5, rows, HALF), (ranks, rows, 2 * width))
            ],
            in_specs=[SCALARS] + [WHOLE] * 4,
            out_specs=[WHOLE] * 3,
            compiler_params=pltpu.CompilerParams(vmem_limit_bytes=40 * 2**20),
        )(spot, qkv_matrix, square_set, ctx_matrix, ff_in)
    else:
        five = [qkv_matrix[:, k * D : (k + 1) * D] for k in range(3)] + [
            square_set[1],
            jnp.concatenate([ctx_matrix[:, :D], ctx_matrix[:, D:]]),
        ]
        five = jnp.stack(five).astype(BF16).reshape(5, rows, grid.ny, 2, -1)
        five_own = pick(five, core, 3).reshape(5, rows, HALF)
        five_other = pick(five, 1 - core, 3).reshape(5, rows, HALF)
        wide_low = jnp.stack(
            [square_set[k, :, side * HALF : (side + 1) * HALF] for k in (0, 2) for side in range(2)]
        ).astype(BF16)
        in_halves = ff_in.reshape(rows, 2, FF)
        in_blocks = jnp.stack(
            [
                lax.dynamic_slice(in_halves, (0, 0, grid.rank(mine, offset) * width), (rows, 2, width))
                for offset in grid.peers
            ]
        ).astype(BF16).reshape(ranks, rows, 2 * width)
    five_other = grid.swap(five_other)
    if not grouped:
        five_low = jnp.where(core == 0, five_own, five_other)
        five_high = jnp.where(core == 0, five_other, five_own)
    lifted = jax.nn.silu(timestep[0].astype(F32)).astype(BF16)
    notes = jnp.concatenate([lifted, norm_gains.astype(BF16).reshape(-1)])
    if grouped:
        size = notes.shape[0]
        notes = jnp.pad(notes, (0, -size % 2048)).reshape(-1, 128)
        notes = gather_notes(notes, grid.na).reshape(count, -1)[:, :size]
    else:
        notes = grid.gather_small(notes)
    origin = []
    for spot_of in grid.spots:
        source = [
            (mine[axis] - step) % grid.sizes[axis] for axis, step in zip(AXES, spot_of)
        ]
        origin.append(grid.line(*source))
    origin = jnp.stack(origin)
    sorter = (jnp.arange(count)[:, None] == origin[None, :]).astype(BF16)
    gain_rows = dot(sorter, notes[:, D:])
    gain_rows = gain_rows.reshape(count, 3, rows).transpose(1, 0, 2).reshape(3, D)
    lifted_own = lax.dynamic_slice(notes, (0, device * rows), (count, rows))
    shift_terms = dot(lifted_own, mod_matrix.astype(BF16))
    cotangent_own = (cotangent[0].astype(F32) * keep_rows).astype(BF16)
    if grouped:
        shift_terms = shift_terms.reshape(grid.ny, 2, grid.na, grid.nb, 6 * D // 128, 128)
        blocks = in_blocks.reshape(grid.ny, 2, grid.nb, rows, 2 * width)
        shifts, cotangents, in_parts = sum_shifts(shift_terms, cotangent_own, blocks, grid.na)
        in_parts = in_parts.reshape(ranks, rows, 2 * width)
        shifts = shifts.reshape(6, D)
    else:
        shifts = grid.scatter_small(shift_terms).reshape(6, D)
        in_parts = grid.swap_ranks(in_blocks)

    tall = (grid.ny, 2, grid.na, grid.nb, rows)
    wide = (grid.ny, grid.na, grid.nb, rows, D)
    both = lambda k, out, at: [(five_low[k], out, 0, at), (five_high[k], out, 1, at)]
    sides = lambda k, out: [
        (wide_low[2 * k], out, None, 0),
        (wide_low[2 * k + 1], out, None, HALF),
    ]
    stream = latents[0].astype(F32)
    normed_one, inverse_one = norm_rows(stream)
    entry_attn = (normed_one * gain_rows[0] * (1.0 + shifts[1]) + shifts[0]).astype(BF16)
    entry_pair = [entry_attn, grid.swap(entry_attn)]
    pair_lengths = jnp.concatenate([lengths, grid.swap(lengths)])
    columns = HALF // PAIR
    if grouped:
        lines = [lax.all_gather(low_own, "z"), lax.all_gather(five_other, "z")]
        in_lines = lax.all_gather(in_parts.reshape(-1, D), "z")
        down_lines = lax.all_gather(ff_down.astype(BF16), "z")
        (
            mixture_attn, qkv, text_both, kv_cross,
            matrix_qkv, matrix_out, matrix_query, matrix_ctx, matrix_cross,
        ) = gather_group(pair_lengths, *entry_pair, *lines, context[0], grid.swap(context[0]))
        matrix_qkv = matrix_qkv.reshape(D, 3 * HALF)
    else:
        first = both(0, 0, 0) + both(1, 0, HALF) + both(2, 0, 2 * HALF)
        (matrix_qkv,), _ = grid.gather_weights(
            [first[:3], first[3:]], [tall + (3 * HALF,)], mine, spot, ()
        )
        matrix_qkv = matrix_qkv.reshape(D, 3 * HALF)
        (matrix_out, matrix_query), _ = grid.gather_weights(
            [sides(0, 0), both(3, 1, 0)], [wide, tall + (HALF,)], mine, spot, ()
        )
        (matrix_ctx, matrix_cross), _ = grid.gather_weights(
            [both(4, 0, 0), sides(1, 1)], [tall + (HALF,), wide], mine, spot, ()
        )
        down_part = grid.to_rank(ff_down.astype(BF16))
        rank_in, rank_down = grid.gather_ranks(in_parts, down_part, mine, spot)
        qkv = pair_in(*entry_pair, matrix_qkv, dot)
        mixture_attn = attend(pair_lengths, *((qkv, frames, 0, k * columns) for k in range(3)))
        text = jnp.concatenate([context[0], grid.swap(context[0])])
        blank = jnp.zeros((2 * words, count, rows // 2), BF16)
        text_cut = text.reshape(2 * words, count, rows // 2)
        text_key = jnp.concatenate([text_cut, blank], axis=-1).reshape(2 * words, -1)
        text_value = jnp.concatenate([blank, text_cut], axis=-1).reshape(2 * words, -1)
        text_both = jnp.concatenate([text_key, text_value])
        kv_cross = dot(text_both, matrix_ctx.reshape(D, HALF)).astype(BF16)
    matrix_out, matrix_cross = matrix_out.reshape(HALF, D), matrix_cross.reshape(HALF, D)
    matrix_query, matrix_ctx = matrix_query.reshape(D, HALF), matrix_ctx.reshape(D, HALF)

    all_words = jnp.full((2,), words, jnp.int32)
    d_result = cotangent[0].astype(F32) * keep_rows

    self_parts = tuple((qkv, frames, 0, k * columns) for k in range(3))
    own, away = pair_out([mixture_attn], matrix_out, dot)
    branch_attn = own + grid.swap(away).astype(F32)
    after_attn = stream + shifts[2] * branch_attn
    normed_two, inverse_two = norm_rows(after_attn)
    entry_cross = (normed_two * gain_rows[1]).astype(BF16)
    cross_pair = [entry_cross, grid.swap(entry_cross)]
    query_cross = pair_in(*cross_pair, matrix_query, dot)
    cross_parts = ((query_cross, frames, 0, 0), (kv_cross, words, 0, 0), (kv_cross, words, 2, 0))
    mixture_cross = attend(all_words, *cross_parts)
    own, away = pair_out([mixture_cross], matrix_cross, dot)
    branch_cross = own + grid.swap(away).astype(F32)
    after_cross = after_attn + branch_cross
    normed_three, inverse_three = norm_rows(after_cross)
    entry_ffn = (normed_three * gain_rows[2] * (1.0 + shifts[4]) + shifts[3]).astype(BF16)

    notes = gate_notes(shifts[5])
    whole = lambda array: (array, array.shape[1], 0)
    chips = grid.chips
    if grouped:
        d_entry_ffn, grad_down, grad_in, branch_ffn, *_ = ffn_group(
            entry_ffn, notes, cotangent_own, cotangents, in_lines, down_lines,
            chips, grid.peers, (grid.ny, grid.nb),
        )
        grad_in = grad_in.reshape(-1, 2 * width)
    else:
        entry_ext = jnp.concatenate([entry_ffn, notes])
        cot_arrived = [grid.move(cotangent_own, y=y, x=x) for y, x in grid.chips]
        (entry_ext,) = after([entry_ext], cot_arrived[1:])
        arrived = [grid.move(entry_ext, y=y, x=x) for y, x in grid.chips]
        entry_parts, hidden_parts, d_gate_up_parts, d_branch_parts = [], [], [], []
        d_entry_sources, folded_rows, branch_own, branch_away = [], [], [], []
        for k, (y, x) in enumerate(grid.chips):
            own_entry, own_cot = arrived[k], cot_arrived[k]
            if k in (1, 2):
                own_entry, own_cot = after([own_entry, own_cot], hidden_parts[:1])
            elif k > 2:
                own_entry, own_cot = after([own_entry, own_cot], folded_rows[k - 2 : k - 1])
            entries = [own_entry, grid.swap(own_entry)]
            hidden, d_gate_up, d_branch, own, other = ffn_both_ways(
                entries, [own_cot, grid.swap(own_cot)], rank_in, rank_down
            )
            other = grid.swap(other)
            folded_rows.append(total([own[0], other[0]]).astype(BF16))
            if k:
                d_entry_sources.append(grid.move(folded_rows[k], y=-y, x=-x))
                branch_away.append(total([own[1], other[1]]).astype(BF16))
            else:
                d_entry_sources += [own[0], other[0]]
                branch_own += [own[1], other[1]]
            entry_parts += entries
            hidden_parts.append(hidden)
            d_gate_up_parts.append(d_gate_up)
            d_branch_parts.append(d_branch)
        hidden_parts[:1] = after(hidden_parts[:1], folded_rows[-2:-1])
        grad_down = outer_sum(
            hidden_parts, [[whole(a) for a in d_branch_parts]], frames, 256 if width % 256 == 0 else 128
        ).reshape(width, D)
        d_gate_up_parts[:1] = after(d_gate_up_parts[:1], folded_rows[-1:])
        in_group = [[whole(a) for a in d_gate_up_parts]]
        if rows % 16 == 0:
            grad_in = outer_sum(
                entry_parts, in_group, frames, D // (2 * grid.ny), grid.nb * rows
            )
        else:
            grad_in = outer_sum(entry_parts, in_group, frames, D // 4)
            grad_in = grad_in.reshape(2 * grid.ny, grid.na, grid.nb * rows, 2 * width)
            grad_in = jnp.swapaxes(grad_in, 0, 1)
        grad_in = grad_in.reshape(-1, 2 * width)
        d_entry_ffn = total(after(d_entry_sources, (grad_down, grad_in)))
        branch_arrived = [
            grid.move(away, y=-y, x=-x) for away, (y, x) in zip(branch_away, chips[1:])
        ]
        branch_ffn = total(branch_own + branch_arrived)
    grad_in = lax.psum_scatter(grad_in, "z", tiled=True)

    d_gain_ffn = jnp.sum(d_entry_ffn * normed_three * (1.0 + shifts[4]), axis=0)
    d_scale_ffn = jnp.sum(d_entry_ffn * normed_three * gain_rows[2], axis=0)
    d_shift_ffn = jnp.sum(d_entry_ffn, axis=0)
    d_after_cross = d_result + norm_back(
        d_entry_ffn * gain_rows[2] * (1.0 + shifts[4]), normed_three, inverse_three
    )

    def join(own, other):
        lead = own.shape[:-1]
        shape = lead + (grid.ny, 1, D // (2 * grid.ny))
        own, other = own.reshape(shape), other.reshape(shape)
        low = jnp.where(core == 0, own, other)
        high = jnp.where(core == 0, other, own)
        return jnp.concatenate([low, high], axis=-2).reshape(lead + (D,))

    d_branch_cross = d_after_cross.astype(BF16)
    d_cross_pair = [d_branch_cross, grid.swap(d_branch_cross)]
    d_mixture_cross = pair_in(*d_cross_pair, matrix_cross, dot_back)
    d_query_cross, d_key_cross, d_value_cross = attend_back(
        all_words, *cross_parts, d_mixture_cross
    )
    own, away = pair_out([d_query_cross], matrix_query, dot_back)
    d_entry_cross = own + grid.swap(away).astype(F32)
    d_gain_cross = jnp.sum(d_entry_cross * normed_two, axis=0)
    d_after_attn = d_after_cross + norm_back(d_entry_cross * gain_rows[1], normed_two, inverse_two)
    d_branch_attn = (d_after_attn * shifts[2]).astype(BF16)
    d_attn_pair = [d_branch_attn, grid.swap(d_branch_attn)]
    d_gate_attn = jnp.sum(d_after_attn * branch_attn, axis=0)
    d_mixture_attn = pair_in(*d_attn_pair, matrix_out, dot_back)
    d_queries, d_keys, d_values = attend_back(pair_lengths, *self_parts, d_mixture_attn)
    own, away = pair_out([d_queries, d_keys, d_values], matrix_qkv, dot_back)
    d_entry_attn = own + grid.swap(away).astype(F32)
    d_gain_attn = jnp.sum(d_entry_attn * normed_one * (1.0 + shifts[1]), axis=0)
    d_scale_attn = jnp.sum(d_entry_attn * normed_one * gain_rows[0], axis=0)
    d_shift_attn = jnp.sum(d_entry_attn, axis=0)
    d_latents = d_after_attn + norm_back(
        d_entry_attn * gain_rows[0] * (1.0 + shifts[1]), normed_one, inverse_one
    )


    d_gate_ffn = jnp.sum(d_result * branch_ffn, axis=0)
    result = after_cross + shifts[5] * branch_ffn
    branches = (result, shifts[2] * branch_attn, branch_cross, shifts[5] * branch_ffn)
    stream_terms = jnp.stack([jnp.sum(keep_rows * branch * branch) for branch in branches])
    vectors = [
        d_shift_attn,
        d_scale_attn,
        d_gate_attn,
        d_shift_ffn,
        d_scale_ffn,
        d_gate_ffn,
        d_gain_attn,
        d_gain_cross,
        d_gain_ffn,
    ]
    small = stack_vectors(vectors)

    beside = lambda halves: jnp.concatenate([halves[0], halves[1]], axis=1)
    if grouped:
        reduced, small, grad_in, grad_down, _ = reduce_group(
            [
                ("wide", [mixture_cross], d_cross_pair, 0),
                ("tall", cross_pair, [d_query_cross], 1),
                ("tall", [text_both], [d_key_cross, d_value_cross], 0),
                ("wide", [mixture_attn], d_attn_pair, 1),
                ("tall", entry_pair, [d_queries], 0),
                ("tall", entry_pair, [d_keys], 1),
                ("tall", entry_pair, [d_values], 0),
            ],
            small, grad_in.reshape(grid.ny, 2, grid.nb, rows, 2 * width),
            grad_down.reshape(grid.na, -1, D), grid.na, rows,
        )
        small = small.reshape(count, -1, 128)[:, : 9 * D // 128].reshape(count, 9, D)
        grad_cross, grad_out = beside(reduced[0]), beside(reduced[3])
        grad_query, grad_ctx = (join(reduced[k, 0], reduced[k, 1]) for k in (1, 2))
        qkv_parts = [reduced[4:, 0], reduced[4:, 1]]
        turn_width = D // (2 * grid.ny)
    else:
        grad_down = lax.psum_scatter(grad_down, "z", tiled=True)
        grad_down = grid.to_rank(grad_down, back=True)
        grad_in = grid.swap_back(grad_in.reshape(grid.ny, 2, grid.nb, rows, 2 * width), mine)
        grad_in = grid.join_columns(grad_in, mine, spot)
        small = grid.gather_small(small[: 9 * D // 128].reshape(9, D))
        block = D // (2 * grid.ny)

        def reduce(lefts, right, piece, halves=1):
            groups = [[whole(array) for array in right]]
            gradient = outer_sum(lefts, groups, piece, block, None, halves)
            gradient = grid.fold(gradient.reshape(tall + (-1,)), "yczx", 0, mine)
            return lax.psum_scatter(jnp.swapaxes(gradient, 0, 1), "z")

        def reduce_tall(lefts, right, piece):
            sums = reduce(lefts, right, piece)
            return join(pick(sums, core, 0), grid.swap(pick(sums, 1 - core, 0)))

        grad_cross = beside(reduce([mixture_cross], d_cross_pair, frames, 2))
        grad_out = beside(reduce([mixture_attn], d_attn_pair, frames, 2))
        grad_query = reduce_tall(cross_pair, [d_query_cross], frames)
        grad_ctx = reduce_tall([text_both], [d_key_cross, d_value_cross], 2 * words)
        qkv_parts = [
            jnp.concatenate(
                [reduce_tall(entry_pair, [d], frames) for d in (d_queries, d_keys, d_values)],
                axis=1,
            )
        ]
        turn_width = D
    grad_ctx = jnp.concatenate([grad_ctx[: rows // 2], grad_ctx[rows // 2 :]], axis=1)
    grad_square = jnp.stack([grad_out, grad_query, grad_cross])
    grad_mod = jnp.einsum("nd,nkm->kdm", lifted_own, small[:, :6], preferred_element_type=F32)
    gain_sums = jnp.sum(small[:, 6:].astype(F32), axis=0)
    grad_gains = lax.dynamic_slice(gain_sums, (0, device * rows), (3, rows))
    lamb = functools.partial(lamb_terms, spot)
    done = {}
    done["qkv"] = lamb(qkv_matrix, qkv_first, qkv_second, qkv_parts, turn_width)
    done["mod"] = lamb(mod_matrix, mod_first, mod_second, [grad_mod], D)
    done["square"] = lamb(square_set, square_first, square_second, [grad_square], HALF)
    done["ctx"] = lamb(ctx_matrix, ctx_first, ctx_second, [grad_ctx], D)
    done["down"] = lamb(ff_down, down_first, down_second, [grad_down], 256)
    done["in"] = lamb(ff_in, in_first, in_second, [grad_in], 1024)
    done["gains"] = lamb_small(norm_gains, gains_first, gains_second, grad_gains)
    names = ("mod", "qkv", "square", "ctx", "in", "down", "gains")
    sums = [done[name][3] for name in names]
    sums.append(jnp.stack([stream_terms, jnp.sum(lengths) * jnp.ones(4)]).T)
    sums = jnp.concatenate(sums)
    if grouped:
        wanted = sums.shape
        sums = jnp.pad(sums, ((0, -wanted[0] % 8), (0, 128 - wanted[1])))
        sums = total_over_devices(sums, grid.na)[: wanted[0], : wanted[1]]
    else:
        sums = grid.sum_small(sums)
    norms = jnp.sqrt(sums[:9])
    weight_norms, update_norms = norms[:, 0], norms[:, 1]
    stream_rms = jnp.sqrt(sums[9:, 0] / (sums[9:, 1] * D))
    factors = RATE * (weight_norms / update_norms)
    masters = [mod_matrix, qkv_matrix, square_set, ctx_matrix, ff_in, ff_down, norm_gains]
    weights_new = step_weights(factors, masters, [done[name][2] for name in names])
    outputs = [result.astype(BF16)[None], d_latents.astype(BF16)[None]]
    for name, weight_new in zip(names, weights_new):
        outputs += [weight_new, done[name][0], done[name][1]]
    outputs.append(weight_norms)
    outputs.append(update_norms)
    outputs.append(stream_rms)
    return tuple(outputs)


def solution(mesh):
    grid = Grid(mesh)
    clip = P(AXES, None, None)
    row = P(AXES, None)
    square = P(None, AXES, None)
    gains = P(None, AXES)
    weights = (row,) * 6 + (square,) * 3 + (row,) * 9 + (gains,) * 3
    in_specs = (clip, clip, row, P(AXES), clip) + weights
    out_specs = (clip, clip) + weights + (P(), P(), P())
    return jax.shard_map(
        functools.partial(shards, grid),
        mesh=grid.mesh,
        in_specs=in_specs,
        out_specs=out_specs,
        check_vma=False,
    )
```

```python
import functools
import itertools

import jax
import jax.numpy as jnp
from jax import lax
from jax.experimental import pallas as pl
from jax.experimental.pallas import tpu as pltpu
from jax.sharding import Mesh, PartitionSpec as P

D = 1536
HEAD_DIM = 64
FF = 6144
STEP = 10


NORM_EPS = 1e-05
BETA_ONE = 0.9
BETA_TWO = 0.999
ADAM_EPS = 1e-06
DECAY = 0.01
RATE = 0.5
SCALE = 0.125

AXES = ("y", "c", "z", "x")
HALF = D // 2
PAIR = 2 * HEAD_DIM
BF16 = jnp.bfloat16
F32 = jnp.float32
ANY = pl.BlockSpec(memory_space=pl.ANY)
WHOLE = pl.BlockSpec(memory_space=pltpu.VMEM)
SCALARS = pl.BlockSpec(memory_space=pltpu.SMEM)
LIGHT = pl.CostEstimate(flops=2**20, bytes_accessed=2**20, transcendentals=0)


def norm_rows(matrix):
    centred = matrix - jnp.mean(matrix, axis=-1, keepdims=True)
    inverse = lax.rsqrt(jnp.mean(centred * centred, axis=-1, keepdims=True) + NORM_EPS)
    return (centred * inverse, inverse)


def norm_back(gradient, normed, inverse):
    return inverse * (
        gradient
        - jnp.mean(gradient, axis=-1, keepdims=True)
        - normed * jnp.mean(gradient * normed, axis=-1, keepdims=True)
    )


def dot(first, second):
    return jnp.dot(first, second, preferred_element_type=F32)


def dot_back(first, second):
    return lax.dot_general(first, second, (((1,), (1,)), ((), ())), preferred_element_type=F32)


def dot_rows(first, second):
    return lax.dot_general(first, second, (((0,), (0,)), ((), ())), preferred_element_type=F32)


def pick(array, index, axis):
    return lax.dynamic_index_in_dim(array, index, axis, keepdims=False)


def no_work(*refs):
    pass


def after(values, others):
    values = list(values)
    return pl.pallas_call(
        no_work,
        out_shape=[jax.ShapeDtypeStruct(value.shape, value.dtype) for value in values],
        in_specs=[ANY] * (len(values) + len(others)),
        out_specs=[ANY] * len(values),
        input_output_aliases={k: k for k in range(len(values))},
    )(*values, *others)


def total(terms):
    return sum(term.astype(F32) for term in terms)


def only(block, head):
    lane = lax.broadcasted_iota(jnp.int32, block.shape, 1)
    mine = lane < HEAD_DIM if head == 0 else lane >= HEAD_DIM
    return jnp.where(mine, block, jnp.zeros_like(block))


def both_heads(first, second):
    lane = lax.broadcasted_iota(jnp.int32, first.shape, 1)
    return jnp.where(lane < HEAD_DIM, first, second)


def attend_heads(valid, query, key, value):
    mixed = []
    for head in range(2):
        scores = dot_back(only(query, head), key) * SCALE
        column = lax.broadcasted_iota(jnp.int32, scores.shape, 1)
        scores = jnp.where(column < valid, scores, -1e30)
        powers = jnp.exp(scores - jnp.max(scores, axis=-1, keepdims=True))
        chances = (powers / jnp.sum(powers, axis=-1, keepdims=True)).astype(BF16)
        mixed.append(dot(chances, value))
    return both_heads(*mixed).astype(BF16)


def attend_kernel(valid_ref, query_ref, key_ref, value_ref, out_ref):
    valid = valid_ref[pl.program_id(0)]
    out_ref[...] = attend_heads(valid, query_ref[...], key_ref[...], value_ref[...])


def attend_back_kernel(
    valid_ref, query_ref, key_ref, value_ref, d_ref, d_query_ref, d_key_ref, d_value_ref
):
    valid = valid_ref[pl.program_id(0)]
    query, key, value, d_mix = query_ref[...], key_ref[...], value_ref[...], d_ref[...]
    parts = []
    for head in range(2):
        scores = dot_back(only(key, head), query) * SCALE
        row = lax.broadcasted_iota(jnp.int32, scores.shape, 0)
        scores = jnp.where(row < valid, scores, -1e30)
        powers = jnp.exp(scores - jnp.max(scores, axis=0, keepdims=True))
        chances = powers / jnp.sum(powers, axis=0, keepdims=True)
        d_chances = dot_back(only(value, head), d_mix)
        mean = jnp.sum(chances * d_chances, axis=0, keepdims=True)
        d_scores = (chances * (d_chances - mean)).astype(BF16)
        d_value = dot(chances.astype(BF16), d_mix)
        d_key = dot(d_scores, query) * SCALE
        d_query = dot_rows(d_scores, key) * SCALE
        parts.append((d_query, d_key, d_value))
    for out_ref, first, second in zip((d_query_ref, d_key_ref, d_value_ref), *parts):
        out_ref[...] = both_heads(first, second).astype(BF16)


def block_of(rows, row_shift, column_shift):
    return pl.BlockSpec((rows, PAIR), lambda b, j: (b + row_shift, j + column_shift))


def attend(valid, query, key, value):
    frames, words = query[1], key[1]
    pairs = HALF // PAIR
    return pl.pallas_call(
        attend_kernel,
        out_shape=jax.ShapeDtypeStruct((2 * frames, HALF), BF16),
        grid=(2, pairs),
        in_specs=[SCALARS] + [block_of(*part[1:]) for part in (query, key, value)],
        out_specs=block_of(frames, 0, 0),
        compiler_params=pltpu.CompilerParams(vmem_limit_bytes=32 * 2**20),
        cost_estimate=LIGHT,
    )(valid, query[0], key[0], value[0])


def attend_back(valid, query, key, value, d_mixture):
    frames, words = query[1], key[1]
    pairs = HALF // PAIR
    return pl.pallas_call(
        attend_back_kernel,
        out_shape=[
            jax.ShapeDtypeStruct((2 * rows, HALF), BF16) for rows in (frames, words, words)
        ],
        grid=(2, pairs),
        in_specs=[SCALARS]
        + [block_of(*part[1:]) for part in (query, key, value)]
        + [block_of(frames, 0, 0)],
        out_specs=[block_of(rows, 0, 0) for rows in (frames, words, words)],
        compiler_params=pltpu.CompilerParams(vmem_limit_bytes=48 * 2**20),
        cost_estimate=LIGHT,
    )(valid, query[0], key[0], value[0], d_mixture)


def copy_all(copies):
    for copy in copies:
        copy.start()
    for copy in copies:
        copy.wait()


def place_pieces(spot_ref, *refs, plan, sizes):
    ny, nb = sizes
    count = len(plan["offsets"]) * len(plan["parts"])
    pieces, sem = refs[:count], refs[-1]
    outs = refs[-1 - plan["outs"] : -1]
    y, x = spot_ref[0], spot_ref[3]
    copies = []
    for part, blocks in enumerate(plan["parts"]):
        for spot, (dy, dx) in enumerate(plan["offsets"]):
            from_y = lax.rem(y - dy + ny, ny)
            from_x = lax.rem(x - dx + nb, nb)
            piece = pieces[part * len(plan["offsets"]) + spot]
            for block, (out, lane, column, width) in enumerate(blocks):
                columns = pl.ds(column, width)
                if lane is None:
                    target = outs[out].at[from_y, :, from_x, :, columns]
                else:
                    target = outs[out].at[from_y, lane, :, from_x, :, columns]
                copies.append(
                    pltpu.make_async_copy(piece.at[:, block], target, sem.at[len(copies)])
                )
    copy_all(copies)


def place_ranks(spot_ref, lines_ref, in_ref, down_ref, sem, *, offsets, sizes, rows, depth):
    ny, na, nb = sizes
    y, c, x = spot_ref[0], spot_ref[1], spot_ref[3]
    copies = []
    for block, (dy, dc, dx) in enumerate(offsets):
        target = in_ref.at[
            lax.rem(y - dy + ny, ny), lax.rem(c + dc, 2), :, lax.rem(x - dx + nb, nb)
        ]
        source = lines_ref.at[:, pl.ds(block * rows, rows)]
        copies.append(pltpu.make_async_copy(source, target, sem.at[len(copies)]))
    source = lines_ref.at[:, pl.ds(len(offsets) * rows, depth)]
    copies.append(pltpu.make_async_copy(source, down_ref, sem.at[len(copies)]))
    copy_all(copies)


def place_columns(spot_ref, pieces_ref, out_ref, sem, *, offsets, sizes, width):
    ny, nb = sizes
    y, c, x = spot_ref[0], spot_ref[1], spot_ref[3]
    copies = []
    for k, (dy, dc, dx) in enumerate(offsets):
        rank = (lax.rem(y - dy + ny, ny) * 2 + lax.rem(c + dc, 2)) * nb + lax.rem(x - dx + nb, nb)
        for half in range(2):
            start = pl.multiple_of(half * FF + rank * width, 128)
            copies.append(
                pltpu.make_async_copy(
                    pieces_ref.at[k, :, pl.ds(half * width, width)],
                    out_ref.at[:, pl.ds(start, width)],
                    sem.at[len(copies)],
                )
            )
    copy_all(copies)


def place(kernel, spot, arrays, shapes, copies):
    size = sum(a.size * a.dtype.itemsize for a in arrays)
    return pl.pallas_call(
        kernel,
        out_shape=[jax.ShapeDtypeStruct(shape, BF16) for shape in shapes],
        in_specs=[SCALARS] + [ANY] * len(arrays),
        out_specs=[WHOLE] * len(shapes),
        scratch_shapes=[pltpu.SemaphoreType.DMA((copies,))],
        compiler_params=pltpu.CompilerParams(vmem_limit_bytes=40 * 2**20),
        cost_estimate=pl.CostEstimate(flops=0, bytes_accessed=2 * size, transcendentals=0),
    )(spot, *arrays)


def prepare_kernel(
    spot_ref, qkv_ref, square_ref, ctx_ref, in_ref, own_ref, other_ref, block_ref,
    *, offsets, sizes
):
    ny, na, nb = sizes
    y, c, x = spot_ref[0], spot_ref[1], spot_ref[3]
    part = D // (2 * ny)
    for out_ref, which in ((own_ref, c), (other_ref, 1 - c)):
        for k in range(5):
            for block in range(ny):
                start = block * 2 * part + which * part
                if k < 3:
                    values = qkv_ref[:, pl.ds(pl.multiple_of(k * D + start, part), part)]
                elif k == 3:
                    values = square_ref[1, :, pl.ds(pl.multiple_of(start, part), part)]
                else:
                    values = jnp.concatenate(
                        [
                            ctx_ref[:, pl.ds(pl.multiple_of(side * D + start, part), part)]
                            for side in range(2)
                        ]
                    )
                out_ref[k, :, block * part : (block + 1) * part] = values.astype(BF16)
    for k, matrix in enumerate((0, 2)):
        for side in range(2):
            values = square_ref[matrix, :, side * HALF : (side + 1) * HALF]
            own_ref[5 + 2 * k + side] = values.astype(BF16)
    width = FF // len(offsets)
    share = width // na
    for k, (dy, dc, dx) in enumerate(offsets):
        rank = lax.rem(y + dy, ny) * 2 + lax.rem(c + dc, 2)
        first = lax.rem(x + dx, nb) == 0
        for side in range(2):
            for z in range(na):
                start = pl.multiple_of(side * FF + (rank * na + z) * nb * share, 128)
                values = in_ref[:, pl.ds(start, nb * share)].astype(BF16)
                values = jnp.where(first, values[:, :share], values[:, share:])
                at = side * width + z * share
                block_ref[k, :, at : at + share] = values


BLOCKS = [(0, lane, k * HALF, lane, k) for k in range(3) for lane in range(2)]
BLOCKS += [(1, None, 0, 0, 5), (1, None, HALF, 0, 6), (2, 0, 0, 0, 3), (2, 1, 0, 1, 3)]
BLOCKS += [(3, 0, 0, 0, 4), (3, 1, 0, 1, 4), (4, None, 0, 0, 7), (4, None, HALF, 0, 8)]
ACROSS = (0, 1, 2, 6, 7, 10, 11)


def gather_kernel(
    valid_ref, own_hbm, other_hbm, lines_hbm, more_lines_hbm, words_ref, more_words_ref,
    mixture_ref, qkv_ref, text_ref, kv_ref, *refs,
):
    outs, arrays = refs[:5], refs[5:10]
    entry, x_send, x_recv, y_send, y_recv, on_send, on_recv, own_sem, load_sem, out_sem = refs[10:]
    y, c, x = (lax.axis_index(axis) for axis in "ycx")
    far_y, far_x = 1 - y, 1 - x
    frames = entry.shape[1]

    def place_of(block, at_y, at_x):
        array, lane, column, _, _ = BLOCKS[block]
        columns = pl.ds(column, HALF)
        if lane is None:
            return arrays[array].at[at_y, :, at_x, :, columns]
        return arrays[array].at[at_y, 1 - c if lane else c, :, at_x, :, columns]

    def remote(source, target, send, recv, device):
        return pltpu.make_async_remote_copy(
            src_ref=source,
            dst_ref=target,
            send_sem=send,
            recv_sem=recv,
            device_id=device,
            device_id_type=pl.DeviceIdType.MESH,
        )

    barrier = pltpu.get_barrier_semaphore()
    for device in ({"y": far_y}, {"x": far_x}):
        pl.semaphore_signal(
            barrier, inc=1, device_id=device, device_id_type=pl.DeviceIdType.MESH
        )
    pl.semaphore_wait(barrier, 2)
    count = len(BLOCKS)
    to_x, to_y, onward, own = [], [], [], []
    for b in range(count):
        here = place_of(b, y, x)
        source = (lines_hbm, more_lines_hbm)[BLOCKS[b][3]].at[:, BLOCKS[b][4]]
        to_x.append(remote(source, here, x_send.at[b], x_recv.at[b], {"x": far_x}))
        to_y.append(remote(source, here, y_send.at[b], y_recv.at[b], {"y": far_y}))
        if b in ACROSS:
            there, device = place_of(b, y, far_x), {"y": far_y}
        else:
            there, device = place_of(b, far_y, x), {"x": far_x}
        onward.append(remote(there, there, on_send.at[b], on_recv.at[b], device))
        own.append(pltpu.make_async_copy(source, here, own_sem.at[b]))

    def send(blocks):
        for b in blocks:
            to_x[b].start()
            to_y[b].start()
            own[b].start()

    def hand_on(blocks):
        for b in blocks:
            (to_x if b in ACROSS else to_y)[b].wait_recv()
            onward[b].start()

    def arrive(blocks):
        for b in blocks:
            own[b].wait()
            (to_y if b in ACROSS else to_x)[b].wait_recv()
            onward[b].wait_recv()

    send(range(6))
    loads = [
        pltpu.make_async_copy(source, entry.at[k], load_sem.at[k])
        for k, source in enumerate((own_hbm, other_hbm))
    ]
    for load in loads:
        load.start()
    text_ref[...] = jnp.zeros_like(text_ref)
    share = arrays[3].shape[-2] // 2
    for k, ref in enumerate((words_ref, more_words_ref)):
        height = ref.shape[0]
        words = ref[...]
        for device in range(D // (2 * share)):
            part = words[:, device * share : (device + 1) * share]
            for side in range(2):
                at, column = (2 * side + k) * height, (2 * device + side) * share
                text_ref[at : at + height, column : column + share] = part
    hand_on(range(6))
    send(range(6, count))
    for load in loads:
        load.wait()
    arrive(range(6))
    copies = [pltpu.make_async_copy(arrays[0], outs[0], out_sem.at[0])]
    copies[0].start()
    for k in range(2):
        weights = arrays[0][...].reshape(D, 3 * HALF)
        qkv_ref[k * frames : (k + 1) * frames, :] = dot(entry[k], weights).astype(BF16)
    pairs = HALF // PAIR

    @pl.loop(0, 2 * pairs)
    def _(step):
        clip, j = step // pairs, step % pairs
        rows = pl.ds(pl.multiple_of(clip * frames, frames), frames)
        lanes = [pl.ds(pl.multiple_of(k * HALF + j * PAIR, PAIR), PAIR) for k in range(3)]
        query, key, value = (qkv_ref[rows, lane] for lane in lanes)
        mixture_ref[rows, lanes[0]] = attend_heads(valid_ref[clip], query, key, value)

    hand_on(range(6, count))
    arrive(range(6, count))
    kv_ref[...] = dot(text_ref[...], arrays[3][...].reshape(D, HALF)).astype(BF16)
    for k in range(1, 5):
        copies.append(pltpu.make_async_copy(arrays[k], outs[k], out_sem.at[k]))
        copies[k].start()
    for copy in copies:
        copy.wait()
    for b in range(count):
        to_x[b].wait_send()
        to_y[b].wait_send()
        onward[b].wait_send()


def gather_group(valid, own, other, lines, more_lines, words, more_words):
    na, _, rows, _ = lines.shape
    count = len(BLOCKS)
    frames = own.shape[0]
    tall = lambda cols: (2, 2, na, 2, rows, cols)
    wide = (2, na, 2, rows, D)
    shapes = [tall(3 * HALF), wide, tall(HALF), tall(HALF), wide]
    sem = lambda size: pltpu.SemaphoreType.DMA((size,))
    return pl.pallas_call(
        gather_kernel,
        out_shape=[
            jax.ShapeDtypeStruct((2 * frames, HALF), BF16),
            jax.ShapeDtypeStruct((2 * frames, 3 * HALF), BF16),
            jax.ShapeDtypeStruct((4 * words.shape[0], D), BF16),
            jax.ShapeDtypeStruct((4 * words.shape[0], HALF), BF16),
        ]
        + [jax.ShapeDtypeStruct(shape, BF16) for shape in shapes],
        in_specs=[SCALARS] + [ANY] * 4 + [WHOLE] * 2,
        out_specs=[WHOLE] * 4 + [ANY] * 5,
        scratch_shapes=[pltpu.VMEM(shape, BF16) for shape in shapes]
        + [pltpu.VMEM((2, frames, D), BF16)]
        + [sem(count)] * 7
        + [sem(2), sem(5)],
        compiler_params=pltpu.CompilerParams(
            vmem_limit_bytes=56 * 2**20, collective_id=4, has_side_effects=True
        ),
        cost_estimate=LIGHT,
    )(valid, own, other, lines, more_lines, words, more_words)


def ffn_kernel(
    entry_a, entry_b, d_a, d_b, in_hbm, down_hbm,
    hidden_ref, d_gate_up_ref, d_branch_ref, own_ref, other_ref,
    entry_ref, d_ref, in_ref, down_ref, sem,
):
    step = pl.program_id(0)
    sources = (entry_a, in_hbm, d_a, down_hbm, entry_b, d_b)
    targets = (entry_ref.at[0], in_ref, d_ref.at[0], down_ref, entry_ref.at[1], d_ref.at[1])
    copies = [
        pltpu.make_async_copy(source, target, sem.at[k])
        for k, (source, target) in enumerate(zip(sources, targets))
    ]

    @pl.when(step == 0)
    def _():
        for copy in copies:
            copy.start()
        for copy in copies[:4]:
            copy.wait()

    @pl.when(step == 1)
    def _():
        for copy in copies[4:]:
            copy.wait()

    width = down_ref.shape[0]
    frames = d_ref.shape[1]
    notes = entry_ref[step, frames:, :].astype(F32)
    gate_row = notes[0:1] + notes[1:2] + notes[2:3]
    d_branch = (d_ref[step].astype(F32) * gate_row).astype(BF16)
    d_branch_ref[...] = d_branch
    gate_up = dot(entry_ref[step, :frames, :], in_ref[...])
    gate, up = gate_up[:, :width], gate_up[:, width:]
    logistic = jax.nn.sigmoid(gate)
    hidden = (gate * logistic * up).astype(BF16)
    hidden_ref[...] = hidden
    d_hidden = dot_back(d_branch, down_ref[...])
    d_gate = d_hidden * up * logistic * (1.0 + gate * (1.0 - logistic))
    d_gate_up_ref[:, :width] = d_gate.astype(BF16)
    d_gate_up_ref[:, width:] = (d_hidden * gate * logistic).astype(BF16)
    d_entry = dot_back(d_gate_up_ref[...], in_ref[...]).astype(BF16)
    branch = dot(hidden, down_ref[...]).astype(BF16)

    @pl.when(step == 0)
    def _():
        own_ref[0] = d_entry
        own_ref[1] = branch

    @pl.when(step == 1)
    def _():
        other_ref[0] = d_entry
        other_ref[1] = branch


NOTE_ROWS = 16


def gate_notes(gate):
    high = gate.astype(BF16)
    rest = gate - high.astype(F32)
    middle = rest.astype(BF16)
    low = (rest - middle.astype(F32)).astype(BF16)
    blank = jnp.zeros((NOTE_ROWS - 3, gate.shape[0]), BF16)
    return jnp.concatenate([jnp.stack([high, middle, low]), blank])


def ffn_both_ways(entries, cotangents, rank_in, rank_down):
    frames = cotangents[0].shape[0]
    width = rank_down.shape[0]
    rows_of = lambda cols: pl.BlockSpec((frames, cols), lambda i: (i, 0))
    whole = pl.BlockSpec((2, frames, D), lambda i: (0, 0, 0))
    shape = lambda *sizes: jax.ShapeDtypeStruct(sizes, BF16)
    return pl.pallas_call(
        ffn_kernel,
        out_shape=[shape(2 * frames, cols) for cols in (width, 2 * width, D)]
        + [shape(2, frames, D)] * 2,
        grid=(2,),
        in_specs=[ANY] * 6,
        out_specs=[rows_of(cols) for cols in (width, 2 * width, D)] + [whole] * 2,
        scratch_shapes=[
            pltpu.VMEM((2, frames + NOTE_ROWS, D), BF16),
            pltpu.VMEM((2, frames, D), BF16),
            pltpu.VMEM((D, 2 * width), BF16),
            pltpu.VMEM((width, D), BF16),
            pltpu.SemaphoreType.DMA((6,)),
        ],
        compiler_params=pltpu.CompilerParams(vmem_limit_bytes=56 * 2**20),
        cost_estimate=LIGHT,
    )(*entries, *cotangents, rank_in, rank_down)


def outer_kernel(*refs, lefts, groups, rows, lanes):
    left_refs, right_refs, out_ref = refs[:lefts], refs[lefts:-1], refs[-1]

    def pieces(group):
        return [ref[k : k + rows, :] for ref in group for k in range(0, ref.shape[0], rows)]

    left_pieces = pieces(left_refs)
    start = column = 0
    for size in groups:
        group = right_refs[start : start + size]
        start += size
        sums = None
        for left, right in zip(left_pieces, pieces(group)):
            term = dot_rows(left, right)
            sums = term if sums is None else sums + term
        sums = sums.astype(BF16)
        end = column + sums.shape[1]
        if lanes is None:
            out_ref[0, :, column:end] = sums
        else:
            for k in range(out_ref.shape[0]):
                out_ref[k, 0, :, column:end] = sums[k * lanes : (k + 1) * lanes]
        column = end


def outer_sum(lefts, groups, rows, block, lanes=None, halves=1):
    depth = lefts[0].shape[1]
    cols = sum(group[0][1] for group in groups) // halves
    blocks = depth // block * halves
    if block % 128:
        left = jnp.concatenate([a[: a.shape[0] // rows * rows] for a in lefts])
        right = jnp.concatenate(
            [
                jnp.concatenate([a[:, at * width : (at + 1) * width] for a, width, at in group])
                for group in groups
            ],
            axis=1,
        )
        out = dot_rows(left, right).astype(BF16).reshape(depth // block, block, halves, cols)
        return jnp.swapaxes(out, 1, 2).reshape(blocks, block, cols)
    if lanes is None:
        out_shape = (blocks, block, cols)
        out_spec = pl.BlockSpec((1, block, cols), lambda i: (i, 0, 0))
    else:
        out_shape = (block // lanes, blocks, lanes, cols)
        out_spec = pl.BlockSpec((block // lanes, 1, lanes, cols), lambda i: (0, i, 0, 0))
    used = lambda array: array.shape[0] // rows * rows

    def right_spec(right):
        array, width, at = right
        if halves > 1:
            return pl.BlockSpec((array.shape[0], width // halves), lambda i: (0, i % halves))
        return pl.BlockSpec(
            (array.shape[0], width), lambda i: (0, at), pipeline_mode=pl.Buffered(1)
        )

    rights = [right for group in groups for right in group]
    return pl.pallas_call(
        functools.partial(
            outer_kernel,
            lefts=len(lefts),
            groups=[len(group) for group in groups],
            rows=rows,
            lanes=lanes,
        ),
        out_shape=jax.ShapeDtypeStruct(out_shape, BF16),
        grid=(blocks,),
        in_specs=[pl.BlockSpec((used(a), block), lambda i: (0, i // halves)) for a in lefts]
        + [right_spec(right) for right in rights],
        out_specs=out_spec,
        compiler_params=pltpu.CompilerParams(vmem_limit_bytes=56 * 2**20),
        cost_estimate=LIGHT,
    )(*lefts, *[right[0] for right in rights])


def reduce_kernel(*refs, plan, inputs):
    arrays, (small_hbm, in_hbm, down_hbm) = refs[:inputs], refs[inputs : inputs + 3]
    out_ref, small_ref, in_ref, down_ref, down_in = refs[inputs + 3 : inputs + 8]
    (
        blocks, first_x, first_y, second, second_in, kept, lines_in, mine, other_in, left_ref, right_ref, notes,
        load_sem, first_send, first_recv, second_send, second_recv, line_send, line_recv,
        core_send, core_recv, note_send, note_recv,
        in_own, in_core, in_y, in_x, in_send, in_recv, down_send, down_recv, down_sem,
    ) = refs[inputs + 8 :]
    y, c, z, x = (lax.axis_index(axis) for axis in AXES)
    na, rows = kept.shape[1], kept.shape[3]
    far_y, far_c, far_x = 1 - y, 1 - c, 1 - x
    count = len(plan)
    names = [("y", far_y), ("c", far_c), ("x", far_x)]
    names += [("z", lax.rem(z + k, na)) for k in range(1, na)]
    slots = {}
    for m, (_, _, _, turn) in enumerate(plan):
        slots[m] = sum(1 for other in plan[:m] if other[3] == turn)

    def remote(source, target, send, recv, axis, at):
        return pltpu.make_async_remote_copy(
            src_ref=source,
            dst_ref=target,
            send_sem=send,
            recv_sem=recv,
            device_id={axis: at},
            device_id_type=pl.DeviceIdType.MESH,
        )

    barrier = pltpu.get_barrier_semaphore()
    for axis, at in names:
        pl.semaphore_signal(
            barrier, inc=1, device_id={axis: at}, device_id_type=pl.DeviceIdType.MESH
        )
    pl.semaphore_wait(barrier, len(names))

    def first_copy(m):
        if plan[m][3]:
            source, target, axis, at = blocks.at[m, far_y], first_y.at[slots[m]], "y", far_y
        else:
            source, target, axis, at = blocks.at[m, :, :, :, far_x], first_x.at[slots[m]], "x", far_x
        return remote(source, target, first_send.at[m], first_recv.at[m], axis, at)

    def second_copy(m):
        axis, at = ("x", far_x) if plan[m][3] else ("y", far_y)
        return remote(
            second.at[m], second_in.at[m], second_send.at[m], second_recv.at[m], axis, at
        )

    def line_copies(m):
        return [
            remote(
                kept.at[m, lax.rem(z + k, na)],
                lines_in.at[m, k - 1],
                line_send.at[m * (na - 1) + k - 1],
                line_recv.at[m * (na - 1) + k - 1],
                "z",
                lax.rem(z + k, na),
            )
            for k in range(1, na)
        ]

    def core_copy(m):
        return remote(
            mine.at[m, far_c], other_in.at[m], core_send.at[m], core_recv.at[m], "c", far_c
        )

    def note_copies(hop):
        if hop == 0:
            hops = [(notes.at[0, 0, 0, 0], notes.at[0, 0, 0, 1], "x", far_x)]
        elif hop == 1:
            hops = [
                (notes.at[0, 0, 0], notes.at[0, 0, k], "z", lax.rem(z + k, na))
                for k in range(1, na)
            ]
        elif hop == 2:
            hops = [(notes.at[0, 0], notes.at[0, 1], "c", far_c)]
        else:
            hops = [(notes.at[0], notes.at[1], "y", far_y)]
        at = 0 if hop == 0 else hop + (na - 2 if hop > 1 else 0)
        return [
            remote(source, target, note_send.at[at + k], note_recv.at[at + k], axis, to)
            for k, (source, target, axis, to) in enumerate(hops)
        ]

    def loads(m):
        copies = []
        for group, buffer in ((plan[m][1], left_ref), (plan[m][2], right_ref)):
            start = 0
            for place_of in group:
                height, width = arrays[place_of].shape
                copies.append(
                    pltpu.make_async_copy(
                        arrays[place_of],
                        buffer.at[m % 2, pl.ds(start, height), pl.ds(0, width)],
                        load_sem.at[m % 2, len(copies)],
                    )
                )
                start += height
        return copies

    def compute(m):
        kind, lefts, rights, _ = plan[m]
        height = sum(arrays[place_of].shape[0] for place_of in lefts)
        depth = na * 2 * rows

        @pl.loop(0, 4)
        def _(step):
            at_y, at_c = step // 2, step % 2
            at, columns = (step, 0) if kind == "tall" else (at_y, at_c)
            left = left_ref[m % 2, :height, pl.ds(pl.multiple_of(at * depth, 128), depth)]
            right = right_ref[m % 2, :height, pl.ds(pl.multiple_of(columns * HALF, 128), HALF)]
            sums = dot_rows(left, right).astype(BF16)
            for k in range(2 * na):
                blocks[m, at_y, at_c, k // 2, k % 2] = sums[k * rows : (k + 1) * rows]

    def arrived(m, at_c, at_z, at_y, at_x):
        if plan[m][3]:
            came = first_y[slots[m], at_c, at_z, at_x]
        else:
            came = first_x[slots[m], at_y, at_c, at_z]
        return blocks[m, at_y, at_c, at_z, at_x].astype(F32) + came.astype(F32)

    load = pltpu.make_async_copy(small_hbm, notes.at[0, 0, 0, 0], load_sem.at[0, 0])
    load.start()
    load.wait()
    hops = [note_copies(hop) for hop in range(4)]
    for copy in hops[0]:
        copy.start()

    load = pltpu.make_async_copy(in_hbm, in_own, load_sem.at[0, 0])
    load.start()
    load.wait()

    def in_copies(first, pairs, axis, at):
        return [
            remote(source, target, in_send.at[first + k], in_recv.at[first + k], axis, at)
            for k, (source, target) in enumerate(pairs)
        ]

    in_hops = [
        in_copies(0, [(in_own.at[:, far_c], in_core)], "c", far_c),
        in_copies(
            1, [(in_own.at[far_y, c], in_y.at[0]), (in_core.at[far_y], in_y.at[1])], "y", far_y
        ),
        in_copies(
            3,
            [
                (in_own.at[y, c, far_x], in_x.at[0]),
                (in_core.at[y, far_x], in_x.at[1]),
                (in_y.at[0, far_x], in_x.at[2]),
                (in_y.at[1, far_x], in_x.at[3]),
            ],
            "x",
            far_x,
        ),
    ]
    for copy in in_hops[0]:
        copy.start()
    down_copies = [
        remote(
            down_hbm.at[lax.rem(z + k, na)], down_in.at[k - 1],
            down_send.at[k - 1], down_recv.at[k - 1], "z", lax.rem(z + k, na),
        )
        for k in range(1, na)
    ]
    for copy in down_copies:
        copy.start()
    for copy in loads(0):
        copy.start()
    def second_step(m):
        first_copy(m).wait_recv()

        @pl.loop(0, 2 * na)
        def _(step):
            at_c, at_z = step // na, step % na
            at_y, at_x = (y, far_x) if plan[m][3] else (far_y, x)
            second[m, at_c, at_z] = arrived(m, at_c, at_z, at_y, at_x).astype(BF16)

        second_copy(m).start()

    def line_step(m):
        second_copy(m).wait_recv()

        @pl.loop(0, 2 * na)
        def _(step):
            at_c, at_z = step // na, step % na
            sums = arrived(m, at_c, at_z, y, x) + second_in[m, at_c, at_z].astype(F32)
            kept[m, at_z, at_c] = sums.astype(BF16)

        for copy in line_copies(m):
            copy.start()

    def last_step(m):
        sums = kept[m, z].astype(F32)
        for k, copy in enumerate(line_copies(m)):
            copy.wait_recv()
            sums += lines_in[m, k].astype(F32)
        mine[m] = sums.astype(BF16)
        if plan[m][0] == "tall":
            core_copy(m).start()

    def rows_back():
        for copy in in_hops[2]:
            copy.wait_recv()
        width = in_own.shape[-1] // 2
        share = width // na
        for at_y in range(2):
            for at_c in range(2):
                if at_y:
                    near = in_y[at_c, x]
                else:
                    near = in_core[y, x] if at_c else in_own[y, c, x]
                across = in_x[at_y * 2 + at_c]
                low = jnp.where(x == 0, near, across)
                high = jnp.where(x == 0, across, near)
                rank = lax.rem(y + at_y, 2) * 2 + lax.rem(c + at_c, 2)
                for half in range(2):
                    for k in range(na):
                        at = half * width + k * share
                        start = pl.multiple_of(half * FF + (rank * na + k) * 2 * share, 128)
                        in_ref[:, pl.ds(start, 2 * share)] = jnp.concatenate(
                            [low[:, at : at + share], high[:, at : at + share]], axis=1
                        )
        depth = down_ref.shape[0]
        sums = None
        for k in range(na):
            if k:
                down_copies[k - 1].wait_recv()
            source = down_in.at[k - 1] if k else down_hbm.at[z]
            copy = pltpu.make_async_copy(source, left_ref.at[0, pl.ds(0, depth)], down_sem.at[0])
            copy.start()
            copy.wait()
            term = left_ref[0, :depth, :].astype(F32)
            sums = term if sums is None else sums + term
        down_ref[...] = sums.astype(BF16)

    for m in range(count + 6):
        if m < count:
            for copy in loads(m):
                copy.wait()
            if m + 1 < count:
                for copy in loads(m + 1):
                    copy.start()
            compute(m)
            first_copy(m).start()
        if m in (1, 3):
            for copy in in_hops[m // 2]:
                copy.wait_recv()
            for copy in in_hops[m // 2 + 1]:
                copy.start()
        if m in (0, 2, 4):
            hop = m // 2
            for copy in hops[hop]:
                copy.wait_recv()
            for copy in hops[hop + 1]:
                copy.start()
        for behind, step in ((2, second_step), (4, line_step), (6, last_step)):
            if 0 <= m - behind < count:
                step(m - behind)
        if m == count - 1:
            rows_back()
    order = range(count)
    for m in order:
        if plan[m][0] == "tall":
            core_copy(m).wait_recv()
            out_ref[m, 0] = mine[m, c]
            out_ref[m, 1] = other_in[m]
        else:
            out_ref[m] = mine[m]
    for copy in hops[3]:
        copy.wait_recv()
    small_ref[...] = notes[...]


    for hop in hops + in_hops + [down_copies]:
        for copy in hop:
            copy.wait_send()
    for m in range(count):
        first_copy(m).wait_send()
        second_copy(m).wait_send()
        for copy in line_copies(m):
            copy.wait_send()
        if plan[m][0] == "tall":
            core_copy(m).wait_send()


def reduce_group(matrices, small, grad_in, grad_down, na, rows):
    arrays, plan = [], []
    for kind, lefts, rights, turn in matrices:
        places = []
        for group in (lefts, rights):
            places.append([])
            for array in group:
                found = [k for k, known in enumerate(arrays) if known is array]
                if not found:
                    arrays.append(array)
                    found = [len(arrays) - 1]
                places[-1].append(found[0])
        plan.append((kind, *places, turn))
    count = len(plan)
    tall = max(sum(a.shape[0] for a in lefts) for _, lefts, _, _ in matrices)
    turns = [turn for *_, turn in plan]
    low = lambda *shape: pltpu.VMEM(shape, BF16)
    sem = lambda *shape: pltpu.SemaphoreType.DMA(shape)
    all_small = (2, 2, na, 2) + small.shape
    return pl.pallas_call(
        functools.partial(reduce_kernel, plan=plan, inputs=len(arrays)),
        out_shape=[
            jax.ShapeDtypeStruct((count, 2, rows, HALF), BF16),
            jax.ShapeDtypeStruct(all_small, BF16),
            jax.ShapeDtypeStruct((rows, 2 * FF), BF16),
            jax.ShapeDtypeStruct(grad_down.shape[1:], BF16),
            jax.ShapeDtypeStruct((na - 1,) + grad_down.shape[1:], BF16),
        ],
        in_specs=[ANY] * (len(arrays) + 3),
        out_specs=[WHOLE] * 4 + [ANY],
        scratch_shapes=[
            low(count, 2, 2, na, 2, rows, HALF),
            low(turns.count(0), 2, 2, na, rows, HALF),
            low(turns.count(1), 2, na, 2, rows, HALF),
            low(count, 2, na, rows, HALF),
            low(count, 2, na, rows, HALF),
            low(count, na, 2, rows, HALF),
            low(count, na - 1, 2, rows, HALF),
            low(count, 2, rows, HALF),
            low(count, rows, HALF),
            low(2, tall, D),
            low(2, tall, D),
            low(*all_small),
            sem(2, 4),
            sem(count),
            sem(count),
            sem(count),
            sem(count),
            sem(count * (na - 1)),
            sem(count * (na - 1)),
            sem(count),
            sem(count),
            sem(na + 2),
            sem(na + 2),
            low(*grad_in.shape),
            low(2, 2, *grad_in.shape[-2:]),
            low(2, 2, *grad_in.shape[-2:]),
            low(4, *grad_in.shape[-2:]),
            sem(7),
            sem(7),
            sem(na - 1),
            sem(na - 1),
            sem(1),
        ],
        compiler_params=pltpu.CompilerParams(
            vmem_limit_bytes=60 * 2**20, collective_id=1, has_side_effects=True
        ),
        cost_estimate=LIGHT,
    )(*arrays, small, grad_in, grad_down)


def pair_in_kernel(own_ref, other_ref, weight_ref, out_ref, *, product):
    for step, ref in enumerate((own_ref, other_ref)):

        @pl.when(pl.program_id(0) == step)
        def _():
            out_ref[...] = product(ref[...], weight_ref[...]).astype(BF16)


def pair_in(own, other, weight, product):
    frames = own.shape[0]
    cols = weight.shape[1] if product is dot else weight.shape[0]
    whole = lambda array: pl.BlockSpec(
        array.shape, lambda i: (0, 0), pipeline_mode=pl.Buffered(1)
    )
    return pl.pallas_call(
        functools.partial(pair_in_kernel, product=product),
        out_shape=jax.ShapeDtypeStruct((2 * frames, cols), BF16),
        grid=(2,),
        in_specs=[whole(own), whole(other), whole(weight)],
        out_specs=pl.BlockSpec((frames, cols), lambda i: (i, 0)),
        compiler_params=pltpu.CompilerParams(vmem_limit_bytes=48 * 2**20),
        cost_estimate=LIGHT,
    )(own, other, weight)


def pair_out_kernel(*refs, product):
    part_refs, weight_ref, own_ref, other_ref = refs[:-3], refs[-3], refs[-2], refs[-1]
    sums = None
    column = 0
    for ref in part_refs:
        weight = weight_ref[...]
        if len(part_refs) > 1:
            weight = weight_ref[:, column : column + ref.shape[1]]
            column += ref.shape[1]
        term = product(ref[...], weight)
        sums = term if sums is None else sums + term

    @pl.when(pl.program_id(0) == 0)
    def _():
        own_ref[...] = sums

    @pl.when(pl.program_id(0) == 1)
    def _():
        other_ref[...] = sums.astype(BF16)


def pair_out(parts, weight, product):
    frames = parts[0].shape[0] // 2
    cols = weight.shape[1] if product is dot else weight.shape[0]
    whole = pl.BlockSpec((frames, cols), lambda i: (0, 0))
    return pl.pallas_call(
        functools.partial(pair_out_kernel, product=product),
        out_shape=[
            jax.ShapeDtypeStruct((frames, cols), F32),
            jax.ShapeDtypeStruct((frames, cols), BF16),
        ],
        grid=(2,),
        in_specs=[pl.BlockSpec((frames, part.shape[1]), lambda i: (i, 0)) for part in parts]
        + [pl.BlockSpec(weight.shape, lambda i: (0, 0), pipeline_mode=pl.Buffered(1))],
        out_specs=[whole, whole],
        compiler_params=pltpu.CompilerParams(vmem_limit_bytes=48 * 2**20),
        cost_estimate=LIGHT,
    )(*parts, weight)


def notes_kernel(own_ref, out_ref, notes, send, recv):
    y, c, z, x = (lax.axis_index(axis) for axis in AXES)
    na = notes.shape[2]
    far_y, far_c, far_x = {"y": 1 - y}, {"c": 1 - c}, {"x": 1 - x}
    lines = [{"z": lax.rem(z + k, na)} for k in range(1, na)]
    barrier = pltpu.get_barrier_semaphore()
    for device in [far_y, far_c, far_x] + lines:
        pl.semaphore_signal(
            barrier, inc=1, device_id=device, device_id_type=pl.DeviceIdType.MESH
        )
    pl.semaphore_wait(barrier, 3 + len(lines))
    notes[0, 0, 0, 0] = own_ref[...]
    hops = [
        [(notes.at[0, 0, 0, 0], notes.at[0, 0, 0, 1], far_x)],
        [(notes.at[0, 0, 0], notes.at[0, 0, k + 1], line) for k, line in enumerate(lines)],
        [(notes.at[0, 0], notes.at[0, 1], far_c)],
        [(notes.at[0], notes.at[1], far_y)],
    ]
    at = 0
    copies = []
    for hop in hops:
        group = []
        for source, target, device in hop:
            group.append(
                pltpu.make_async_remote_copy(
                    src_ref=source,
                    dst_ref=target,
                    send_sem=send.at[at],
                    recv_sem=recv.at[at],
                    device_id=device,
                    device_id_type=pl.DeviceIdType.MESH,
                )
            )
            at += 1
        for copy in group:
            copy.start()
        for copy in group:
            copy.wait_recv()
        copies += group
    for copy in copies:
        copy.wait_send()
    out_ref[...] = notes[...]


def gather_notes(notes, na):
    all_notes = (2, 2, na, 2) + notes.shape
    sem = pltpu.SemaphoreType.DMA((na + 2,))
    return pl.pallas_call(
        notes_kernel,
        out_shape=jax.ShapeDtypeStruct(all_notes, BF16),
        in_specs=[WHOLE],
        out_specs=WHOLE,
        scratch_shapes=[pltpu.VMEM(all_notes, BF16), sem, sem],
        compiler_params=pltpu.CompilerParams(collective_id=5, has_side_effects=True),
        cost_estimate=LIGHT,
    )(notes)


def shift_kernel(
    terms_ref, cot_hbm, in_ref, shifts_ref, cots_hbm, parts_ref,
    from_core, line_out, line_in, y_out, y_in, x_out, x_in,
    in_core, in_y, in_x,
    core_sem, line_send, line_recv, step_sem, cot_send, cot_recv, relay_send, relay_recv,
    in_send, in_recv,
):
    y, c, z, x = (lax.axis_index(axis) for axis in AXES)
    na = terms_ref.shape[2]
    far_y, far_c, far_x = 1 - y, 1 - c, 1 - x

    def remote(source, target, send, recv, device):
        return pltpu.make_async_remote_copy(
            src_ref=source,
            dst_ref=target,
            send_sem=send,
            recv_sem=recv,
            device_id=device,
            device_id_type=pl.DeviceIdType.MESH,
        )

    devices = [{"y": far_y}, {"c": far_c}, {"x": far_x}]
    devices += [{"z": lax.rem(z + k, na)} for k in range(1, na)]
    barrier = pltpu.get_barrier_semaphore()
    for device in devices:
        pl.semaphore_signal(
            barrier, inc=1, device_id=device, device_id_type=pl.DeviceIdType.MESH
        )
    pl.semaphore_wait(barrier, len(devices))

    to_core = remote(terms_ref.at[:, 1], from_core, core_sem.at[0], core_sem.at[1], {"c": far_c})
    to_core.start()

    def block_copies(first, pairs, device):
        return [
            remote(source, target, in_send.at[first + k], in_recv.at[first + k], device)
            for k, (source, target) in enumerate(pairs)
        ]

    in_hops = [
        block_copies(0, [(in_ref.at[:, 1], in_core)], {"c": far_c}),
        block_copies(1, [(in_ref.at[1, 0], in_y.at[0]), (in_core.at[1], in_y.at[1])], {"y": far_y}),
        block_copies(
            3,
            [
                (in_ref.at[0, 0, 1], in_x.at[0]),
                (in_core.at[0, 1], in_x.at[1]),
                (in_y.at[0, 1], in_x.at[2]),
                (in_y.at[1, 1], in_x.at[3]),
            ],
            {"x": far_x},
        ),
    ]
    for copy in in_hops[0]:
        copy.start()
    chips = {1: {"x": far_x}, 2: {"y": far_y}}
    cots = {
        2 * k: remote(cot_hbm, cots_hbm.at[2 * k], cot_send.at[2 * k], cot_recv.at[2 * k], chips[k])
        for k in chips
    }
    cots[1] = remote(cot_hbm, cots_hbm.at[1], cot_send.at[1], cot_recv.at[1], {"c": far_c})
    for k in (1, 2, 3):
        cots[2 * k + 1] = remote(
            cots_hbm.at[2 * k], cots_hbm.at[2 * k + 1],
            cot_send.at[2 * k + 1], cot_recv.at[2 * k + 1], {"c": far_c},
        )
    relays = []
    for k, (part, size) in enumerate(halves_of(cot_hbm.shape[0])):
        near, next_to = (1, 2) if k == 0 else (2, 1)
        here = pl.ds(part, size)
        relays.append(
            remote(
                cots_hbm.at[2 * near, here], cots_hbm.at[6, here],
                relay_send.at[k], relay_recv.at[k], chips[next_to],
            )
        )
    cots[2].start()
    cots[4].start()
    cots[1].start()

    to_core.wait_recv()
    for copy in in_hops[0]:
        copy.wait_recv()
    for copy in in_hops[1]:
        copy.start()
    lines = []
    for k in range(1, na):
        line_out[k - 1] = terms_ref[:, 0, k] + from_core[:, k]
        lines.append(
            remote(
                line_out.at[k - 1], line_in.at[k - 1], line_send.at[k - 1], line_recv.at[k - 1],
                {"z": lax.rem(z - k + na, na)},
            )
        )
        lines[-1].start()
    here = terms_ref[:, 0, 0] + from_core[:, 0]
    for k, copy in enumerate(lines):
        copy.wait_recv()
        here = here + line_in[k]
    y_out[...] = here[1]
    to_y = remote(y_out, y_in, step_sem.at[0], step_sem.at[1], {"y": far_y})
    to_y.start()
    for k in (1, 2):
        cots[2 * k].wait_recv()
    for copy in relays:
        copy.start()
    for k in (1, 2):
        cots[2 * k + 1].start()
    to_y.wait_recv()
    here = here[0] + y_in[...]
    x_out[...] = here[1]
    to_x = remote(x_out, x_in, step_sem.at[2], step_sem.at[3], {"x": far_x})
    to_x.start()
    for copy in in_hops[1]:
        copy.wait_recv()
    for copy in in_hops[2]:
        copy.start()
    to_x.wait_recv()
    shifts_ref[...] = here[0] + x_in[...]

    for copy in relays:
        copy.wait_recv()
    cots[7].start()
    for copy in in_hops[2]:
        copy.wait_recv()
    for at_y in range(2):
        for at_c in range(2):
            near = in_ref[0, 0, 0] if not at_y and not at_c else None
            if near is None:
                near = in_y[at_c, 0] if at_y else in_core[0, 0]
            parts_ref[at_y, at_c, 0] = near
            parts_ref[at_y, at_c, 1] = in_x[at_y * 2 + at_c]
    for k in (1, 3, 5, 7):
        cots[k].wait_recv()
        cots[k].wait_send()
    for copy in [to_core, to_y, to_x, cots[2], cots[4]] + lines + relays + sum(in_hops, []):
        copy.wait_send()


def sum_shifts(terms, cotangent, blocks, na):
    rows = terms.shape[-2]
    full = lambda *shape: pltpu.VMEM(shape + (rows, 128), F32)
    sem = lambda size: pltpu.SemaphoreType.DMA((size,))
    block = blocks.shape[-2:]
    low = lambda *shape: pltpu.VMEM(shape + block, BF16)
    return pl.pallas_call(
        shift_kernel,
        out_shape=[
            jax.ShapeDtypeStruct((rows, 128), F32),
            jax.ShapeDtypeStruct((8,) + cotangent.shape, BF16),
            jax.ShapeDtypeStruct(blocks.shape, BF16),
        ],
        in_specs=[WHOLE, ANY, WHOLE],
        out_specs=[WHOLE, ANY, WHOLE],
        scratch_shapes=[
            full(2, na, 2),
            full(na - 1, 2, 2),
            full(na - 1, 2, 2),
            full(2),
            full(2),
            full(),
            full(),
            low(2, 2),
            low(2, 2),
            low(4),
            sem(2),
            sem(na - 1),
            sem(na - 1),
            sem(4),
            sem(8),
            sem(8),
            sem(2),
            sem(2),
            sem(7),
            sem(7),
        ],
        compiler_params=pltpu.CompilerParams(
            vmem_limit_bytes=32 * 2**20, collective_id=2, has_side_effects=True
        ),
        cost_estimate=LIGHT,
    )(terms, cotangent, blocks)


def halves_of(height):
    cut = height // 32 * 16
    return (0, cut), (cut, height - cut)


def ffn_group_kernel(
    entry_hbm, notes_hbm, cot_hbm, cots_hbm, lines_hbm, down_hbm,
    d_entry_hbm, grad_down_hbm, grad_in_hbm, branch_hbm, own_hbm, other_hbm, pair_hbm, back_hbm,
    sum_hbm, branch_back_hbm,
    entry, d_branch, hidden, d_gate_up, in_lines, down_lines, partial, away, branch, loaded, sums,
    local_sem, entry_send, entry_recv, cot_sem,
    pair_send, pair_recv, back_send, back_recv, branch_sem, out_sem,
    relay_send, relay_recv, branch_pair_send, branch_pair_recv, branch_send, branch_recv,
    *, chips, peers, sizes,
):
    ny, nb = sizes
    y, c, x = lax.axis_index("y"), lax.axis_index("c"), lax.axis_index("x")
    frames = cot_hbm.shape[0]
    rows = frames // 2
    own_rows = in_lines.shape[-2]
    width = down_lines.shape[0] * down_lines.shape[1]
    in_all = lambda: in_lines[...].reshape(D, 2 * width)
    down_all = lambda: down_lines[...].reshape(width, D)
    count = len(chips)
    sibling = {"c": 1 - c}
    ahead = [{"y": lax.rem(y + dy, ny), "x": lax.rem(x + dx, nb)} for dy, dx in chips]
    behind = [
        {"y": lax.rem(y - dy + ny, ny), "x": lax.rem(x - dx + nb, nb)} for dy, dx in chips
    ]

    def remote(source, target, send, recv, device):
        return pltpu.make_async_remote_copy(
            src_ref=source,
            dst_ref=target,
            send_sem=send,
            recv_sem=recv,
            device_id=device,
            device_id_type=pl.DeviceIdType.MESH,
        )

    barrier = pltpu.get_barrier_semaphore()
    for device in [sibling] + behind[1:]:
        pl.semaphore_signal(
            barrier, inc=1, device_id=device, device_id_type=pl.DeviceIdType.MESH
        )
    pl.semaphore_wait(barrier, count)

    loads = [
        pltpu.make_async_copy(source, target, local_sem.at[k])
        for k, (source, target) in enumerate(
            [
                (entry_hbm, entry.at[0, pl.ds(0, frames)]),
                (notes_hbm, entry.at[0, pl.ds(frames, NOTE_ROWS)]),
                (down_hbm, down_lines),
            ]
        )
    ]
    for k, (dy, dc, dx) in enumerate(peers):
        target = in_lines.at[
            lax.rem(y + dy, ny), lax.rem(c + dc, 2), :, lax.rem(x + dx, nb)
        ]
        source = lines_hbm.at[:, pl.ds(k * own_rows, own_rows)]
        loads.append(pltpu.make_async_copy(source, target, local_sem.at[3 + k]))
    for load in loads:
        load.start()
    cot_loads = [
        pltpu.make_async_copy(
            cots_hbm.at[k] if k else cot_hbm, d_branch.at[k], cot_sem.at[k]
        )
        for k in range(2 * count)
    ]
    for load in cot_loads:
        load.start()
    entry_copies = {
        1: remote(entry.at[0], entry.at[1], entry_send.at[1], entry_recv.at[1], sibling)
    }
    for k in range(1, count):
        entry_copies[2 * k] = remote(
            entry.at[0], entry.at[2 * k], entry_send.at[2 * k], entry_recv.at[2 * k], ahead[k]
        )
        entry_copies[2 * k + 1] = remote(
            entry.at[2 * k], entry.at[2 * k + 1],
            entry_send.at[2 * k + 1], entry_recv.at[2 * k + 1], sibling,
        )
    for load in loads[:2]:
        load.wait()
    for k in (2, 4, 1):
        entry_copies[k].start()

    relays = []
    height = entry.shape[1]
    for k, (part, size) in enumerate(halves_of(height)):
        near, next_to = (1, 2) if k == 0 else (2, 1)
        here = pl.ds(part, size)
        relays.append(
            remote(
                entry.at[2 * near, here], entry.at[2 * 3, here],
                relay_send.at[k], relay_recv.at[k], ahead[next_to],
            )
        )

    def branch_copies(k):
        copies = []
        if k == 0:
            copies.append(pltpu.make_async_copy(branch.at[0], own_hbm, branch_sem.at[0]))
        copies.append(
            remote(
                branch.at[1], other_hbm.at[k], branch_pair_send.at[k], branch_pair_recv.at[k], sibling
            )
        )
        return copies

    def branch_wait(k):
        for copy in branch_copies(k)[:-1]:
            copy.wait()
        branch_copies(k)[-1].wait_send()

    def branch_copy(k):
        return remote(
            sum_hbm.at[k - 1], branch_back_hbm.at[k - 1], branch_send.at[k], branch_recv.at[k],
            behind[k],
        )

    order = (0, 3, 1, 2)
    turn = {k: order.index(k) % 2 for k in order}

    def pair_copy(k):
        return remote(
            away.at[turn[k]], pair_hbm.at[k], pair_send.at[k], pair_recv.at[k], sibling
        )

    def back_copy(k):
        return remote(
            partial.at[k], back_hbm.at[k - 1], back_send.at[k], back_recv.at[k], behind[k]
        )

    def compute(k, i):
        @pl.loop(0, 2)
        def _(part):
            slot = 2 * k + i
            here = pl.ds(pl.multiple_of(part * rows, rows), rows)
            notes = entry[slot, frames:, :].astype(F32)
            gate_row = notes[0:1] + notes[1:2] + notes[2:3]
            d_here = (d_branch[slot, here, :].astype(F32) * gate_row).astype(BF16)
            d_branch[slot, here, :] = d_here
            gate_up = dot(entry[slot, here, :], in_all())
            gate, up = gate_up[:, :width], gate_up[:, width:]
            logistic = jax.nn.sigmoid(gate)
            hidden_here = (gate * logistic * up).astype(BF16)
            hidden[slot, here, :] = hidden_here
            d_hidden = dot_back(d_here, down_all())
            d_gate = d_hidden * up * logistic * (1.0 + gate * (1.0 - logistic))
            d_gate_up[slot, here, :width] = d_gate.astype(BF16)
            d_gate_up[slot, here, width:] = (d_hidden * gate * logistic).astype(BF16)
            d_entry = dot_back(d_gate_up[slot, here, :], in_all()).astype(BF16)
            branch[i, here, :] = dot(hidden_here, down_all()).astype(BF16)

            if i == 0:
                partial[k, here, :] = d_entry
            else:
                away[turn[k], here, :] = d_entry

    def move(source, target):
        copy = pltpu.make_async_copy(source, target, out_sem.at[0])
        copy.start()
        copy.wait()

    def fetch(source):
        move(source, loaded)
        return loaded[...].astype(F32)

    def branch_terms(k):
        branch_copies(k)[-1].wait_recv()
        own = branch[0].astype(F32) if k else fetch(own_hbm)
        return own + fetch(other_hbm.at[k])

    def finish(k):
        pair_copy(k).wait_recv()
        partial[k] = (partial[k].astype(F32) + fetch(pair_hbm.at[k])).astype(BF16)
        if k:
            back_copy(k).start()
            pair_copy(k).wait_send()
            away[turn[k]] = branch_terms(k).astype(BF16)
            move(away.at[turn[k]], sum_hbm.at[k - 1])
            branch_copy(k).start()
        else:
            pair_copy(k).wait_send()

    before = None
    for k in order:
        if k == 0:
            for load in loads[2:]:
                load.wait()
        elif k == 3:
            entry_copies[2].wait_recv()
            entry_copies[4].wait_recv()
            for copy in relays:
                copy.start()
            for near in (3, 5):
                entry_copies[near].start()
            for copy in relays:
                copy.wait_recv()
            entry_copies[7].start()
        entry_copies[2 * k + 1].wait_recv()
        cot_loads[2 * k].wait()
        cot_loads[2 * k + 1].wait()
        if before is not None:
            branch_wait(before)
        compute(k, 0)
        if before == 0:
            finish(0)
        compute(k, 1)
        pair_copy(k).start()
        for copy in branch_copies(k):
            copy.start()
        if k:
            finish(k)
        before = k
    branch_wait(before)

    down_rows = 256 if width % 256 == 0 else 128

    @pl.loop(0, width // down_rows)
    def _(block):
        columns = pl.ds(pl.multiple_of(block * down_rows, down_rows), down_rows)
        term = dot_rows(hidden[0, :, columns], d_branch[0])
        for slot in range(1, 2 * count):
            term += dot_rows(hidden[slot, :, columns], d_branch[slot])
        branch[0, :down_rows, :] = term.astype(BF16)
        copy = pltpu.make_async_copy(
            branch.at[0, pl.ds(0, down_rows)], grad_down_hbm.at[columns], out_sem.at[1]
        )
        copy.start()
        copy.wait()

    na, _, lanes, _ = grad_in_hbm.shape
    in_rows = na * lanes

    @pl.loop(0, D // in_rows)
    def _(block):
        columns = pl.ds(pl.multiple_of(block * in_rows, 128), in_rows)
        term = dot_rows(entry[0, :frames, columns], d_gate_up[0])
        for slot in range(1, 2 * count):
            term += dot_rows(entry[slot, :frames, columns], d_gate_up[slot])
        branch[1, :in_rows, :] = term.astype(BF16)
        copies = [
            pltpu.make_async_copy(
                branch.at[1, pl.ds(z * lanes, lanes)], grad_in_hbm.at[z, block], out_sem.at[2 + z]
            )
            for z in range(na)
        ]
        copy_all(copies)

    total_here = partial[0].astype(F32)
    for k in range(1, count):
        back_copy(k).wait_recv()
        total_here += fetch(back_hbm.at[k - 1])
    sums[...] = total_here
    move(sums, d_entry_hbm)
    total_here = branch_terms(0)
    for k in range(1, count):
        branch_copy(k).wait_recv()
        total_here += fetch(branch_back_hbm.at[k - 1])
    sums[...] = total_here
    move(sums, branch_hbm)

    entry_copies[1].wait_send()
    for k in range(1, count):
        if k < 3:
            entry_copies[2 * k].wait_send()
            relays[k - 1].wait_send()
        entry_copies[2 * k + 1].wait_send()
        back_copy(k).wait_send()
        branch_copy(k).wait_send()


def ffn_group(entry, notes, cotangent, cotangents, lines, down, chips, peers, sizes):
    frames = cotangent.shape[0]
    na, depth = down.shape[:2]
    width = na * depth
    rows = lines.shape[1] // len(peers)
    lanes = sizes[1] * rows
    count = len(chips)
    low = lambda *shape: jax.ShapeDtypeStruct(shape, BF16)
    sem = lambda size: pltpu.SemaphoreType.DMA((size,))
    clip = (frames, D)
    return pl.pallas_call(
        functools.partial(ffn_group_kernel, chips=chips, peers=peers, sizes=sizes),
        out_shape=[
            jax.ShapeDtypeStruct(clip, F32),
            low(width, D),
            low(na, D // (na * lanes), lanes, 2 * width),
            jax.ShapeDtypeStruct(clip, F32),
            low(*clip),
            low(count, *clip),
            low(count, *clip),
            low(count - 1, *clip),
            low(count - 1, *clip),
            low(count - 1, *clip),
        ],
        in_specs=[ANY] * 6,
        out_specs=[ANY] * 10,
        scratch_shapes=[
            pltpu.VMEM((2 * count, frames + NOTE_ROWS, D), BF16),
            pltpu.VMEM((2 * count, frames, D), BF16),
            pltpu.VMEM((2 * count, frames, width), BF16),
            pltpu.VMEM((2 * count, frames, 2 * width), BF16),
            pltpu.VMEM((sizes[0], 2, na, sizes[1], rows, 2 * width), BF16),
            pltpu.VMEM((na, depth, D), BF16),
            pltpu.VMEM((count, frames, D), BF16),
            pltpu.VMEM((2, frames, D), BF16),
            pltpu.VMEM((2, frames, D), BF16),
            pltpu.VMEM(clip, BF16),
            pltpu.VMEM(clip, F32),
            sem(3 + len(peers)),
            sem(2 * count),
            sem(2 * count),
            sem(2 * count),
            sem(count),
            sem(count),
            sem(count),
            sem(count),
            sem(2),
            sem(2 + na),
            sem(2),
            sem(2),
            sem(count),
            sem(count),
            sem(count),
            sem(count),
        ],
        compiler_params=pltpu.CompilerParams(
            vmem_limit_bytes=60 * 2**20, collective_id=0, has_side_effects=True
        ),
        cost_estimate=LIGHT,
    )(entry, notes, cotangent, cotangents, lines, down)


def stack_kernel(*refs):
    out_ref = refs[-1]
    out_ref[...] = jnp.zeros_like(out_ref)
    rows = refs[0].shape[0]
    for k, ref in enumerate(refs[:-1]):
        out_ref[k * rows : (k + 1) * rows, :] = ref[...].astype(BF16)


def stack_vectors(vectors):
    parts = [vector.reshape(-1, 128) for vector in vectors]
    rows = sum(part.shape[0] for part in parts)
    return pl.pallas_call(
        stack_kernel,
        out_shape=jax.ShapeDtypeStruct((rows + -rows % 16, 128), BF16),
        in_specs=[WHOLE] * len(parts),
        out_specs=WHOLE,
        cost_estimate=LIGHT,
    )(*parts)


def total_kernel(sums_ref, out_ref, steps, lines, step_send, step_recv, line_send, line_recv):
    y, c, z, x = (lax.axis_index(axis) for axis in AXES)
    na = lines.shape[0]

    def remote(source, target, send, recv, device):
        return pltpu.make_async_remote_copy(
            src_ref=source,
            dst_ref=target,
            send_sem=send,
            recv_sem=recv,
            device_id=device,
            device_id_type=pl.DeviceIdType.MESH,
        )

    near = [{"c": 1 - c}, {"x": 1 - x}, {"y": 1 - y}]
    far = [{"z": lax.rem(z + k, na)} for k in range(1, na)]
    barrier = pltpu.get_barrier_semaphore()
    for device in near + far:
        pl.semaphore_signal(
            barrier, inc=1, device_id=device, device_id_type=pl.DeviceIdType.MESH
        )
    pl.semaphore_wait(barrier, len(near) + len(far))
    steps[0, 0] = sums_ref[...]
    for k, device in enumerate(near):
        copy = remote(steps.at[k, 0], steps.at[k, 1], step_send.at[k], step_recv.at[k], device)
        copy.start()
        copy.wait()
        both = steps[k, 0] + steps[k, 1]
        if k < 2:
            steps[k + 1, 0] = both
    lines[z] = both
    copies = [
        remote(lines.at[z], lines.at[z], line_send.at[k], line_recv.at[k], device)
        for k, device in enumerate(far)
    ]
    for copy in copies:
        copy.start()
    for copy in copies:
        copy.wait()
    whole = lines[0]
    for k in range(1, na):
        whole = whole + lines[k]
    out_ref[...] = whole


def total_over_devices(sums, na):
    sem = lambda size: pltpu.SemaphoreType.DMA((size,))
    return pl.pallas_call(
        total_kernel,
        out_shape=jax.ShapeDtypeStruct(sums.shape, F32),
        in_specs=[WHOLE],
        out_specs=WHOLE,
        scratch_shapes=[
            pltpu.VMEM((3, 2) + sums.shape, F32),
            pltpu.VMEM((na,) + sums.shape, F32),
            sem(3),
            sem(3),
            sem(na - 1),
            sem(na - 1),
        ],
        compiler_params=pltpu.CompilerParams(collective_id=3, has_side_effects=True),
        cost_estimate=LIGHT,
    )(sums)


def step_kernel(factor_ref, *refs):
    count = len(refs) // 3
    at = 0
    for weight_ref, direction_ref, out_ref in zip(refs[:count], refs[count : 2 * count], refs[2 * count :]):
        if len(weight_ref.shape) == 3:
            for k in range(weight_ref.shape[0]):
                out_ref[k] = weight_ref[k] - factor_ref[at] * direction_ref[k]
                at += 1
        else:
            out_ref[...] = weight_ref[...] - factor_ref[at] * direction_ref[...]
            at += 1


def step_weights(factors, weights, directions):
    return pl.pallas_call(
        step_kernel,
        out_shape=[jax.ShapeDtypeStruct(weight.shape, F32) for weight in weights],
        in_specs=[SCALARS] + [WHOLE] * (2 * len(weights)),
        out_specs=[WHOLE] * len(weights),
        compiler_params=pltpu.CompilerParams(vmem_limit_bytes=56 * 2**20),
        cost_estimate=LIGHT,
    )(factors, *weights, *directions)


def lamb_kernel(spot_ref, weight_ref, first_ref, second_ref, *refs):
    gradient_refs = refs[:-4]
    first_out, second_out, direction_out, sums_ref = refs[-4:]
    gradient = gradient_refs[0][...].astype(F32)
    if len(gradient_refs) == 2:
        ours = pl.program_id(1) % 2 == spot_ref[1]
        gradient = jnp.where(ours, gradient, gradient_refs[1][...].astype(F32))
    weight = weight_ref[...]
    first_new = BETA_ONE * first_ref[...] + (1.0 - BETA_ONE) * gradient
    second_new = BETA_TWO * second_ref[...] + (1.0 - BETA_TWO) * gradient * gradient
    direction = (
        first_new
        / (1.0 - BETA_ONE**STEP)
        / (jnp.sqrt(second_new / (1.0 - BETA_TWO**STEP)) + ADAM_EPS)
        + DECAY * weight
    )
    first_out[...] = first_new
    second_out[...] = second_new
    direction_out[...] = direction

    @pl.when(pl.program_id(1) == 0)
    def _():
        sums_ref[...] = jnp.zeros_like(sums_ref)

    for row, values in enumerate((weight, direction)):
        squares = jnp.sum(values * values, axis=1)
        for start in range(0, squares.shape[1], 128):
            sums_ref[:, row, :] += squares[:, start : start + 128]


def lamb_terms(spot, weight, first_moment, second_moment, gradients, block):
    shape = weight.shape
    arrays = [
        array.reshape((-1,) + array.shape[-2:])
        for array in (weight, first_moment, second_moment, *gradients)
    ]
    groups, rows, cols = arrays[0].shape
    in_blocks = len(gradients) == 1 and arrays[3].shape != arrays[0].shape
    spec = pl.BlockSpec((1, rows, block), lambda i, j: (i, 0, j))
    turns = 2 * HALF // block
    halves = pl.BlockSpec((1, rows, block), lambda i, j: (j // turns, 0, j % turns // 2))
    by_block = pl.BlockSpec((1, rows, block), lambda i, j: (j, 0, 0))
    full = jax.ShapeDtypeStruct((groups, rows, cols), F32)
    out = pl.pallas_call(
        lamb_kernel,
        out_shape=[full, full, full, jax.ShapeDtypeStruct((groups, 8, 128), F32)],
        grid=(groups, cols // block),
        in_specs=[SCALARS]
        + [spec] * 3
        + [by_block if in_blocks else spec if len(gradients) == 1 else halves] * len(gradients),
        out_specs=[spec] * 3 + [pl.BlockSpec((1, 8, 128), lambda i, j: (i, 0, 0))],
        compiler_params=pltpu.CompilerParams(vmem_limit_bytes=40 * 2**20),
        cost_estimate=pl.CostEstimate(
            flops=20 * weight.size, bytes_accessed=28 * weight.size, transcendentals=weight.size
        ),
    )(spot, *arrays)
    return [array.reshape(shape) for array in out[:3]] + [jnp.sum(out[3][:, :2], axis=-1)]


class Grid:
    def __init__(self, mesh):
        self.ny = mesh.shape["dp"] // 2
        self.nb = 2
        self.na = mesh.shape["fsdp"] // 2
        self.sizes = dict(y=self.ny, c=2, z=self.na, x=self.nb)
        self.count = self.ny * 2 * self.na * self.nb
        self.spots = list(itertools.product(*(range(self.sizes[axis]) for axis in AXES)))
        self.peers = list(itertools.product(range(self.ny), range(2), range(self.nb)))
        self.chips = list(itertools.product(range(self.ny), range(self.nb)))
        self.back = [
            (dy, dc, dx)
            for dx in range(self.nb)
            for dy in range(self.ny)
            for dc in range(2)
        ]
        self.mesh = Mesh(mesh.devices.reshape(self.ny, 2, self.na, self.nb), AXES)

    def line(self, y, c, z, x):
        return ((y * 2 + c) * self.na + z) * self.nb + x

    def here(self):
        return {axis: lax.axis_index(axis) for axis in AXES}

    def move(self, array, **steps):
        steps = {axis: step % self.sizes[axis] for axis, step in steps.items()}
        steps = {axis: step for axis, step in steps.items() if step}
        if not steps:
            return array
        names = tuple(axis for axis in AXES if axis in steps)
        lengths = [self.sizes[axis] for axis in names]
        pairs = []
        for spot in itertools.product(*(range(n) for n in lengths)):
            source = target = 0
            for axis, at, n in zip(names, spot, lengths):
                source, target = source * n + at, target * n + (at + steps[axis]) % n
            pairs.append((source, target))
        return lax.ppermute(array, names, pairs)

    def rank(self, mine, offset):
        y, c, x = ((mine[axis] + step) % self.sizes[axis] for axis, step in zip("ycx", offset))
        return (y * 2 + c) * self.nb + x

    def swap(self, array):
        return self.move(array, c=1)

    def gather_small(self, array):
        shape = array.shape
        for axis in "xzcy":
            parts = [self.move(array, **{axis: k}) for k in range(self.sizes[axis])]
            array = jnp.concatenate([part.reshape((-1,) + shape) for part in parts])
        return array

    def scatter_small(self, array):
        sources = [array]
        for axis in "cyxz":
            where = 0
            arrays = []
            size = self.sizes[axis]
            sources = [s.reshape(self.small_shape(axis, s)) for s in sources]
            for k in range(1, size):
                part = total([s[:, k] for s in sources])
                arrays.append(self.move(part, **{axis: -k}))
            sources = [s[:, 0] for s in sources] + arrays
        return total(sources).reshape(array.shape[1:])

    def small_shape(self, axis, array):
        before = {"c": self.ny, "y": 1, "x": self.na, "z": 1}[axis]
        return (before, self.sizes[axis], -1, array.shape[-1])

    def sum_small(self, array):
        bit = 1
        while bit < self.count:
            array = array + lax.ppermute(array, AXES, [(d, d ^ bit) for d in range(self.count)])
            bit *= 2
        return array

    def spread(self, lines, turn, between):
        held, marks = {(0, 0): lines}, []
        for axis in ("x", "y") if turn else ("y", "x"):
            for (y, x), piece in list(held.items()):
                for k in range(1, self.sizes[axis]):
                    step = dict(y=y, x=x)
                    step[axis] = k
                    held[(step["y"], step["x"])] = self.move(piece, **{axis: k})
            if not marks:
                marks = list(held.values())[1:]
                if between:
                    held.update(zip(list(held)[1:], after(marks, between)))
        return held, marks

    def gather_weights(self, parts, shapes, mine, spot, first, between=(), behind=()):
        rows = parts[0][0][0].shape[0]
        mixed = jnp.stack([shard for part in parts for shard, *_ in part])
        lines = lax.all_gather(mixed, "z")
        if first:
            (lines,) = after([lines], first)
        start = 0
        held, marks, plan = [], [], dict(parts=[], outs=len(shapes))
        for turn, part in enumerate(parts):
            end = start + len(part)
            pieces, arrived = self.spread(lines[:, start:end], turn, between)
            held.append(pieces)
            marks += arrived
            start = end
            plan["parts"].append(
                [(out, lane, column, shard.shape[1]) for shard, out, lane, column in part]
            )
        plan["offsets"] = sorted(held[0])
        if rows % 16 == 0:
            arrays = [pieces[offset] for pieces in held for offset in plan["offsets"]]
            arrays += behind
            copies = len(plan["offsets"]) * sum(len(part) for part in parts)
            kernel = functools.partial(place_pieces, plan=plan, sizes=(self.ny, self.nb))
            return place(kernel, spot, arrays, shapes, copies), marks
        outs = [jnp.zeros(shape, BF16) for shape in shapes]
        for pieces, blocks in zip(held, plan["parts"]):
            for (dy, dx), piece in pieces.items():
                y = (mine["y"] - dy + self.ny) % self.ny
                x = (mine["x"] - dx + self.nb) % self.nb
                for block, (out, lane, column, width) in enumerate(blocks):
                    update = piece[:, block][None, :, None]
                    if lane is None:
                        at = (y, 0, x, 0, column)
                    else:
                        update = update[:, None]
                        at = (y, lane, 0, x, 0, column)
                    outs[out] = lax.dynamic_update_slice(outs[out], update, at)
        return outs, marks

    def swap_ranks(self, blocks):
        shape = blocks.shape[1:]
        blocks = blocks.reshape((self.ny, 2, self.nb) + shape)
        for where, axis in ((1, "c"), (0, "y"), (2, "x")):
            parts = [
                self.move(lax.index_in_dim(blocks, k, where), **{axis: k})
                for k in range(self.sizes[axis])
            ]
            blocks = jnp.concatenate(parts, axis=where)
        return blocks.reshape((-1,) + shape)

    def swap_back(self, blocks, mine):
        for where, axis in ((1, "c"), (1, "y"), (2, "x")):
            parts = [
                self.move(pick(blocks, (mine[axis] + k) % self.sizes[axis], where), **{axis: k})
                for k in range(self.sizes[axis])
            ]
            blocks = jnp.stack(parts)
        return blocks.reshape((-1,) + blocks.shape[-2:])

    def gather_ranks(self, in_parts, down_part, mine, spot):
        peers, rows, width = in_parts.shape
        depth = down_part.shape[0]
        in_shape = (self.ny, 2, self.na, self.nb, rows, width)
        down_shape = (self.na, depth, D)
        if rows % 16 == 0 and width == D:
            mixed = jnp.concatenate([in_parts.reshape(-1, D), down_part])
            lines = lax.all_gather(mixed, "z")
            kernel = functools.partial(
                place_ranks,
                offsets=self.peers,
                sizes=(self.ny, self.na, self.nb),
                rows=rows,
                depth=depth,
            )
            rank_in, rank_down = place(kernel, spot, [lines], [in_shape, down_shape], peers + 1)
        else:
            rank_down = lax.all_gather(down_part, "z")
            lines = lax.all_gather(in_parts, "z")
            rank_in = jnp.zeros(in_shape, BF16)
            for k, (dy, dc, dx) in enumerate(self.peers):
                at = ((mine["y"] - dy) % self.ny, (mine["c"] + dc) % 2, 0, (mine["x"] - dx) % self.nb, 0, 0)
                rank_in = lax.dynamic_update_slice(rank_in, lines[:, k][None, None, :, None], at)
        return rank_in.reshape(-1, width), rank_down.reshape(-1, D)

    def join_columns(self, pieces, mine, spot):
        peers, rows, width = pieces.shape
        width = width // 2
        if rows % 16 == 0:
            kernel = functools.partial(
                place_columns, offsets=self.back, sizes=(self.ny, self.nb), width=width
            )
            return place(kernel, spot, [pieces], [(rows, 2 * FF)], 2 * peers)[0]
        out = jnp.zeros((rows, 2, FF), BF16)
        for k, (dy, dc, dx) in enumerate(self.back):
            y, x = (mine["y"] - dy) % self.ny, (mine["x"] - dx) % self.nb
            rank = (y * 2 + (mine["c"] + dc) % 2) * self.nb + x
            piece = pieces[k].reshape(rows, 2, width)
            out = lax.dynamic_update_slice(out, piece, (0, 0, rank * width))
        return out.reshape(rows, 2 * FF)

    def fold(self, array, names, turn, mine, between=(), behind=(), marks=None):
        names = list(names)
        sources = [array]
        for axis, waits in zip("yx" if turn else "xy", (between, behind)):
            where = names.index(axis)
            size = self.sizes[axis]
            arrived = []
            for k in range(1, size):
                away = total([pick(s, (mine[axis] + k) % size, where) for s in sources])
                arrived.append(self.move(away.astype(BF16), **{axis: k}))
            if waits:
                arrived = after(arrived, waits)
            if marks is not None and len(names) > len(array.shape) - 3:
                marks += arrived
            sources = [pick(s, mine[axis], where) for s in sources] + list(arrived)
            names.remove(axis)
        return total(sources).astype(BF16)

    def to_rank(self, array, back=False):
        pairs = []
        for d in range(self.count):
            rank, z = divmod(d, self.na)
            y, c, x = self.peers[rank]
            pairs.append((d, self.line(y, c, z, x)))
        if back:
            pairs = [(b, a) for a, b in pairs]
        return lax.ppermute(array, AXES, pairs)


def lamb_small(weight, first_moment, second_moment, gradient):
    first_new = BETA_ONE * first_moment + (1.0 - BETA_ONE) * gradient
    second_new = BETA_TWO * second_moment + (1.0 - BETA_TWO) * gradient * gradient
    direction = (
        first_new
        / (1.0 - BETA_ONE**STEP)
        / (jnp.sqrt(second_new / (1.0 - BETA_TWO**STEP)) + ADAM_EPS)
        + DECAY * weight
    )
    sums = jnp.stack([jnp.sum(weight * weight), jnp.sum(direction * direction)])
    return [first_new, second_new, direction, sums[None]]


def shards(
    grid,
    latents,
    context,
    timestep,
    lengths,
    cotangent,
    mod_matrix,
    mod_first,
    mod_second,
    qkv_matrix,
    qkv_first,
    qkv_second,
    square_set,
    square_first,
    square_second,
    ctx_matrix,
    ctx_first,
    ctx_second,
    ff_in,
    in_first,
    in_second,
    ff_down,
    down_first,
    down_second,
    norm_gains,
    gains_first,
    gains_second,
):
    mine = grid.here()
    core = mine["c"]
    spot = jnp.stack([mine[axis] for axis in AXES]).astype(jnp.int32)
    device = grid.line(*(mine[axis] for axis in AXES))
    count, ranks = grid.count, len(grid.peers)
    rows = mod_matrix.shape[0]
    frames = latents.shape[1]
    words = context.shape[1]
    valid = lengths[0]
    keep_rows = (jnp.arange(frames) < valid).astype(F32)[:, None]

    width = FF // ranks
    grouped = rows % 16 == 0 and grid.ny == 2 and grid.nb == 2
    if grouped:
        prepare = functools.partial(prepare_kernel, offsets=grid.peers, sizes=(grid.ny, grid.na, grid.nb))
        low_own, five_other, in_blocks = pl.pallas_call(
            prepare,
            out_shape=[
                jax.ShapeDtypeStruct(shape, BF16)
                for shape in ((9, rows, HALF), (5, rows, HALF), (ranks, rows, 2 * width))
            ],
            in_specs=[SCALARS] + [WHOLE] * 4,
            out_specs=[WHOLE] * 3,
            compiler_params=pltpu.CompilerParams(vmem_limit_bytes=40 * 2**20),
        )(spot, qkv_matrix, square_set, ctx_matrix, ff_in)
    else:
        five = [qkv_matrix[:, k * D : (k + 1) * D] for k in range(3)] + [
            square_set[1],
            jnp.concatenate([ctx_matrix[:, :D], ctx_matrix[:, D:]]),
        ]
        five = jnp.stack(five).astype(BF16).reshape(5, rows, grid.ny, 2, -1)
        five_own = pick(five, core, 3).reshape(5, rows, HALF)
        five_other = pick(five, 1 - core, 3).reshape(5, rows, HALF)
        wide_low = jnp.stack(
            [square_set[k, :, side * HALF : (side + 1) * HALF] for k in (0, 2) for side in range(2)]
        ).astype(BF16)
        in_halves = ff_in.reshape(rows, 2, FF)
        in_blocks = jnp.stack(
            [
                lax.dynamic_slice(in_halves, (0, 0, grid.rank(mine, offset) * width), (rows, 2, width))
                for offset in grid.peers
            ]
        ).astype(BF16).reshape(ranks, rows, 2 * width)
    five_other = grid.swap(five_other)
    if not grouped:
        five_low = jnp.where(core == 0, five_own, five_other)
        five_high = jnp.where(core == 0, five_other, five_own)
    lifted = jax.nn.silu(timestep[0].astype(F32)).astype(BF16)
    notes = jnp.concatenate([lifted, norm_gains.astype(BF16).reshape(-1)])
    if grouped:
        size = notes.shape[0]
        notes = jnp.pad(notes, (0, -size % 2048)).reshape(-1, 128)
        notes = gather_notes(notes, grid.na).reshape(count, -1)[:, :size]
    else:
        notes = grid.gather_small(notes)
    origin = []
    for spot_of in grid.spots:
        source = [
            (mine[axis] - step) % grid.sizes[axis] for axis, step in zip(AXES, spot_of)
        ]
        origin.append(grid.line(*source))
    origin = jnp.stack(origin)
    sorter = (jnp.arange(count)[:, None] == origin[None, :]).astype(BF16)
    gain_rows = dot(sorter, notes[:, D:])
    gain_rows = gain_rows.reshape(count, 3, rows).transpose(1, 0, 2).reshape(3, D)
    lifted_own = lax.dynamic_slice(notes, (0, device * rows), (count, rows))
    shift_terms = dot(lifted_own, mod_matrix.astype(BF16))
    cotangent_own = (cotangent[0].astype(F32) * keep_rows).astype(BF16)
    if grouped:
        shift_terms = shift_terms.reshape(grid.ny, 2, grid.na, grid.nb, 6 * D // 128, 128)
        blocks = in_blocks.reshape(grid.ny, 2, grid.nb, rows, 2 * width)
        shifts, cotangents, in_parts = sum_shifts(shift_terms, cotangent_own, blocks, grid.na)
        in_parts = in_parts.reshape(ranks, rows, 2 * width)
        shifts = shifts.reshape(6, D)
    else:
        shifts = grid.scatter_small(shift_terms).reshape(6, D)
        in_parts = grid.swap_ranks(in_blocks)

    tall = (grid.ny, 2, grid.na, grid.nb, rows)
    wide = (grid.ny, grid.na, grid.nb, rows, D)
    both = lambda k, out, at: [(five_low[k], out, 0, at), (five_high[k], out, 1, at)]
    sides = lambda k, out: [
        (wide_low[2 * k], out, None, 0),
        (wide_low[2 * k + 1], out, None, HALF),
    ]
    stream = latents[0].astype(F32)
    normed_one, inverse_one = norm_rows(stream)
    entry_attn = (normed_one * gain_rows[0] * (1.0 + shifts[1]) + shifts[0]).astype(BF16)
    entry_pair = [entry_attn, grid.swap(entry_attn)]
    pair_lengths = jnp.concatenate([lengths, grid.swap(lengths)])
    columns = HALF // PAIR
    if grouped:
        lines = [lax.all_gather(low_own, "z"), lax.all_gather(five_other, "z")]
        in_lines = lax.all_gather(in_parts.reshape(-1, D), "z")
        down_lines = lax.all_gather(ff_down.astype(BF16), "z")
        (
            mixture_attn, qkv, text_both, kv_cross,
            matrix_qkv, matrix_out, matrix_query, matrix_ctx, matrix_cross,
        ) = gather_group(pair_lengths, *entry_pair, *lines, context[0], grid.swap(context[0]))
        matrix_qkv = matrix_qkv.reshape(D, 3 * HALF)
    else:
        first = both(0, 0, 0) + both(1, 0, HALF) + both(2, 0, 2 * HALF)
        (matrix_qkv,), _ = grid.gather_weights(
            [first[:3], first[3:]], [tall + (3 * HALF,)], mine, spot, ()
        )
        matrix_qkv = matrix_qkv.reshape(D, 3 * HALF)
        (matrix_out, matrix_query), _ = grid.gather_weights(
            [sides(0, 0), both(3, 1, 0)], [wide, tall + (HALF,)], mine, spot, ()
        )
        (matrix_ctx, matrix_cross), _ = grid.gather_weights(
            [both(4, 0, 0), sides(1, 1)], [tall + (HALF,), wide], mine, spot, ()
        )
        down_part = grid.to_rank(ff_down.astype(BF16))
        rank_in, rank_down = grid.gather_ranks(in_parts, down_part, mine, spot)
        qkv = pair_in(*entry_pair, matrix_qkv, dot)
        mixture_attn = attend(pair_lengths, *((qkv, frames, 0, k * columns) for k in range(3)))
        text = jnp.concatenate([context[0], grid.swap(context[0])])
        blank = jnp.zeros((2 * words, count, rows // 2), BF16)
        text_cut = text.reshape(2 * words, count, rows // 2)
        text_key = jnp.concatenate([text_cut, blank], axis=-1).reshape(2 * words, -1)
        text_value = jnp.concatenate([blank, text_cut], axis=-1).reshape(2 * words, -1)
        text_both = jnp.concatenate([text_key, text_value])
        kv_cross = dot(text_both, matrix_ctx.reshape(D, HALF)).astype(BF16)
    matrix_out, matrix_cross = matrix_out.reshape(HALF, D), matrix_cross.reshape(HALF, D)
    matrix_query, matrix_ctx = matrix_query.reshape(D, HALF), matrix_ctx.reshape(D, HALF)

    all_words = jnp.full((2,), words, jnp.int32)
    d_result = cotangent[0].astype(F32) * keep_rows

    self_parts = tuple((qkv, frames, 0, k * columns) for k in range(3))
    own, away = pair_out([mixture_attn], matrix_out, dot)
    branch_attn = own + grid.swap(away).astype(F32)
    after_attn = stream + shifts[2] * branch_attn
    normed_two, inverse_two = norm_rows(after_attn)
    entry_cross = (normed_two * gain_rows[1]).astype(BF16)
    cross_pair = [entry_cross, grid.swap(entry_cross)]
    query_cross = pair_in(*cross_pair, matrix_query, dot)
    cross_parts = ((query_cross, frames, 0, 0), (kv_cross, words, 0, 0), (kv_cross, words, 2, 0))
    mixture_cross = attend(all_words, *cross_parts)
    own, away = pair_out([mixture_cross], matrix_cross, dot)
    branch_cross = own + grid.swap(away).astype(F32)
    after_cross = after_attn + branch_cross
    normed_three, inverse_three = norm_rows(after_cross)
    entry_ffn = (normed_three * gain_rows[2] * (1.0 + shifts[4]) + shifts[3]).astype(BF16)

    notes = gate_notes(shifts[5])
    whole = lambda array: (array, array.shape[1], 0)
    chips = grid.chips
    if grouped:
        d_entry_ffn, grad_down, grad_in, branch_ffn, *_ = ffn_group(
            entry_ffn, notes, cotangent_own, cotangents, in_lines, down_lines,
            chips, grid.peers, (grid.ny, grid.nb),
        )
        grad_in = grad_in.reshape(-1, 2 * width)
    else:
        entry_ext = jnp.concatenate([entry_ffn, notes])
        cot_arrived = [grid.move(cotangent_own, y=y, x=x) for y, x in grid.chips]
        (entry_ext,) = after([entry_ext], cot_arrived[1:])
        arrived = [grid.move(entry_ext, y=y, x=x) for y, x in grid.chips]
        entry_parts, hidden_parts, d_gate_up_parts, d_branch_parts = [], [], [], []
        d_entry_sources, folded_rows, branch_own, branch_away = [], [], [], []
        for k, (y, x) in enumerate(grid.chips):
            own_entry, own_cot = arrived[k], cot_arrived[k]
            if k in (1, 2):
                own_entry, own_cot = after([own_entry, own_cot], hidden_parts[:1])
            elif k > 2:
                own_entry, own_cot = after([own_entry, own_cot], folded_rows[k - 2 : k - 1])
            entries = [own_entry, grid.swap(own_entry)]
            hidden, d_gate_up, d_branch, own, other = ffn_both_ways(
                entries, [own_cot, grid.swap(own_cot)], rank_in, rank_down
            )
            other = grid.swap(other)
            folded_rows.append(total([own[0], other[0]]).astype(BF16))
            if k:
                d_entry_sources.append(grid.move(folded_rows[k], y=-y, x=-x))
                branch_away.append(total([own[1], other[1]]).astype(BF16))
            else:
                d_entry_sources += [own[0], other[0]]
                branch_own += [own[1], other[1]]
            entry_parts += entries
            hidden_parts.append(hidden)
            d_gate_up_parts.append(d_gate_up)
            d_branch_parts.append(d_branch)
        hidden_parts[:1] = after(hidden_parts[:1], folded_rows[-2:-1])
        grad_down = outer_sum(
            hidden_parts, [[whole(a) for a in d_branch_parts]], frames, 256 if width % 256 == 0 else 128
        ).reshape(width, D)
        d_gate_up_parts[:1] = after(d_gate_up_parts[:1], folded_rows[-1:])
        in_group = [[whole(a) for a in d_gate_up_parts]]
        if rows % 16 == 0:
            grad_in = outer_sum(
                entry_parts, in_group, frames, D // (2 * grid.ny), grid.nb * rows
            )
        else:
            grad_in = outer_sum(entry_parts, in_group, frames, D // 4)
            grad_in = grad_in.reshape(2 * grid.ny, grid.na, grid.nb * rows, 2 * width)
            grad_in = jnp.swapaxes(grad_in, 0, 1)
        grad_in = grad_in.reshape(-1, 2 * width)
        d_entry_ffn = total(after(d_entry_sources, (grad_down, grad_in)))
        branch_arrived = [
            grid.move(away, y=-y, x=-x) for away, (y, x) in zip(branch_away, chips[1:])
        ]
        branch_ffn = total(branch_own + branch_arrived)
    grad_in = lax.psum_scatter(grad_in, "z", tiled=True)

    d_gain_ffn = jnp.sum(d_entry_ffn * normed_three * (1.0 + shifts[4]), axis=0)
    d_scale_ffn = jnp.sum(d_entry_ffn * normed_three * gain_rows[2], axis=0)
    d_shift_ffn = jnp.sum(d_entry_ffn, axis=0)
    d_after_cross = d_result + norm_back(
        d_entry_ffn * gain_rows[2] * (1.0 + shifts[4]), normed_three, inverse_three
    )

    def join(own, other):
        lead = own.shape[:-1]
        shape = lead + (grid.ny, 1, D // (2 * grid.ny))
        own, other = own.reshape(shape), other.reshape(shape)
        low = jnp.where(core == 0, own, other)
        high = jnp.where(core == 0, other, own)
        return jnp.concatenate([low, high], axis=-2).reshape(lead + (D,))

    d_branch_cross = d_after_cross.astype(BF16)
    d_cross_pair = [d_branch_cross, grid.swap(d_branch_cross)]
    d_mixture_cross = pair_in(*d_cross_pair, matrix_cross, dot_back)
    d_query_cross, d_key_cross, d_value_cross = attend_back(
        all_words, *cross_parts, d_mixture_cross
    )
    own, away = pair_out([d_query_cross], matrix_query, dot_back)
    d_entry_cross = own + grid.swap(away).astype(F32)
    d_gain_cross = jnp.sum(d_entry_cross * normed_two, axis=0)
    d_after_attn = d_after_cross + norm_back(d_entry_cross * gain_rows[1], normed_two, inverse_two)
    d_branch_attn = (d_after_attn * shifts[2]).astype(BF16)
    d_attn_pair = [d_branch_attn, grid.swap(d_branch_attn)]
    d_gate_attn = jnp.sum(d_after_attn * branch_attn, axis=0)
    d_mixture_attn = pair_in(*d_attn_pair, matrix_out, dot_back)
    d_queries, d_keys, d_values = attend_back(pair_lengths, *self_parts, d_mixture_attn)
    own, away = pair_out([d_queries, d_keys, d_values], matrix_qkv, dot_back)
    d_entry_attn = own + grid.swap(away).astype(F32)
    d_gain_attn = jnp.sum(d_entry_attn * normed_one * (1.0 + shifts[1]), axis=0)
    d_scale_attn = jnp.sum(d_entry_attn * normed_one * gain_rows[0], axis=0)
    d_shift_attn = jnp.sum(d_entry_attn, axis=0)
    d_latents = d_after_attn + norm_back(
        d_entry_attn * gain_rows[0] * (1.0 + shifts[1]), normed_one, inverse_one
    )


    d_gate_ffn = jnp.sum(d_result * branch_ffn, axis=0)
    result = after_cross + shifts[5] * branch_ffn
    branches = (result, shifts[2] * branch_attn, branch_cross, shifts[5] * branch_ffn)
    stream_terms = jnp.stack([jnp.sum(keep_rows * branch * branch) for branch in branches])
    vectors = [
        d_shift_attn,
        d_scale_attn,
        d_gate_attn,
        d_shift_ffn,
        d_scale_ffn,
        d_gate_ffn,
        d_gain_attn,
        d_gain_cross,
        d_gain_ffn,
    ]
    small = stack_vectors(vectors)

    beside = lambda halves: jnp.concatenate([halves[0], halves[1]], axis=1)
    if grouped:
        reduced, small, grad_in, grad_down, _ = reduce_group(
            [
                ("wide", [mixture_cross], d_cross_pair, 0),
                ("tall", cross_pair, [d_query_cross], 1),
                ("tall", [text_both], [d_key_cross, d_value_cross], 0),
                ("wide", [mixture_attn], d_attn_pair, 1),
                ("tall", entry_pair, [d_queries], 0),
                ("tall", entry_pair, [d_keys], 1),
                ("tall", entry_pair, [d_values], 0),
            ],
            small, grad_in.reshape(grid.ny, 2, grid.nb, rows, 2 * width),
            grad_down.reshape(grid.na, -1, D), grid.na, rows,
        )
        small = small.reshape(count, -1, 128)[:, : 9 * D // 128].reshape(count, 9, D)
        grad_cross, grad_out = beside(reduced[0]), beside(reduced[3])
        grad_query, grad_ctx = (join(reduced[k, 0], reduced[k, 1]) for k in (1, 2))
        qkv_parts = [reduced[4:, 0], reduced[4:, 1]]
        turn_width = D // (2 * grid.ny)
    else:
        grad_down = lax.psum_scatter(grad_down, "z", tiled=True)
        grad_down = grid.to_rank(grad_down, back=True)
        grad_in = grid.swap_back(grad_in.reshape(grid.ny, 2, grid.nb, rows, 2 * width), mine)
        grad_in = grid.join_columns(grad_in, mine, spot)
        small = grid.gather_small(small[: 9 * D // 128].reshape(9, D))
        block = D // (2 * grid.ny)

        def reduce(lefts, right, piece, halves=1):
            groups = [[whole(array) for array in right]]
            gradient = outer_sum(lefts, groups, piece, block, None, halves)
            gradient = grid.fold(gradient.reshape(tall + (-1,)), "yczx", 0, mine)
            return lax.psum_scatter(jnp.swapaxes(gradient, 0, 1), "z")

        def reduce_tall(lefts, right, piece):
            sums = reduce(lefts, right, piece)
            return join(pick(sums, core, 0), grid.swap(pick(sums, 1 - core, 0)))

        grad_cross = beside(reduce([mixture_cross], d_cross_pair, frames, 2))
        grad_out = beside(reduce([mixture_attn], d_attn_pair, frames, 2))
        grad_query = reduce_tall(cross_pair, [d_query_cross], frames)
        grad_ctx = reduce_tall([text_both], [d_key_cross, d_value_cross], 2 * words)
        qkv_parts = [
            jnp.concatenate(
                [reduce_tall(entry_pair, [d], frames) for d in (d_queries, d_keys, d_values)],
                axis=1,
            )
        ]
        turn_width = D
    grad_ctx = jnp.concatenate([grad_ctx[: rows // 2], grad_ctx[rows // 2 :]], axis=1)
    grad_square = jnp.stack([grad_out, grad_query, grad_cross])
    grad_mod = jnp.einsum("nd,nkm->kdm", lifted_own, small[:, :6], preferred_element_type=F32)
    gain_sums = jnp.sum(small[:, 6:].astype(F32), axis=0)
    grad_gains = lax.dynamic_slice(gain_sums, (0, device * rows), (3, rows))
    lamb = functools.partial(lamb_terms, spot)
    done = {}
    done["qkv"] = lamb(qkv_matrix, qkv_first, qkv_second, qkv_parts, turn_width)
    done["mod"] = lamb(mod_matrix, mod_first, mod_second, [grad_mod], D)
    done["square"] = lamb(square_set, square_first, square_second, [grad_square], HALF)
    done["ctx"] = lamb(ctx_matrix, ctx_first, ctx_second, [grad_ctx], D)
    done["down"] = lamb(ff_down, down_first, down_second, [grad_down], 256)
    done["in"] = lamb(ff_in, in_first, in_second, [grad_in], 1024)
    done["gains"] = lamb_small(norm_gains, gains_first, gains_second, grad_gains)
    names = ("mod", "qkv", "square", "ctx", "in", "down", "gains")
    sums = [done[name][3] for name in names]
    sums.append(jnp.stack([stream_terms, jnp.sum(lengths) * jnp.ones(4)]).T)
    sums = jnp.concatenate(sums)
    if grouped:
        wanted = sums.shape
        sums = jnp.pad(sums, ((0, -wanted[0] % 8), (0, 128 - wanted[1])))
        sums = total_over_devices(sums, grid.na)[: wanted[0], : wanted[1]]
    else:
        sums = grid.sum_small(sums)
    norms = jnp.sqrt(sums[:9])
    weight_norms, update_norms = norms[:, 0], norms[:, 1]
    stream_rms = jnp.sqrt(sums[9:, 0] / (sums[9:, 1] * D))
    factors = RATE * (weight_norms / update_norms)
    masters = [mod_matrix, qkv_matrix, square_set, ctx_matrix, ff_in, ff_down, norm_gains]
    weights_new = step_weights(factors, masters, [done[name][2] for name in names])
    outputs = [result.astype(BF16)[None], d_latents.astype(BF16)[None]]
    for name, weight_new in zip(names, weights_new):
        outputs += [weight_new, done[name][0], done[name][1]]
    outputs.append(weight_norms)
    outputs.append(update_norms)
    outputs.append(stream_rms)
    return tuple(outputs)


def solution(mesh):
    grid = Grid(mesh)
    clip = P(AXES, None, None)
    row = P(AXES, None)
    square = P(None, AXES, None)
    gains = P(None, AXES)
    weights = (row,) * 6 + (square,) * 3 + (row,) * 9 + (gains,) * 3
    in_specs = (clip, clip, row, P(AXES), clip) + weights
    out_specs = (clip, clip) + weights + (P(), P(), P())
    return jax.shard_map(
        functools.partial(shards, grid),
        mesh=grid.mesh,
        in_specs=in_specs,
        out_specs=out_specs,
        check_vma=False,
    )
```
